32 devices in a mesh: head: 4 (over y, x), tok: 8 (over z, core).
Axes of the slice: x: 2, y: 2, z: 4, core: 2. Of those that a mesh axis runs over, the one named last changes fastest.
Arguments:
- query_input: bfloat16 [2048, 2048], P('tok', 'head'), may hold values from -6 to 6
- key_input: bfloat16 [2048, 2048], P('tok', 'head'), may hold values from -6 to 6
- value_input: bfloat16 [2048, 2048], P('tok', 'head'), may hold values from -6 to 6
- out_grad: bfloat16 [2048, 2048], P('tok', 'head'), may hold values from -0.890625 to 0.890625
- token_rates: float32 [2048, 4], P('tok', 'head'), may hold values from 0.00088388345 to 0.008838835
- out_gain: float32 [2048], P('head'), may hold values from 0.1 to 1.9
- gate_prior: bfloat16 [4, 512, 256], P('head'), may hold values from -0.8242256 to 0.8242256
- up_prior: bfloat16 [4, 512, 256], P('head'), may hold values from -0.8242256 to 0.8242256
- down_prior: bfloat16 [4, 256, 512], P('head'), may hold values from -3.496893 to 3.496893
Outputs:
- query_grad: bfloat16 [2048, 2048], P('tok', 'head')
- key_grad: bfloat16 [2048, 2048], P('tok', 'head')
- value_grad: bfloat16 [2048, 2048], P('tok', 'head')
- gate_prior_grad: float32 [4, 512, 256], P('head', None, 'tok')
- up_prior_grad: float32 [4, 512, 256], P('head', None, 'tok')
- down_prior_grad: float32 [4, 256, 512], P('head', None, 'tok')
The draws below stay inside these ranges and needn't reach their ends.
All inputs are finite; a program needn't handle non-finite values.
Results may differ from the reference program's by a relative error of at most 0.014.
Values may be sent and summed in bfloat16 or wider, within the bound.
No kernel may reach another device: no remote copies, remote signals or barrier semaphores. Data moves between devices by JAX's collectives and lax.ppermute only.
A program may use at most 64 MiB of HBM per device.

```python
import math
import jax
import jax.numpy as jnp
from jax import lax

DH = 512
FH = 256
HEADS = 4
WIDTH = 2048
TOKENS = 2048


def scaled_weight(base_key, row_count, col_count, fan_in, head_rise):
    draw_key, row_key, col_key = jax.random.split(base_key, 3)
    base_draw = jnp.clip(jax.random.normal(draw_key, (HEADS, row_count, col_count), jnp.float32), -4.0, 4.0)
    row_scale = jnp.exp(jax.random.uniform(row_key, (HEADS, row_count, 1), jnp.float32, -1.15, 1.15))
    col_scale = jnp.exp(jax.random.uniform(col_key, (HEADS, 1, col_count), jnp.float32, -1.15, 1.15))
    head_scale = head_rise ** (jnp.arange(HEADS, dtype=jnp.float32) / max(HEADS - 1, 1))
    return base_draw * row_scale * col_scale * head_scale[:, None, None] / jnp.sqrt(4.6 * fan_in)


def draw_gate_prior(key, part):
    return scaled_weight(jax.random.fold_in(key, 101), DH, FH, DH, 1.0).astype(jnp.bfloat16)


def draw_up_prior(key, part):
    return scaled_weight(jax.random.fold_in(key, 202), DH, FH, DH, 1.0).astype(jnp.bfloat16)


def draw_down_prior(key, part):
    return scaled_weight(jax.random.fold_in(key, 303), FH, DH, FH, 3.0).astype(jnp.bfloat16)


def levels(stream_key, dims, pieces, low, top_value):
    level, own = 1.0, jax.random.fold_in(stream_key, 6)
    for axis_at, parts in pieces:
        draws = jnp.exp(jax.random.uniform(jax.random.fold_in(own, axis_at), (parts,), jnp.float32, low / len(pieces), top_value / len(pieces)))
        level = level * jnp.repeat(draws, dims[axis_at] // parts).reshape([-1 if axis == axis_at else 1 for axis in range(len(dims))])
    return level


def normal_values(rng, dims, spread, reach, shards=(), held_as=jnp.bfloat16):
    array = jax.random.normal(rng, dims, jnp.float32) * spread
    if len(shards) > 0:
        array = levels(rng, dims, shards, -0.22, 0.18) * array
    return jnp.clip(array, min=-reach, max=reach).astype(held_as)


def setup_inputs(seed: int = 0) -> dict:
    keys = jax.random.split(jax.random.key(seed), 10)
    return {
        "query_input": normal_values(keys[0], (TOKENS, WIDTH), 1.0, 6.0, ((0, 8), (1, 4))),
        "key_input": normal_values(keys[1], (TOKENS, WIDTH), 1.0, 6.0, ((0, 8), (1, 4))),
        "value_input": normal_values(keys[2], (TOKENS, WIDTH), 1.0, 6.0, ((0, 8), (1, 4))),
        "out_grad": normal_values(keys[3], (TOKENS, WIDTH), (TOKENS ** -0.25), 0.890625, ((0, 8), (1, 4))),
        "token_rates": jnp.clip(jnp.exp(math.log(0.008838835) - 2.3025852 * jax.random.uniform(keys[4], (TOKENS, HEADS), jnp.float32) ** levels(keys[4], (TOKENS, HEADS), ((0, 8), (1, 4)), -0.2, 0.2)), 0.00088388345, 0.008838835),
        "out_gain": jnp.clip(1.0 + 0.18 * jax.random.normal(keys[5], (WIDTH,), jnp.float32), 0.1, 1.9),
        "gate_prior": draw_gate_prior(jax.random.fold_in(keys[9], 71), 0),
        "up_prior": draw_up_prior(jax.random.fold_in(keys[9], 71), 0),
        "down_prior": draw_down_prior(jax.random.fold_in(keys[9], 71), 0),
    }


EPSILON = 1e-06

def matmul(first_op, second_op):
    return jnp.dot(first_op, second_op, preferred_element_type=jnp.float32)

def contract_rows(first_op, second_op):
    return lax.dot_general(first_op, second_op, (((0,), (0,)), ((), ())), preferred_element_type=jnp.float32)

def contract_cols(first_op, second_op):
    return lax.dot_general(first_op, second_op, (((1,), (1,)), ((), ())), preferred_element_type=jnp.float32)

def silu_parts(hidden):
    sigmoid_value = jax.nn.sigmoid(hidden)
    silu_value = hidden * sigmoid_value
    silu_slope = sigmoid_value * (1.0 + hidden * (1.0 - sigmoid_value))
    curvature = sigmoid_value * (1.0 - sigmoid_value) * (2.0 + hidden * (1.0 - 2.0 * sigmoid_value))
    return (silu_value, silu_slope, curvature)

def update_forward(key_head, value_head, rate_head, priors):
    gate_weight, up_weight, down_weight = priors
    gate_pre = matmul(key_head, gate_weight)
    up_pre = matmul(key_head, up_weight)
    silu_value, silu_slope, curvature = silu_parts(gate_pre)
    mixed_act = (silu_value * up_pre).astype(jnp.bfloat16)
    value_push = (-rate_head[:, None] * value_head.astype(jnp.float32)).astype(jnp.bfloat16)
    down_update = contract_rows(mixed_act, value_push)
    down_back = contract_cols(value_push, down_weight)
    gate_back = (down_back * up_pre * silu_slope).astype(jnp.bfloat16)
    up_back = (down_back * silu_value).astype(jnp.bfloat16)
    gate_update = contract_rows(key_head, gate_back)
    up_update = contract_rows(key_head, up_back)
    update_saved = (up_pre, silu_value, silu_slope, curvature, mixed_act, value_push, down_back, gate_back, up_back)
    return ((gate_update, up_update, down_update), update_saved)

def renormalize(prior, update):
    prior_f = prior.astype(jnp.float32)
    moved_weight = prior_f - update
    prior_norm = jnp.sqrt(lax.optimization_barrier(jnp.sum(prior_f * prior_f, axis=0)) + EPSILON)
    moved_norm = jnp.sqrt(lax.optimization_barrier(jnp.sum(moved_weight * moved_weight, axis=0)) + EPSILON)
    return (moved_weight, prior_norm, moved_norm)

def apply_forward(query_head, fast_weights):
    gate_pre = matmul(query_head, fast_weights[0])
    up_pre = matmul(query_head, fast_weights[1])
    silu_value, silu_slope, curvature = silu_parts(gate_pre)
    mixed_act = (silu_value * up_pre).astype(jnp.bfloat16)
    output = matmul(mixed_act, fast_weights[2])
    return (output, (up_pre, silu_value, silu_slope, mixed_act))

def apply_backward(query_head, fast_weights, apply_saved, out_back):
    up_pre, silu_value, silu_slope, mixed_act = apply_saved
    down_grad = contract_rows(mixed_act, out_back)
    mixed_back = contract_cols(out_back, fast_weights[2])
    gate_back = (mixed_back * up_pre * silu_slope).astype(jnp.bfloat16)
    up_back = (mixed_back * silu_value).astype(jnp.bfloat16)
    gate_grad = contract_rows(query_head, gate_back)
    up_grad = contract_rows(query_head, up_back)
    query_back = (contract_cols(gate_back, fast_weights[0]) + contract_cols(up_back, fast_weights[1])).astype(jnp.bfloat16)
    return ((gate_grad, up_grad, down_grad), query_back)

def norm_adjoint(prior, moved_weight, prior_norm, moved_norm, fast_grad, column_dot):
    moved_grad = prior_norm / moved_norm * (fast_grad - moved_weight * (column_dot / (moved_norm * moved_norm)))
    direct = prior.astype(jnp.float32) * (column_dot / (moved_norm * prior_norm))
    return (moved_grad, direct)

def second_adjoint(key_head, rate_head, priors, update_saved, cotangent):
    gate_weight, up_weight, down_weight = priors
    up_pre, silu_value, silu_slope, curvature, mixed_act, value_push, down_back, gate_back, up_back = update_saved
    gate_cot, up_cot, down_cot = cotangent
    gate_bar = matmul(key_head, gate_cot)
    up_bar = matmul(key_head, up_cot)
    mixed_bar = contract_cols(value_push, down_cot)
    push_bar = matmul(mixed_act, down_cot)
    down_back_bar = (gate_bar * up_pre * silu_slope + up_bar * silu_value).astype(jnp.bfloat16)
    up_pre_bar = (gate_bar * down_back * silu_slope + mixed_bar * silu_value).astype(jnp.bfloat16)
    gate_pre_bar = ((up_bar * down_back + mixed_bar * up_pre) * silu_slope + gate_bar * down_back * up_pre * curvature).astype(jnp.bfloat16)
    down_prior_bar = contract_rows(down_back_bar, value_push)
    gate_prior_bar = contract_rows(key_head, gate_pre_bar)
    up_prior_bar = contract_rows(key_head, up_pre_bar)
    value_grad = (rate_head[:, None] * (push_bar + matmul(down_back_bar, down_weight))).astype(jnp.bfloat16)
    key_total = contract_cols(gate_back, gate_cot) + contract_cols(up_back, up_cot) + contract_cols(gate_pre_bar, gate_weight) + contract_cols(up_pre_bar, up_weight)
    key_grad = (-key_total).astype(jnp.bfloat16)
    return ((gate_prior_bar, up_prior_bar, down_prior_bar), key_grad, value_grad)

def reference(query_input, key_input, value_input, out_grad, token_rates, out_gain, gate_prior, up_prior, down_prior):
    head_states = []
    outputs = []
    for head_index in range(HEADS):
        lower = head_index * DH
        key_head = key_input[:, lower:lower + DH]
        value_head = value_input[:, lower:lower + DH]
        query_head = query_input[:, lower:lower + DH]
        rate_head = token_rates[:, head_index]
        priors = (gate_prior[head_index], up_prior[head_index], down_prior[head_index])
        updates, update_saved = update_forward(key_head, value_head, rate_head, priors)
        renormed = [renormalize(priors[matrix_index], updates[matrix_index]) for matrix_index in range(3)]
        fast_weights = tuple(((moved_weight * (prior_norm / moved_norm)).astype(jnp.bfloat16) for moved_weight, prior_norm, moved_norm in renormed))
        output, apply_saved = apply_forward(query_head, fast_weights)
        outputs.append(output)
        head_states.append((key_head, query_head, rate_head, priors, update_saved, renormed, fast_weights, apply_saved))
    output_all = jnp.concatenate(outputs, axis=1)
    gain_weighted = out_grad.astype(jnp.float32) * out_gain
    square_sum = lax.optimization_barrier(jnp.sum(output_all * output_all, axis=1))
    dot_sum = lax.optimization_barrier(jnp.sum(gain_weighted * output_all, axis=1))
    inverse = lax.rsqrt(square_sum / WIDTH + EPSILON)
    out_back_all = (inverse[:, None] * gain_weighted - output_all * (inverse * inverse * inverse * dot_sum / WIDTH)[:, None]).astype(jnp.bfloat16)
    query_grads, key_grads, value_grads = ([], [], [])
    gate_grads, up_grads, down_grads = ([], [], [])
    for head_index in range(HEADS):
        key_head, query_head, rate_head, priors, update_saved, renormed, fast_weights, apply_saved = head_states[head_index]
        lower = head_index * DH
        fast_grads, query_back = apply_backward(query_head, fast_weights, apply_saved, out_back_all[:, lower:lower + DH])
        cotangent = []
        global_parts = []
        for matrix_index in range(3):
            moved_weight, prior_norm, moved_norm = renormed[matrix_index]
            column_dot = lax.optimization_barrier(jnp.sum(fast_grads[matrix_index] * moved_weight, axis=0))
            moved_grad, direct = norm_adjoint(priors[matrix_index], moved_weight, prior_norm, moved_norm, fast_grads[matrix_index], column_dot)
            cotangent.append(moved_grad.astype(jnp.bfloat16))
            global_parts.append(moved_grad + direct)
        prior_bars, key_grad, value_grad = second_adjoint(key_head, rate_head, priors, update_saved, tuple(cotangent))
        query_grads.append(query_back)
        key_grads.append(key_grad)
        value_grads.append(value_grad)
        gate_grads.append(global_parts[0] - prior_bars[0])
        up_grads.append(global_parts[1] - prior_bars[1])
        down_grads.append(global_parts[2] - prior_bars[2])
    return (jnp.concatenate(query_grads, axis=1), jnp.concatenate(key_grads, axis=1), jnp.concatenate(value_grads, axis=1), jnp.stack(gate_grads), jnp.stack(up_grads), jnp.stack(down_grads))
```

```python
import jax
import jax.numpy as jnp
from jax import lax
from jax.sharding import PartitionSpec as P

EPSILON = 1e-06
CORES = 2


def nn(a, b):
    return lax.dot_general(a, b, (((1,), (0,)), ((), ())), preferred_element_type=jnp.float32)


def nt(a, b):
    return lax.dot_general(a, b, (((1,), (1,)), ((), ())), preferred_element_type=jnp.float32)


def tn(a, b):
    return lax.dot_general(a, b, (((0,), (0,)), ((), ())), preferred_element_type=jnp.float32)


def silu_parts(hidden):
    sigmoid_value = jax.nn.sigmoid(hidden)
    silu_value = hidden * sigmoid_value
    silu_slope = sigmoid_value * (1.0 + hidden * (1.0 - sigmoid_value))
    curvature = sigmoid_value * (1.0 - sigmoid_value) * (2.0 + hidden * (1.0 - 2.0 * sigmoid_value))
    return silu_value, silu_slope, curvature


def chip_perm(count, shift):
    chips = count // CORES
    return [(t, ((t // CORES + shift) % chips) * CORES + t % CORES) for t in range(count)]


def core_perm(count):
    return [(t, t ^ 1) for t in range(count)]


def pack(gate, up, down):
    folds = gate.shape[1] // down.shape[1]
    rows = down.shape[0] // folds
    down = jnp.concatenate([down[i * rows : (i + 1) * rows] for i in range(folds)], axis=1)
    return jnp.concatenate([gate, up, down], axis=0)


def unpack(packed, fh):
    g = packed.shape[0] // 3
    folds = packed.shape[1] // fh
    down = packed[2 * g :]
    down = jnp.concatenate([down[:, i * fh : (i + 1) * fh] for i in range(folds)], axis=0)
    return packed[:g], packed[g : 2 * g], down


def scatter_sum(gate, up, down, tok):
    count = lax.axis_size("tok")
    chips = count // CORES
    chip, core = tok // CORES, tok % CORES
    g, d = gate.shape[0] // count, down.shape[0] // count

    def piece(shift):
        t = lax.rem(chip + shift, chips) * CORES + core
        return pack(
            lax.dynamic_slice_in_dim(gate, t * g, g, 0),
            lax.dynamic_slice_in_dim(up, t * g, g, 0),
            lax.dynamic_slice_in_dim(down, t * d, d, 0),
        )

    total = piece(0)
    for shift in range(1, chips):
        sent = piece(shift).astype(jnp.bfloat16)
        total = total + lax.ppermute(sent, "tok", chip_perm(count, shift)).astype(jnp.float32)
    return total


def gather(packed, tok, fh):
    count = lax.axis_size("tok")
    chips = count // CORES
    chip, core = tok // CORES, tok % CORES
    held = jnp.zeros((count,) + packed.shape, packed.dtype)
    for shift in range(chips):
        mine = packed if shift == 0 else lax.ppermute(packed, "tok", chip_perm(count, shift))
        other = lax.ppermute(mine, "tok", core_perm(count))
        source = lax.rem(chip + chips - shift, chips) * CORES
        held = lax.dynamic_update_index_in_dim(held, mine, source + core, 0)
        held = lax.dynamic_update_index_in_dim(held, other, source + 1 - core, 0)
    gate, up, down = jax.vmap(lambda x: unpack(x, fh))(held)
    return tuple(x.reshape((-1, x.shape[-1])) for x in (gate, up, down))


def norm_of(rows):
    return jnp.sqrt(jnp.sum(rows * rows, axis=1, keepdims=True) + EPSILON)


def per_device(
    query_input,
    key_input,
    value_input,
    out_grad,
    token_rates,
    out_gain,
    gate_prior,
    up_prior,
    down_prior,
):
    count = lax.axis_size("tok")
    tok = lax.axis_index("tok")
    own = key_input.shape[0]
    w1t, w3t, w2 = gate_prior[0].T, up_prior[0].T, down_prior[0]
    fh = w2.shape[0]
    g, d = fh // count, w2.shape[1] // count
    rates = token_rates.T

    pair = lambda x: lax.ppermute(x, "tok", core_perm(count))
    keys = jnp.concatenate([key_input, pair(key_input)], axis=0)
    values = jnp.concatenate([value_input, pair(value_input)], axis=0)
    rate = jnp.concatenate([rates, pair(rates)], axis=1)
    queries = jnp.concatenate([query_input, pair(query_input)], axis=0)
    grads = jnp.concatenate([out_grad, pair(out_grad)], axis=0)

    gate_pre, up_pre = nt(w1t, keys), nt(w3t, keys)
    silu_value, silu_slope, curvature = silu_parts(gate_pre)
    mixed = (silu_value * up_pre).astype(jnp.bfloat16)
    push = (-rate * values.T.astype(jnp.float32)).astype(jnp.bfloat16)
    down_update = nt(push, mixed)
    down_back = nn(w2, push)
    gate_back = (down_back * up_pre * silu_slope).astype(jnp.bfloat16)
    up_back = (down_back * silu_value).astype(jnp.bfloat16)
    update = unpack(scatter_sum(nn(gate_back, keys), nn(up_back, keys), down_update, tok), fh)

    priors = [
        lax.dynamic_slice_in_dim(x, tok * n, n, 0).astype(jnp.float32)
        for x, n in ((w1t, g), (w3t, g), (w2.T, d))
    ]
    moved = [p - u for p, u in zip(priors, update)]
    prior_norm = [norm_of(p) for p in priors]
    moved_norm = [norm_of(m) for m in moved]
    fast = [
        (m * (p / n)).astype(jnp.bfloat16) for m, p, n in zip(moved, prior_norm, moved_norm)
    ]
    f1t, f3t, f2t = gather(pack(*fast), tok, fh)

    q_gate, q_up = nt(f1t, queries), nt(f3t, queries)
    q_silu, q_slope, _ = silu_parts(q_gate)
    q_mixed = (q_silu * q_up).astype(jnp.bfloat16)
    output = nn(f2t, q_mixed)
    weighted = grads.T.astype(jnp.float32) * out_gain[:, None]
    sums = lax.psum(
        jnp.stack([jnp.sum(output * output, axis=0), jnp.sum(weighted * output, axis=0)]), "head"
    )
    full_width = lax.axis_size("head") * output.shape[0]
    inverse = lax.rsqrt(sums[0:1] / full_width + EPSILON)
    out_back = (
        inverse * weighted - output * (inverse * inverse * inverse * sums[1:2] / full_width)
    ).astype(jnp.bfloat16)
    q_back = tn(f2t, out_back)
    q_gate_back = (q_back * q_up * q_slope).astype(jnp.bfloat16)
    q_up_back = (q_back * q_silu).astype(jnp.bfloat16)
    fast_grad = unpack(
        scatter_sum(nn(q_gate_back, queries), nn(q_up_back, queries), nt(out_back, q_mixed), tok),
        fh,
    )
    query_grad = (tn(q_gate_back[:, :own], f1t) + tn(q_up_back[:, :own], f3t)).astype(jnp.bfloat16)

    cotangent, owned = [], []
    for p, m, pn, mn, fg in zip(priors, moved, prior_norm, moved_norm, fast_grad):
        column_dot = jnp.sum(fg * m, axis=1, keepdims=True)
        moved_grad = pn / mn * (fg - m * (column_dot / (mn * mn)))
        cotangent.append(moved_grad.astype(jnp.bfloat16))
        owned.append(moved_grad + p * (column_dot / (mn * pn)))
    c1t, c3t, c2t = gather(pack(*cotangent), tok, fh)

    gate_bar, up_bar, mixed_bar = nt(c1t, keys), nt(c3t, keys), tn(c2t, push)
    down_back_bar = (gate_bar * up_pre * silu_slope + up_bar * silu_value).astype(jnp.bfloat16)
    up_pre_bar = (gate_bar * down_back * silu_slope + mixed_bar * silu_value).astype(jnp.bfloat16)
    gate_pre_bar = (
        (up_bar * down_back + mixed_bar * up_pre) * silu_slope
        + gate_bar * down_back * up_pre * curvature
    ).astype(jnp.bfloat16)
    bars = unpack(
        scatter_sum(nn(gate_pre_bar, keys), nn(up_pre_bar, keys), nt(push, down_back_bar), tok), fh
    )
    value_grad = (
        rates * (nn(c2t, mixed[:, :own]) + tn(w2, down_back_bar[:, :own]))
    ).astype(jnp.bfloat16).T
    key_grad = (
        -(
            tn(gate_back[:, :own], c1t)
            + tn(up_back[:, :own], c3t)
            + tn(gate_pre_bar[:, :own], w1t)
            + tn(up_pre_bar[:, :own], w3t)
        )
    ).astype(jnp.bfloat16)
    results = [(o - b).T[None] for o, b in zip(owned, bars)]
    return (query_grad, key_grad, value_grad, *results)


def solution(mesh):
    tokens = P("tok", "head")
    in_specs = (tokens,) * 5 + (P("head"),) + (P("head", None, None),) * 3
    out_specs = (tokens,) * 3 + (P("head", None, "tok"),) * 3
    return jax.shard_map(
        per_device, mesh=mesh, in_specs=in_specs, out_specs=out_specs, check_vma=False
    )
```

```python
import jax
import jax.numpy as jnp
from jax import lax
from jax.sharding import PartitionSpec as P

EPSILON = 1e-06
CORES = 2


def nn(a, b):
    return lax.dot_general(a, b, (((1,), (0,)), ((), ())), preferred_element_type=jnp.float32)


def nt(a, b):
    return lax.dot_general(a, b, (((1,), (1,)), ((), ())), preferred_element_type=jnp.float32)


def tn(a, b):
    return lax.dot_general(a, b, (((0,), (0,)), ((), ())), preferred_element_type=jnp.float32)


def silu_parts(hidden):
    sigmoid_value = jax.nn.sigmoid(hidden)
    silu_value = hidden * sigmoid_value
    silu_slope = sigmoid_value * (1.0 + hidden * (1.0 - sigmoid_value))
    curvature = sigmoid_value * (1.0 - sigmoid_value) * (2.0 + hidden * (1.0 - 2.0 * sigmoid_value))
    return silu_value, silu_slope, curvature


def partner(index, step, count):
    return index ^ step if count & (count - 1) == 0 else (index + step) % count


def source(index, step, count):
    return index ^ step if count & (count - 1) == 0 else (index + count - step) % count


def chip_perm(count, step):
    chips = count // CORES
    return [(t, partner(t // CORES, step, chips) * CORES + t % CORES) for t in range(count)]


def core_perm(count):
    return [(t, t ^ 1) for t in range(count)]


def pack(gate, up, down):
    folds = gate.shape[1] // down.shape[1]
    rows = down.shape[0] // folds
    down = jnp.concatenate([down[i * rows : (i + 1) * rows] for i in range(folds)], axis=1)
    return jnp.concatenate([gate, up, down], axis=0)


def unpack(packed, fh):
    g = packed.shape[0] // 3
    folds = packed.shape[1] // fh
    down = packed[2 * g :]
    down = jnp.concatenate([down[:, i * fh : (i + 1) * fh] for i in range(folds)], axis=0)
    return packed[:g], packed[g : 2 * g], down


def scatter_sum(gate, up, down, tok):
    count = lax.axis_size("tok")
    chips = count // CORES
    chip, core = tok // CORES, tok % CORES
    g, d = gate.shape[0] // count, down.shape[0] // count

    def piece(shift):
        t = partner(chip, shift, chips) * CORES + core
        return pack(
            lax.dynamic_slice_in_dim(gate, t * g, g, 0),
            lax.dynamic_slice_in_dim(up, t * g, g, 0),
            lax.dynamic_slice_in_dim(down, t * d, d, 0),
        )

    total = piece(0)
    for shift in reversed(range(1, chips)):
        sent = piece(shift).astype(jnp.bfloat16)
        total = total + lax.ppermute(sent, "tok", chip_perm(count, shift)).astype(jnp.float32)
    return total


def gather(packed, tok, fh):
    count = lax.axis_size("tok")
    chips = count // CORES
    chip, core = tok // CORES, tok % CORES
    held = jnp.zeros((count,) + packed.shape, packed.dtype)
    for shift in (0, *reversed(range(1, chips))):
        mine = packed if shift == 0 else lax.ppermute(packed, "tok", chip_perm(count, shift))
        other = lax.ppermute(mine, "tok", core_perm(count))
        origin = source(chip, shift, chips) * CORES
        held = lax.dynamic_update_index_in_dim(held, mine, origin + core, 0)
        held = lax.dynamic_update_index_in_dim(held, other, origin + 1 - core, 0)
    gate, up, down = jax.vmap(lambda x: unpack(x, fh))(held)
    return tuple(x.reshape((-1, x.shape[-1])) for x in (gate, up, down))


def norm_of(rows):
    return jnp.sqrt(jnp.sum(rows * rows, axis=1, keepdims=True) + EPSILON)


def per_device(
    query_input,
    key_input,
    value_input,
    out_grad,
    token_rates,
    out_gain,
    gate_prior,
    up_prior,
    down_prior,
):
    count = lax.axis_size("tok")
    tok = lax.axis_index("tok")
    own = key_input.shape[0]
    w1t, w3t, w2 = gate_prior[0].T, up_prior[0].T, down_prior[0]
    fh = w2.shape[0]
    g, d = fh // count, w2.shape[1] // count
    rates = token_rates.T

    pair = lambda x: lax.ppermute(x, "tok", core_perm(count))
    keys = jnp.concatenate([key_input, pair(key_input)], axis=0)
    values = jnp.concatenate([value_input, pair(value_input)], axis=0)
    rate = jnp.concatenate([rates, pair(rates)], axis=1)
    queries = jnp.concatenate([query_input, pair(query_input)], axis=0)
    grads = jnp.concatenate([out_grad, pair(out_grad)], axis=0)

    gate_pre, up_pre = nt(w1t, keys), nt(w3t, keys)
    silu_value, silu_slope, curvature = silu_parts(gate_pre)
    mixed = (silu_value * up_pre).astype(jnp.bfloat16)
    push = (-rate * values.T.astype(jnp.float32)).astype(jnp.bfloat16)
    down_update = nt(push, mixed)
    down_back = nn(w2, push)
    gate_back = (down_back * up_pre * silu_slope).astype(jnp.bfloat16)
    up_back = (down_back * silu_value).astype(jnp.bfloat16)
    update = unpack(scatter_sum(nn(gate_back, keys), nn(up_back, keys), down_update, tok), fh)

    priors = [
        lax.dynamic_slice_in_dim(x, tok * n, n, 0).astype(jnp.float32)
        for x, n in ((w1t, g), (w3t, g), (w2.T, d))
    ]
    moved = [p - u for p, u in zip(priors, update)]
    prior_norm = [norm_of(p) for p in priors]
    moved_norm = [norm_of(m) for m in moved]
    fast = [
        (m * (p / n)).astype(jnp.bfloat16) for m, p, n in zip(moved, prior_norm, moved_norm)
    ]
    f1t, f3t, f2t = gather(pack(*fast), tok, fh)

    q_gate, q_up = nt(f1t, queries), nt(f3t, queries)
    q_silu, q_slope, _ = silu_parts(q_gate)
    q_mixed = (q_silu * q_up).astype(jnp.bfloat16)
    output = nn(f2t, q_mixed)
    weighted = grads.T.astype(jnp.float32) * out_gain[:, None]
    part = jnp.stack([jnp.sum(output * output, axis=0), jnp.sum(weighted * output, axis=0)])
    heads = lax.axis_size("head")
    sums = part
    for step in range(1, heads):
        perm = [(h, partner(h, step, heads)) for h in range(heads)]
        sums = sums + lax.ppermute(part, "head", perm)
    full_width = heads * output.shape[0]
    inverse = lax.rsqrt(sums[0:1] / full_width + EPSILON)
    out_back = (
        inverse * weighted - output * (inverse * inverse * inverse * sums[1:2] / full_width)
    ).astype(jnp.bfloat16)
    q_back = tn(f2t, out_back)
    q_gate_back = (q_back * q_up * q_slope).astype(jnp.bfloat16)
    q_up_back = (q_back * q_silu).astype(jnp.bfloat16)
    fast_grad = unpack(
        scatter_sum(nn(q_gate_back, queries), nn(q_up_back, queries), nt(out_back, q_mixed), tok),
        fh,
    )
    query_grad = (tn(q_gate_back[:, :own], f1t) + tn(q_up_back[:, :own], f3t)).astype(jnp.bfloat16)

    cotangent, owned = [], []
    for p, m, pn, mn, fg in zip(priors, moved, prior_norm, moved_norm, fast_grad):
        column_dot = jnp.sum(fg * m, axis=1, keepdims=True)
        moved_grad = pn / mn * (fg - m * (column_dot / (mn * mn)))
        cotangent.append(moved_grad.astype(jnp.bfloat16))
        owned.append(moved_grad + p * (column_dot / (mn * pn)))
    c1t, c3t, c2t = gather(pack(*cotangent), tok, fh)

    gate_bar, up_bar, mixed_bar = nt(c1t, keys), nt(c3t, keys), tn(c2t, push)
    down_back_bar = (gate_bar * up_pre * silu_slope + up_bar * silu_value).astype(jnp.bfloat16)
    up_pre_bar = (gate_bar * down_back * silu_slope + mixed_bar * silu_value).astype(jnp.bfloat16)
    gate_pre_bar = (
        (up_bar * down_back + mixed_bar * up_pre) * silu_slope
        + gate_bar * down_back * up_pre * curvature
    ).astype(jnp.bfloat16)
    bars = unpack(
        scatter_sum(nn(gate_pre_bar, keys), nn(up_pre_bar, keys), nt(push, down_back_bar), tok), fh
    )
    value_grad = (
        rates * (nn(c2t, mixed[:, :own]) + tn(w2, down_back_bar[:, :own]))
    ).astype(jnp.bfloat16).T
    key_grad = (
        -(
            tn(gate_back[:, :own], c1t)
            + tn(up_back[:, :own], c3t)
            + tn(gate_pre_bar[:, :own], w1t)
            + tn(up_pre_bar[:, :own], w3t)
        )
    ).astype(jnp.bfloat16)
    results = [(o - b).T[None] for o, b in zip(owned, bars)]
    return (query_grad, key_grad, value_grad, *results)


def solution(mesh):
    tokens = P("tok", "head")
    in_specs = (tokens,) * 5 + (P("head"),) + (P("head", None, None),) * 3
    out_specs = (tokens,) * 3 + (P("head", None, "tok"),) * 3
    return jax.shard_map(
        per_device, mesh=mesh, in_specs=in_specs, out_specs=out_specs, check_vma=False
    )
```

```python
import functools

import jax
import jax.numpy as jnp
from jax import lax
from jax.experimental import pallas as pl
from jax.experimental.pallas import tpu as pltpu
from jax.sharding import PartitionSpec as P

EPSILON = 1e-06
CORES = 2
ROW_TILE = 16
VMEM_LIMIT = 24 * 1024 * 1024
BF16, F32 = jnp.bfloat16, jnp.float32


def nn(a, b):
    return lax.dot_general(a, b, (((1,), (0,)), ((), ())), preferred_element_type=F32)


def nt(a, b):
    return lax.dot_general(a, b, (((1,), (1,)), ((), ())), preferred_element_type=F32)


def tn(a, b):
    return lax.dot_general(a, b, (((0,), (0,)), ((), ())), preferred_element_type=F32)


def silu_parts(hidden):
    sigmoid_value = jax.nn.sigmoid(hidden)
    silu_value = hidden * sigmoid_value
    silu_slope = sigmoid_value * (1.0 + hidden * (1.0 - sigmoid_value))
    curvature = sigmoid_value * (1.0 - sigmoid_value) * (2.0 + hidden * (1.0 - 2.0 * sigmoid_value))
    return silu_value, silu_slope, curvature


def partner(index, step, count):
    return index ^ step if count & (count - 1) == 0 else (index + step) % count


def source(index, step, count):
    return index ^ step if count & (count - 1) == 0 else (index + count - step) % count


def chip_perm(count, step):
    chips = count // CORES
    return [(t, partner(t // CORES, step, chips) * CORES + t % CORES) for t in range(count)]


def core_perm(count):
    return [(t, t ^ 1) for t in range(count)]


def pack(gate, up, down):
    folds = gate.shape[1] // down.shape[1]
    rows = down.shape[0] // folds
    down = jnp.concatenate([down[i * rows : (i + 1) * rows] for i in range(folds)], axis=1)
    return jnp.concatenate([gate, up, down], axis=0)


def unpack(packed, fh):
    g = packed.shape[0] // 3
    folds = packed.shape[1] // fh
    down = packed[2 * g :]
    down = jnp.concatenate([down[:, i * fh : (i + 1) * fh] for i in range(folds)], axis=0)
    return packed[:g], packed[g : 2 * g], down


def update_forward(w1t, w3t, w2, keys, push):
    gate_pre, up_pre = nt(w1t, keys), nt(w3t, keys)
    silu, slope, curvature = silu_parts(gate_pre)
    mixed = (silu * up_pre).astype(BF16)
    down_back = nn(w2, push)
    back_slope = down_back * slope
    gate_back = (down_back * up_pre * slope).astype(BF16)
    up_back = (down_back * silu).astype(BF16)
    return up_pre, silu, slope, curvature, mixed, down_back, back_slope, gate_back, up_back


def apply_forward(f1t, f3t, f2t, queries, weighted):
    q_gate, q_up = nt(f1t, queries), nt(f3t, queries)
    silu, slope, _ = silu_parts(q_gate)
    mixed = (silu * q_up).astype(BF16)
    output = nn(f2t, mixed)
    square = jnp.sum(output * output, axis=0, keepdims=True)
    dot = jnp.sum(weighted * output, axis=0, keepdims=True)
    return output, mixed, q_up * slope, silu, jnp.concatenate([square, dot], axis=0)


def apply_backward(f2t, sums, full_width, output, weighted, mixed, up_slope, silu, queries):
    inverse = lax.rsqrt(sums[0:1] / full_width + EPSILON)
    scale = inverse * inverse * inverse * sums[1:2] / full_width
    out_back = (inverse * weighted - output * scale).astype(BF16)
    q_back = tn(f2t, out_back)
    gate_back = (q_back * up_slope).astype(BF16)
    up_back = (q_back * silu).astype(BF16)
    return gate_back, up_back, nn(gate_back, queries), nn(up_back, queries), nt(out_back, mixed)


def second_adjoint(c1t, c3t, c2t, keys, push, up_slope, silu, back_slope, back_curve):
    gate_bar, up_bar, mixed_bar = nt(c1t, keys), nt(c3t, keys), tn(c2t, push)
    down_back_bar = (gate_bar * up_slope + up_bar * silu).astype(BF16)
    up_pre_bar = (gate_bar * back_slope + mixed_bar * silu).astype(BF16)
    gate_pre_bar = (up_bar * back_slope + mixed_bar * up_slope + gate_bar * back_curve).astype(BF16)
    return (
        down_back_bar,
        up_pre_bar,
        gate_pre_bar,
        nn(gate_pre_bar, keys),
        nn(up_pre_bar, keys),
        nt(push, down_back_bar),
    )


def push_of(rates, values):
    return (-rates * values.T.astype(F32)).astype(BF16)


def both(own_ref, other_ref, axis=0):
    return jnp.concatenate([own_ref[...], other_ref[...]], axis=axis)


def send_pieces(chips, gate_ref, up_ref, down_ref, outs):
    tok = lax.axis_index("tok")
    chip, core = tok // CORES, tok % CORES
    g = gate_ref.shape[0] // (chips * CORES)
    d = down_ref.shape[0] // (chips * CORES)
    fh = down_ref.shape[1]
    for step, out in enumerate(outs):
        t = partner(chip, step, chips) * CORES + core
        out[:g] = gate_ref[pl.ds(pl.multiple_of(t * g, g), g), :].astype(out.dtype)
        out[g : 2 * g] = up_ref[pl.ds(pl.multiple_of(t * g, g), g), :].astype(out.dtype)
        for i in range(d // g):
            rows = pl.ds(pl.multiple_of(t * d + i * g, g), g)
            out[2 * g :, i * fh : (i + 1) * fh] = down_ref[rows, :].astype(out.dtype)


def place_pieces(chips, pieces, gate_ref, up_ref, down_ref):
    tok = lax.axis_index("tok")
    chip, core = tok // CORES, tok % CORES
    g = gate_ref.shape[0] // (chips * CORES)
    d = down_ref.shape[0] // (chips * CORES)
    fh = down_ref.shape[1]
    for step in range(chips):
        first = source(chip, step, chips) * CORES
        for piece, t in ((pieces[2 * step], first + core), (pieces[2 * step + 1], first + 1 - core)):
            gate_ref[pl.ds(pl.multiple_of(t * g, g), g), :] = piece[:g]
            up_ref[pl.ds(pl.multiple_of(t * g, g), g), :] = piece[g : 2 * g]
            for i in range(d // g):
                rows = pl.ds(pl.multiple_of(t * d + i * g, g), g)
                down_ref[rows, :] = piece[2 * g :, i * fh : (i + 1) * fh]


def update_kernel(chips, ko, kx, vo, vx, ro, rx, w1t, w3t, w2, *rest):
    outs, (gate, up, down) = rest[:chips], rest[chips:]
    keys = both(ko, kx)
    push = push_of(both(ro, rx, 1), both(vo, vx))
    *_, mixed, _, _, gate_back, up_back = update_forward(w1t[...], w3t[...], w2[...], keys, push)
    down[...] = nt(push, mixed)
    gate[...] = nn(gate_back, keys)
    up[...] = nn(up_back, keys)
    send_pieces(chips, gate, up, down, outs)


def saved_kernel(
    ko, kx, vo, vx, ro, rx, w1t, w3t, w2, go, gx, gain,
    push_ref, up_slope_ref, silu_ref, back_slope_ref, back_curve_ref,
    mixed_ref, gate_back_ref, up_back_ref, weighted_ref,
):
    push = push_of(both(ro, rx, 1), both(vo, vx))
    push_ref[...] = push
    up_pre, silu, slope, curvature, mixed, down_back, back_slope, gate_back, up_back = (
        update_forward(w1t[...], w3t[...], w2[...], both(ko, kx), push)
    )
    up_slope_ref[...] = up_pre * slope
    silu_ref[...] = silu
    back_slope_ref[...] = back_slope
    back_curve_ref[...] = down_back * up_pre * curvature
    own = mixed_ref.shape[1]
    mixed_ref[...] = mixed[:, :own]
    gate_back_ref[...] = gate_back[:, :own]
    up_back_ref[...] = up_back[:, :own]
    weighted_ref[...] = both(go, gx).T.astype(F32) * gain[...]


def apply_kernel(chips, *refs):
    pieces, refs = refs[: 2 * chips], refs[2 * chips :]
    qo, qx, weighted, f1t, f3t, f2t, output, mixed, up_slope, silu, sums = refs
    place_pieces(chips, pieces, f1t, f3t, f2t)
    output[...], mixed[...], up_slope[...], silu[...], sums[...] = apply_forward(
        f1t[...], f3t[...], f2t[...], both(qo, qx), weighted[...]
    )


def back_kernel(chips, heads, *refs):
    sums = sum(r[...] for r in refs[1:heads]) + refs[0][...]
    f2t, output, weighted, mixed, up_slope, silu, qo, qx, gate_back, up_back = refs[heads : heads + 10]
    outs, (gate, up, down) = refs[heads + 10 : heads + 10 + chips], refs[heads + 10 + chips :]
    width = heads * output.shape[0]
    gb, ub, gate[...], up[...], down[...] = apply_backward(
        f2t[...], sums, width, output[...], weighted[...], mixed[...], up_slope[...], silu[...],
        both(qo, qx),
    )
    send_pieces(chips, gate, up, down, outs)
    own = gate_back.shape[1]
    gate_back[...], up_back[...] = gb[:, :own], ub[:, :own]


def query_kernel(gate_back, up_back, f1t, f3t, out):
    out[...] = (tn(gate_back[...], f1t[...]) + tn(up_back[...], f3t[...])).astype(BF16)


def second_kernel(chips, *refs):
    pieces, refs = refs[: 2 * chips], refs[2 * chips :]
    ko, kx, push, up_slope, silu, back_slope, back_curve = refs[:7]
    c1t, c3t, c2t, dbb_ref, upb_ref, gpb_ref = refs[7:13]
    outs, (gate, up, down) = refs[13 : 13 + chips], refs[13 + chips :]
    place_pieces(chips, pieces, c1t, c3t, c2t)
    dbb, upb, gpb, gate[...], up[...], down[...] = second_adjoint(
        c1t[...], c3t[...], c2t[...], both(ko, kx), push[...],
        up_slope[...], silu[...], back_slope[...], back_curve[...],
    )
    send_pieces(chips, gate, up, down, outs)
    own = dbb_ref.shape[1]
    dbb_ref[...], upb_ref[...], gpb_ref[...] = dbb[:, :own], upb[:, :own], gpb[:, :own]


def token_grads(rates, mixed, dbb, upb, gpb, gate_back, up_back, c1t, c3t, c2t, w1t, w3t, w2):
    value_grad = (rates * (nn(c2t, mixed) + tn(w2, dbb))).T.astype(BF16)
    key_total = tn(gate_back, c1t) + tn(up_back, c3t) + tn(gpb, w1t) + tn(upb, w3t)
    return value_grad, (-key_total).astype(BF16)


def token_kernel(*refs):
    value_grad, key_grad = refs[-2:]
    value_grad[...], key_grad[...] = token_grads(*(r[...] for r in refs[:-2]))


def call(kernel, outs, args, scratch=(), name=None):
    vmem = pl.BlockSpec(memory_space=pltpu.VMEM)
    return pl.pallas_call(
        kernel,
        out_shape=[jax.ShapeDtypeStruct(s, t) for s, t in outs],
        in_specs=[vmem] * len(args),
        out_specs=[vmem] * len(outs),
        scratch_shapes=[pltpu.VMEM(s, t) for s, t in scratch],
        compiler_params=pltpu.CompilerParams(vmem_limit_bytes=VMEM_LIMIT),
        name=name,
    )(*args)


def exchange_sum(pieces, chips):
    count = chips * CORES
    got = {s: lax.ppermute(pieces[s], "tok", chip_perm(count, s)) for s in reversed(range(1, chips))}
    total = pieces[0]
    for step in range(1, chips):
        total = total + got[step].astype(F32)
    return total


def gather(packed, chips):
    count = chips * CORES
    pieces = [None] * count
    for step in (0, *reversed(range(1, chips))):
        mine = packed if step == 0 else lax.ppermute(packed, "tok", chip_perm(count, step))
        pieces[2 * step] = mine
        pieces[2 * step + 1] = lax.ppermute(mine, "tok", core_perm(count))
    return pieces


def sliced_pieces(gate, up, down, tok, chips):
    chip, core = tok // CORES, tok % CORES
    g, d = gate.shape[0] // (chips * CORES), down.shape[0] // (chips * CORES)
    pieces = []
    for step in range(chips):
        t = partner(chip, step, chips) * CORES + core
        piece = pack(
            lax.dynamic_slice_in_dim(gate, t * g, g, 0),
            lax.dynamic_slice_in_dim(up, t * g, g, 0),
            lax.dynamic_slice_in_dim(down, t * d, d, 0),
        )
        pieces.append(piece if step == 0 else piece.astype(BF16))
    return pieces


def whole_matrices(pieces, tok, chips, fh):
    chip, core = tok // CORES, tok % CORES
    held = jnp.zeros((chips * CORES,) + pieces[0].shape, pieces[0].dtype)
    for step in range(chips):
        first = source(chip, step, chips) * CORES
        held = lax.dynamic_update_index_in_dim(held, pieces[2 * step], first + core, 0)
        held = lax.dynamic_update_index_in_dim(held, pieces[2 * step + 1], first + 1 - core, 0)
    parts = jax.vmap(lambda x: unpack(x, fh))(held)
    return tuple(x.reshape((-1, x.shape[-1])) for x in parts)


def norm_of(rows):
    return jnp.sqrt(jnp.sum(rows * rows, axis=1, keepdims=True) + EPSILON)


def per_device(
    query_input,
    key_input,
    value_input,
    out_grad,
    token_rates,
    out_gain,
    gate_prior,
    up_prior,
    down_prior,
):
    count, heads = lax.axis_size("tok"), lax.axis_size("head")
    tok = lax.axis_index("tok")
    chips = count // CORES
    own, dh = key_input.shape
    n = own * CORES
    w1t, w3t, w2 = gate_prior[0].T, up_prior[0].T, down_prior[0]
    fh = w2.shape[0]
    g, d = fh // count, dh // count
    tiled = g % ROW_TILE == 0 and d % g == 0 and dh // g == fh // g * (d // g)
    rates = token_rates.T
    gain = out_gain[:, None]

    pair = lambda x: lax.ppermute(x, "tok", core_perm(count))
    key_other, value_other, rate_other = pair(key_input), pair(value_input), pair(rates)
    query_other, grad_other = pair(query_input), pair(out_grad)
    messages = [((3 * g, dh), F32)] + [((3 * g, dh), BF16)] * (chips - 1)
    matrices = [((fh, dh), BF16), ((fh, dh), BF16), ((dh, fh), BF16)]
    sums_scratch = [((fh, dh), F32), ((fh, dh), F32), ((dh, fh), F32)]
    hidden = ((fh, n), F32)
    own_hidden = ((fh, own), BF16)
    joined = lambda a, b, axis=0: jnp.concatenate([a, b], axis=axis)

    inputs = (
        key_input, key_other, value_input, value_other, rates, rate_other, w1t, w3t, w2,
    )
    if tiled:
        pieces = call(
            functools.partial(update_kernel, chips), messages, inputs, sums_scratch, "update"
        )
        push, up_slope, silu, back_slope, back_curve, mixed, gate_back, up_back, weighted = call(
            saved_kernel,
            [((dh, n), BF16)] + [hidden] * 4 + [own_hidden] * 3 + [((dh, n), F32)],
            (*inputs, out_grad, grad_other, gain),
            name="saved",
        )
    else:
        keys = joined(key_input, key_other)
        queries = joined(query_input, query_other)
        push = push_of(joined(rates, rate_other, 1), joined(value_input, value_other))
        up_pre, silu, slope, curvature, mixed, down_back, back_slope, gate_back, up_back = (
            update_forward(w1t, w3t, w2, keys, push)
        )
        up_slope, back_curve = up_pre * slope, down_back * up_pre * curvature
        weighted = joined(out_grad, grad_other).T.astype(F32) * gain
        pieces = sliced_pieces(nn(gate_back, keys), nn(up_back, keys), nt(push, mixed), tok, chips)
        mixed, gate_back, up_back = mixed[:, :own], gate_back[:, :own], up_back[:, :own]
    update = unpack(exchange_sum(pieces, chips), fh)

    priors = [
        lax.dynamic_slice_in_dim(x, tok * rows, rows, 0).astype(F32)
        for x, rows in ((w1t, g), (w3t, g), (w2.T, d))
    ]
    moved = [p - u for p, u in zip(priors, update)]
    prior_norm = [norm_of(p) for p in priors]
    moved_norm = [norm_of(m) for m in moved]
    fast = [(m * (p / q)).astype(BF16) for m, p, q in zip(moved, prior_norm, moved_norm)]
    pieces = gather(pack(*fast), chips)

    if tiled:
        f1t, f3t, f2t, output, q_mixed, q_slope, q_silu, part = call(
            functools.partial(apply_kernel, chips),
            matrices + [((dh, n), F32), ((fh, n), BF16), hidden, hidden, ((2, n), F32)],
            (*pieces, query_input, query_other, weighted),
            name="apply",
        )
    else:
        f1t, f3t, f2t = whole_matrices(pieces, tok, chips, fh)
        output, q_mixed, q_slope, q_silu, part = apply_forward(f1t, f3t, f2t, queries, weighted)
    sums = [part] + [
        lax.ppermute(part, "head", [(h, partner(h, step, heads)) for h in range(heads)])
        for step in range(1, heads)
    ]
    if tiled:
        q_gate_back, q_up_back, *pieces = call(
            functools.partial(back_kernel, chips, heads),
            [own_hidden] * 2 + messages,
            (*sums, f2t, output, weighted, q_mixed, q_slope, q_silu, query_input, query_other),
            sums_scratch,
            "apply_back",
        )
        (query_grad,) = call(
            query_kernel, [((own, dh), BF16)], (q_gate_back, q_up_back, f1t, f3t), name="query_grad"
        )
    else:
        q_gate_back, q_up_back, *grads = apply_backward(
            f2t, sum(sums[1:], sums[0]), heads * dh, output, weighted, q_mixed, q_slope, q_silu, queries
        )
        pieces = sliced_pieces(*grads, tok, chips)
        query_grad = (tn(q_gate_back[:, :own], f1t) + tn(q_up_back[:, :own], f3t)).astype(BF16)
    fast_grad = unpack(exchange_sum(pieces, chips), fh)

    cotangent, owned = [], []
    for p, m, pn, mn, fg in zip(priors, moved, prior_norm, moved_norm, fast_grad):
        column_dot = jnp.sum(fg * m, axis=1, keepdims=True)
        moved_grad = pn / mn * (fg - m * (column_dot / (mn * mn)))
        cotangent.append(moved_grad.astype(BF16))
        owned.append(moved_grad + p * (column_dot / (mn * pn)))
    pieces = gather(pack(*cotangent), chips)

    if tiled:
        c1t, c3t, c2t, dbb, upb, gpb, *pieces = call(
            functools.partial(second_kernel, chips),
            matrices + [own_hidden] * 3 + messages,
            (*pieces, key_input, key_other, push, up_slope, silu, back_slope, back_curve),
            sums_scratch,
            "second_adjoint",
        )
    else:
        c1t, c3t, c2t = whole_matrices(pieces, tok, chips, fh)
        dbb, upb, gpb, *bars = second_adjoint(
            c1t, c3t, c2t, keys, push, up_slope, silu, back_slope, back_curve
        )
        pieces = sliced_pieces(*bars, tok, chips)
        dbb, upb, gpb = dbb[:, :own], upb[:, :own], gpb[:, :own]
    token_args = (
        rates, mixed, dbb, upb, gpb, gate_back, up_back, c1t, c3t, c2t, w1t, w3t, w2,
    )
    if tiled:
        value_grad, key_grad = call(
            token_kernel, [((own, dh), BF16)] * 2, token_args, name="token_grads"
        )
    else:
        value_grad, key_grad = token_grads(*token_args)
    bars = unpack(exchange_sum(pieces, chips), fh)
    results = [(o - b).T[None] for o, b in zip(owned, bars)]
    return (query_grad, key_grad, value_grad, *results)


def solution(mesh):
    tokens = P("tok", "head")
    in_specs = (tokens,) * 5 + (P("head"),) + (P("head", None, None),) * 3
    out_specs = (tokens,) * 3 + (P("head", None, "tok"),) * 3
    return jax.shard_map(
        per_device, mesh=mesh, in_specs=in_specs, out_specs=out_specs, check_vma=False
    )
```

```python
import functools

import jax
import jax.numpy as jnp
from jax import lax
from jax.experimental import pallas as pl
from jax.experimental.pallas import tpu as pltpu
from jax.sharding import PartitionSpec as P

EPSILON = 1e-06
CORES = 2
ROW_TILE = 16
VMEM_LIMIT = 24 * 1024 * 1024
BF16, F32 = jnp.bfloat16, jnp.float32


def nn(a, b):
    return lax.dot_general(a, b, (((1,), (0,)), ((), ())), preferred_element_type=F32)


def nt(a, b):
    return lax.dot_general(a, b, (((1,), (1,)), ((), ())), preferred_element_type=F32)


def tn(a, b):
    return lax.dot_general(a, b, (((0,), (0,)), ((), ())), preferred_element_type=F32)


def silu_parts(hidden):
    sigmoid_value = jax.nn.sigmoid(hidden)
    silu_value = hidden * sigmoid_value
    silu_slope = sigmoid_value * (1.0 + hidden * (1.0 - sigmoid_value))
    curvature = sigmoid_value * (1.0 - sigmoid_value) * (2.0 + hidden * (1.0 - 2.0 * sigmoid_value))
    return silu_value, silu_slope, curvature


def partner(index, step, count):
    return index ^ step if count & (count - 1) == 0 else (index + step) % count


def source(index, step, count):
    return index ^ step if count & (count - 1) == 0 else (index + count - step) % count


def chip_perm(count, step):
    chips = count // CORES
    return [(t, partner(t // CORES, step, chips) * CORES + t % CORES) for t in range(count)]


def core_perm(count):
    return [(t, t ^ 1) for t in range(count)]


def pack(gate, up, down):
    folds = gate.shape[1] // down.shape[1]
    rows = down.shape[0] // folds
    down = jnp.concatenate([down[i * rows : (i + 1) * rows] for i in range(folds)], axis=1)
    return jnp.concatenate([gate, up, down], axis=0)


def unpack(packed, fh):
    g = packed.shape[0] // 3
    folds = packed.shape[1] // fh
    down = packed[2 * g :]
    down = jnp.concatenate([down[:, i * fh : (i + 1) * fh] for i in range(folds)], axis=0)
    return packed[:g], packed[g : 2 * g], down


def update_forward(w1t, w3t, w2, keys, push):
    gate_pre, up_pre = nt(w1t, keys), nt(w3t, keys)
    silu, slope, curvature = silu_parts(gate_pre)
    mixed = (silu * up_pre).astype(BF16)
    down_back = nn(w2, push)
    back_slope = down_back * slope
    gate_back = (down_back * up_pre * slope).astype(BF16)
    up_back = (down_back * silu).astype(BF16)
    return up_pre, silu, slope, curvature, mixed, down_back, back_slope, gate_back, up_back


def apply_forward(f1t, f3t, f2t, queries, weighted):
    q_gate, q_up = nt(f1t, queries), nt(f3t, queries)
    silu, slope, _ = silu_parts(q_gate)
    mixed = (silu * q_up).astype(BF16)
    output = nn(f2t, mixed)
    square = jnp.sum(output * output, axis=0, keepdims=True)
    dot = jnp.sum(weighted * output, axis=0, keepdims=True)
    return output, mixed, q_up * slope, silu, jnp.concatenate([square, dot], axis=0)


def apply_backward(f2t, sums, full_width, output, weighted, mixed, up_slope, silu, queries):
    inverse = lax.rsqrt(sums[0:1] / full_width + EPSILON)
    scale = inverse * inverse * inverse * sums[1:2] / full_width
    out_back = (inverse * weighted - output * scale).astype(BF16)
    q_back = tn(f2t, out_back)
    gate_back = (q_back * up_slope).astype(BF16)
    up_back = (q_back * silu).astype(BF16)
    return gate_back, up_back, nn(gate_back, queries), nn(up_back, queries), nt(out_back, mixed)


def second_adjoint(c1t, c3t, c2t, keys, push, up_slope, silu, back_slope, back_curve):
    gate_bar, up_bar, mixed_bar = nt(c1t, keys), nt(c3t, keys), tn(c2t, push)
    down_back_bar = (gate_bar * up_slope + up_bar * silu).astype(BF16)
    up_pre_bar = (gate_bar * back_slope + mixed_bar * silu).astype(BF16)
    gate_pre_bar = (up_bar * back_slope + mixed_bar * up_slope + gate_bar * back_curve).astype(BF16)
    return (
        down_back_bar,
        up_pre_bar,
        gate_pre_bar,
        nn(gate_pre_bar, keys),
        nn(up_pre_bar, keys),
        nt(push, down_back_bar),
    )


def norm_of(rows):
    return jnp.sqrt(jnp.sum(rows * rows, axis=1, keepdims=True) + EPSILON)


def owner_forward(prior, update, fh):
    moved = prior - update
    fast = [m * (norm_of(p) / norm_of(m)) for p, m in zip(unpack(prior, fh), unpack(moved, fh))]
    return pack(*fast).astype(BF16), moved


def owner_backward(prior, moved, fast_grad, fh):
    cotangent, owned = [], []
    for p, m, fg in zip(unpack(prior, fh), unpack(moved, fh), unpack(fast_grad, fh)):
        prior_norm, moved_norm = norm_of(p), norm_of(m)
        column_dot = jnp.sum(fg * m, axis=1, keepdims=True)
        moved_grad = (prior_norm / moved_norm) * (fg - m * (column_dot / (moved_norm * moved_norm)))
        cotangent.append(moved_grad)
        owned.append(moved_grad + p * (column_dot / (moved_norm * prior_norm)))
    return pack(*cotangent).astype(BF16), pack(*owned)


def total_of(pieces):
    total = pieces[0]
    for piece in pieces[1:]:
        total = total + piece.astype(F32)
    return total


def push_of(rates, values):
    return (-rates * values.T.astype(F32)).astype(BF16)


def both(own_ref, other_ref, axis=0):
    return jnp.concatenate([own_ref[...], other_ref[...]], axis=axis)


def send_pieces(chips, gate_ref, up_ref, down_ref, outs):
    tok = lax.axis_index("tok")
    chip, core = tok // CORES, tok % CORES
    g = gate_ref.shape[0] // (chips * CORES)
    d = down_ref.shape[0] // (chips * CORES)
    fh = down_ref.shape[1]
    for step, out in enumerate(outs):
        t = partner(chip, step, chips) * CORES + core
        out[:g] = gate_ref[pl.ds(pl.multiple_of(t * g, g), g), :].astype(out.dtype)
        out[g : 2 * g] = up_ref[pl.ds(pl.multiple_of(t * g, g), g), :].astype(out.dtype)
        for i in range(d // g):
            rows = pl.ds(pl.multiple_of(t * d + i * g, g), g)
            out[2 * g :, i * fh : (i + 1) * fh] = down_ref[rows, :].astype(out.dtype)


def place_pieces(chips, pieces, gate_ref, up_ref, down_ref):
    tok = lax.axis_index("tok")
    chip, core = tok // CORES, tok % CORES
    g = gate_ref.shape[0] // (chips * CORES)
    d = down_ref.shape[0] // (chips * CORES)
    fh = down_ref.shape[1]
    for step in range(chips):
        first = source(chip, step, chips) * CORES
        for piece, t in ((pieces[2 * step], first + core), (pieces[2 * step + 1], first + 1 - core)):
            gate_ref[pl.ds(pl.multiple_of(t * g, g), g), :] = piece[:g]
            up_ref[pl.ds(pl.multiple_of(t * g, g), g), :] = piece[g : 2 * g]
            for i in range(d // g):
                rows = pl.ds(pl.multiple_of(t * d + i * g, g), g)
                down_ref[rows, :] = piece[2 * g :, i * fh : (i + 1) * fh]


def update_kernel(chips, ko, kx, vo, vx, ro, rx, w1t, w3t, w2, *rest):
    outs, (gate, up, down) = rest[:chips], rest[chips:]
    keys = both(ko, kx)
    push = push_of(both(ro, rx, 1), both(vo, vx))
    *_, mixed, _, _, gate_back, up_back = update_forward(w1t[...], w3t[...], w2[...], keys, push)
    down[...] = nt(push, mixed)
    gate[...] = nn(gate_back, keys)
    up[...] = nn(up_back, keys)
    send_pieces(chips, gate, up, down, outs)


def saved_kernel(
    chips, ko, kx, vo, vx, ro, rx, w1t, w3t, w2, go, gx, gain,
    push_ref, up_slope_ref, silu_ref, back_slope_ref, back_curve_ref,
    mixed_ref, gate_back_ref, up_back_ref, weighted_ref, prior_ref, down_ref,
):
    push = push_of(both(ro, rx, 1), both(vo, vx))
    push_ref[...] = push
    up_pre, silu, slope, curvature, mixed, down_back, back_slope, gate_back, up_back = (
        update_forward(w1t[...], w3t[...], w2[...], both(ko, kx), push)
    )
    up_slope_ref[...] = up_pre * slope
    silu_ref[...] = silu
    back_slope_ref[...] = back_slope
    back_curve_ref[...] = down_back * up_pre * curvature
    own = mixed_ref.shape[1]
    mixed_ref[...] = mixed[:, :own]
    gate_back_ref[...] = gate_back[:, :own]
    up_back_ref[...] = up_back[:, :own]
    weighted_ref[...] = (both(go, gx).astype(F32) * gain[...]).T
    tok = lax.axis_index("tok")
    g, (d, fh) = prior_ref.shape[0] // 3, (down_ref.shape[0] // (chips * CORES), down_ref.shape[1])
    rows = pl.ds(pl.multiple_of(tok * g, g), g)
    prior_ref[:g] = w1t[rows, :].astype(F32)
    prior_ref[g : 2 * g] = w3t[rows, :].astype(F32)
    down_ref[...] = w2[...].astype(F32).T
    for i in range(d // g):
        rows = pl.ds(pl.multiple_of(tok * d + i * g, g), g)
        prior_ref[2 * g :, i * fh : (i + 1) * fh] = down_ref[rows, :]


def owner_forward_kernel(fh, prior, *refs):
    fast, moved = refs[-2:]
    fast[...], moved[...] = owner_forward(prior[...], total_of([r[...] for r in refs[:-2]]), fh)


def owner_backward_kernel(fh, prior, moved, *refs):
    cotangent, owned = refs[-2:]
    fast_grad = total_of([r[...] for r in refs[:-2]])
    cotangent[...], owned[...] = owner_backward(prior[...], moved[...], fast_grad, fh)


def owner_result_kernel(fh, owned, *refs):
    gate, up, down = refs[-3:]
    bars = total_of([r[...] for r in refs[:-3]])
    gate[...], up[...], down[...] = unpack(owned[...] - bars, fh)


def apply_kernel(chips, *refs):
    pieces, refs = refs[: 2 * chips], refs[2 * chips :]
    qo, qx, weighted, f1t, f3t, f2t, output, mixed, up_slope, silu, sums = refs
    place_pieces(chips, pieces, f1t, f3t, f2t)
    output[...], mixed[...], up_slope[...], silu[...], sums[...] = apply_forward(
        f1t[...], f3t[...], f2t[...], both(qo, qx), weighted[...]
    )


def back_kernel(chips, heads, *refs):
    sums, f2t, output, weighted, mixed, up_slope, silu, qo, qx, gate_back, up_back = refs[:11]
    outs, (gate, up, down) = refs[11 : 11 + chips], refs[11 + chips :]
    width = heads * output.shape[0]
    gb, ub, gate[...], up[...], down[...] = apply_backward(
        f2t[...], sums[...], width, output[...], weighted[...], mixed[...], up_slope[...], silu[...],
        both(qo, qx),
    )
    send_pieces(chips, gate, up, down, outs)
    own = gate_back.shape[1]
    gate_back[...], up_back[...] = gb[:, :own], ub[:, :own]


def query_kernel(gate_back, up_back, f1t, f3t, out):
    out[...] = (tn(gate_back[...], f1t[...]) + tn(up_back[...], f3t[...])).astype(BF16)


def second_kernel(chips, *refs):
    pieces, refs = refs[: 2 * chips], refs[2 * chips :]
    ko, kx, push, up_slope, silu, back_slope, back_curve = refs[:7]
    c1t, c3t, c2t, dbb_ref, upb_ref, gpb_ref = refs[7:13]
    outs, (gate, up, down) = refs[13 : 13 + chips], refs[13 + chips :]
    place_pieces(chips, pieces, c1t, c3t, c2t)
    dbb, upb, gpb, gate[...], up[...], down[...] = second_adjoint(
        c1t[...], c3t[...], c2t[...], both(ko, kx), push[...],
        up_slope[...], silu[...], back_slope[...], back_curve[...],
    )
    send_pieces(chips, gate, up, down, outs)
    own = dbb_ref.shape[1]
    dbb_ref[...], upb_ref[...], gpb_ref[...] = dbb[:, :own], upb[:, :own], gpb[:, :own]


def token_grads(rates, mixed, dbb, upb, gpb, gate_back, up_back, c1t, c3t, c2t, w1t, w3t, w2):
    value_grad = (rates * (nn(c2t, mixed) + tn(w2, dbb))).T.astype(BF16)
    key_total = tn(gate_back, c1t) + tn(up_back, c3t) + tn(gpb, w1t) + tn(upb, w3t)
    return value_grad, (-key_total).astype(BF16)


def token_kernel(*refs):
    value_grad, key_grad = refs[-2:]
    value_grad[...], key_grad[...] = token_grads(*(r[...] for r in refs[:-2]))


def call(kernel, outs, args, scratch=(), name=None, flops=0):
    vmem = pl.BlockSpec(memory_space=pltpu.VMEM)
    return pl.pallas_call(
        kernel,
        out_shape=[jax.ShapeDtypeStruct(s, t) for s, t in outs],
        in_specs=[vmem] * len(args),
        out_specs=[vmem] * len(outs),
        scratch_shapes=[pltpu.VMEM(s, t) for s, t in scratch],
        compiler_params=pltpu.CompilerParams(vmem_limit_bytes=VMEM_LIMIT),
        cost_estimate=pl.CostEstimate(
            flops=flops,
            bytes_accessed=sum(a.size * a.dtype.itemsize for a in args),
            transcendentals=0,
        ),
        name=name,
    )(*args)


def exchange(pieces, chips):
    count = chips * CORES
    got = [lax.ppermute(pieces[s], "tok", chip_perm(count, s)) for s in reversed(range(1, chips))]
    return [pieces[0], *got]


def head_sum(part, heads):
    if heads & (heads - 1) == 0:
        step = 1
        while step < heads:
            part = part + lax.ppermute(part, "head", [(h, h ^ step) for h in range(heads)])
            step *= 2
        return part
    return lax.psum(part, "head")


def gather(packed, chips):
    count = chips * CORES
    pieces = [None] * count
    for step in range(chips):
        mine = packed if step == 0 else lax.ppermute(packed, "tok", chip_perm(count, step))
        pieces[2 * step] = mine
        pieces[2 * step + 1] = lax.ppermute(mine, "tok", core_perm(count))
    return pieces


def sliced_pieces(gate, up, down, tok, chips):
    chip, core = tok // CORES, tok % CORES
    g, d = gate.shape[0] // (chips * CORES), down.shape[0] // (chips * CORES)
    pieces = []
    for step in range(chips):
        t = partner(chip, step, chips) * CORES + core
        piece = pack(
            lax.dynamic_slice_in_dim(gate, t * g, g, 0),
            lax.dynamic_slice_in_dim(up, t * g, g, 0),
            lax.dynamic_slice_in_dim(down, t * d, d, 0),
        )
        pieces.append(piece if step == 0 else piece.astype(BF16))
    return pieces


def whole_matrices(pieces, tok, chips, fh):
    chip, core = tok // CORES, tok % CORES
    held = jnp.zeros((chips * CORES,) + pieces[0].shape, pieces[0].dtype)
    for step in range(chips):
        first = source(chip, step, chips) * CORES
        held = lax.dynamic_update_index_in_dim(held, pieces[2 * step], first + core, 0)
        held = lax.dynamic_update_index_in_dim(held, pieces[2 * step + 1], first + 1 - core, 0)
    parts = jax.vmap(lambda x: unpack(x, fh))(held)
    return tuple(x.reshape((-1, x.shape[-1])) for x in parts)


def per_device(
    query_input,
    key_input,
    value_input,
    out_grad,
    token_rates,
    out_gain,
    gate_prior,
    up_prior,
    down_prior,
):
    count, heads = lax.axis_size("tok"), lax.axis_size("head")
    tok = lax.axis_index("tok")
    chips = count // CORES
    own, dh = key_input.shape
    n = own * CORES
    w1t, w3t, w2 = gate_prior[0].T, up_prior[0].T, down_prior[0]
    fh = w2.shape[0]
    g, d = fh // count, dh // count
    tiled = g % ROW_TILE == 0 and d % g == 0 and dh // g == fh // g * (d // g)
    rates = token_rates.T
    gain = out_gain[None, :]
    product = 2 * n * dh * fh
    owner = ((3 * g, dh), BF16), ((3 * g, dh), F32)

    pair = lambda x: lax.ppermute(x, "tok", core_perm(count))
    key_other, value_other, rate_other = pair(key_input), pair(value_input), pair(rates)
    query_other, grad_other = pair(query_input), pair(out_grad)
    messages = [((3 * g, dh), F32)] + [((3 * g, dh), BF16)] * (chips - 1)
    matrices = [((fh, dh), BF16), ((fh, dh), BF16), ((dh, fh), BF16)]
    sums_scratch = [((fh, dh), F32), ((fh, dh), F32), ((dh, fh), F32)]
    hidden = ((fh, n), F32)
    own_hidden = ((fh, own), BF16)
    joined = lambda a, b, axis=0: jnp.concatenate([a, b], axis=axis)

    inputs = (
        key_input, key_other, value_input, value_other, rates, rate_other, w1t, w3t, w2,
    )
    if tiled:
        pieces = call(
            functools.partial(update_kernel, chips),
            messages,
            inputs,
            sums_scratch,
            "update",
            6 * product,
        )
        push, up_slope, silu, back_slope, back_curve, mixed, gate_back, up_back, weighted, prior = call(
            functools.partial(saved_kernel, chips),
            [((dh, n), BF16)] + [hidden] * 4 + [own_hidden] * 3 + [((dh, n), F32), owner[1]],
            (*inputs, out_grad, grad_other, gain),
            [((dh, fh), F32)],
            "saved",
            3 * product,
        )
    else:
        keys = joined(key_input, key_other)
        queries = joined(query_input, query_other)
        push = push_of(joined(rates, rate_other, 1), joined(value_input, value_other))
        up_pre, silu, slope, curvature, mixed, down_back, back_slope, gate_back, up_back = (
            update_forward(w1t, w3t, w2, keys, push)
        )
        up_slope, back_curve = up_pre * slope, down_back * up_pre * curvature
        weighted = (joined(out_grad, grad_other).astype(F32) * gain).T
        pieces = sliced_pieces(nn(gate_back, keys), nn(up_back, keys), nt(push, mixed), tok, chips)
        mixed, gate_back, up_back = mixed[:, :own], gate_back[:, :own], up_back[:, :own]
        prior = pack(
            *(
                lax.dynamic_slice_in_dim(x, tok * rows, rows, 0).astype(F32)
                for x, rows in ((w1t, g), (w3t, g), (w2.T, d))
            )
        )
    pieces = exchange(pieces, chips)
    if tiled:
        fast, moved = call(
            functools.partial(owner_forward_kernel, fh), owner, (prior, *pieces), name="owner_forward"
        )
    else:
        fast, moved = owner_forward(prior, total_of(pieces), fh)
    pieces = gather(fast, chips)

    if tiled:
        f1t, f3t, f2t, output, q_mixed, q_slope, q_silu, part = call(
            functools.partial(apply_kernel, chips),
            matrices + [((dh, n), F32), ((fh, n), BF16), hidden, hidden, ((2, n), F32)],
            (*pieces, query_input, query_other, weighted),
            name="apply",
            flops=3 * product,
        )
    else:
        f1t, f3t, f2t = whole_matrices(pieces, tok, chips, fh)
        output, q_mixed, q_slope, q_silu, part = apply_forward(f1t, f3t, f2t, queries, weighted)
    sums = head_sum(part, heads)
    if tiled:
        q_gate_back, q_up_back, *pieces = call(
            functools.partial(back_kernel, chips, heads),
            [own_hidden] * 2 + messages,
            (sums, f2t, output, weighted, q_mixed, q_slope, q_silu, query_input, query_other),
            sums_scratch,
            "apply_back",
            4 * product,
        )
        (query_grad,) = call(
            query_kernel,
            [((own, dh), BF16)],
            (q_gate_back, q_up_back, f1t, f3t),
            name="query_grad",
            flops=product,
        )
    else:
        q_gate_back, q_up_back, *grads = apply_backward(
            f2t, sums, heads * dh, output, weighted, q_mixed, q_slope, q_silu, queries
        )
        pieces = sliced_pieces(*grads, tok, chips)
        query_grad = (tn(q_gate_back[:, :own], f1t) + tn(q_up_back[:, :own], f3t)).astype(BF16)
    pieces = exchange(pieces, chips)
    if tiled:
        cotangent, owned = call(
            functools.partial(owner_backward_kernel, fh),
            owner,
            (prior, moved, *pieces),
            name="owner_backward",
        )
    else:
        cotangent, owned = owner_backward(prior, moved, total_of(pieces), fh)
    pieces = gather(cotangent, chips)

    if tiled:
        c1t, c3t, c2t, dbb, upb, gpb, *pieces = call(
            functools.partial(second_kernel, chips),
            matrices + [own_hidden] * 3 + messages,
            (*pieces, key_input, key_other, push, up_slope, silu, back_slope, back_curve),
            sums_scratch,
            "second_adjoint",
            6 * product,
        )
    else:
        c1t, c3t, c2t = whole_matrices(pieces, tok, chips, fh)
        dbb, upb, gpb, *bars = second_adjoint(
            c1t, c3t, c2t, keys, push, up_slope, silu, back_slope, back_curve
        )
        pieces = sliced_pieces(*bars, tok, chips)
        dbb, upb, gpb = dbb[:, :own], upb[:, :own], gpb[:, :own]
    token_args = (
        rates, mixed, dbb, upb, gpb, gate_back, up_back, c1t, c3t, c2t, w1t, w3t, w2,
    )
    if tiled:
        value_grad, key_grad = call(
            token_kernel, [((own, dh), BF16)] * 2, token_args, name="token_grads", flops=3 * product
        )
    else:
        value_grad, key_grad = token_grads(*token_args)
    pieces = exchange(pieces, chips)
    if tiled:
        results = call(
            functools.partial(owner_result_kernel, fh),
            [((g, dh), F32)] * 2 + [((d, fh), F32)],
            (owned, *pieces),
            name="owner_result",
        )
    else:
        results = unpack(owned - total_of(pieces), fh)
    results = [r.T[None] for r in results]
    return (query_grad, key_grad, value_grad, *results)


def solution(mesh):
    tokens = P("tok", "head")
    in_specs = (tokens,) * 5 + (P("head"),) + (P("head", None, None),) * 3
    out_specs = (tokens,) * 3 + (P("head", None, "tok"),) * 3
    return jax.shard_map(
        per_device, mesh=mesh, in_specs=in_specs, out_specs=out_specs, check_vma=False
    )
```

```python
import functools

import jax
import jax.numpy as jnp
from jax import lax
from jax.experimental import pallas as pl
from jax.experimental.pallas import tpu as pltpu
from jax.sharding import PartitionSpec as P

EPSILON = 1e-06
CORES = 2
ROW_TILE = 16
VMEM_LIMIT = 24 * 1024 * 1024
BF16, F32 = jnp.bfloat16, jnp.float32


def nn(a, b):
    return lax.dot_general(a, b, (((1,), (0,)), ((), ())), preferred_element_type=F32)


def nt(a, b):
    return lax.dot_general(a, b, (((1,), (1,)), ((), ())), preferred_element_type=F32)


def tn(a, b):
    return lax.dot_general(a, b, (((0,), (0,)), ((), ())), preferred_element_type=F32)


def silu_parts(hidden):
    sigmoid_value = jax.nn.sigmoid(hidden)
    silu_value = hidden * sigmoid_value
    silu_slope = sigmoid_value * (1.0 + hidden * (1.0 - sigmoid_value))
    curvature = sigmoid_value * (1.0 - sigmoid_value) * (2.0 + hidden * (1.0 - 2.0 * sigmoid_value))
    return silu_value, silu_slope, curvature


def core_perm(count):
    return [(t, t ^ 1) for t in range(count)]


def pack(gate, up, down):
    folds = gate.shape[1] // down.shape[1]
    rows = down.shape[0] // folds
    down = jnp.concatenate([down[i * rows : (i + 1) * rows] for i in range(folds)], axis=1)
    return jnp.concatenate([gate, up, down], axis=0)


def unpack(packed, fh):
    g = packed.shape[0] // 3
    folds = packed.shape[1] // fh
    down = packed[2 * g :]
    down = jnp.concatenate([down[:, i * fh : (i + 1) * fh] for i in range(folds)], axis=0)
    return packed[:g], packed[g : 2 * g], down


def update_forward(w1t, w3t, w2, keys, push):
    gate_pre, up_pre = nt(w1t, keys), nt(w3t, keys)
    silu, slope, curvature = silu_parts(gate_pre)
    mixed = (silu * up_pre).astype(BF16)
    down_back = nn(w2, push)
    back_slope = down_back * slope
    gate_back = (down_back * up_pre * slope).astype(BF16)
    up_back = (down_back * silu).astype(BF16)
    return up_pre, silu, slope, curvature, mixed, down_back, back_slope, gate_back, up_back


def apply_forward(f1t, f3t, f2t, queries, weighted):
    q_gate, q_up = nt(f1t, queries), nt(f3t, queries)
    silu, slope, _ = silu_parts(q_gate)
    mixed = (silu * q_up).astype(BF16)
    output = nn(f2t, mixed)
    square = jnp.sum(output * output, axis=0, keepdims=True)
    dot = jnp.sum(weighted * output, axis=0, keepdims=True)
    return output, mixed, q_up * slope, silu, jnp.concatenate([square, dot], axis=0)


def apply_backward(f2t, sums, full_width, output, weighted, mixed, up_slope, silu, queries):
    inverse = lax.rsqrt(sums[0:1] / full_width + EPSILON)
    scale = inverse * inverse * inverse * sums[1:2] / full_width
    out_back = (inverse * weighted - output * scale).astype(BF16)
    q_back = tn(f2t, out_back)
    gate_back = (q_back * up_slope).astype(BF16)
    up_back = (q_back * silu).astype(BF16)
    return gate_back, up_back, nn(gate_back, queries), nn(up_back, queries), nt(out_back, mixed)


def second_adjoint(c1t, c3t, c2t, keys, push, up_slope, silu, back_slope, back_curve):
    gate_bar, up_bar, mixed_bar = nt(c1t, keys), nt(c3t, keys), tn(c2t, push)
    down_back_bar = (gate_bar * up_slope + up_bar * silu).astype(BF16)
    up_pre_bar = (gate_bar * back_slope + mixed_bar * silu).astype(BF16)
    gate_pre_bar = (up_bar * back_slope + mixed_bar * up_slope + gate_bar * back_curve).astype(BF16)
    return (
        down_back_bar,
        up_pre_bar,
        gate_pre_bar,
        nn(gate_pre_bar, keys),
        nn(up_pre_bar, keys),
        nt(push, down_back_bar),
    )


def norm_of(rows):
    return jnp.sqrt(jnp.sum(rows * rows, axis=1, keepdims=True) + EPSILON)


def owner_forward(prior, update, fh):
    moved = prior - update
    fast = [m * (norm_of(p) / norm_of(m)) for p, m in zip(unpack(prior, fh), unpack(moved, fh))]
    return pack(*fast).astype(BF16), moved


def owner_backward(prior, moved, fast_grad, fh):
    cotangent, owned = [], []
    for p, m, fg in zip(unpack(prior, fh), unpack(moved, fh), unpack(fast_grad, fh)):
        prior_norm, moved_norm = norm_of(p), norm_of(m)
        column_dot = jnp.sum(fg * m, axis=1, keepdims=True)
        moved_grad = (prior_norm / moved_norm) * (fg - m * (column_dot / (moved_norm * moved_norm)))
        cotangent.append(moved_grad)
        owned.append(moved_grad + p * (column_dot / (moved_norm * prior_norm)))
    return pack(*cotangent).astype(BF16), pack(*owned)


def push_of(rates, values):
    return (-rates * values.T.astype(F32)).astype(BF16)


def both(own_ref, other_ref, axis=0):
    return jnp.concatenate([own_ref[...], other_ref[...]], axis=axis)


def cut_piece(out, at, t, g, d, gate_ref, up_ref, down_ref):
    fh = down_ref.shape[1]
    out[at : at + g] = gate_ref[pl.ds(pl.multiple_of(t * g, g), g), :].astype(out.dtype)
    out[at + g : at + 2 * g] = up_ref[pl.ds(pl.multiple_of(t * g, g), g), :].astype(out.dtype)
    for i in range(d // g):
        rows = pl.ds(pl.multiple_of(t * d + i * g, g), g)
        out[at + 2 * g : at + 3 * g, i * fh : (i + 1) * fh] = down_ref[rows, :].astype(out.dtype)


def send_pieces(chips, gate_ref, up_ref, down_ref, own, sent):
    tok = lax.axis_index("tok")
    g = gate_ref.shape[0] // (chips * CORES)
    d = down_ref.shape[0] // (chips * CORES)
    cut_piece(own, 0, tok, g, d, gate_ref, up_ref, down_ref)
    for chip in range(chips):
        t = chip * CORES + tok % CORES
        cut_piece(sent, 3 * g * chip, t, g, d, gate_ref, up_ref, down_ref)


def place_pieces(chips, mine, other, gate_ref, up_ref, down_ref):
    core = lax.axis_index("tok") % CORES
    g = gate_ref.shape[0] // (chips * CORES)
    d = down_ref.shape[0] // (chips * CORES)
    fh = down_ref.shape[1]
    for chip in range(chips):
        at = 3 * g * chip
        for piece, c in ((mine, core), (other, 1 - core)):
            t = chip * CORES + c
            gate_ref[pl.ds(pl.multiple_of(t * g, g), g), :] = piece[at : at + g]
            up_ref[pl.ds(pl.multiple_of(t * g, g), g), :] = piece[at + g : at + 2 * g]
            for i in range(d // g):
                rows = pl.ds(pl.multiple_of(t * d + i * g, g), g)
                down_ref[rows, :] = piece[at + 2 * g : at + 3 * g, i * fh : (i + 1) * fh]


def total_in_kernel(own, got):
    chip = lax.axis_index("tok") // CORES
    rows = own.shape[0]
    chips = got.shape[0] // rows
    total = own[...]
    for step in range(1, chips):
        at = lax.rem(chip + step, chips) * rows
        total = total + got[pl.ds(pl.multiple_of(at, rows), rows), :].astype(F32)
    return total


def update_kernel(chips, ko, kx, vo, vx, ro, rx, w1, w3, w2, *rest):
    outs, (gate, up, down) = rest[:2], rest[2:]
    keys = both(ko, kx)
    push = push_of(both(ro, rx, 1), both(vo, vx))
    *_, mixed, _, _, gate_back, up_back = update_forward(w1[...].T, w3[...].T, w2[...], keys, push)
    down[...] = nt(push, mixed)
    gate[...] = nn(gate_back, keys)
    up[...] = nn(up_back, keys)
    send_pieces(chips, gate, up, down, *outs)


def saved_kernel(
    chips, ko, kx, vo, vx, ro, rx, w1, w3, w2, go, gx, gain,
    push_ref, up_slope_ref, silu_ref, back_slope_ref, back_curve_ref,
    mixed_ref, gate_back_ref, up_back_ref, weighted_ref, prior_ref, gate_ref, up_ref, down_ref,
):
    push = push_of(both(ro, rx, 1), both(vo, vx))
    push_ref[...] = push
    up_pre, silu, slope, curvature, mixed, down_back, back_slope, gate_back, up_back = (
        update_forward(w1[...].T, w3[...].T, w2[...], both(ko, kx), push)
    )
    up_slope_ref[...] = up_pre * slope
    silu_ref[...] = silu
    back_slope_ref[...] = back_slope
    back_curve_ref[...] = down_back * up_pre * curvature
    own = mixed_ref.shape[1]
    mixed_ref[...] = mixed[:, :own]
    gate_back_ref[...] = gate_back[:, :own]
    up_back_ref[...] = up_back[:, :own]
    weighted_ref[...] = (both(go, gx).astype(F32) * gain[...]).T
    tok = lax.axis_index("tok")
    g, (d, fh) = prior_ref.shape[0] // 3, (down_ref.shape[0] // (chips * CORES), down_ref.shape[1])
    rows = pl.ds(pl.multiple_of(tok * g, g), g)
    gate_ref[...] = w1[...].astype(F32).T
    up_ref[...] = w3[...].astype(F32).T
    prior_ref[:g] = gate_ref[rows, :]
    prior_ref[g : 2 * g] = up_ref[rows, :]
    down_ref[...] = w2[...].astype(F32).T
    for i in range(d // g):
        rows = pl.ds(pl.multiple_of(tok * d + i * g, g), g)
        prior_ref[2 * g :, i * fh : (i + 1) * fh] = down_ref[rows, :]


def repeat(out, piece):
    rows = piece.shape[0]
    for chip in range(out.shape[0] // rows):
        out[chip * rows : (chip + 1) * rows] = piece


def owner_forward_kernel(fh, prior, *refs):
    fast, moved = refs[-2:]
    piece, moved[...] = owner_forward(prior[...], total_in_kernel(*refs[:-2]), fh)
    repeat(fast, piece)


def owner_backward_kernel(fh, prior, moved, *refs):
    cotangent, owned = refs[-2:]
    fast_grad = total_in_kernel(*refs[:-2])
    piece, owned[...] = owner_backward(prior[...], moved[...], fast_grad, fh)
    repeat(cotangent, piece)


def owner_result_kernel(fh, owned, *refs):
    gate, up, down = refs[-3:]
    bars = total_in_kernel(*refs[:-3])
    gate[...], up[...], down[...] = unpack(owned[...] - bars, fh)


def apply_kernel(chips, *refs):
    pieces, refs = refs[:2], refs[2:]
    qo, qx, weighted, f1t, f3t, f2t, output, mixed, up_slope, silu, sums = refs
    place_pieces(chips, *pieces, f1t, f3t, f2t)
    output[...], mixed[...], up_slope[...], silu[...], sums[...] = apply_forward(
        f1t[...], f3t[...], f2t[...], both(qo, qx), weighted[...]
    )


def back_kernel(chips, heads, *refs):
    sums, f2t, output, weighted, mixed, up_slope, silu, qo, qx, gate_back, up_back = refs[:11]
    outs, (gate, up, down) = refs[11:13], refs[13:]
    width = heads * output.shape[0]
    gb, ub, gate[...], up[...], down[...] = apply_backward(
        f2t[...], sums[...], width, output[...], weighted[...], mixed[...], up_slope[...], silu[...],
        both(qo, qx),
    )
    send_pieces(chips, gate, up, down, *outs)
    own = gate_back.shape[1]
    gate_back[...], up_back[...] = gb[:, :own], ub[:, :own]


def query_kernel(gate_back, up_back, f1t, f3t, out):
    out[...] = (tn(gate_back[...], f1t[...]) + tn(up_back[...], f3t[...])).astype(BF16)


def second_kernel(chips, *refs):
    pieces, refs = refs[:2], refs[2:]
    ko, kx, push, up_slope, silu, back_slope, back_curve = refs[:7]
    c1t, c3t, c2t, dbb_ref, upb_ref, gpb_ref = refs[7:13]
    outs, (gate, up, down) = refs[13:15], refs[15:]
    place_pieces(chips, *pieces, c1t, c3t, c2t)
    dbb, upb, gpb, gate[...], up[...], down[...] = second_adjoint(
        c1t[...], c3t[...], c2t[...], both(ko, kx), push[...],
        up_slope[...], silu[...], back_slope[...], back_curve[...],
    )
    send_pieces(chips, gate, up, down, *outs)
    own = dbb_ref.shape[1]
    dbb_ref[...], upb_ref[...], gpb_ref[...] = dbb[:, :own], upb[:, :own], gpb[:, :own]


def token_grads(rates, mixed, dbb, upb, gpb, gate_back, up_back, c1t, c3t, c2t, w1, w3, w2):
    value_grad = (rates * (nn(c2t, mixed) + tn(w2, dbb))).T.astype(BF16)
    key_total = tn(gate_back, c1t) + tn(up_back, c3t) + tn(gpb, w1.T) + tn(upb, w3.T)
    return value_grad, (-key_total).astype(BF16)


def token_kernel(*refs):
    value_grad, key_grad = refs[-2:]
    value_grad[...], key_grad[...] = token_grads(*(r[...] for r in refs[:-2]))


def call(kernel, outs, args, scratch=(), name=None, flops=0):
    vmem = pl.BlockSpec(memory_space=pltpu.VMEM)
    return pl.pallas_call(
        kernel,
        out_shape=[jax.ShapeDtypeStruct(s, t) for s, t in outs],
        in_specs=[vmem] * len(args),
        out_specs=[vmem] * len(outs),
        scratch_shapes=[pltpu.VMEM(s, t) for s, t in scratch],
        compiler_params=pltpu.CompilerParams(vmem_limit_bytes=VMEM_LIMIT),
        cost_estimate=pl.CostEstimate(
            flops=flops,
            bytes_accessed=sum(a.size * a.dtype.itemsize for a in args),
            transcendentals=0,
        ),
        name=name,
    )(*args)


def over_chips(blocks, count):
    groups = [list(range(core, count, CORES)) for core in range(CORES)]
    return lax.all_to_all(blocks, "tok", 0, 0, axis_index_groups=groups, tiled=True)


def gather(copies, count):
    mine = over_chips(copies, count)
    return mine, lax.ppermute(mine, "tok", core_perm(count))


def head_sum(part, heads):
    total = part
    for step in range(1, heads):
        total = total + lax.ppermute(part, "head", [(h, (h + step) % heads) for h in range(heads)])
    return total


def sliced_pieces(gate, up, down, tok, count):
    g, d = gate.shape[0] // count, down.shape[0] // count
    rows = lambda x, size, t: lax.dynamic_slice_in_dim(x, t * size, size, 0)
    piece = lambda t: pack(rows(gate, g, t), rows(up, g, t), rows(down, d, t))
    sent = [piece(t + tok % CORES) for t in range(0, count, CORES)]
    return piece(tok), jnp.concatenate(sent, axis=0).astype(BF16)


def total_of(own, got, tok):
    blocks = got.reshape((-1,) + own.shape)
    chip = lax.broadcasted_iota(jnp.int32, (blocks.shape[0], 1, 1), 0)
    others = jnp.where(chip == tok // CORES, 0.0, blocks.astype(F32))
    return own + jnp.sum(others, axis=0)


def whole_matrices(mine, other, tok, count, fh):
    shape = (count // CORES, -1, mine.shape[1])
    pair = jnp.stack([mine.reshape(shape), other.reshape(shape)], axis=1)
    pair = jnp.where(tok % CORES == 0, pair, pair[:, ::-1])
    held = pair.reshape((count, -1, mine.shape[1]))
    parts = jax.vmap(lambda x: unpack(x, fh))(held)
    return tuple(x.reshape((-1, x.shape[-1])) for x in parts)


def per_device(
    query_input,
    key_input,
    value_input,
    out_grad,
    token_rates,
    out_gain,
    gate_prior,
    up_prior,
    down_prior,
):
    count, heads = lax.axis_size("tok"), lax.axis_size("head")
    tok = lax.axis_index("tok")
    chips = count // CORES
    own, dh = key_input.shape
    n = own * CORES
    w1, w3, w2 = gate_prior[0], up_prior[0], down_prior[0]
    fh = w2.shape[0]
    g, d = fh // count, dh // count
    tiled = g % ROW_TILE == 0 and d % g == 0 and dh // g == fh // g * (d // g)
    rates = token_rates.T
    gain = out_gain[None, :]
    product = 2 * n * dh * fh
    owner = ((3 * g * chips, dh), BF16), ((3 * g, dh), F32)

    pair = lambda x: lax.ppermute(x, "tok", core_perm(count))
    key_other, value_other, rate_other = pair(key_input), pair(value_input), pair(rates)
    messages = [((3 * g, dh), F32), ((3 * g * chips, dh), BF16)]
    matrices = [((fh, dh), BF16), ((fh, dh), BF16), ((dh, fh), BF16)]
    sums_scratch = [((fh, dh), F32), ((fh, dh), F32), ((dh, fh), F32)]
    hidden = ((fh, n), F32)
    own_hidden = ((fh, own), BF16)
    joined = lambda a, b, axis=0: jnp.concatenate([a, b], axis=axis)

    inputs = (
        key_input, key_other, value_input, value_other, rates, rate_other, w1, w3, w2,
    )
    if tiled:
        pieces = call(
            functools.partial(update_kernel, chips),
            messages,
            inputs,
            sums_scratch,
            "update",
            6 * product,
        )
        query_later, grad_later, *pieces = lax.optimization_barrier(
            (query_input, out_grad, *pieces)
        )
        query_other, grad_other = pair(query_later), pair(grad_later)
        push, up_slope, silu, back_slope, back_curve, mixed, gate_back, up_back, weighted, prior = call(
            functools.partial(saved_kernel, chips),
            [((dh, n), BF16)] + [hidden] * 4 + [own_hidden] * 3 + [((dh, n), F32), owner[1]],
            (*inputs, out_grad, grad_other, gain),
            sums_scratch,
            "saved",
            3 * product,
        )
    else:
        query_other, grad_other = pair(query_input), pair(out_grad)
        keys = joined(key_input, key_other)
        queries = joined(query_input, query_other)
        push = push_of(joined(rates, rate_other, 1), joined(value_input, value_other))
        up_pre, silu, slope, curvature, mixed, down_back, back_slope, gate_back, up_back = (
            update_forward(w1.T, w3.T, w2, keys, push)
        )
        up_slope, back_curve = up_pre * slope, down_back * up_pre * curvature
        weighted = (joined(out_grad, grad_other).astype(F32) * gain).T
        pieces = sliced_pieces(nn(gate_back, keys), nn(up_back, keys), nt(push, mixed), tok, count)
        mixed, gate_back, up_back = mixed[:, :own], gate_back[:, :own], up_back[:, :own]
        prior = pack(
            *(
                lax.dynamic_slice_in_dim(x, tok * rows, rows, 0).astype(F32)
                for x, rows in ((w1.T, g), (w3.T, g), (w2.T, d))
            )
        )
    pieces = pieces[0], over_chips(pieces[1], count)
    if tiled:
        fast, moved = call(
            functools.partial(owner_forward_kernel, fh), owner, (prior, *pieces), name="owner_forward"
        )
    else:
        fast, moved = owner_forward(prior, total_of(*pieces, tok), fh)
        fast = jnp.tile(fast, (chips, 1))
    pieces = gather(fast, count)

    if tiled:
        f1t, f3t, f2t, output, q_mixed, q_slope, q_silu, part = call(
            functools.partial(apply_kernel, chips),
            matrices + [((dh, n), F32), ((fh, n), BF16), hidden, hidden, ((2, n), F32)],
            (*pieces, query_input, query_other, weighted),
            name="apply",
            flops=3 * product,
        )
    else:
        f1t, f3t, f2t = whole_matrices(*pieces, tok, count, fh)
        output, q_mixed, q_slope, q_silu, part = apply_forward(f1t, f3t, f2t, queries, weighted)
    sums = head_sum(part, heads)
    if tiled:
        q_gate_back, q_up_back, *pieces = call(
            functools.partial(back_kernel, chips, heads),
            [own_hidden] * 2 + messages,
            (sums, f2t, output, weighted, q_mixed, q_slope, q_silu, query_input, query_other),
            sums_scratch,
            "apply_back",
            4 * product,
        )
        (query_grad,) = call(
            query_kernel,
            [((own, dh), BF16)],
            (q_gate_back, q_up_back, f1t, f3t),
            name="query_grad",
            flops=product,
        )
    else:
        q_gate_back, q_up_back, *grads = apply_backward(
            f2t, sums, heads * dh, output, weighted, q_mixed, q_slope, q_silu, queries
        )
        pieces = sliced_pieces(*grads, tok, count)
        query_grad = (tn(q_gate_back[:, :own], f1t) + tn(q_up_back[:, :own], f3t)).astype(BF16)
    pieces = pieces[0], over_chips(pieces[1], count)
    if tiled:
        cotangent, owned = call(
            functools.partial(owner_backward_kernel, fh),
            owner,
            (prior, moved, *pieces),
            name="owner_backward",
        )
    else:
        cotangent, owned = owner_backward(prior, moved, total_of(*pieces, tok), fh)
        cotangent = jnp.tile(cotangent, (chips, 1))
    pieces = gather(cotangent, count)

    if tiled:
        c1t, c3t, c2t, dbb, upb, gpb, *pieces = call(
            functools.partial(second_kernel, chips),
            matrices + [own_hidden] * 3 + messages,
            (*pieces, key_input, key_other, push, up_slope, silu, back_slope, back_curve),
            sums_scratch,
            "second_adjoint",
            6 * product,
        )
    else:
        c1t, c3t, c2t = whole_matrices(*pieces, tok, count, fh)
        dbb, upb, gpb, *bars = second_adjoint(
            c1t, c3t, c2t, keys, push, up_slope, silu, back_slope, back_curve
        )
        pieces = sliced_pieces(*bars, tok, count)
        dbb, upb, gpb = dbb[:, :own], upb[:, :own], gpb[:, :own]
    token_args = (
        rates, mixed, dbb, upb, gpb, gate_back, up_back, c1t, c3t, c2t, w1, w3, w2,
    )
    if tiled:
        value_grad, key_grad = call(
            token_kernel, [((own, dh), BF16)] * 2, token_args, name="token_grads", flops=3 * product
        )
    else:
        value_grad, key_grad = token_grads(*token_args)
    pieces = pieces[0], over_chips(pieces[1], count)
    if tiled:
        results = call(
            functools.partial(owner_result_kernel, fh),
            [((g, dh), F32)] * 2 + [((d, fh), F32)],
            (owned, *pieces),
            name="owner_result",
        )
    else:
        results = unpack(owned - total_of(*pieces, tok), fh)
    results = [r.T[None] for r in results]
    return (query_grad, key_grad, value_grad, *results)


def solution(mesh):
    tokens = P("tok", "head")
    in_specs = (tokens,) * 5 + (P("head"),) + (P("head", None, None),) * 3
    out_specs = (tokens,) * 3 + (P("head", None, "tok"),) * 3
    return jax.shard_map(
        per_device, mesh=mesh, in_specs=in_specs, out_specs=out_specs, check_vma=False
    )
```

```python
import functools

import jax
import jax.numpy as jnp
from jax import lax
from jax.experimental import pallas as pl
from jax.experimental.pallas import tpu as pltpu
from jax.sharding import PartitionSpec as P

EPSILON = 1e-06
CORES = 2
ROW_TILE = 16
VMEM_LIMIT = 24 * 1024 * 1024
BF16, F32 = jnp.bfloat16, jnp.float32


def nn(a, b):
    return lax.dot_general(a, b, (((1,), (0,)), ((), ())), preferred_element_type=F32)


def nt(a, b):
    return lax.dot_general(a, b, (((1,), (1,)), ((), ())), preferred_element_type=F32)


def tn(a, b):
    return lax.dot_general(a, b, (((0,), (0,)), ((), ())), preferred_element_type=F32)


def silu_parts(hidden):
    sigmoid_value = jax.nn.sigmoid(hidden)
    silu_value = hidden * sigmoid_value
    silu_slope = sigmoid_value * (1.0 + hidden * (1.0 - sigmoid_value))
    curvature = sigmoid_value * (1.0 - sigmoid_value) * (2.0 + hidden * (1.0 - 2.0 * sigmoid_value))
    return silu_value, silu_slope, curvature


def partner(index, step, count):
    return index ^ step if count & (count - 1) == 0 else (index + step) % count


def source(index, step, count):
    return index ^ step if count & (count - 1) == 0 else (index + count - step) % count


def chip_perm(count, step):
    chips = count // CORES
    return [(t, partner(t // CORES, step, chips) * CORES + t % CORES) for t in range(count)]


def core_perm(count):
    return [(t, t ^ 1) for t in range(count)]


def pack(gate, up, down):
    folds = gate.shape[1] // down.shape[1]
    rows = down.shape[0] // folds
    down = jnp.concatenate([down[i * rows : (i + 1) * rows] for i in range(folds)], axis=1)
    return jnp.concatenate([gate, up, down], axis=0)


def unpack(packed, fh):
    g = packed.shape[0] // 3
    folds = packed.shape[1] // fh
    down = packed[2 * g :]
    down = jnp.concatenate([down[:, i * fh : (i + 1) * fh] for i in range(folds)], axis=0)
    return packed[:g], packed[g : 2 * g], down


def update_forward(w1t, w3t, w2, keys, push):
    gate_pre, up_pre = nt(w1t, keys), nt(w3t, keys)
    silu, slope, curvature = silu_parts(gate_pre)
    mixed = (silu * up_pre).astype(BF16)
    down_back = nn(w2, push)
    back_slope = down_back * slope
    gate_back = (down_back * up_pre * slope).astype(BF16)
    up_back = (down_back * silu).astype(BF16)
    return up_pre, silu, slope, curvature, mixed, down_back, back_slope, gate_back, up_back


def apply_forward(f1t, f3t, f2t, queries, weighted):
    q_gate, q_up = nt(f1t, queries), nt(f3t, queries)
    silu, slope, _ = silu_parts(q_gate)
    mixed = (silu * q_up).astype(BF16)
    output = nn(f2t, mixed)
    square = jnp.sum(output * output, axis=0, keepdims=True)
    dot = jnp.sum(weighted * output, axis=0, keepdims=True)
    return output, mixed, q_up * slope, silu, jnp.concatenate([square, dot], axis=0)


def apply_backward(f2t, sums, full_width, output, weighted, mixed, up_slope, silu, queries):
    inverse = lax.rsqrt(sums[0:1] / full_width + EPSILON)
    scale = inverse * inverse * inverse * sums[1:2] / full_width
    out_back = (inverse * weighted - output * scale).astype(BF16)
    q_back = tn(f2t, out_back)
    gate_back = (q_back * up_slope).astype(BF16)
    up_back = (q_back * silu).astype(BF16)
    return gate_back, up_back, nn(gate_back, queries), nn(up_back, queries), nt(out_back, mixed)


def second_adjoint(c1t, c3t, c2t, keys, push, up_slope, silu, back_slope, back_curve):
    gate_bar, up_bar, mixed_bar = nt(c1t, keys), nt(c3t, keys), tn(c2t, push)
    down_back_bar = (gate_bar * up_slope + up_bar * silu).astype(BF16)
    up_pre_bar = (gate_bar * back_slope + mixed_bar * silu).astype(BF16)
    gate_pre_bar = (up_bar * back_slope + mixed_bar * up_slope + gate_bar * back_curve).astype(BF16)
    return (
        down_back_bar,
        up_pre_bar,
        gate_pre_bar,
        nn(gate_pre_bar, keys),
        nn(up_pre_bar, keys),
        nt(push, down_back_bar),
    )


def folds_of(rows, folds):
    width = rows.shape[1] // folds
    return [rows[:, i * width : (i + 1) * width] for i in range(folds)]


def norm_of(rows):
    return jnp.sqrt(jnp.sum(rows * rows, axis=1, keepdims=True) + EPSILON)


def owner_forward(prior, update, folds):
    moved = prior - update
    fast = [
        m * (norm_of(p) / norm_of(m)) for p, m in zip(folds_of(prior, folds), folds_of(moved, folds))
    ]
    return jnp.concatenate(fast, axis=1).astype(BF16), moved


def owner_backward(prior, moved, fast_grad, folds):
    cotangent, owned = [], []
    for p, m, fg in zip(*(folds_of(x, folds) for x in (prior, moved, fast_grad))):
        prior_norm, moved_norm = norm_of(p), norm_of(m)
        column_dot = jnp.sum(fg * m, axis=1, keepdims=True)
        moved_grad = (prior_norm / moved_norm) * (fg - m * (column_dot / (moved_norm * moved_norm)))
        cotangent.append(moved_grad)
        owned.append(moved_grad + p * (column_dot / (moved_norm * prior_norm)))
    return jnp.concatenate(cotangent, axis=1).astype(BF16), jnp.concatenate(owned, axis=1)


def push_of(rates, values):
    return (-rates * values.T.astype(F32)).astype(BF16)


def both(own_ref, other_ref, axis=0):
    return jnp.concatenate([own_ref[...], other_ref[...]], axis=axis)


def cut_share(out, ref, chips, folds):
    core = lax.axis_index("tok") % CORES
    rows, width = ref.shape[0] // (chips * CORES), ref.shape[1]
    height = rows // folds
    for chip in range(chips):
        for i in range(folds):
            at = pl.multiple_of((chip * CORES + core) * rows + i * height, height)
            out[chip * height : (chip + 1) * height, i * width : (i + 1) * width] = ref[
                pl.ds(at, height), :
            ].astype(out.dtype)


def place_shares(ref, mine, other, chips, folds):
    core = lax.axis_index("tok") % CORES
    rows, width = ref.shape[0] // (chips * CORES), ref.shape[1]
    height = rows // folds
    for share, c in ((mine, core), (other, 1 - core)):
        for chip in range(chips):
            for i in range(folds):
                at = pl.multiple_of((chip * CORES + c) * rows + i * height, height)
                ref[pl.ds(at, height), :] = share[
                    chip * height : (chip + 1) * height, i * width : (i + 1) * width
                ]


def send_pieces(chips, folds, owned, gate_ref, up_ref, down_ref, outs):
    tok = lax.axis_index("tok")
    chip, core = tok // CORES, tok % CORES
    half = chips // 2
    g, width = gate_ref.shape[0] // (chips * CORES), down_ref.shape[1]
    for step, out in enumerate(outs):
        to = partner(chip, step, chips)
        holds = ((chip == half - 1) & (to < half)) | ((chip == half) & (to >= half))
        first = (to * CORES + core) * g
        for k, ref in enumerate((gate_ref, up_ref, down_ref)):
            if k < 2:
                rows = ref[pl.ds(pl.multiple_of(first, g), g), :]
            else:
                parts = [
                    ref[pl.ds(pl.multiple_of(first * folds + i * g, g), g), :] for i in range(folds)
                ]
                rows = jnp.concatenate(parts, axis=1)
            rest = owned[k][pl.ds(pl.multiple_of(to * g, g), g), :]
            out[k * g : (k + 1) * g] = jnp.where(holds, rest - rows, -rows).astype(out.dtype)


def cut_matrices(chips, folds, gate_ref, up_ref, down_ref, outs):
    for k, ref in enumerate((gate_ref, up_ref, down_ref)):
        folded = folds if k == 2 else 1
        cut_share(outs[k], ref, chips, folded)
        outs[3 + k][...] = outs[k][...].astype(BF16)


def update_kernel(chips, folds, ko, kx, vo, vx, ro, rx, w1t, w3t, w2, *rest):
    outs, (gate, up, down) = rest[:6], rest[6:]
    keys = both(ko, kx)
    push = push_of(both(ro, rx, 1), both(vo, vx))
    *_, mixed, _, _, gate_back, up_back = update_forward(w1t[...], w3t[...], w2[...], keys, push)
    down[...] = nt(push, mixed)
    gate[...] = nn(gate_back, keys)
    up[...] = nn(up_back, keys)
    cut_matrices(chips, folds, gate, up, down, outs)


def saved_kernel(
    chips, folds, ko, kx, vo, vx, ro, rx, w1t, w3t, w2, go, gx, gain,
    push_ref, up_slope_ref, silu_ref, back_slope_ref, back_curve_ref,
    mixed_ref, gate_back_ref, up_back_ref, weighted_ref, p1_ref, p3_ref, p2_ref,
    gate_ref, up_ref, down_ref,
):
    push = push_of(both(ro, rx, 1), both(vo, vx))
    push_ref[...] = push
    up_pre, silu, slope, curvature, mixed, down_back, back_slope, gate_back, up_back = (
        update_forward(w1t[...], w3t[...], w2[...], both(ko, kx), push)
    )
    up_slope_ref[...] = up_pre * slope
    silu_ref[...] = silu
    back_slope_ref[...] = back_slope
    back_curve_ref[...] = down_back * up_pre * curvature
    own = mixed_ref.shape[1]
    mixed_ref[...] = mixed[:, :own]
    gate_back_ref[...] = gate_back[:, :own]
    up_back_ref[...] = up_back[:, :own]
    weighted_ref[...] = (both(go, gx).astype(F32) * gain[...]).T
    gate_ref[...] = w1t[...].astype(F32)
    up_ref[...] = w3t[...].astype(F32)
    down_ref[...] = w2[...].astype(F32).T
    cut_share(p1_ref, gate_ref, chips, 1)
    cut_share(p3_ref, up_ref, chips, 1)
    cut_share(p2_ref, down_ref, chips, folds)


def carry_kernel(own, got, out):
    out[...] = (own[...] + got[...].astype(F32)).astype(BF16)


def owner_forward_kernel(folds, prior, mine, other, fast, moved):
    total = mine[...].astype(F32) + other[...].astype(F32)
    fast[...], moved[...] = owner_forward(prior[...], total, folds)


def owner_backward_kernel(folds, prior, moved, mine, other, cotangent, owned):
    total = mine[...].astype(F32) + other[...].astype(F32)
    cotangent[...], owned[...] = owner_backward(prior[...], moved[...], total, folds)


def owner_result_kernel(folds, own, *refs):
    gate, up, down = refs[-3:]
    total = own[...]
    for piece in refs[:-3]:
        total = total + piece[...].astype(F32)
    g = gate.shape[0]
    gate[...], up[...] = total[:g], total[g : 2 * g]
    for i, rows in enumerate(folds_of(total[2 * g :], folds)):
        down[i * g : (i + 1) * g] = rows


def apply_kernel(chips, folds, *refs):
    pieces, refs = refs[:6], refs[6:]
    qo, qx, weighted, f1t, f3t, f2t, output, mixed, up_slope, silu, sums = refs
    for k, ref in enumerate((f1t, f3t, f2t)):
        place_shares(ref, pieces[k], pieces[3 + k], chips, folds if k == 2 else 1)
    output[...], mixed[...], up_slope[...], silu[...], sums[...] = apply_forward(
        f1t[...], f3t[...], f2t[...], both(qo, qx), weighted[...]
    )


def back_kernel(chips, folds, heads, *refs):
    parts, refs = refs[:heads], refs[heads:]
    sums = parts[0][...]
    for part in parts[1:]:
        sums = sums + part[...]
    f2t, output, weighted, mixed, up_slope, silu, qo, qx, gate_back, up_back = refs[:10]
    outs, (gate, up, down) = refs[10:16], refs[16:]
    width = heads * output.shape[0]
    gb, ub, gate[...], up[...], down[...] = apply_backward(
        f2t[...], sums, width, output[...], weighted[...], mixed[...], up_slope[...], silu[...],
        both(qo, qx),
    )
    cut_matrices(chips, folds, gate, up, down, outs)
    own = gate_back.shape[1]
    gate_back[...], up_back[...] = gb[:, :own], ub[:, :own]


def query_kernel(gate_back, up_back, f1t, f3t, out):
    out[...] = (tn(gate_back[...], f1t[...]) + tn(up_back[...], f3t[...])).astype(BF16)


def second_kernel(chips, folds, *refs):
    pieces, owned, refs = refs[:6], refs[6:9], refs[9:]
    ko, kx, push, up_slope, silu, back_slope, back_curve = refs[:7]
    c1t, c3t, c2t, dbb_ref, upb_ref, gpb_ref = refs[7:13]
    outs, (gate, up, down) = refs[13 : 13 + chips], refs[13 + chips :]
    for k, ref in enumerate((c1t, c3t, c2t)):
        place_shares(ref, pieces[k], pieces[3 + k], chips, folds if k == 2 else 1)
    dbb, upb, gpb, gate[...], up[...], down[...] = second_adjoint(
        c1t[...], c3t[...], c2t[...], both(ko, kx), push[...],
        up_slope[...], silu[...], back_slope[...], back_curve[...],
    )
    send_pieces(chips, folds, owned, gate, up, down, outs)
    own = dbb_ref.shape[1]
    dbb_ref[...], upb_ref[...], gpb_ref[...] = dbb[:, :own], upb[:, :own], gpb[:, :own]


def token_grads(rates, mixed, dbb, upb, gpb, gate_back, up_back, c1t, c3t, c2t, w1t, w3t, w2):
    value_grad = (rates * (nn(c2t, mixed) + tn(w2, dbb))).T.astype(BF16)
    key_total = tn(gate_back, c1t) + tn(up_back, c3t) + tn(gpb, w1t) + tn(upb, w3t)
    return value_grad, (-key_total).astype(BF16)


def token_kernel(*refs):
    value_grad, key_grad = refs[-2:]
    value_grad[...], key_grad[...] = token_grads(*(r[...] for r in refs[:-2]))


def call(kernel, outs, args, scratch=(), name=None, flops=0):
    vmem = pl.BlockSpec(memory_space=pltpu.VMEM)
    return pl.pallas_call(
        kernel,
        out_shape=[jax.ShapeDtypeStruct(s, t) for s, t in outs],
        in_specs=[vmem] * len(args),
        out_specs=[vmem] * len(outs),
        scratch_shapes=[pltpu.VMEM(s, t) for s, t in scratch],
        compiler_params=pltpu.CompilerParams(vmem_limit_bytes=VMEM_LIMIT),
        cost_estimate=pl.CostEstimate(
            flops=flops,
            bytes_accessed=sum(a.size * a.dtype.itemsize for a in args),
            transcendentals=0,
        ),
        name=name,
    )(*args)


def exchange(pieces, chips):
    count = chips * CORES
    got = [lax.ppermute(pieces[s], "tok", chip_perm(count, s)) for s in reversed(range(1, chips))]
    return [pieces[0], *got]


def between_chips(x, pairs):
    perm = [(a * CORES + c, b * CORES + c) for a, b in pairs for c in range(CORES)]
    return lax.ppermute(x, "tok", perm)


def outer_pairs(chips, hop):
    return [(hop, hop + 1), (chips - 1 - hop, chips - 2 - hop)]


def half_sums(own, own_rounded, chips):
    carried, shape = own_rounded, [(own.shape, BF16)]
    for hop in range(chips // 2 - 1):
        got = between_chips(carried, outer_pairs(chips, hop))
        (carried,) = call(carry_kernel, shape, (own, got), name="carry")
    half = chips // 2
    return carried, between_chips(carried, [(half - 1, half), (half, half - 1)])


def from_inner(x, chip, chips):
    for hop in reversed(range(chips // 2 - 1)):
        pairs = outer_pairs(chips, hop)
        got = between_chips(x, [(b, a) for a, b in pairs])
        x = jnp.where((chip == pairs[0][0]) | (chip == pairs[1][0]), got, x)
    return x, lax.ppermute(x, "tok", core_perm(chips * CORES))


def head_parts(part, heads):
    got = [
        lax.ppermute(part, "head", [(h, partner(h, step, heads)) for h in range(heads)])
        for step in range(1, heads)
    ]
    return [part, *got]


def over_chips(blocks, count):
    groups = [list(range(core, count, CORES)) for core in range(CORES)]
    return lax.all_to_all(blocks, "tok", 0, 0, axis_index_groups=groups, tiled=True)


def gather_blocks(copies, count):
    mine = over_chips(copies, count)
    return mine, lax.ppermute(mine, "tok", core_perm(count))


def sliced_pieces(gate, up, down, tok, count):
    g, d = gate.shape[0] // count, down.shape[0] // count
    rows = lambda x, size, t: lax.dynamic_slice_in_dim(x, t * size, size, 0)
    piece = lambda t: pack(rows(gate, g, t), rows(up, g, t), rows(down, d, t))
    sent = [piece(t + tok % CORES) for t in range(0, count, CORES)]
    return piece(tok), jnp.concatenate(sent, axis=0).astype(BF16)


def total_of(own, got, tok):
    blocks = got.reshape((-1,) + own.shape)
    chip = lax.broadcasted_iota(jnp.int32, (blocks.shape[0], 1, 1), 0)
    others = jnp.where(chip == tok // CORES, 0.0, blocks.astype(F32))
    return own + jnp.sum(others, axis=0)


def whole_matrices(mine, other, tok, count, fh):
    shape = (count // CORES, -1, mine.shape[1])
    pair = jnp.stack([mine.reshape(shape), other.reshape(shape)], axis=1)
    pair = jnp.where(tok % CORES == 0, pair, pair[:, ::-1])
    held = pair.reshape((count, -1, mine.shape[1]))
    parts = jax.vmap(lambda x: unpack(x, fh))(held)
    return tuple(x.reshape((-1, x.shape[-1])) for x in parts)


def packed_owner_forward(prior, update, fh):
    fast, moved = zip(*(owner_forward(p, u, 1) for p, u in zip(unpack(prior, fh), unpack(update, fh))))
    return pack(*fast), pack(*moved)


def packed_owner_backward(prior, moved, fast_grad, fh):
    parts = (unpack(x, fh) for x in (prior, moved, fast_grad))
    cotangent, owned = zip(*(owner_backward(p, m, f, 1) for p, m, f in zip(*parts)))
    return pack(*cotangent), pack(*owned)


def per_device(
    query_input,
    key_input,
    value_input,
    out_grad,
    token_rates,
    out_gain,
    gate_prior,
    up_prior,
    down_prior,
):
    count, heads = lax.axis_size("tok"), lax.axis_size("head")
    tok = lax.axis_index("tok")
    chips, chip = count // CORES, tok // CORES
    own, dh = key_input.shape
    n = own * CORES
    w1, w3, w2 = gate_prior[0], up_prior[0], down_prior[0]
    fh = w2.shape[0]
    g, d = fh // count, dh // count
    rates = token_rates.T
    gain = out_gain[None, :]
    inputs = query_input, key_input, value_input, out_grad, rates, gain, w1, w3, w2

    if g % ROW_TILE or d % g or dh * g != fh * d or chips % 2:
        query_grad, key_grad, value_grad, *results = by_blocks(inputs, tok, count, heads)
    else:
        query_grad, key_grad, value_grad, *results = by_line(inputs, chip, chips, heads)
    return (query_grad, key_grad, value_grad, *(r.T[None] for r in results))


def by_line(inputs, chip, chips, heads):
    query_input, key_input, value_input, out_grad, rates, gain, w1, w3, w2 = inputs
    count = chips * CORES
    own, dh = key_input.shape
    n, fh = own * CORES, w2.shape[0]
    g, d, folds = fh // count, dh // count, dh // fh
    w1t, w3t = w1.T, w3.T
    product = 2 * n * dh * fh

    share = (g * chips, dh)
    share_sums = [(share, F32)] * 3 + [(share, BF16)] * 3
    matrices = [((fh, dh), BF16), ((fh, dh), BF16), ((dh, fh), BF16)]
    sums_scratch = [((fh, dh), F32), ((fh, dh), F32), ((dh, fh), F32)]
    hidden = ((fh, n), F32)
    own_hidden = ((fh, own), BF16)
    folds_by_matrix = (1, 1, folds)

    pair = lambda x: lax.ppermute(x, "tok", core_perm(count))
    key_other, value_other, rate_other = pair(key_input), pair(value_input), pair(rates)
    keys_values = (
        key_input, key_other, value_input, value_other, rates, rate_other, w1t, w3t, w2,
    )
    sums = call(
        functools.partial(update_kernel, chips, folds),
        share_sums,
        keys_values,
        sums_scratch,
        "update",
        6 * product,
    )
    query_later, grad_later, *sums = lax.optimization_barrier((query_input, out_grad, *sums))
    query_other, grad_other = pair(query_later), pair(grad_later)
    *saved, weighted, p1, p3, p2 = call(
        functools.partial(saved_kernel, chips, folds),
        [((dh, n), BF16)] + [hidden] * 4 + [own_hidden] * 3 + [((dh, n), F32)] + [(share, F32)] * 3,
        (*keys_values, out_grad, grad_other, gain),
        sums_scratch,
        "saved",
        3 * product,
    )
    push, up_slope, silu, back_slope, back_curve, mixed, gate_back, up_back = saved
    priors = p1, p3, p2

    fast, moved = [], []
    for k in range(3):
        mine, other = half_sums(sums[k], sums[3 + k], chips)
        rows, rows_moved = call(
            functools.partial(owner_forward_kernel, folds_by_matrix[k]),
            [(share, BF16), (share, F32)],
            (priors[k], mine, other),
            name="owner_forward",
        )
        moved.append(rows_moved)
        fast.append(from_inner(rows, chip, chips))
    f1t, f3t, f2t, output, q_mixed, q_slope, q_silu, part = call(
        functools.partial(apply_kernel, chips, folds),
        matrices + [((dh, n), F32), ((fh, n), BF16), hidden, hidden, ((2, n), F32)],
        (*(f[0] for f in fast), *(f[1] for f in fast), query_input, query_other, weighted),
        name="apply",
        flops=3 * product,
    )
    q_gate_back, q_up_back, *sums = call(
        functools.partial(back_kernel, chips, folds, heads),
        [own_hidden] * 2 + share_sums,
        (
            *head_parts(part, heads),
            f2t, output, weighted, q_mixed, q_slope, q_silu, query_input, query_other,
        ),
        sums_scratch,
        "apply_back",
        4 * product,
    )
    (query_grad,) = call(
        query_kernel,
        [((own, dh), BF16)],
        (q_gate_back, q_up_back, f1t, f3t),
        name="query_grad",
        flops=product,
    )

    cotangent, owned = [], []
    for k in range(3):
        mine, other = half_sums(sums[k], sums[3 + k], chips)
        rows, rows_owned = call(
            functools.partial(owner_backward_kernel, folds_by_matrix[k]),
            [(share, BF16), (share, F32)],
            (priors[k], moved[k], mine, other),
            name="owner_backward",
        )
        owned.append(rows_owned)
        cotangent.append(from_inner(rows, chip, chips))
    c1t, c3t, c2t, dbb, upb, gpb, *pieces = call(
        functools.partial(second_kernel, chips, folds),
        matrices + [own_hidden] * 3 + [((3 * g, dh), F32)] + [((3 * g, dh), BF16)] * (chips - 1),
        (
            *(c[0] for c in cotangent), *(c[1] for c in cotangent), *owned,
            key_input, key_other, push, up_slope, silu, back_slope, back_curve,
        ),
        sums_scratch,
        "second_adjoint",
        6 * product,
    )
    value_grad, key_grad = call(
        token_kernel,
        [((own, dh), BF16)] * 2,
        (rates, mixed, dbb, upb, gpb, gate_back, up_back, c1t, c3t, c2t, w1t, w3t, w2),
        name="token_grads",
        flops=3 * product,
    )
    results = call(
        functools.partial(owner_result_kernel, folds),
        [((g, dh), F32)] * 2 + [((d, fh), F32)],
        exchange(pieces, chips),
        name="owner_result",
    )
    return query_grad, key_grad, value_grad, *results


def by_blocks(inputs, tok, count, heads):
    query_input, key_input, value_input, out_grad, rates, gain, w1, w3, w2 = inputs
    own, dh = key_input.shape
    fh, chips = w2.shape[0], count // CORES
    g, d = fh // count, dh // count
    w1t, w3t = w1.T, w3.T
    pair = lambda x, axis=0: jnp.concatenate(
        [x, lax.ppermute(x, "tok", core_perm(count))], axis=axis
    )
    keys, values, queries, rate = pair(key_input), pair(value_input), pair(query_input), pair(rates, 1)
    weighted = (pair(out_grad).astype(F32) * gain).T
    push = push_of(rate, values)
    up_pre, silu, slope, curvature, mixed, down_back, back_slope, gate_back, up_back = (
        update_forward(w1t, w3t, w2, keys, push)
    )
    up_slope, back_curve = up_pre * slope, down_back * up_pre * curvature
    piece, sent = sliced_pieces(
        nn(gate_back, keys), nn(up_back, keys), nt(push, mixed), tok, count
    )
    prior = pack(
        *(
            lax.dynamic_slice_in_dim(x, tok * rows, rows, 0).astype(F32)
            for x, rows in ((w1t, g), (w3t, g), (w2.T, d))
        )
    )
    update = total_of(piece, over_chips(sent, count), tok)
    fast, moved = packed_owner_forward(prior, update, fh)
    blocks = gather_blocks(jnp.tile(fast, (chips, 1)), count)
    f1t, f3t, f2t = whole_matrices(*blocks, tok, count, fh)
    output, q_mixed, q_slope, q_silu, part = apply_forward(f1t, f3t, f2t, queries, weighted)
    sums = lax.psum(part, "head")
    q_gate_back, q_up_back, *grads = apply_backward(
        f2t, sums, heads * dh, output, weighted, q_mixed, q_slope, q_silu, queries
    )
    piece, sent = sliced_pieces(*grads, tok, count)
    query_grad = (tn(q_gate_back[:, :own], f1t) + tn(q_up_back[:, :own], f3t)).astype(BF16)
    fast_grad = total_of(piece, over_chips(sent, count), tok)
    cotangent, owned = packed_owner_backward(prior, moved, fast_grad, fh)
    blocks = gather_blocks(jnp.tile(cotangent, (chips, 1)), count)
    c1t, c3t, c2t = whole_matrices(*blocks, tok, count, fh)
    dbb, upb, gpb, *bars = second_adjoint(
        c1t, c3t, c2t, keys, push, up_slope, silu, back_slope, back_curve
    )
    piece, sent = sliced_pieces(*bars, tok, count)
    value_grad, key_grad = token_grads(
        rates, mixed[:, :own], dbb[:, :own], upb[:, :own], gpb[:, :own],
        gate_back[:, :own], up_back[:, :own], c1t, c3t, c2t, w1t, w3t, w2,
    )
    results = unpack(owned - total_of(piece, over_chips(sent, count), tok), fh)
    return query_grad, key_grad, value_grad, *results


def solution(mesh):
    tokens = P("tok", "head")
    in_specs = (tokens,) * 5 + (P("head"),) + (P("head", None, None),) * 3
    out_specs = (tokens,) * 3 + (P("head", None, "tok"),) * 3
    return jax.shard_map(
        per_device, mesh=mesh, in_specs=in_specs, out_specs=out_specs, check_vma=False
    )
```

```python
import functools

import jax
import jax.numpy as jnp
from jax import lax
from jax.experimental import pallas as pl
from jax.experimental.pallas import tpu as pltpu
from jax.sharding import PartitionSpec as P

EPSILON = 1e-06
CORES = 2
ROW_TILE = 16
VMEM_LIMIT = 16 * 1024 * 1024
BF16, F32 = jnp.bfloat16, jnp.float32


def nn(a, b):
    return lax.dot_general(a, b, (((1,), (0,)), ((), ())), preferred_element_type=F32)


def nt(a, b):
    return lax.dot_general(a, b, (((1,), (1,)), ((), ())), preferred_element_type=F32)


def tn(a, b):
    return lax.dot_general(a, b, (((0,), (0,)), ((), ())), preferred_element_type=F32)


def silu_parts(hidden):
    sigmoid_value = jax.nn.sigmoid(hidden)
    silu_value = hidden * sigmoid_value
    silu_slope = sigmoid_value * (1.0 + hidden * (1.0 - sigmoid_value))
    curvature = sigmoid_value * (1.0 - sigmoid_value) * (2.0 + hidden * (1.0 - 2.0 * sigmoid_value))
    return silu_value, silu_slope, curvature


def partner(index, step, count):
    return index ^ step if count & (count - 1) == 0 else (index + step) % count


def source(index, step, count):
    return index ^ step if count & (count - 1) == 0 else (index + count - step) % count


def chip_perm(count, step):
    chips = count // CORES
    return [(t, partner(t // CORES, step, chips) * CORES + t % CORES) for t in range(count)]


def core_perm(count):
    return [(t, t ^ 1) for t in range(count)]


def pack(gate, up, down):
    folds = gate.shape[1] // down.shape[1]
    rows = down.shape[0] // folds
    down = jnp.concatenate([down[i * rows : (i + 1) * rows] for i in range(folds)], axis=1)
    return jnp.concatenate([gate, up, down], axis=0)


def unpack(packed, fh):
    g = packed.shape[0] // 3
    folds = packed.shape[1] // fh
    down = packed[2 * g :]
    down = jnp.concatenate([down[:, i * fh : (i + 1) * fh] for i in range(folds)], axis=0)
    return packed[:g], packed[g : 2 * g], down


def update_forward(w1t, w3t, w2, keys, push):
    gate_pre, up_pre = nt(w1t, keys), nt(w3t, keys)
    silu, slope, curvature = silu_parts(gate_pre)
    mixed = (silu * up_pre).astype(BF16)
    down_back = nn(w2, push)
    back_slope = down_back * slope
    gate_back = (down_back * up_pre * slope).astype(BF16)
    up_back = (down_back * silu).astype(BF16)
    return up_pre, silu, slope, curvature, mixed, down_back, back_slope, gate_back, up_back


def apply_forward(f1t, f3t, f2t, queries, weighted):
    q_gate, q_up = nt(f1t, queries), nt(f3t, queries)
    silu, slope, _ = silu_parts(q_gate)
    mixed = (silu * q_up).astype(BF16)
    output = nn(f2t, mixed)
    square = jnp.sum(output * output, axis=0, keepdims=True)
    dot = jnp.sum(weighted * output, axis=0, keepdims=True)
    return output, mixed, q_up * slope, silu, jnp.concatenate([square, dot], axis=0)


def apply_backward(f2t, sums, full_width, output, weighted, mixed, up_slope, silu, queries):
    inverse = lax.rsqrt(sums[0:1] / full_width + EPSILON)
    scale = inverse * inverse * inverse * sums[1:2] / full_width
    out_back = (inverse * weighted - output * scale).astype(BF16)
    q_back = tn(f2t, out_back)
    gate_back = (q_back * up_slope).astype(BF16)
    up_back = (q_back * silu).astype(BF16)
    return gate_back, up_back, nn(gate_back, queries), nn(up_back, queries), nt(out_back, mixed)


def second_adjoint(c1t, c3t, c2t, keys, push, up_slope, silu, back_slope, back_curve):
    gate_bar, up_bar, mixed_bar = nt(c1t, keys), nt(c3t, keys), tn(c2t, push)
    down_back_bar = (gate_bar * up_slope + up_bar * silu).astype(BF16)
    up_pre_bar = (gate_bar * back_slope + mixed_bar * silu).astype(BF16)
    gate_pre_bar = (up_bar * back_slope + mixed_bar * up_slope + gate_bar * back_curve).astype(BF16)
    return (
        down_back_bar,
        up_pre_bar,
        gate_pre_bar,
        nn(gate_pre_bar, keys),
        nn(up_pre_bar, keys),
        nt(push, down_back_bar),
    )


def folds_of(rows, folds):
    width = rows.shape[1] // folds
    return [rows[:, i * width : (i + 1) * width] for i in range(folds)]


def norm_of(rows):
    return jnp.sqrt(jnp.sum(rows * rows, axis=1, keepdims=True) + EPSILON)


def owner_forward(prior, update, folds):
    moved = prior - update
    fast = [
        m * (norm_of(p) / norm_of(m)) for p, m in zip(folds_of(prior, folds), folds_of(moved, folds))
    ]
    return jnp.concatenate(fast, axis=1).astype(BF16), moved


def owner_backward(prior, moved, fast_grad, folds):
    cotangent, owned = [], []
    for p, m, fg in zip(*(folds_of(x, folds) for x in (prior, moved, fast_grad))):
        prior_norm, moved_norm = norm_of(p), norm_of(m)
        column_dot = jnp.sum(fg * m, axis=1, keepdims=True)
        moved_grad = (prior_norm / moved_norm) * (fg - m * (column_dot / (moved_norm * moved_norm)))
        cotangent.append(moved_grad)
        owned.append(moved_grad + p * (column_dot / (moved_norm * prior_norm)))
    return jnp.concatenate(cotangent, axis=1).astype(BF16), jnp.concatenate(owned, axis=1)


def update_sums(w1t, w3t, w2, keys, rates, values):
    push = push_of(rates, values)
    *_, mixed, _, _, gate_back, up_back = update_forward(w1t, w3t, w2, keys, push)
    return nn(gate_back, keys), nn(up_back, keys), nt(push, mixed)


def push_of(rates, values):
    return (-rates * values.T.astype(F32)).astype(BF16)


def both(own_ref, other_ref, axis=0):
    return jnp.concatenate([own_ref[...], other_ref[...]], axis=axis)


def rows_of(ref, chip, core, chips, folds, i):
    rows = ref.shape[0] // (chips * CORES)
    height = rows // folds
    return pl.ds(pl.multiple_of((chip * CORES + core) * rows + i * height, height), height)


def cut_half(out, ref, parity, chips, folds):
    core = lax.axis_index("tok") % CORES
    height, width = ref.shape[0] // (chips * CORES * folds), ref.shape[1]
    for k in range(chips // 2):
        for i in range(folds):
            out[k * height : (k + 1) * height, i * width : (i + 1) * width] = ref[
                rows_of(ref, 2 * k + parity, core, chips, folds, i), :
            ].astype(out.dtype)


def place_half(ref, half, parity, core, chips, folds):
    height, width = ref.shape[0] // (chips * CORES * folds), ref.shape[1]
    for k in range(chips // 2):
        for i in range(folds):
            ref[rows_of(ref, 2 * k + parity, core, chips, folds, i), :] = half[
                k * height : (k + 1) * height, i * width : (i + 1) * width
            ]


def place_halves(chips, folds, halves, matrices):
    tok = lax.axis_index("tok")
    parity, core = tok // CORES % 2, tok % CORES
    for k, ref in enumerate(matrices):
        whose = ((parity, core), (1 - parity, core), (parity, 1 - core), (1 - parity, 1 - core))
        for half, (p, c) in zip(halves[4 * k : 4 * k + 4], whose):
            place_half(ref, half, p, c, chips, folds if k == 2 else 1)


def send_pieces(chips, folds, matrices, outs):
    tok = lax.axis_index("tok")
    chip, core = tok // CORES, tok % CORES
    for step, out in enumerate(outs):
        to = partner(chip, step, chips)
        at = 0
        for k, ref in enumerate(matrices):
            folded = folds if k == 2 else 1
            parts = [ref[rows_of(ref, to, core, chips, folded, i), :] for i in range(folded)]
            rows = jnp.concatenate(parts, axis=1).astype(out.dtype)
            out[at : at + rows.shape[0]] = rows
            at += rows.shape[0]


def cut_matrices(chips, folds, matrices, outs):
    parity = lax.axis_index("tok") // CORES % 2
    for k, ref in enumerate(matrices):
        cut_half(outs[k], ref, parity, chips, folds if k == 2 else 1)
        cut_half(outs[3 + k], ref, 1 - parity, chips, folds if k == 2 else 1)


def prep_kernel(keys, values, rates, w1, w3, w2, w1t, w3t, gate, up, down):
    w1t[...], w3t[...] = w1[...].T, w3[...].T
    gate[...], up[...], down[...] = update_sums(
        w1t[...], w3t[...], w2[...], keys[...], rates[...], values[...]
    )


def update_kernel(chips, folds, keys, values, rates, w1t, w3t, w2, own_gate, own_up, own_down, *rest):
    outs, matrices = rest[:6], rest[6:]
    sums = update_sums(w1t[...], w3t[...], w2[...], keys[...], rates[...], values[...])
    for ref, own, total in zip(matrices, (own_gate, own_up, own_down), sums):
        ref[...] = own[...] + total
    cut_matrices(chips, folds, matrices, outs)


def saved_kernel(
    chips, folds, ko, kx, vo, vx, ro, rx, w1t, w3t, w2, go, gx, gain,
    push_ref, up_slope_ref, silu_ref, back_slope_ref, back_curve_ref,
    mixed_ref, gate_back_ref, up_back_ref, weighted_ref, p1_ref, p3_ref, p2_ref,
    gate_ref, up_ref, down_ref,
):
    push = push_of(both(ro, rx, 1), both(vo, vx))
    push_ref[...] = push
    up_pre, silu, slope, curvature, mixed, down_back, back_slope, gate_back, up_back = (
        update_forward(w1t[...], w3t[...], w2[...], both(ko, kx), push)
    )
    up_slope_ref[...] = up_pre * slope
    silu_ref[...] = silu
    back_slope_ref[...] = back_slope
    back_curve_ref[...] = down_back * up_pre * curvature
    own = mixed_ref.shape[1]
    mixed_ref[...] = mixed[:, :own]
    gate_back_ref[...] = gate_back[:, :own]
    up_back_ref[...] = up_back[:, :own]
    weighted_ref[...] = (both(go, gx).astype(F32) * gain[...]).T
    gate_ref[...] = w1t[...].astype(F32)
    up_ref[...] = w3t[...].astype(F32)
    down_ref[...] = w2[...].astype(F32).T
    parity = lax.axis_index("tok") // CORES % 2
    cut_half(p1_ref, gate_ref, parity, chips, 1)
    cut_half(p3_ref, up_ref, parity, chips, 1)
    cut_half(p2_ref, down_ref, parity, chips, folds)


def carry_kernel(own, got, out):
    out[...] = (own[...] + got[...].astype(F32)).astype(BF16)


def total_of_halves(halves):
    total = halves[0][...].astype(F32)
    for half in halves[1:]:
        total = total + half[...].astype(F32)
    return total


def owner_forward_kernel(folds, prior, *refs):
    fast, moved = refs[-2:]
    total = total_of_halves(refs[:-2])
    fast[...], moved[...] = owner_forward(prior[...], total, folds)


def owner_backward_kernel(folds, prior, moved, *refs):
    cotangent, owned = refs[-2:]
    total = total_of_halves(refs[:-2])
    cotangent[...], owned[...] = owner_backward(prior[...], moved[...], total, folds)


def owner_result_kernel(chips, folds, *refs):
    owned, pieces, outs = refs[:3], refs[3:-3], refs[-3:]
    bars = pieces[0][...]
    for piece in pieces[1:]:
        bars = bars + piece[...].astype(F32)
    g = outs[0].shape[0]
    block = lax.axis_index("tok") // (2 * CORES)
    for k, out in enumerate(outs):
        result = owned[k][pl.ds(pl.multiple_of(block * g, g), g), :] - bars[k * g : (k + 1) * g]
        for i, rows in enumerate(folds_of(result, folds if k == 2 else 1)):
            out[i * g : (i + 1) * g] = rows


def apply_kernel(chips, folds, *refs):
    halves, refs = refs[:12], refs[12:]
    qo, qx, weighted, f1t, f3t, f2t, output, mixed, up_slope, silu, sums = refs
    place_halves(chips, folds, halves, (f1t, f3t, f2t))
    output[...], mixed[...], up_slope[...], silu[...], sums[...] = apply_forward(
        f1t[...], f3t[...], f2t[...], both(qo, qx), weighted[...]
    )


def back_kernel(chips, folds, heads, *refs):
    parts, refs = refs[:heads], refs[heads:]
    sums = parts[0][...]
    for part in parts[1:]:
        sums = sums + part[...]
    f2t, output, weighted, mixed, up_slope, silu, qo, qx, gate_back, up_back = refs[:10]
    outs, (gate, up, down) = refs[10:16], refs[16:]
    width = heads * output.shape[0]
    gb, ub, gate[...], up[...], down[...] = apply_backward(
        f2t[...], sums, width, output[...], weighted[...], mixed[...], up_slope[...], silu[...],
        both(qo, qx),
    )
    cut_matrices(chips, folds, (gate, up, down), outs)
    own = gate_back.shape[1]
    gate_back[...], up_back[...] = gb[:, :own], ub[:, :own]


def query_kernel(gate_back, up_back, f1t, f3t, out):
    out[...] = (tn(gate_back[...], f1t[...]) + tn(up_back[...], f3t[...])).astype(BF16)


def second_kernel(chips, folds, *refs):
    halves, refs = refs[:12], refs[12:]
    ko, kx, push, up_slope, silu, back_slope, back_curve = refs[:7]
    c1t, c3t, c2t, dbb_ref, upb_ref, gpb_ref = refs[7:13]
    outs, (gate, up, down) = refs[13 : 13 + chips], refs[13 + chips :]
    place_halves(chips, folds, halves, (c1t, c3t, c2t))
    dbb, upb, gpb, gate[...], up[...], down[...] = second_adjoint(
        c1t[...], c3t[...], c2t[...], both(ko, kx), push[...],
        up_slope[...], silu[...], back_slope[...], back_curve[...],
    )
    send_pieces(chips, folds, (gate, up, down), outs)
    own = dbb_ref.shape[1]
    dbb_ref[...], upb_ref[...], gpb_ref[...] = dbb[:, :own], upb[:, :own], gpb[:, :own]


def token_grads(rates, mixed, dbb, upb, gpb, gate_back, up_back, c1t, c3t, c2t, w1t, w3t, w2):
    value_grad = (rates * (nn(c2t, mixed) + tn(w2, dbb))).T.astype(BF16)
    key_total = tn(gate_back, c1t) + tn(up_back, c3t) + tn(gpb, w1t) + tn(upb, w3t)
    return value_grad, (-key_total).astype(BF16)


def token_kernel(*refs):
    value_grad, key_grad = refs[-2:]
    value_grad[...], key_grad[...] = token_grads(*(r[...] for r in refs[:-2]))


def call(kernel, outs, args, scratch=(), name=None, flops=0):
    vmem = pl.BlockSpec(memory_space=pltpu.VMEM)
    return pl.pallas_call(
        kernel,
        out_shape=[jax.ShapeDtypeStruct(s, t) for s, t in outs],
        in_specs=[vmem] * len(args),
        out_specs=[vmem] * len(outs),
        scratch_shapes=[pltpu.VMEM(s, t) for s, t in scratch],
        compiler_params=pltpu.CompilerParams(vmem_limit_bytes=VMEM_LIMIT),
        cost_estimate=pl.CostEstimate(
            flops=flops,
            bytes_accessed=sum(a.size * a.dtype.itemsize for a in args),
            transcendentals=0,
        ),
        name=name,
    )(*args)


def exchange(pieces, chips):
    count = chips * CORES
    got = [lax.ppermute(pieces[s], "tok", chip_perm(count, s)) for s in reversed(range(1, chips))]
    return [pieces[0], *got]


def to_chip(x, step, chips):
    return lax.ppermute(x, "tok", chip_perm(chips * CORES, step))


def half_sums(kept, given, chips):
    (mine,) = call(carry_kernel, [(given.shape, BF16)], (kept, to_chip(given, 1, chips)), name="carry")
    return [mine, *(to_chip(mine, step, chips) for step in range(2, chips, 2))]


def from_owners(half, chips):
    other = to_chip(half, 1, chips)
    perm = core_perm(chips * CORES)
    return [half, other, lax.ppermute(half, "tok", perm), lax.ppermute(other, "tok", perm)]


def head_parts(part, heads):
    got = [
        lax.ppermute(part, "head", [(h, partner(h, step, heads)) for h in range(heads)])
        for step in range(1, heads)
    ]
    return [part, *got]


def over_chips(blocks, count):
    groups = [list(range(core, count, CORES)) for core in range(CORES)]
    return lax.all_to_all(blocks, "tok", 0, 0, axis_index_groups=groups, tiled=True)


def gather_blocks(copies, count):
    mine = over_chips(copies, count)
    return mine, lax.ppermute(mine, "tok", core_perm(count))


def sliced_pieces(gate, up, down, tok, count):
    g, d = gate.shape[0] // count, down.shape[0] // count
    rows = lambda x, size, t: lax.dynamic_slice_in_dim(x, t * size, size, 0)
    piece = lambda t: pack(rows(gate, g, t), rows(up, g, t), rows(down, d, t))
    sent = [piece(t + tok % CORES) for t in range(0, count, CORES)]
    return piece(tok), jnp.concatenate(sent, axis=0).astype(BF16)


def total_of(own, got, tok):
    blocks = got.reshape((-1,) + own.shape)
    chip = lax.broadcasted_iota(jnp.int32, (blocks.shape[0], 1, 1), 0)
    others = jnp.where(chip == tok // CORES, 0.0, blocks.astype(F32))
    return own + jnp.sum(others, axis=0)


def whole_matrices(mine, other, tok, count, fh):
    shape = (count // CORES, -1, mine.shape[1])
    pair = jnp.stack([mine.reshape(shape), other.reshape(shape)], axis=1)
    pair = jnp.where(tok % CORES == 0, pair, pair[:, ::-1])
    held = pair.reshape((count, -1, mine.shape[1]))
    parts = jax.vmap(lambda x: unpack(x, fh))(held)
    return tuple(x.reshape((-1, x.shape[-1])) for x in parts)


def packed_owner_forward(prior, update, fh):
    fast, moved = zip(*(owner_forward(p, u, 1) for p, u in zip(unpack(prior, fh), unpack(update, fh))))
    return pack(*fast), pack(*moved)


def packed_owner_backward(prior, moved, fast_grad, fh):
    parts = (unpack(x, fh) for x in (prior, moved, fast_grad))
    cotangent, owned = zip(*(owner_backward(p, m, f, 1) for p, m, f in zip(*parts)))
    return pack(*cotangent), pack(*owned)


def per_device(
    query_input,
    key_input,
    value_input,
    out_grad,
    token_rates,
    out_gain,
    gate_prior,
    up_prior,
    down_prior,
):
    count, heads = lax.axis_size("tok"), lax.axis_size("head")
    tok = lax.axis_index("tok")
    chips = count // CORES
    own, dh = key_input.shape
    n = own * CORES
    w1, w3, w2 = gate_prior[0], up_prior[0], down_prior[0]
    fh = w2.shape[0]
    g, d = fh // count, dh // count
    rates = token_rates.T
    gain = out_gain[None, :]
    inputs = query_input, key_input, value_input, out_grad, rates, gain, w1, w3, w2

    if g % ROW_TILE or d % g or dh * g != fh * d or chips & (chips - 1) or chips < 2:
        query_grad, key_grad, value_grad, *results = by_blocks(inputs, tok, count, heads)
    else:
        query_grad, key_grad, value_grad, *results = by_line(inputs, chips, heads)
    return (query_grad, key_grad, value_grad, *(r.T[None] for r in results))


def by_line(inputs, chips, heads):
    query_input, key_input, value_input, out_grad, rates, gain, w1, w3, w2 = inputs
    count = chips * CORES
    own, dh = key_input.shape
    n, fh = own * CORES, w2.shape[0]
    g, d, folds = fh // count, dh // count, dh // fh
    product = 2 * n * dh * fh

    half = (g * chips // 2, dh)
    half_shares = [(half, F32)] * 3 + [(half, BF16)] * 3
    matrices = [((fh, dh), BF16), ((fh, dh), BF16), ((dh, fh), BF16)]
    sums_scratch = [((fh, dh), F32), ((fh, dh), F32), ((dh, fh), F32)]
    hidden = ((fh, n), F32)
    own_hidden = ((fh, own), BF16)
    folds_by_matrix = (1, 1, folds)

    pair = lambda x: lax.ppermute(x, "tok", core_perm(count))
    key_other, value_other, rate_other = pair(key_input), pair(value_input), pair(rates)
    w1t, w3t, *own_sums = call(
        prep_kernel,
        [((fh, dh), BF16)] * 2 + sums_scratch,
        (key_input, value_input, rates, w1, w3, w2),
        name="own_tokens",
        flops=3 * product,
    )
    sums = call(
        functools.partial(update_kernel, chips, folds),
        half_shares,
        (key_other, value_other, rate_other, w1t, w3t, w2, *own_sums),
        sums_scratch,
        "update",
        3 * product,
    )
    keys_values = (
        key_input, key_other, value_input, value_other, rates, rate_other, w1t, w3t, w2,
    )
    query_later, grad_later, *sums = lax.optimization_barrier((query_input, out_grad, *sums))
    query_other, grad_other = pair(query_later), pair(grad_later)
    *saved, weighted, p1, p3, p2 = call(
        functools.partial(saved_kernel, chips, folds),
        [((dh, n), BF16)] + [hidden] * 4 + [own_hidden] * 3 + [((dh, n), F32)] + [(half, F32)] * 3,
        (*keys_values, out_grad, grad_other, gain),
        sums_scratch,
        "saved",
        3 * product,
    )
    push, up_slope, silu, back_slope, back_curve, mixed, gate_back, up_back = saved
    priors = p1, p3, p2

    fast, moved = [], []
    for k in range(3):
        totals = half_sums(sums[k], sums[3 + k], chips)
        rows, rows_moved = call(
            functools.partial(owner_forward_kernel, folds_by_matrix[k]),
            [(half, BF16), (half, F32)],
            (priors[k], *totals),
            name="owner_forward",
        )
        moved.append(rows_moved)
        fast += from_owners(rows, chips)
    f1t, f3t, f2t, output, q_mixed, q_slope, q_silu, part = call(
        functools.partial(apply_kernel, chips, folds),
        matrices + [((dh, n), F32), ((fh, n), BF16), hidden, hidden, ((2, n), F32)],
        (*fast, query_input, query_other, weighted),
        name="apply",
        flops=3 * product,
    )
    q_gate_back, q_up_back, *sums = call(
        functools.partial(back_kernel, chips, folds, heads),
        [own_hidden] * 2 + half_shares,
        (
            *head_parts(part, heads),
            f2t, output, weighted, q_mixed, q_slope, q_silu, query_input, query_other,
        ),
        sums_scratch,
        "apply_back",
        4 * product,
    )
    (query_grad,) = call(
        query_kernel,
        [((own, dh), BF16)],
        (q_gate_back, q_up_back, f1t, f3t),
        name="query_grad",
        flops=product,
    )

    cotangent, owned = [], []
    for k in range(3):
        totals = half_sums(sums[k], sums[3 + k], chips)
        rows, rows_owned = call(
            functools.partial(owner_backward_kernel, folds_by_matrix[k]),
            [(half, BF16), (half, F32)],
            (priors[k], moved[k], *totals),
            name="owner_backward",
        )
        owned.append(rows_owned)
        cotangent += from_owners(rows, chips)
    c1t, c3t, c2t, dbb, upb, gpb, *pieces = call(
        functools.partial(second_kernel, chips, folds),
        matrices + [own_hidden] * 3 + [((3 * g, dh), F32)] + [((3 * g, dh), BF16)] * (chips - 1),
        (
            *cotangent,
            key_input, key_other, push, up_slope, silu, back_slope, back_curve,
        ),
        sums_scratch,
        "second_adjoint",
        6 * product,
    )
    value_grad, key_grad = call(
        token_kernel,
        [((own, dh), BF16)] * 2,
        (rates, mixed, dbb, upb, gpb, gate_back, up_back, c1t, c3t, c2t, w1t, w3t, w2),
        name="token_grads",
        flops=3 * product,
    )
    results = call(
        functools.partial(owner_result_kernel, chips, folds),
        [((g, dh), F32)] * 2 + [((d, fh), F32)],
        (*owned, *exchange(pieces, chips)),
        name="owner_result",
    )
    return query_grad, key_grad, value_grad, *results


def by_blocks(inputs, tok, count, heads):
    query_input, key_input, value_input, out_grad, rates, gain, w1, w3, w2 = inputs
    own, dh = key_input.shape
    fh, chips = w2.shape[0], count // CORES
    g, d = fh // count, dh // count
    w1t, w3t = w1.T, w3.T
    pair = lambda x, axis=0: jnp.concatenate(
        [x, lax.ppermute(x, "tok", core_perm(count))], axis=axis
    )
    keys, values, queries, rate = pair(key_input), pair(value_input), pair(query_input), pair(rates, 1)
    weighted = (pair(out_grad).astype(F32) * gain).T
    push = push_of(rate, values)
    up_pre, silu, slope, curvature, mixed, down_back, back_slope, gate_back, up_back = (
        update_forward(w1t, w3t, w2, keys, push)
    )
    up_slope, back_curve = up_pre * slope, down_back * up_pre * curvature
    piece, sent = sliced_pieces(
        nn(gate_back, keys), nn(up_back, keys), nt(push, mixed), tok, count
    )
    prior = pack(
        *(
            lax.dynamic_slice_in_dim(x, tok * rows, rows, 0).astype(F32)
            for x, rows in ((w1t, g), (w3t, g), (w2.T, d))
        )
    )
    update = total_of(piece, over_chips(sent, count), tok)
    fast, moved = packed_owner_forward(prior, update, fh)
    blocks = gather_blocks(jnp.tile(fast, (chips, 1)), count)
    f1t, f3t, f2t = whole_matrices(*blocks, tok, count, fh)
    output, q_mixed, q_slope, q_silu, part = apply_forward(f1t, f3t, f2t, queries, weighted)
    sums = lax.psum(part, "head")
    q_gate_back, q_up_back, *grads = apply_backward(
        f2t, sums, heads * dh, output, weighted, q_mixed, q_slope, q_silu, queries
    )
    piece, sent = sliced_pieces(*grads, tok, count)
    query_grad = (tn(q_gate_back[:, :own], f1t) + tn(q_up_back[:, :own], f3t)).astype(BF16)
    fast_grad = total_of(piece, over_chips(sent, count), tok)
    cotangent, owned = packed_owner_backward(prior, moved, fast_grad, fh)
    blocks = gather_blocks(jnp.tile(cotangent, (chips, 1)), count)
    c1t, c3t, c2t = whole_matrices(*blocks, tok, count, fh)
    dbb, upb, gpb, *bars = second_adjoint(
        c1t, c3t, c2t, keys, push, up_slope, silu, back_slope, back_curve
    )
    piece, sent = sliced_pieces(*bars, tok, count)
    value_grad, key_grad = token_grads(
        rates, mixed[:, :own], dbb[:, :own], upb[:, :own], gpb[:, :own],
        gate_back[:, :own], up_back[:, :own], c1t, c3t, c2t, w1t, w3t, w2,
    )
    results = unpack(owned - total_of(piece, over_chips(sent, count), tok), fh)
    return query_grad, key_grad, value_grad, *results


def solution(mesh):
    tokens = P("tok", "head")
    in_specs = (tokens,) * 5 + (P("head"),) + (P("head", None, None),) * 3
    out_specs = (tokens,) * 3 + (P("head", None, "tok"),) * 3
    return jax.shard_map(
        per_device, mesh=mesh, in_specs=in_specs, out_specs=out_specs, check_vma=False
    )
```

```python
import functools

import jax
import jax.numpy as jnp
from jax import lax
from jax.experimental import pallas as pl
from jax.experimental.pallas import tpu as pltpu
from jax.sharding import PartitionSpec as P

EPSILON = 1e-06
CORES = 2
ROW_TILE = 16
VMEM_LIMIT = 24 * 1024 * 1024
BF16, F32 = jnp.bfloat16, jnp.float32


def nn(a, b):
    return lax.dot_general(a, b, (((1,), (0,)), ((), ())), preferred_element_type=F32)


def nt(a, b):
    return lax.dot_general(a, b, (((1,), (1,)), ((), ())), preferred_element_type=F32)


def tn(a, b):
    return lax.dot_general(a, b, (((0,), (0,)), ((), ())), preferred_element_type=F32)


def silu_parts(hidden):
    sigmoid_value = jax.nn.sigmoid(hidden)
    silu_value = hidden * sigmoid_value
    silu_slope = sigmoid_value * (1.0 + hidden * (1.0 - sigmoid_value))
    curvature = sigmoid_value * (1.0 - sigmoid_value) * (2.0 + hidden * (1.0 - 2.0 * sigmoid_value))
    return silu_value, silu_slope, curvature


def partner(index, step, count):
    return index ^ step if count & (count - 1) == 0 else (index + step) % count


def source(index, step, count):
    return index ^ step if count & (count - 1) == 0 else (index + count - step) % count


def chip_perm(count, step):
    chips = count // CORES
    return [(t, partner(t // CORES, step, chips) * CORES + t % CORES) for t in range(count)]


def core_perm(count):
    return [(t, t ^ 1) for t in range(count)]


def pack(gate, up, down):
    folds = gate.shape[1] // down.shape[1]
    rows = down.shape[0] // folds
    down = jnp.concatenate([down[i * rows : (i + 1) * rows] for i in range(folds)], axis=1)
    return jnp.concatenate([gate, up, down], axis=0)


def unpack(packed, fh):
    g = packed.shape[0] // 3
    folds = packed.shape[1] // fh
    down = packed[2 * g :]
    down = jnp.concatenate([down[:, i * fh : (i + 1) * fh] for i in range(folds)], axis=0)
    return packed[:g], packed[g : 2 * g], down


def update_forward(w1t, w3t, w2, keys, push):
    gate_pre, up_pre = nt(w1t, keys), nt(w3t, keys)
    silu, slope, curvature = silu_parts(gate_pre)
    mixed = (silu * up_pre).astype(BF16)
    down_back = nn(w2, push)
    back_slope = down_back * slope
    gate_back = (down_back * up_pre * slope).astype(BF16)
    up_back = (down_back * silu).astype(BF16)
    return up_pre, silu, slope, curvature, mixed, down_back, back_slope, gate_back, up_back


def apply_forward(f1t, f3t, f2t, queries, weighted):
    q_gate, q_up = nt(f1t, queries), nt(f3t, queries)
    silu, slope, _ = silu_parts(q_gate)
    mixed = (silu * q_up).astype(BF16)
    output = nn(f2t, mixed)
    square = jnp.sum(output * output, axis=0, keepdims=True)
    dot = jnp.sum(weighted * output, axis=0, keepdims=True)
    return output, mixed, q_up * slope, silu, jnp.concatenate([square, dot], axis=0)


def apply_backward(f2t, sums, full_width, output, weighted, mixed, up_slope, silu, queries):
    inverse = lax.rsqrt(sums[0:1] / full_width + EPSILON)
    scale = inverse * inverse * inverse * sums[1:2] / full_width
    out_back = (inverse * weighted - output * scale).astype(BF16)
    q_back = tn(f2t, out_back)
    gate_back = (q_back * up_slope).astype(BF16)
    up_back = (q_back * silu).astype(BF16)
    return gate_back, up_back, nn(gate_back, queries), nn(up_back, queries), nt(out_back, mixed)


def second_adjoint(c1t, c3t, c2t, keys, push, up_slope, silu, back_slope, back_curve):
    gate_bar, up_bar, mixed_bar = nt(c1t, keys), nt(c3t, keys), tn(c2t, push)
    down_back_bar = (gate_bar * up_slope + up_bar * silu).astype(BF16)
    up_pre_bar = (gate_bar * back_slope + mixed_bar * silu).astype(BF16)
    gate_pre_bar = (up_bar * back_slope + mixed_bar * up_slope + gate_bar * back_curve).astype(BF16)
    return (
        down_back_bar,
        up_pre_bar,
        gate_pre_bar,
        nn(gate_pre_bar, keys),
        nn(up_pre_bar, keys),
        nt(push, down_back_bar),
    )


def folds_of(rows, folds):
    width = rows.shape[1] // folds
    return [rows[:, i * width : (i + 1) * width] for i in range(folds)]


def norm_of(rows):
    return jnp.sqrt(jnp.sum(rows * rows, axis=1, keepdims=True) + EPSILON)


def owner_forward(prior, update, folds):
    moved = prior - update
    fast = [
        m * (norm_of(p) / norm_of(m)) for p, m in zip(folds_of(prior, folds), folds_of(moved, folds))
    ]
    return jnp.concatenate(fast, axis=1).astype(BF16), moved


def owner_backward(prior, moved, fast_grad, folds):
    cotangent, owned = [], []
    for p, m, fg in zip(*(folds_of(x, folds) for x in (prior, moved, fast_grad))):
        prior_norm, moved_norm = norm_of(p), norm_of(m)
        column_dot = jnp.sum(fg * m, axis=1, keepdims=True)
        moved_grad = (prior_norm / moved_norm) * (fg - m * (column_dot / (moved_norm * moved_norm)))
        cotangent.append(moved_grad)
        owned.append(moved_grad + p * (column_dot / (moved_norm * prior_norm)))
    return jnp.concatenate(cotangent, axis=1).astype(BF16), jnp.concatenate(owned, axis=1)


def update_sums(w1t, w3t, w2, keys, rates, values):
    push = push_of(rates, values)
    *_, mixed, _, _, gate_back, up_back = update_forward(w1t, w3t, w2, keys, push)
    return nn(gate_back, keys), nn(up_back, keys), nt(push, mixed)


def push_of(rates, values):
    return (-rates * values.T.astype(F32)).astype(BF16)


def both(own_ref, other_ref, axis=0):
    return jnp.concatenate([own_ref[...], other_ref[...]], axis=axis)


def rows_of(ref, chip, core, chips, folds, i):
    rows = ref.shape[0] // (chips * CORES)
    height = rows // folds
    return pl.ds(pl.multiple_of((chip * CORES + core) * rows + i * height, height), height)


def cut_half(out, ref, parity, chips, folds):
    core = lax.axis_index("tok") % CORES
    height, width = ref.shape[0] // (chips * CORES * folds), ref.shape[1]
    for k in range(chips // 2):
        for i in range(folds):
            out[k * height : (k + 1) * height, i * width : (i + 1) * width] = ref[
                rows_of(ref, 2 * k + parity, core, chips, folds, i), :
            ].astype(out.dtype)


def place_half(ref, half, parity, core, chips, folds):
    height, width = ref.shape[0] // (chips * CORES * folds), ref.shape[1]
    for k in range(chips // 2):
        for i in range(folds):
            ref[rows_of(ref, 2 * k + parity, core, chips, folds, i), :] = half[
                k * height : (k + 1) * height, i * width : (i + 1) * width
            ]


def place_halves(chips, folds, halves, matrices):
    tok = lax.axis_index("tok")
    parity, core = tok // CORES % 2, tok % CORES
    for k, ref in enumerate(matrices):
        whose = ((parity, core), (1 - parity, core), (parity, 1 - core), (1 - parity, 1 - core))
        for half, (p, c) in zip(halves[4 * k : 4 * k + 4], whose):
            place_half(ref, half, p, c, chips, folds if k == 2 else 1)


def send_pieces(chips, folds, matrices, outs):
    tok = lax.axis_index("tok")
    chip, core = tok // CORES, tok % CORES
    for step, out in enumerate(outs):
        to = partner(chip, step, chips)
        at = 0
        for k, ref in enumerate(matrices):
            folded = folds if k == 2 else 1
            parts = [ref[rows_of(ref, to, core, chips, folded, i), :] for i in range(folded)]
            rows = jnp.concatenate(parts, axis=1).astype(out.dtype)
            out[at : at + rows.shape[0]] = rows
            at += rows.shape[0]


def cut_matrices(chips, folds, matrices, outs):
    parity = lax.axis_index("tok") // CORES % 2
    for k, ref in enumerate(matrices):
        cut_half(outs[k], ref, parity, chips, folds if k == 2 else 1)
        cut_half(outs[3 + k], ref, 1 - parity, chips, folds if k == 2 else 1)


def update_kernel(chips, folds, ko, kx, vo, vx, ro, rx, w1t, w3t, w2, *rest):
    outs, matrices = rest[:6], rest[6:]
    sums = update_sums(
        w1t[...], w3t[...], w2[...], both(ko, kx), both(ro, rx, 1), both(vo, vx)
    )
    for ref, total in zip(matrices, sums):
        ref[...] = total
    cut_matrices(chips, folds, matrices, outs)


def saved_kernel(
    chips, folds, ko, kx, vo, vx, ro, rx, w1t, w3t, w2, go, gx, gain,
    push_ref, up_slope_ref, silu_ref, back_slope_ref, back_curve_ref,
    mixed_ref, gate_back_ref, up_back_ref, weighted_ref, p1_ref, p3_ref, p2_ref,
    gate_ref, up_ref, down_ref,
):
    push = push_of(both(ro, rx, 1), both(vo, vx))
    push_ref[...] = push
    up_pre, silu, slope, curvature, mixed, down_back, back_slope, gate_back, up_back = (
        update_forward(w1t[...], w3t[...], w2[...], both(ko, kx), push)
    )
    up_slope_ref[...] = up_pre * slope
    silu_ref[...] = silu
    back_slope_ref[...] = back_slope
    back_curve_ref[...] = down_back * up_pre * curvature
    own = mixed_ref.shape[1]
    mixed_ref[...] = mixed[:, :own]
    gate_back_ref[...] = gate_back[:, :own]
    up_back_ref[...] = up_back[:, :own]
    weighted_ref[...] = (both(go, gx).astype(F32) * gain[...]).T
    gate_ref[...] = w1t[...].astype(F32)
    up_ref[...] = w3t[...].astype(F32)
    down_ref[...] = w2[...].astype(F32).T
    parity = lax.axis_index("tok") // CORES % 2
    cut_half(p1_ref, gate_ref, parity, chips, 1)
    cut_half(p3_ref, up_ref, parity, chips, 1)
    cut_half(p2_ref, down_ref, parity, chips, folds)


def carry_kernel(own, got, out):
    out[...] = (own[...] + got[...].astype(F32)).astype(BF16)


def total_of_halves(halves):
    total = halves[0][...].astype(F32)
    for half in halves[1:]:
        total = total + half[...].astype(F32)
    return total


def owner_forward_kernel(folds, prior, *refs):
    fast, moved = refs[-2:]
    total = total_of_halves(refs[:-2])
    fast[...], moved[...] = owner_forward(prior[...], total, folds)


def owner_backward_kernel(folds, prior, moved, *refs):
    cotangent, owned = refs[-2:]
    total = total_of_halves(refs[:-2])
    cotangent[...], owned[...] = owner_backward(prior[...], moved[...], total, folds)


def owner_result_kernel(chips, folds, *refs):
    owned, pieces, outs = refs[:3], refs[3:-3], refs[-3:]
    bars = pieces[0][...]
    for piece in pieces[1:]:
        bars = bars + piece[...].astype(F32)
    g = outs[0].shape[0]
    block = lax.axis_index("tok") // (2 * CORES)
    for k, out in enumerate(outs):
        result = owned[k][pl.ds(pl.multiple_of(block * g, g), g), :] - bars[k * g : (k + 1) * g]
        for i, rows in enumerate(folds_of(result, folds if k == 2 else 1)):
            out[i * g : (i + 1) * g] = rows


def apply_kernel(chips, folds, *refs):
    halves, refs = refs[:12], refs[12:]
    qo, qx, weighted, f1t, f3t, f2t, output, mixed, up_slope, silu, sums = refs
    place_halves(chips, folds, halves, (f1t, f3t, f2t))
    output[...], mixed[...], up_slope[...], silu[...], sums[...] = apply_forward(
        f1t[...], f3t[...], f2t[...], both(qo, qx), weighted[...]
    )


def back_kernel(chips, folds, heads, *refs):
    parts, refs = refs[:heads], refs[heads:]
    sums = parts[0][...]
    for part in parts[1:]:
        sums = sums + part[...]
    f2t, output, weighted, mixed, up_slope, silu, qo, qx, gate_back, up_back = refs[:10]
    outs, (gate, up, down) = refs[10:16], refs[16:]
    width = heads * output.shape[0]
    gb, ub, gate[...], up[...], down[...] = apply_backward(
        f2t[...], sums, width, output[...], weighted[...], mixed[...], up_slope[...], silu[...],
        both(qo, qx),
    )
    cut_matrices(chips, folds, (gate, up, down), outs)
    own = gate_back.shape[1]
    gate_back[...], up_back[...] = gb[:, :own], ub[:, :own]


def query_kernel(gate_back, up_back, f1t, f3t, out):
    out[...] = (tn(gate_back[...], f1t[...]) + tn(up_back[...], f3t[...])).astype(BF16)


def second_kernel(chips, folds, *refs):
    halves, refs = refs[:12], refs[12:]
    ko, kx, push, up_slope, silu, back_slope, back_curve = refs[:7]
    c1t, c3t, c2t, dbb_ref, upb_ref, gpb_ref = refs[7:13]
    outs, (gate, up, down) = refs[13 : 13 + chips], refs[13 + chips :]
    place_halves(chips, folds, halves, (c1t, c3t, c2t))
    dbb, upb, gpb, gate[...], up[...], down[...] = second_adjoint(
        c1t[...], c3t[...], c2t[...], both(ko, kx), push[...],
        up_slope[...], silu[...], back_slope[...], back_curve[...],
    )
    send_pieces(chips, folds, (gate, up, down), outs)
    own = dbb_ref.shape[1]
    dbb_ref[...], upb_ref[...], gpb_ref[...] = dbb[:, :own], upb[:, :own], gpb[:, :own]


def token_grads(rates, mixed, dbb, upb, gpb, gate_back, up_back, c1t, c3t, c2t, w1t, w3t, w2):
    value_grad = (rates * (nn(c2t, mixed) + tn(w2, dbb))).T.astype(BF16)
    key_total = tn(gate_back, c1t) + tn(up_back, c3t) + tn(gpb, w1t) + tn(upb, w3t)
    return value_grad, (-key_total).astype(BF16)


def token_kernel(*refs):
    value_grad, key_grad = refs[-2:]
    value_grad[...], key_grad[...] = token_grads(*(r[...] for r in refs[:-2]))


def call(kernel, outs, args, scratch=(), name=None, flops=0):
    vmem = pl.BlockSpec(memory_space=pltpu.VMEM)
    return pl.pallas_call(
        kernel,
        out_shape=[jax.ShapeDtypeStruct(s, t) for s, t in outs],
        in_specs=[vmem] * len(args),
        out_specs=[vmem] * len(outs),
        scratch_shapes=[pltpu.VMEM(s, t) for s, t in scratch],
        compiler_params=pltpu.CompilerParams(vmem_limit_bytes=VMEM_LIMIT),
        cost_estimate=pl.CostEstimate(
            flops=flops,
            bytes_accessed=sum(a.size * a.dtype.itemsize for a in args),
            transcendentals=0,
        ),
        name=name,
    )(*args)


def exchange(pieces, chips):
    count = chips * CORES
    got = [lax.ppermute(pieces[s], "tok", chip_perm(count, s)) for s in reversed(range(1, chips))]
    return [pieces[0], *got]


def to_chip(x, step, chips):
    return lax.ppermute(x, "tok", chip_perm(chips * CORES, step))


def half_sums(kept, given, chips):
    (mine,) = call(carry_kernel, [(given.shape, BF16)], (kept, to_chip(given, 1, chips)), name="carry")
    return [mine, *(to_chip(mine, step, chips) for step in range(2, chips, 2))]


def from_owners(halves, chips):
    others = [to_chip(half, 1, chips) for half in halves]
    *later, others[0] = lax.optimization_barrier((*halves, others[0]))
    cross = lambda x: lax.ppermute(x, "tok", core_perm(chips * CORES))
    parts = zip(halves, others, map(cross, later), map(cross, others))
    return [x for part in parts for x in part]


def head_parts(part, heads):
    got = [
        lax.ppermute(part, "head", [(h, partner(h, step, heads)) for h in range(heads)])
        for step in reversed(range(1, heads))
    ]
    return [part, *got]


def over_chips(blocks, count):
    groups = [list(range(core, count, CORES)) for core in range(CORES)]
    return lax.all_to_all(blocks, "tok", 0, 0, axis_index_groups=groups, tiled=True)


def gather_blocks(copies, count):
    mine = over_chips(copies, count)
    return mine, lax.ppermute(mine, "tok", core_perm(count))


def sliced_pieces(gate, up, down, tok, count):
    g, d = gate.shape[0] // count, down.shape[0] // count
    rows = lambda x, size, t: lax.dynamic_slice_in_dim(x, t * size, size, 0)
    piece = lambda t: pack(rows(gate, g, t), rows(up, g, t), rows(down, d, t))
    sent = [piece(t + tok % CORES) for t in range(0, count, CORES)]
    return piece(tok), jnp.concatenate(sent, axis=0).astype(BF16)


def total_of(own, got, tok):
    blocks = got.reshape((-1,) + own.shape)
    chip = lax.broadcasted_iota(jnp.int32, (blocks.shape[0], 1, 1), 0)
    others = jnp.where(chip == tok // CORES, 0.0, blocks.astype(F32))
    return own + jnp.sum(others, axis=0)


def whole_matrices(mine, other, tok, count, fh):
    shape = (count // CORES, -1, mine.shape[1])
    pair = jnp.stack([mine.reshape(shape), other.reshape(shape)], axis=1)
    pair = jnp.where(tok % CORES == 0, pair, pair[:, ::-1])
    held = pair.reshape((count, -1, mine.shape[1]))
    parts = jax.vmap(lambda x: unpack(x, fh))(held)
    return tuple(x.reshape((-1, x.shape[-1])) for x in parts)


def packed_owner_forward(prior, update, fh):
    fast, moved = zip(*(owner_forward(p, u, 1) for p, u in zip(unpack(prior, fh), unpack(update, fh))))
    return pack(*fast), pack(*moved)


def packed_owner_backward(prior, moved, fast_grad, fh):
    parts = (unpack(x, fh) for x in (prior, moved, fast_grad))
    cotangent, owned = zip(*(owner_backward(p, m, f, 1) for p, m, f in zip(*parts)))
    return pack(*cotangent), pack(*owned)


def per_device(
    query_input,
    key_input,
    value_input,
    out_grad,
    token_rates,
    out_gain,
    gate_prior,
    up_prior,
    down_prior,
):
    count, heads = lax.axis_size("tok"), lax.axis_size("head")
    tok = lax.axis_index("tok")
    chips = count // CORES
    own, dh = key_input.shape
    n = own * CORES
    w1, w3, w2 = gate_prior[0], up_prior[0], down_prior[0]
    fh = w2.shape[0]
    g, d = fh // count, dh // count
    rates = token_rates.T
    gain = out_gain[None, :]
    inputs = query_input, key_input, value_input, out_grad, rates, gain, w1, w3, w2

    if g % ROW_TILE or d % g or dh * g != fh * d or chips & (chips - 1) or chips < 2:
        query_grad, key_grad, value_grad, *results = by_blocks(inputs, tok, count, heads)
    else:
        query_grad, key_grad, value_grad, *results = by_line(inputs, chips, heads)
    return (query_grad, key_grad, value_grad, *(r.T[None] for r in results))


def by_line(inputs, chips, heads):
    query_input, key_input, value_input, out_grad, rates, gain, w1, w3, w2 = inputs
    count = chips * CORES
    own, dh = key_input.shape
    n, fh = own * CORES, w2.shape[0]
    g, d, folds = fh // count, dh // count, dh // fh
    product = 2 * n * dh * fh

    half = (g * chips // 2, dh)
    half_shares = [(half, F32)] * 3 + [(half, BF16)] * 3
    matrices = [((fh, dh), BF16), ((fh, dh), BF16), ((dh, fh), BF16)]
    sums_scratch = [((fh, dh), F32), ((fh, dh), F32), ((dh, fh), F32)]
    hidden = ((fh, n), F32)
    own_hidden = ((fh, own), BF16)
    folds_by_matrix = (1, 1, folds)

    pair = lambda x: lax.ppermute(x, "tok", core_perm(count))
    key_other, value_other, rate_other = pair(key_input), pair(value_input), pair(rates)
    w1t, w3t = w1.T, w3.T
    query_other, grad_other = pair(query_input), pair(out_grad)
    keys_values = (
        key_input, key_other, value_input, value_other, rates, rate_other, w1t, w3t, w2,
    )
    sums = call(
        functools.partial(update_kernel, chips, folds),
        half_shares,
        keys_values,
        sums_scratch,
        "update",
        6 * product,
    )
    *saved, weighted, p1, p3, p2 = call(
        functools.partial(saved_kernel, chips, folds),
        [((dh, n), BF16)] + [hidden] * 4 + [own_hidden] * 3 + [((dh, n), F32)] + [(half, F32)] * 3,
        (*keys_values, out_grad, grad_other, gain),
        sums_scratch,
        "saved",
        3 * product,
    )
    push, up_slope, silu, back_slope, back_curve, mixed, gate_back, up_back = saved
    priors = p1, p3, p2

    fast, moved = [], []
    for k in range(3):
        totals = half_sums(sums[k], sums[3 + k], chips)
        rows, rows_moved = call(
            functools.partial(owner_forward_kernel, folds_by_matrix[k]),
            [(half, BF16), (half, F32)],
            (priors[k], *totals),
            name="owner_forward",
        )
        moved.append(rows_moved)
        fast.append(rows)
    f1t, f3t, f2t, output, q_mixed, q_slope, q_silu, part = call(
        functools.partial(apply_kernel, chips, folds),
        matrices + [((dh, n), F32), ((fh, n), BF16), hidden, hidden, ((2, n), F32)],
        (*from_owners(fast, chips), query_input, query_other, weighted),
        name="apply",
        flops=3 * product,
    )
    q_gate_back, q_up_back, *sums = call(
        functools.partial(back_kernel, chips, folds, heads),
        [own_hidden] * 2 + half_shares,
        (
            *head_parts(part, heads),
            f2t, output, weighted, q_mixed, q_slope, q_silu, query_input, query_other,
        ),
        sums_scratch,
        "apply_back",
        4 * product,
    )
    (query_grad,) = call(
        query_kernel,
        [((own, dh), BF16)],
        (q_gate_back, q_up_back, f1t, f3t),
        name="query_grad",
        flops=product,
    )

    cotangent, owned = [], []
    for k in range(3):
        totals = half_sums(sums[k], sums[3 + k], chips)
        rows, rows_owned = call(
            functools.partial(owner_backward_kernel, folds_by_matrix[k]),
            [(half, BF16), (half, F32)],
            (priors[k], moved[k], *totals),
            name="owner_backward",
        )
        owned.append(rows_owned)
        cotangent.append(rows)
    c1t, c3t, c2t, dbb, upb, gpb, *pieces = call(
        functools.partial(second_kernel, chips, folds),
        matrices + [own_hidden] * 3 + [((3 * g, dh), F32)] + [((3 * g, dh), BF16)] * (chips - 1),
        (
            *from_owners(cotangent, chips),
            key_input, key_other, push, up_slope, silu, back_slope, back_curve,
        ),
        sums_scratch,
        "second_adjoint",
        6 * product,
    )
    value_grad, key_grad = call(
        token_kernel,
        [((own, dh), BF16)] * 2,
        (rates, mixed, dbb, upb, gpb, gate_back, up_back, c1t, c3t, c2t, w1t, w3t, w2),
        name="token_grads",
        flops=3 * product,
    )
    results = call(
        functools.partial(owner_result_kernel, chips, folds),
        [((g, dh), F32)] * 2 + [((d, fh), F32)],
        (*owned, *exchange(pieces, chips)),
        name="owner_result",
    )
    return query_grad, key_grad, value_grad, *results


def by_blocks(inputs, tok, count, heads):
    query_input, key_input, value_input, out_grad, rates, gain, w1, w3, w2 = inputs
    own, dh = key_input.shape
    fh, chips = w2.shape[0], count // CORES
    g, d = fh // count, dh // count
    w1t, w3t = w1.T, w3.T
    pair = lambda x, axis=0: jnp.concatenate(
        [x, lax.ppermute(x, "tok", core_perm(count))], axis=axis
    )
    keys, values, queries, rate = pair(key_input), pair(value_input), pair(query_input), pair(rates, 1)
    weighted = (pair(out_grad).astype(F32) * gain).T
    push = push_of(rate, values)
    up_pre, silu, slope, curvature, mixed, down_back, back_slope, gate_back, up_back = (
        update_forward(w1t, w3t, w2, keys, push)
    )
    up_slope, back_curve = up_pre * slope, down_back * up_pre * curvature
    piece, sent = sliced_pieces(
        nn(gate_back, keys), nn(up_back, keys), nt(push, mixed), tok, count
    )
    prior = pack(
        *(
            lax.dynamic_slice_in_dim(x, tok * rows, rows, 0).astype(F32)
            for x, rows in ((w1t, g), (w3t, g), (w2.T, d))
        )
    )
    update = total_of(piece, over_chips(sent, count), tok)
    fast, moved = packed_owner_forward(prior, update, fh)
    blocks = gather_blocks(jnp.tile(fast, (chips, 1)), count)
    f1t, f3t, f2t = whole_matrices(*blocks, tok, count, fh)
    output, q_mixed, q_slope, q_silu, part = apply_forward(f1t, f3t, f2t, queries, weighted)
    sums = lax.psum(part, "head")
    q_gate_back, q_up_back, *grads = apply_backward(
        f2t, sums, heads * dh, output, weighted, q_mixed, q_slope, q_silu, queries
    )
    piece, sent = sliced_pieces(*grads, tok, count)
    query_grad = (tn(q_gate_back[:, :own], f1t) + tn(q_up_back[:, :own], f3t)).astype(BF16)
    fast_grad = total_of(piece, over_chips(sent, count), tok)
    cotangent, owned = packed_owner_backward(prior, moved, fast_grad, fh)
    blocks = gather_blocks(jnp.tile(cotangent, (chips, 1)), count)
    c1t, c3t, c2t = whole_matrices(*blocks, tok, count, fh)
    dbb, upb, gpb, *bars = second_adjoint(
        c1t, c3t, c2t, keys, push, up_slope, silu, back_slope, back_curve
    )
    piece, sent = sliced_pieces(*bars, tok, count)
    value_grad, key_grad = token_grads(
        rates, mixed[:, :own], dbb[:, :own], upb[:, :own], gpb[:, :own],
        gate_back[:, :own], up_back[:, :own], c1t, c3t, c2t, w1t, w3t, w2,
    )
    results = unpack(owned - total_of(piece, over_chips(sent, count), tok), fh)
    return query_grad, key_grad, value_grad, *results


def solution(mesh):
    tokens = P("tok", "head")
    in_specs = (tokens,) * 5 + (P("head"),) + (P("head", None, None),) * 3
    out_specs = (tokens,) * 3 + (P("head", None, "tok"),) * 3
    return jax.shard_map(
        per_device, mesh=mesh, in_specs=in_specs, out_specs=out_specs, check_vma=False
    )
```

```python
import functools

import jax
import jax.numpy as jnp
from jax import lax
from jax.experimental import pallas as pl
from jax.experimental.pallas import tpu as pltpu
from jax.sharding import PartitionSpec as P

EPSILON = 1e-06
CORES = 2
ROW_TILE = 16
VMEM_LIMIT = 24 * 1024 * 1024
BF16, F32 = jnp.bfloat16, jnp.float32


def nn(a, b):
    return lax.dot_general(a, b, (((1,), (0,)), ((), ())), preferred_element_type=F32)


def nt(a, b):
    return lax.dot_general(a, b, (((1,), (1,)), ((), ())), preferred_element_type=F32)


def tn(a, b):
    return lax.dot_general(a, b, (((0,), (0,)), ((), ())), preferred_element_type=F32)


def silu_parts(hidden):
    sigmoid_value = jax.nn.sigmoid(hidden)
    silu_value = hidden * sigmoid_value
    silu_slope = sigmoid_value * (1.0 + hidden * (1.0 - sigmoid_value))
    curvature = sigmoid_value * (1.0 - sigmoid_value) * (2.0 + hidden * (1.0 - 2.0 * sigmoid_value))
    return silu_value, silu_slope, curvature


def partner(index, step, count):
    return index ^ step if count & (count - 1) == 0 else (index + step) % count


def source(index, step, count):
    return index ^ step if count & (count - 1) == 0 else (index + count - step) % count


def chip_perm(count, step):
    chips = count // CORES
    return [(t, partner(t // CORES, step, chips) * CORES + t % CORES) for t in range(count)]


def core_perm(count):
    return [(t, t ^ 1) for t in range(count)]


def pack(gate, up, down):
    folds = gate.shape[1] // down.shape[1]
    rows = down.shape[0] // folds
    down = jnp.concatenate([down[i * rows : (i + 1) * rows] for i in range(folds)], axis=1)
    return jnp.concatenate([gate, up, down], axis=0)


def unpack(packed, fh):
    g = packed.shape[0] // 3
    folds = packed.shape[1] // fh
    down = packed[2 * g :]
    down = jnp.concatenate([down[:, i * fh : (i + 1) * fh] for i in range(folds)], axis=0)
    return packed[:g], packed[g : 2 * g], down


def update_forward(w1t, w3t, w2, keys, push):
    gate_pre, up_pre = nt(w1t, keys), nt(w3t, keys)
    silu, slope, curvature = silu_parts(gate_pre)
    mixed = (silu * up_pre).astype(BF16)
    down_back = nn(w2, push)
    back_slope = down_back * slope
    gate_back = (down_back * up_pre * slope).astype(BF16)
    up_back = (down_back * silu).astype(BF16)
    return up_pre, silu, slope, curvature, mixed, down_back, back_slope, gate_back, up_back


def apply_forward(f1t, f3t, f2t, queries, weighted):
    q_gate, q_up = nt(f1t, queries), nt(f3t, queries)
    silu, slope, _ = silu_parts(q_gate)
    mixed = (silu * q_up).astype(BF16)
    output = nn(f2t, mixed)
    square = jnp.sum(output * output, axis=0, keepdims=True)
    dot = jnp.sum(weighted * output, axis=0, keepdims=True)
    return output, mixed, q_up * slope, silu, jnp.concatenate([square, dot], axis=0)


def apply_backward(f2t, sums, full_width, output, weighted, mixed, up_slope, silu, queries):
    inverse = lax.rsqrt(sums[0:1] / full_width + EPSILON)
    scale = inverse * inverse * inverse * sums[1:2] / full_width
    out_back = (inverse * weighted - output * scale).astype(BF16)
    q_back = tn(f2t, out_back)
    gate_back = (q_back * up_slope).astype(BF16)
    up_back = (q_back * silu).astype(BF16)
    return gate_back, up_back, nn(gate_back, queries), nn(up_back, queries), nt(out_back, mixed)


def second_adjoint(c1t, c3t, c2t, keys, push, up_slope, silu, back_slope, back_curve):
    gate_bar, up_bar, mixed_bar = nt(c1t, keys), nt(c3t, keys), tn(c2t, push)
    down_back_bar = (gate_bar * up_slope + up_bar * silu).astype(BF16)
    up_pre_bar = (gate_bar * back_slope + mixed_bar * silu).astype(BF16)
    gate_pre_bar = (up_bar * back_slope + mixed_bar * up_slope + gate_bar * back_curve).astype(BF16)
    return (
        down_back_bar,
        up_pre_bar,
        gate_pre_bar,
        nn(gate_pre_bar, keys),
        nn(up_pre_bar, keys),
        nt(push, down_back_bar),
    )


def folds_of(rows, folds):
    width = rows.shape[1] // folds
    return [rows[:, i * width : (i + 1) * width] for i in range(folds)]


def norm_of(rows):
    return jnp.sqrt(jnp.sum(rows * rows, axis=1, keepdims=True) + EPSILON)


def owner_forward(prior, update, folds):
    moved = prior - update
    fast = [
        m * (norm_of(p) / norm_of(m)) for p, m in zip(folds_of(prior, folds), folds_of(moved, folds))
    ]
    return jnp.concatenate(fast, axis=1).astype(BF16), moved


def owner_backward(prior, moved, fast_grad, folds):
    cotangent, owned = [], []
    for p, m, fg in zip(*(folds_of(x, folds) for x in (prior, moved, fast_grad))):
        prior_norm, moved_norm = norm_of(p), norm_of(m)
        column_dot = jnp.sum(fg * m, axis=1, keepdims=True)
        moved_grad = (prior_norm / moved_norm) * (fg - m * (column_dot / (moved_norm * moved_norm)))
        cotangent.append(moved_grad)
        owned.append(moved_grad + p * (column_dot / (moved_norm * prior_norm)))
    return jnp.concatenate(cotangent, axis=1).astype(BF16), jnp.concatenate(owned, axis=1)


def update_sums(w1t, w3t, w2, keys, rates, values):
    push = push_of(rates, values)
    *_, mixed, _, _, gate_back, up_back = update_forward(w1t, w3t, w2, keys, push)
    return nn(gate_back, keys), nn(up_back, keys), nt(push, mixed)


def push_of(rates, values):
    return (-rates * values.T.astype(F32)).astype(BF16)


def both(own_ref, other_ref, axis=0):
    return jnp.concatenate([own_ref[...], other_ref[...]], axis=axis)


def rows_of(ref, chip, core, chips, folds, i):
    rows = ref.shape[0] // (chips * CORES)
    height = rows // folds
    return pl.ds(pl.multiple_of((chip * CORES + core) * rows + i * height, height), height)


def cut_half(out, ref, parity, chips, folds):
    core = lax.axis_index("tok") % CORES
    height, width = ref.shape[0] // (chips * CORES * folds), ref.shape[1]
    for k in range(chips // 2):
        for i in range(folds):
            out[k * height : (k + 1) * height, i * width : (i + 1) * width] = ref[
                rows_of(ref, 2 * k + parity, core, chips, folds, i), :
            ].astype(out.dtype)


def place_half(ref, half, parity, core, chips, folds):
    height, width = ref.shape[0] // (chips * CORES * folds), ref.shape[1]
    for k in range(chips // 2):
        for i in range(folds):
            ref[rows_of(ref, 2 * k + parity, core, chips, folds, i), :] = half[
                k * height : (k + 1) * height, i * width : (i + 1) * width
            ]


def place_halves(chips, folds, halves, matrices):
    tok = lax.axis_index("tok")
    parity, core = tok // CORES % 2, tok % CORES
    for k, ref in enumerate(matrices):
        whose = ((parity, core), (1 - parity, core), (parity, 1 - core), (1 - parity, 1 - core))
        for half, (p, c) in zip(halves[4 * k : 4 * k + 4], whose):
            place_half(ref, half, p, c, chips, folds if k == 2 else 1)


def send_pieces(chips, folds, matrices, outs):
    tok = lax.axis_index("tok")
    chip, core = tok // CORES, tok % CORES
    for step, out in enumerate(outs):
        to = partner(chip, step, chips)
        at = 0
        for k, ref in enumerate(matrices):
            folded = folds if k == 2 else 1
            parts = [ref[rows_of(ref, to, core, chips, folded, i), :] for i in range(folded)]
            rows = jnp.concatenate(parts, axis=1).astype(out.dtype)
            out[at : at + rows.shape[0]] = rows
            at += rows.shape[0]


def cut_matrices(chips, folds, matrices, outs):
    parity = lax.axis_index("tok") // CORES % 2
    for k, ref in enumerate(matrices):
        cut_half(outs[k], ref, parity, chips, folds if k == 2 else 1)
        cut_half(outs[3 + k], ref, 1 - parity, chips, folds if k == 2 else 1)


def update_kernel(chips, folds, ko, kx, vo, vx, ro, rx, w1t, w3t, w2, *rest):
    outs, matrices = rest[:6], rest[6:]
    sums = update_sums(
        w1t[...], w3t[...], w2[...], both(ko, kx), both(ro, rx, 1), both(vo, vx)
    )
    for ref, total in zip(matrices, sums):
        ref[...] = total
    cut_matrices(chips, folds, matrices, outs)


def saved_kernel(
    chips, folds, ko, kx, vo, vx, ro, rx, w1t, w3t, w2, go, gx, gain,
    push_ref, up_slope_ref, silu_ref, back_slope_ref, back_curve_ref,
    mixed_ref, gate_back_ref, up_back_ref, weighted_ref, p1_ref, p3_ref, p2_ref,
    gate_ref, up_ref, down_ref,
):
    push = push_of(both(ro, rx, 1), both(vo, vx))
    push_ref[...] = push
    up_pre, silu, slope, curvature, mixed, down_back, back_slope, gate_back, up_back = (
        update_forward(w1t[...], w3t[...], w2[...], both(ko, kx), push)
    )
    up_slope_ref[...] = up_pre * slope
    silu_ref[...] = silu
    back_slope_ref[...] = back_slope
    back_curve_ref[...] = down_back * up_pre * curvature
    own = mixed_ref.shape[1]
    mixed_ref[...] = mixed[:, :own]
    gate_back_ref[...] = gate_back[:, :own]
    up_back_ref[...] = up_back[:, :own]
    weighted_ref[...] = (both(go, gx).astype(F32) * gain[...]).T
    gate_ref[...] = w1t[...].astype(F32)
    up_ref[...] = w3t[...].astype(F32)
    down_ref[...] = w2[...].astype(F32).T
    parity = lax.axis_index("tok") // CORES % 2
    cut_half(p1_ref, gate_ref, parity, chips, 1)
    cut_half(p3_ref, up_ref, parity, chips, 1)
    cut_half(p2_ref, down_ref, parity, chips, folds)


def carry_kernel(own, got, out):
    out[...] = (own[...] + got[...].astype(F32)).astype(BF16)


def total_of_halves(halves):
    total = halves[0][...].astype(F32)
    for half in halves[1:]:
        total = total + half[...].astype(F32)
    return total


def owner_forward_kernel(folds, prior, *refs):
    fast, moved = refs[-2:]
    total = total_of_halves(refs[:-2])
    fast[...], moved[...] = owner_forward(prior[...], total, folds)


def owner_backward_kernel(folds, prior, moved, *refs):
    cotangent, owned = refs[-2:]
    total = total_of_halves(refs[:-2])
    cotangent[...], owned[...] = owner_backward(prior[...], moved[...], total, folds)


def owner_result_kernel(chips, folds, *refs):
    owned, pieces, outs = refs[:3], refs[3:-3], refs[-3:]
    bars = pieces[0][...]
    for piece in pieces[1:]:
        bars = bars + piece[...].astype(F32)
    g = outs[0].shape[0]
    block = lax.axis_index("tok") // (2 * CORES)
    for k, out in enumerate(outs):
        result = owned[k][pl.ds(pl.multiple_of(block * g, g), g), :] - bars[k * g : (k + 1) * g]
        for i, rows in enumerate(folds_of(result, folds if k == 2 else 1)):
            out[i * g : (i + 1) * g] = rows


def apply_kernel(chips, folds, *refs):
    halves, refs = refs[:12], refs[12:]
    qo, qx, weighted, f1t, f3t, f2t, output, mixed, up_slope, silu, sums = refs
    place_halves(chips, folds, halves, (f1t, f3t, f2t))
    output[...], mixed[...], up_slope[...], silu[...], sums[...] = apply_forward(
        f1t[...], f3t[...], f2t[...], both(qo, qx), weighted[...]
    )


def back_kernel(chips, folds, heads, *refs):
    total, other, refs = refs[0][...], refs[1][...], refs[2:]
    own = total.shape[1] // CORES
    other = jnp.concatenate([other[:, own:], other[:, :own]], axis=1)
    sums = jnp.where(lax.axis_index("tok") % CORES == 0, other, total)
    f2t, output, weighted, mixed, up_slope, silu, qo, qx, gate_back, up_back = refs[:10]
    outs, (gate, up, down) = refs[10:16], refs[16:]
    width = heads * output.shape[0]
    gb, ub, gate[...], up[...], down[...] = apply_backward(
        f2t[...], sums, width, output[...], weighted[...], mixed[...], up_slope[...], silu[...],
        both(qo, qx),
    )
    cut_matrices(chips, folds, (gate, up, down), outs)
    own = gate_back.shape[1]
    gate_back[...], up_back[...] = gb[:, :own], ub[:, :own]


def query_kernel(gate_back, up_back, f1t, f3t, out):
    out[...] = (tn(gate_back[...], f1t[...]) + tn(up_back[...], f3t[...])).astype(BF16)


def second_kernel(chips, folds, *refs):
    halves, refs = refs[:12], refs[12:]
    ko, kx, push, up_slope, silu, back_slope, back_curve = refs[:7]
    c1t, c3t, c2t, dbb_ref, upb_ref, gpb_ref = refs[7:13]
    outs, (gate, up, down) = refs[13 : 13 + chips], refs[13 + chips :]
    place_halves(chips, folds, halves, (c1t, c3t, c2t))
    dbb, upb, gpb, gate[...], up[...], down[...] = second_adjoint(
        c1t[...], c3t[...], c2t[...], both(ko, kx), push[...],
        up_slope[...], silu[...], back_slope[...], back_curve[...],
    )
    send_pieces(chips, folds, (gate, up, down), outs)
    own = dbb_ref.shape[1]
    dbb_ref[...], upb_ref[...], gpb_ref[...] = dbb[:, :own], upb[:, :own], gpb[:, :own]


def token_grads(rates, mixed, dbb, upb, gpb, gate_back, up_back, c1t, c3t, c2t, w1t, w3t, w2):
    value_grad = (rates * (nn(c2t, mixed) + tn(w2, dbb))).T.astype(BF16)
    key_total = tn(gate_back, c1t) + tn(up_back, c3t) + tn(gpb, w1t) + tn(upb, w3t)
    return value_grad, (-key_total).astype(BF16)


def token_kernel(*refs):
    value_grad, key_grad = refs[-2:]
    value_grad[...], key_grad[...] = token_grads(*(r[...] for r in refs[:-2]))


def call(kernel, outs, args, scratch=(), name=None, flops=0):
    vmem = pl.BlockSpec(memory_space=pltpu.VMEM)
    return pl.pallas_call(
        kernel,
        out_shape=[jax.ShapeDtypeStruct(s, t) for s, t in outs],
        in_specs=[vmem] * len(args),
        out_specs=[vmem] * len(outs),
        scratch_shapes=[pltpu.VMEM(s, t) for s, t in scratch],
        compiler_params=pltpu.CompilerParams(vmem_limit_bytes=VMEM_LIMIT),
        cost_estimate=pl.CostEstimate(
            flops=flops,
            bytes_accessed=sum(a.size * a.dtype.itemsize for a in args),
            transcendentals=0,
        ),
        name=name,
    )(*args)


def exchange(pieces, chips):
    count = chips * CORES
    got = [lax.ppermute(pieces[s], "tok", chip_perm(count, s)) for s in reversed(range(1, chips))]
    return [pieces[0], *got]


def to_chip(x, step, chips):
    return lax.ppermute(x, "tok", chip_perm(chips * CORES, step))


def half_sums(kept, given, chips):
    (mine,) = call(carry_kernel, [(given.shape, BF16)], (kept, to_chip(given, 1, chips)), name="carry")
    return [mine, *(to_chip(mine, step, chips) for step in range(2, chips, 2))]


def from_owners(halves, chips):
    others = [to_chip(half, 1, chips) for half in halves]
    *later, others[0] = lax.optimization_barrier((*halves, others[0]))
    cross = lambda x: lax.ppermute(x, "tok", core_perm(chips * CORES))
    parts = zip(halves, others, map(cross, later), map(cross, others))
    return [x for part in parts for x in part]


def head_sums(part, count, heads):
    total, step = part, 1
    while step < heads:
        perm = [
            (h * count + t, (h ^ step if t % CORES else h) * count + t)
            for h in range(heads)
            for t in range(count)
        ]
        total = total + lax.ppermute(total, ("head", "tok"), perm)
        step *= 2
    return [total, lax.ppermute(total, "tok", core_perm(count))]


def over_chips(blocks, count):
    groups = [list(range(core, count, CORES)) for core in range(CORES)]
    return lax.all_to_all(blocks, "tok", 0, 0, axis_index_groups=groups, tiled=True)


def gather_blocks(copies, count):
    mine = over_chips(copies, count)
    return mine, lax.ppermute(mine, "tok", core_perm(count))


def sliced_pieces(gate, up, down, tok, count):
    g, d = gate.shape[0] // count, down.shape[0] // count
    rows = lambda x, size, t: lax.dynamic_slice_in_dim(x, t * size, size, 0)
    piece = lambda t: pack(rows(gate, g, t), rows(up, g, t), rows(down, d, t))
    sent = [piece(t + tok % CORES) for t in range(0, count, CORES)]
    return piece(tok), jnp.concatenate(sent, axis=0).astype(BF16)


def total_of(own, got, tok):
    blocks = got.reshape((-1,) + own.shape)
    chip = lax.broadcasted_iota(jnp.int32, (blocks.shape[0], 1, 1), 0)
    others = jnp.where(chip == tok // CORES, 0.0, blocks.astype(F32))
    return own + jnp.sum(others, axis=0)


def whole_matrices(mine, other, tok, count, fh):
    shape = (count // CORES, -1, mine.shape[1])
    pair = jnp.stack([mine.reshape(shape), other.reshape(shape)], axis=1)
    pair = jnp.where(tok % CORES == 0, pair, pair[:, ::-1])
    held = pair.reshape((count, -1, mine.shape[1]))
    parts = jax.vmap(lambda x: unpack(x, fh))(held)
    return tuple(x.reshape((-1, x.shape[-1])) for x in parts)


def packed_owner_forward(prior, update, fh):
    fast, moved = zip(*(owner_forward(p, u, 1) for p, u in zip(unpack(prior, fh), unpack(update, fh))))
    return pack(*fast), pack(*moved)


def packed_owner_backward(prior, moved, fast_grad, fh):
    parts = (unpack(x, fh) for x in (prior, moved, fast_grad))
    cotangent, owned = zip(*(owner_backward(p, m, f, 1) for p, m, f in zip(*parts)))
    return pack(*cotangent), pack(*owned)


def per_device(
    query_input,
    key_input,
    value_input,
    out_grad,
    token_rates,
    out_gain,
    gate_prior,
    up_prior,
    down_prior,
):
    count, heads = lax.axis_size("tok"), lax.axis_size("head")
    tok = lax.axis_index("tok")
    chips = count // CORES
    own, dh = key_input.shape
    n = own * CORES
    w1, w3, w2 = gate_prior[0], up_prior[0], down_prior[0]
    fh = w2.shape[0]
    g, d = fh // count, dh // count
    rates = token_rates.T
    gain = out_gain[None, :]
    inputs = query_input, key_input, value_input, out_grad, rates, gain, w1, w3, w2

    if g % ROW_TILE or d % g or dh * g != fh * d or chips & (chips - 1) or chips < 2 or heads & (heads - 1):
        query_grad, key_grad, value_grad, *results = by_blocks(inputs, tok, count, heads)
    else:
        query_grad, key_grad, value_grad, *results = by_line(inputs, chips, heads)
    return (query_grad, key_grad, value_grad, *(r.T[None] for r in results))


def by_line(inputs, chips, heads):
    query_input, key_input, value_input, out_grad, rates, gain, w1, w3, w2 = inputs
    count = chips * CORES
    own, dh = key_input.shape
    n, fh = own * CORES, w2.shape[0]
    g, d, folds = fh // count, dh // count, dh // fh
    product = 2 * n * dh * fh

    half = (g * chips // 2, dh)
    half_shares = [(half, F32)] * 3 + [(half, BF16)] * 3
    matrices = [((fh, dh), BF16), ((fh, dh), BF16), ((dh, fh), BF16)]
    sums_scratch = [((fh, dh), F32), ((fh, dh), F32), ((dh, fh), F32)]
    hidden = ((fh, n), F32)
    own_hidden = ((fh, own), BF16)
    folds_by_matrix = (1, 1, folds)

    pair = lambda x: lax.ppermute(x, "tok", core_perm(count))
    key_other, value_other, rate_other = pair(key_input), pair(value_input), pair(rates)
    w1t, w3t = w1.T, w3.T
    query_other, grad_other = pair(query_input), pair(out_grad)
    keys_values = (
        key_input, key_other, value_input, value_other, rates, rate_other, w1t, w3t, w2,
    )
    sums = call(
        functools.partial(update_kernel, chips, folds),
        half_shares,
        keys_values,
        sums_scratch,
        "update",
        6 * product,
    )
    *saved, weighted, p1, p3, p2 = call(
        functools.partial(saved_kernel, chips, folds),
        [((dh, n), BF16)] + [hidden] * 4 + [own_hidden] * 3 + [((dh, n), F32)] + [(half, F32)] * 3,
        (*keys_values, out_grad, grad_other, gain),
        sums_scratch,
        "saved",
        3 * product,
    )
    push, up_slope, silu, back_slope, back_curve, mixed, gate_back, up_back = saved
    priors = p1, p3, p2

    fast, moved = [], []
    for k in range(3):
        totals = half_sums(sums[k], sums[3 + k], chips)
        rows, rows_moved = call(
            functools.partial(owner_forward_kernel, folds_by_matrix[k]),
            [(half, BF16), (half, F32)],
            (priors[k], *totals),
            name="owner_forward",
        )
        moved.append(rows_moved)
        fast.append(rows)
    f1t, f3t, f2t, output, q_mixed, q_slope, q_silu, part = call(
        functools.partial(apply_kernel, chips, folds),
        matrices + [((dh, n), F32), ((fh, n), BF16), hidden, hidden, ((2, n), F32)],
        (*from_owners(fast, chips), query_input, query_other, weighted),
        name="apply",
        flops=3 * product,
    )
    q_gate_back, q_up_back, *sums = call(
        functools.partial(back_kernel, chips, folds, heads),
        [own_hidden] * 2 + half_shares,
        (
            *head_sums(part, count, heads),
            f2t, output, weighted, q_mixed, q_slope, q_silu, query_input, query_other,
        ),
        sums_scratch,
        "apply_back",
        4 * product,
    )
    (query_grad,) = call(
        query_kernel,
        [((own, dh), BF16)],
        (q_gate_back, q_up_back, f1t, f3t),
        name="query_grad",
        flops=product,
    )

    cotangent, owned = [], []
    for k in range(3):
        totals = half_sums(sums[k], sums[3 + k], chips)
        rows, rows_owned = call(
            functools.partial(owner_backward_kernel, folds_by_matrix[k]),
            [(half, BF16), (half, F32)],
            (priors[k], moved[k], *totals),
            name="owner_backward",
        )
        owned.append(rows_owned)
        cotangent.append(rows)
    c1t, c3t, c2t, dbb, upb, gpb, *pieces = call(
        functools.partial(second_kernel, chips, folds),
        matrices + [own_hidden] * 3 + [((3 * g, dh), F32)] + [((3 * g, dh), BF16)] * (chips - 1),
        (
            *from_owners(cotangent, chips),
            key_input, key_other, push, up_slope, silu, back_slope, back_curve,
        ),
        sums_scratch,
        "second_adjoint",
        6 * product,
    )
    value_grad, key_grad = call(
        token_kernel,
        [((own, dh), BF16)] * 2,
        (rates, mixed, dbb, upb, gpb, gate_back, up_back, c1t, c3t, c2t, w1t, w3t, w2),
        name="token_grads",
        flops=3 * product,
    )
    results = call(
        functools.partial(owner_result_kernel, chips, folds),
        [((g, dh), F32)] * 2 + [((d, fh), F32)],
        (*owned, *exchange(pieces, chips)),
        name="owner_result",
    )
    return query_grad, key_grad, value_grad, *results


def by_blocks(inputs, tok, count, heads):
    query_input, key_input, value_input, out_grad, rates, gain, w1, w3, w2 = inputs
    own, dh = key_input.shape
    fh, chips = w2.shape[0], count // CORES
    g, d = fh // count, dh // count
    w1t, w3t = w1.T, w3.T
    pair = lambda x, axis=0: jnp.concatenate(
        [x, lax.ppermute(x, "tok", core_perm(count))], axis=axis
    )
    keys, values, queries, rate = pair(key_input), pair(value_input), pair(query_input), pair(rates, 1)
    weighted = (pair(out_grad).astype(F32) * gain).T
    push = push_of(rate, values)
    up_pre, silu, slope, curvature, mixed, down_back, back_slope, gate_back, up_back = (
        update_forward(w1t, w3t, w2, keys, push)
    )
    up_slope, back_curve = up_pre * slope, down_back * up_pre * curvature
    piece, sent = sliced_pieces(
        nn(gate_back, keys), nn(up_back, keys), nt(push, mixed), tok, count
    )
    prior = pack(
        *(
            lax.dynamic_slice_in_dim(x, tok * rows, rows, 0).astype(F32)
            for x, rows in ((w1t, g), (w3t, g), (w2.T, d))
        )
    )
    update = total_of(piece, over_chips(sent, count), tok)
    fast, moved = packed_owner_forward(prior, update, fh)
    blocks = gather_blocks(jnp.tile(fast, (chips, 1)), count)
    f1t, f3t, f2t = whole_matrices(*blocks, tok, count, fh)
    output, q_mixed, q_slope, q_silu, part = apply_forward(f1t, f3t, f2t, queries, weighted)
    sums = lax.psum(part, "head")
    q_gate_back, q_up_back, *grads = apply_backward(
        f2t, sums, heads * dh, output, weighted, q_mixed, q_slope, q_silu, queries
    )
    piece, sent = sliced_pieces(*grads, tok, count)
    query_grad = (tn(q_gate_back[:, :own], f1t) + tn(q_up_back[:, :own], f3t)).astype(BF16)
    fast_grad = total_of(piece, over_chips(sent, count), tok)
    cotangent, owned = packed_owner_backward(prior, moved, fast_grad, fh)
    blocks = gather_blocks(jnp.tile(cotangent, (chips, 1)), count)
    c1t, c3t, c2t = whole_matrices(*blocks, tok, count, fh)
    dbb, upb, gpb, *bars = second_adjoint(
        c1t, c3t, c2t, keys, push, up_slope, silu, back_slope, back_curve
    )
    piece, sent = sliced_pieces(*bars, tok, count)
    value_grad, key_grad = token_grads(
        rates, mixed[:, :own], dbb[:, :own], upb[:, :own], gpb[:, :own],
        gate_back[:, :own], up_back[:, :own], c1t, c3t, c2t, w1t, w3t, w2,
    )
    results = unpack(owned - total_of(piece, over_chips(sent, count), tok), fh)
    return query_grad, key_grad, value_grad, *results


def solution(mesh):
    tokens = P("tok", "head")
    in_specs = (tokens,) * 5 + (P("head"),) + (P("head", None, None),) * 3
    out_specs = (tokens,) * 3 + (P("head", None, "tok"),) * 3
    return jax.shard_map(
        per_device, mesh=mesh, in_specs=in_specs, out_specs=out_specs, check_vma=False
    )
```

```python
import functools

import jax
import jax.numpy as jnp
from jax import lax
from jax.experimental import pallas as pl
from jax.experimental.pallas import tpu as pltpu
from jax.sharding import PartitionSpec as P

EPSILON = 1e-06
CORES = 2
ROW_TILE = 16
VMEM_LIMIT = 24 * 1024 * 1024
BF16, F32 = jnp.bfloat16, jnp.float32


def nn(a, b):
    return lax.dot_general(a, b, (((1,), (0,)), ((), ())), preferred_element_type=F32)


def nt(a, b):
    return lax.dot_general(a, b, (((1,), (1,)), ((), ())), preferred_element_type=F32)


def tn(a, b):
    return lax.dot_general(a, b, (((0,), (0,)), ((), ())), preferred_element_type=F32)


def silu_parts(hidden):
    sigmoid_value = jax.nn.sigmoid(hidden)
    silu_value = hidden * sigmoid_value
    silu_slope = sigmoid_value * (1.0 + hidden * (1.0 - sigmoid_value))
    curvature = sigmoid_value * (1.0 - sigmoid_value) * (2.0 + hidden * (1.0 - 2.0 * sigmoid_value))
    return silu_value, silu_slope, curvature


def partner(index, step, count):
    return index ^ step if count & (count - 1) == 0 else (index + step) % count


def source(index, step, count):
    return index ^ step if count & (count - 1) == 0 else (index + count - step) % count


def chip_perm(count, step):
    chips = count // CORES
    return [(t, partner(t // CORES, step, chips) * CORES + t % CORES) for t in range(count)]


def core_perm(count):
    return [(t, t ^ 1) for t in range(count)]


def pack(gate, up, down):
    folds = gate.shape[1] // down.shape[1]
    rows = down.shape[0] // folds
    down = jnp.concatenate([down[i * rows : (i + 1) * rows] for i in range(folds)], axis=1)
    return jnp.concatenate([gate, up, down], axis=0)


def unpack(packed, fh):
    g = packed.shape[0] // 3
    folds = packed.shape[1] // fh
    down = packed[2 * g :]
    down = jnp.concatenate([down[:, i * fh : (i + 1) * fh] for i in range(folds)], axis=0)
    return packed[:g], packed[g : 2 * g], down


def update_forward(w1t, w3t, w2, keys, push):
    gate_pre, up_pre = nt(w1t, keys), nt(w3t, keys)
    silu, slope, curvature = silu_parts(gate_pre)
    mixed = (silu * up_pre).astype(BF16)
    down_back = nn(w2, push)
    back_slope = down_back * slope
    gate_back = (down_back * up_pre * slope).astype(BF16)
    up_back = (down_back * silu).astype(BF16)
    return up_pre, silu, slope, curvature, mixed, down_back, back_slope, gate_back, up_back


def apply_forward(f1t, f3t, f2t, queries, weighted):
    q_gate, q_up = nt(f1t, queries), nt(f3t, queries)
    silu, slope, _ = silu_parts(q_gate)
    mixed = (silu * q_up).astype(BF16)
    output = nn(f2t, mixed)
    square = jnp.sum(output * output, axis=0, keepdims=True)
    dot = jnp.sum(weighted * output, axis=0, keepdims=True)
    return output, mixed, q_up * slope, silu, jnp.concatenate([square, dot], axis=0)


def apply_backward(f2t, sums, full_width, output, weighted, up_slope, silu):
    inverse = lax.rsqrt(sums[0:1] / full_width + EPSILON)
    scale = inverse * inverse * inverse * sums[1:2] / full_width
    out_back = (inverse * weighted - output * scale).astype(BF16)
    q_back = tn(f2t, out_back)
    gate_back = (q_back * up_slope).astype(BF16)
    up_back = (q_back * silu).astype(BF16)
    return gate_back, up_back, out_back


def second_adjoint(c1t, c3t, c2t, keys, push, up_slope, silu, back_slope, back_curve):
    gate_bar, up_bar, mixed_bar = nt(c1t, keys), nt(c3t, keys), tn(c2t, push)
    down_back_bar = (gate_bar * up_slope + up_bar * silu).astype(BF16)
    up_pre_bar = (gate_bar * back_slope + mixed_bar * silu).astype(BF16)
    gate_pre_bar = (up_bar * back_slope + mixed_bar * up_slope + gate_bar * back_curve).astype(BF16)
    return down_back_bar, up_pre_bar, gate_pre_bar


def folds_of(rows, folds):
    width = rows.shape[1] // folds
    return [rows[:, i * width : (i + 1) * width] for i in range(folds)]


def norm_of(rows):
    return jnp.sqrt(jnp.sum(rows * rows, axis=1, keepdims=True) + EPSILON)


def owner_forward(prior, update, folds):
    moved = prior - update
    fast = [
        m * (norm_of(p) / norm_of(m)) for p, m in zip(folds_of(prior, folds), folds_of(moved, folds))
    ]
    return jnp.concatenate(fast, axis=1).astype(BF16), moved


def owner_backward(prior, moved, fast_grad, folds):
    cotangent, owned = [], []
    for p, m, fg in zip(*(folds_of(x, folds) for x in (prior, moved, fast_grad))):
        prior_norm, moved_norm = norm_of(p), norm_of(m)
        column_dot = jnp.sum(fg * m, axis=1, keepdims=True)
        moved_grad = (prior_norm / moved_norm) * (fg - m * (column_dot / (moved_norm * moved_norm)))
        cotangent.append(moved_grad)
        owned.append(moved_grad + p * (column_dot / (moved_norm * prior_norm)))
    return jnp.concatenate(cotangent, axis=1).astype(BF16), jnp.concatenate(owned, axis=1)


def push_of(rates, values):
    return (-rates * values.T.astype(F32)).astype(BF16)


def both(own_ref, other_ref, axis=0):
    return jnp.concatenate([own_ref[...], other_ref[...]], axis=axis)


def rows_of(ref, chip, core, chips, folds, i):
    rows = ref.shape[0] // (chips * CORES)
    height = rows // folds
    return pl.ds(pl.multiple_of((chip * CORES + core) * rows + i * height, height), height)


def cut_half(out, ref, parity, chips, folds):
    core = lax.axis_index("tok") % CORES
    height, width = ref.shape[0] // (chips * CORES * folds), ref.shape[1]
    for k in range(chips // 2):
        for i in range(folds):
            out[k * height : (k + 1) * height, i * width : (i + 1) * width] = ref[
                rows_of(ref, 2 * k + parity, core, chips, folds, i), :
            ].astype(out.dtype)


def place_half(ref, half, parity, core, chips, folds):
    height, width = ref.shape[0] // (chips * CORES * folds), ref.shape[1]
    for k in range(chips // 2):
        for i in range(folds):
            ref[rows_of(ref, 2 * k + parity, core, chips, folds, i), :] = half[
                k * height : (k + 1) * height, i * width : (i + 1) * width
            ]


def place_halves(chips, folds, halves, matrices):
    tok = lax.axis_index("tok")
    parity, core = tok // CORES % 2, tok % CORES
    for k, ref in enumerate(matrices):
        whose = ((parity, core), (1 - parity, core), (parity, 1 - core), (1 - parity, 1 - core))
        for half, (p, c) in zip(halves[4 * k : 4 * k + 4], whose):
            place_half(ref, half, p, c, chips, folds if k == 2 else 1)


def products_of_core(chips, folds, order, gate_ref, up_ref, down_ref, tokens, hidden):
    core = lax.axis_index("tok") % CORES

    def picked(ref):
        rows = ref.shape[0] // (chips * CORES)
        blocks = [
            ref[pl.ds(pl.multiple_of((chip * CORES + core) * rows, rows), rows), :] for chip in order
        ]
        return jnp.concatenate(blocks, axis=0)

    gate, up = nn(picked(gate_ref), tokens), nn(picked(up_ref), tokens)
    down = nt(picked(down_ref), hidden)
    g, d = gate.shape[0] // chips, down.shape[0] // chips
    pieces = []
    for k in range(chips):
        parts = [down[k * d + i * g : k * d + (i + 1) * g] for i in range(folds)]
        pieces.append(
            (gate[k * g : (k + 1) * g], up[k * g : (k + 1) * g], jnp.concatenate(parts, axis=1))
        )
    return pieces


def send_pieces(chips, folds, operands, outs):
    chip = lax.axis_index("tok") // CORES
    order = [partner(chip, step, chips) for step in range(chips)]
    for out, parts in zip(outs, products_of_core(chips, folds, order, *operands)):
        out[...] = jnp.concatenate(parts, axis=0).astype(out.dtype)


def send_halves(chips, folds, operands, outs):
    parity = lax.axis_index("tok") // CORES % 2
    half = chips // 2
    order = [2 * k + p for p in (parity, 1 - parity) for k in range(half)]
    pieces = products_of_core(chips, folds, order, *operands)
    for k in range(3):
        kept, given = ([p[k] for p in part] for part in (pieces[:half], pieces[half:]))
        outs[k][...] = jnp.concatenate(kept, axis=0)
        outs[3 + k][...] = jnp.concatenate(given, axis=0).astype(BF16)


def update_kernel(chips, folds, ko, kx, vo, vx, ro, rx, w1t, w3t, w2, *rest):
    outs, (gate, up, push) = rest[:6], rest[6:]
    keys = both(ko, kx)
    push[...] = push_of(both(ro, rx, 1), both(vo, vx))
    *_, mixed, _, _, gate[...], up[...] = update_forward(w1t[...], w3t[...], w2[...], keys, push[...])
    send_halves(chips, folds, (gate, up, push, keys, mixed), outs)


def saved_kernel(
    chips, folds, ko, kx, vo, vx, ro, rx, w1t, w3t, w2, go, gx, gain,
    push_ref, up_slope_ref, silu_ref, back_slope_ref, back_curve_ref,
    mixed_ref, gate_back_ref, up_back_ref, weighted_ref, p1_ref, p3_ref, p2_ref,
    gate_ref, up_ref, down_ref,
):
    push = push_of(both(ro, rx, 1), both(vo, vx))
    push_ref[...] = push
    up_pre, silu, slope, curvature, mixed, down_back, back_slope, gate_back, up_back = (
        update_forward(w1t[...], w3t[...], w2[...], both(ko, kx), push)
    )
    up_slope_ref[...] = up_pre * slope
    silu_ref[...] = silu
    back_slope_ref[...] = back_slope
    back_curve_ref[...] = down_back * up_pre * curvature
    own = mixed_ref.shape[1]
    mixed_ref[...] = mixed[:, :own]
    gate_back_ref[...] = gate_back[:, :own]
    up_back_ref[...] = up_back[:, :own]
    weighted_ref[...] = (both(go, gx).astype(F32) * gain[...]).T
    gate_ref[...] = w1t[...].astype(F32)
    up_ref[...] = w3t[...].astype(F32)
    down_ref[...] = w2[...].astype(F32).T
    parity = lax.axis_index("tok") // CORES % 2
    cut_half(p1_ref, gate_ref, parity, chips, 1)
    cut_half(p3_ref, up_ref, parity, chips, 1)
    cut_half(p2_ref, down_ref, parity, chips, folds)


def carry_kernel(own, got, out):
    out[...] = (own[...] + got[...].astype(F32)).astype(BF16)


def total_of_halves(halves):
    total = halves[0][...].astype(F32)
    for half in halves[1:]:
        total = total + half[...].astype(F32)
    return total


def owner_forward_kernel(folds, prior, *refs):
    fast, moved = refs[-2:]
    total = total_of_halves(refs[:-2])
    fast[...], moved[...] = owner_forward(prior[...], total, folds)


def owner_backward_kernel(folds, prior, moved, *refs):
    cotangent, owned = refs[-2:]
    total = total_of_halves(refs[:-2])
    cotangent[...], owned[...] = owner_backward(prior[...], moved[...], total, folds)


def owner_result_kernel(chips, folds, *refs):
    owned, pieces, outs = refs[:3], refs[3:-3], refs[-3:]
    bars = pieces[0][...]
    for piece in pieces[1:]:
        bars = bars + piece[...].astype(F32)
    g = outs[0].shape[0]
    block = lax.axis_index("tok") // (2 * CORES)
    for k, out in enumerate(outs):
        result = owned[k][pl.ds(pl.multiple_of(block * g, g), g), :] - bars[k * g : (k + 1) * g]
        for i, rows in enumerate(folds_of(result, folds if k == 2 else 1)):
            out[i * g : (i + 1) * g] = rows


def apply_kernel(chips, folds, *refs):
    halves, refs = refs[:12], refs[12:]
    qo, qx, weighted, f1t, f3t, f2t, output, mixed, up_slope, silu, sums = refs
    place_halves(chips, folds, halves, (f1t, f3t, f2t))
    output[...], mixed[...], up_slope[...], silu[...], sums[...] = apply_forward(
        f1t[...], f3t[...], f2t[...], both(qo, qx), weighted[...]
    )


def back_kernel(chips, folds, heads, *refs):
    parts, refs = refs[:heads], refs[heads:]
    sums = parts[0][...]
    for part in parts[1:]:
        sums = sums + part[...]
    f2t, output, weighted, mixed, up_slope, silu, qo, qx, gate_back, up_back = refs[:10]
    outs, (gate, up, down) = refs[10:16], refs[16:]
    width = heads * output.shape[0]
    gate[...], up[...], down[...] = apply_backward(
        f2t[...], sums, width, output[...], weighted[...], up_slope[...], silu[...]
    )
    send_halves(chips, folds, (gate, up, down, both(qo, qx), mixed[...]), outs)
    own = gate_back.shape[1]
    gate_back[...], up_back[...] = gate[:, :own], up[:, :own]


def query_kernel(gate_back, up_back, f1t, f3t, out):
    out[...] = (tn(gate_back[...], f1t[...]) + tn(up_back[...], f3t[...])).astype(BF16)


def second_kernel(chips, folds, *refs):
    halves, refs = refs[:12], refs[12:]
    ko, kx, push, up_slope, silu, back_slope, back_curve = refs[:7]
    c1t, c3t, c2t, dbb_ref, upb_ref, gpb_ref = refs[7:13]
    outs, (gate, up) = refs[13 : 13 + chips], refs[13 + chips :]
    place_halves(chips, folds, halves, (c1t, c3t, c2t))
    keys = both(ko, kx)
    dbb, up[...], gate[...] = second_adjoint(
        c1t[...], c3t[...], c2t[...], keys, push[...],
        up_slope[...], silu[...], back_slope[...], back_curve[...],
    )
    send_pieces(chips, folds, (gate, up, push, keys, dbb), outs)
    own = dbb_ref.shape[1]
    dbb_ref[...], upb_ref[...], gpb_ref[...] = dbb[:, :own], up[:, :own], gate[:, :own]


def token_grads(rates, mixed, dbb, upb, gpb, gate_back, up_back, c1t, c3t, c2t, w1t, w3t, w2):
    value_grad = (rates * (nn(c2t, mixed) + tn(w2, dbb))).T.astype(BF16)
    key_total = tn(gate_back, c1t) + tn(up_back, c3t) + tn(gpb, w1t) + tn(upb, w3t)
    return value_grad, (-key_total).astype(BF16)


def token_kernel(*refs):
    value_grad, key_grad = refs[-2:]
    value_grad[...], key_grad[...] = token_grads(*(r[...] for r in refs[:-2]))


def call(kernel, outs, args, scratch=(), name=None, flops=0):
    vmem = pl.BlockSpec(memory_space=pltpu.VMEM)
    return pl.pallas_call(
        kernel,
        out_shape=[jax.ShapeDtypeStruct(s, t) for s, t in outs],
        in_specs=[vmem] * len(args),
        out_specs=[vmem] * len(outs),
        scratch_shapes=[pltpu.VMEM(s, t) for s, t in scratch],
        compiler_params=pltpu.CompilerParams(vmem_limit_bytes=VMEM_LIMIT),
        cost_estimate=pl.CostEstimate(
            flops=flops,
            bytes_accessed=sum(a.size * a.dtype.itemsize for a in args),
            transcendentals=0,
        ),
        name=name,
    )(*args)


def exchange(pieces, chips):
    count = chips * CORES
    got = [lax.ppermute(pieces[s], "tok", chip_perm(count, s)) for s in reversed(range(1, chips))]
    return [pieces[0], *got]


def to_chip(x, step, chips):
    return lax.ppermute(x, "tok", chip_perm(chips * CORES, step))


def half_sums(kept, given, chips):
    (mine,) = call(carry_kernel, [(given.shape, BF16)], (kept, to_chip(given, 1, chips)), name="carry")
    return [mine, *(to_chip(mine, step, chips) for step in range(2, chips, 2))]


def from_owners(halves, chips):
    others = [to_chip(half, 1, chips) for half in halves]
    *later, others[0] = lax.optimization_barrier((*halves, others[0]))
    cross = lambda x: lax.ppermute(x, "tok", core_perm(chips * CORES))
    parts = zip(halves, others, map(cross, later), map(cross, others))
    return [x for part in parts for x in part]


def head_parts(part, heads):
    got = [
        lax.ppermute(part, "head", [(h, partner(h, step, heads)) for h in range(heads)])
        for step in range(1, heads)
    ]
    return [part, *got]


def over_chips(blocks, count):
    groups = [list(range(core, count, CORES)) for core in range(CORES)]
    return lax.all_to_all(blocks, "tok", 0, 0, axis_index_groups=groups, tiled=True)


def gather_blocks(copies, count):
    mine = over_chips(copies, count)
    return mine, lax.ppermute(mine, "tok", core_perm(count))


def sliced_pieces(gate, up, down, tok, count):
    g, d = gate.shape[0] // count, down.shape[0] // count
    rows = lambda x, size, t: lax.dynamic_slice_in_dim(x, t * size, size, 0)
    piece = lambda t: pack(rows(gate, g, t), rows(up, g, t), rows(down, d, t))
    sent = [piece(t + tok % CORES) for t in range(0, count, CORES)]
    return piece(tok), jnp.concatenate(sent, axis=0).astype(BF16)


def total_of(own, got, tok):
    blocks = got.reshape((-1,) + own.shape)
    chip = lax.broadcasted_iota(jnp.int32, (blocks.shape[0], 1, 1), 0)
    others = jnp.where(chip == tok // CORES, 0.0, blocks.astype(F32))
    return own + jnp.sum(others, axis=0)


def whole_matrices(mine, other, tok, count, fh):
    shape = (count // CORES, -1, mine.shape[1])
    pair = jnp.stack([mine.reshape(shape), other.reshape(shape)], axis=1)
    pair = jnp.where(tok % CORES == 0, pair, pair[:, ::-1])
    held = pair.reshape((count, -1, mine.shape[1]))
    parts = jax.vmap(lambda x: unpack(x, fh))(held)
    return tuple(x.reshape((-1, x.shape[-1])) for x in parts)


def packed_owner_forward(prior, update, fh):
    fast, moved = zip(*(owner_forward(p, u, 1) for p, u in zip(unpack(prior, fh), unpack(update, fh))))
    return pack(*fast), pack(*moved)


def packed_owner_backward(prior, moved, fast_grad, fh):
    parts = (unpack(x, fh) for x in (prior, moved, fast_grad))
    cotangent, owned = zip(*(owner_backward(p, m, f, 1) for p, m, f in zip(*parts)))
    return pack(*cotangent), pack(*owned)


def per_device(
    query_input,
    key_input,
    value_input,
    out_grad,
    token_rates,
    out_gain,
    gate_prior,
    up_prior,
    down_prior,
):
    count, heads = lax.axis_size("tok"), lax.axis_size("head")
    tok = lax.axis_index("tok")
    chips = count // CORES
    own, dh = key_input.shape
    n = own * CORES
    w1, w3, w2 = gate_prior[0], up_prior[0], down_prior[0]
    fh = w2.shape[0]
    g, d = fh // count, dh // count
    rates = token_rates.T
    gain = out_gain[None, :]
    inputs = query_input, key_input, value_input, out_grad, rates, gain, w1, w3, w2

    if g % ROW_TILE or d % g or dh * g != fh * d or chips & (chips - 1) or chips < 2:
        query_grad, key_grad, value_grad, *results = by_blocks(inputs, tok, count, heads)
    else:
        query_grad, key_grad, value_grad, *results = by_line(inputs, chips, heads)
    return (query_grad, key_grad, value_grad, *(r.T[None] for r in results))


def by_line(inputs, chips, heads):
    query_input, key_input, value_input, out_grad, rates, gain, w1, w3, w2 = inputs
    count = chips * CORES
    own, dh = key_input.shape
    n, fh = own * CORES, w2.shape[0]
    g, d, folds = fh // count, dh // count, dh // fh
    product = 2 * n * dh * fh

    half = (g * chips // 2, dh)
    half_shares = [(half, F32)] * 3 + [(half, BF16)] * 3
    matrices = [((fh, dh), BF16), ((fh, dh), BF16), ((dh, fh), BF16)]
    sums_scratch = [((fh, dh), F32), ((fh, dh), F32), ((dh, fh), F32)]
    operands = [((fh, n), BF16), ((fh, n), BF16), ((dh, n), BF16)]
    hidden = ((fh, n), F32)
    own_hidden = ((fh, own), BF16)
    folds_by_matrix = (1, 1, folds)

    pair = lambda x: lax.ppermute(x, "tok", core_perm(count))
    key_other, value_other, rate_other = pair(key_input), pair(value_input), pair(rates)
    w1t, w3t = w1.T, w3.T
    query_other, grad_other = pair(query_input), pair(out_grad)
    keys_values = (
        key_input, key_other, value_input, value_other, rates, rate_other, w1t, w3t, w2,
    )
    sums = call(
        functools.partial(update_kernel, chips, folds),
        half_shares,
        keys_values,
        operands,
        "update",
        6 * product,
    )
    *saved, weighted, p1, p3, p2 = call(
        functools.partial(saved_kernel, chips, folds),
        [((dh, n), BF16)] + [hidden] * 4 + [own_hidden] * 3 + [((dh, n), F32)] + [(half, F32)] * 3,
        (*keys_values, out_grad, grad_other, gain),
        sums_scratch,
        "saved",
        3 * product,
    )
    push, up_slope, silu, back_slope, back_curve, mixed, gate_back, up_back = saved
    priors = p1, p3, p2

    fast, moved = [], []
    for k in range(3):
        totals = half_sums(sums[k], sums[3 + k], chips)
        rows, rows_moved = call(
            functools.partial(owner_forward_kernel, folds_by_matrix[k]),
            [(half, BF16), (half, F32)],
            (priors[k], *totals),
            name="owner_forward",
        )
        moved.append(rows_moved)
        fast.append(rows)
    f1t, f3t, f2t, output, q_mixed, q_slope, q_silu, part = call(
        functools.partial(apply_kernel, chips, folds),
        matrices + [((dh, n), F32), ((fh, n), BF16), hidden, hidden, ((2, n), F32)],
        (*from_owners(fast, chips), query_input, query_other, weighted),
        name="apply",
        flops=3 * product,
    )
    q_gate_back, q_up_back, *sums = call(
        functools.partial(back_kernel, chips, folds, heads),
        [own_hidden] * 2 + half_shares,
        (
            *head_parts(part, heads),
            f2t, output, weighted, q_mixed, q_slope, q_silu, query_input, query_other,
        ),
        operands,
        "apply_back",
        4 * product,
    )
    (query_grad,) = call(
        query_kernel,
        [((own, dh), BF16)],
        (q_gate_back, q_up_back, f1t, f3t),
        name="query_grad",
        flops=product,
    )

    cotangent, owned = [], []
    for k in range(3):
        totals = half_sums(sums[k], sums[3 + k], chips)
        rows, rows_owned = call(
            functools.partial(owner_backward_kernel, folds_by_matrix[k]),
            [(half, BF16), (half, F32)],
            (priors[k], moved[k], *totals),
            name="owner_backward",
        )
        owned.append(rows_owned)
        cotangent.append(rows)
    c1t, c3t, c2t, dbb, upb, gpb, *pieces = call(
        functools.partial(second_kernel, chips, folds),
        matrices + [own_hidden] * 3 + [((3 * g, dh), F32)] + [((3 * g, dh), BF16)] * (chips - 1),
        (
            *from_owners(cotangent, chips),
            key_input, key_other, push, up_slope, silu, back_slope, back_curve,
        ),
        operands[:2],
        "second_adjoint",
        6 * product,
    )
    value_grad, key_grad = call(
        token_kernel,
        [((own, dh), BF16)] * 2,
        (rates, mixed, dbb, upb, gpb, gate_back, up_back, c1t, c3t, c2t, w1t, w3t, w2),
        name="token_grads",
        flops=3 * product,
    )
    results = call(
        functools.partial(owner_result_kernel, chips, folds),
        [((g, dh), F32)] * 2 + [((d, fh), F32)],
        (*owned, *exchange(pieces, chips)),
        name="owner_result",
    )
    return query_grad, key_grad, value_grad, *results


def by_blocks(inputs, tok, count, heads):
    query_input, key_input, value_input, out_grad, rates, gain, w1, w3, w2 = inputs
    own, dh = key_input.shape
    fh, chips = w2.shape[0], count // CORES
    g, d = fh // count, dh // count
    w1t, w3t = w1.T, w3.T
    pair = lambda x, axis=0: jnp.concatenate(
        [x, lax.ppermute(x, "tok", core_perm(count))], axis=axis
    )
    keys, values, queries, rate = pair(key_input), pair(value_input), pair(query_input), pair(rates, 1)
    weighted = (pair(out_grad).astype(F32) * gain).T
    push = push_of(rate, values)
    up_pre, silu, slope, curvature, mixed, down_back, back_slope, gate_back, up_back = (
        update_forward(w1t, w3t, w2, keys, push)
    )
    up_slope, back_curve = up_pre * slope, down_back * up_pre * curvature
    sums = nn(gate_back, keys), nn(up_back, keys), nt(push, mixed)
    piece, sent = sliced_pieces(*sums, tok, count)
    prior = pack(
        *(
            lax.dynamic_slice_in_dim(x, tok * rows, rows, 0).astype(F32)
            for x, rows in ((w1t, g), (w3t, g), (w2.T, d))
        )
    )
    update = total_of(piece, over_chips(sent, count), tok)
    fast, moved = packed_owner_forward(prior, update, fh)
    blocks = gather_blocks(jnp.tile(fast, (chips, 1)), count)
    f1t, f3t, f2t = whole_matrices(*blocks, tok, count, fh)
    output, q_mixed, q_slope, q_silu, part = apply_forward(f1t, f3t, f2t, queries, weighted)
    sums = lax.psum(part, "head")
    q_gate_back, q_up_back, out_back = apply_backward(
        f2t, sums, heads * dh, output, weighted, q_slope, q_silu
    )
    grads = nn(q_gate_back, queries), nn(q_up_back, queries), nt(out_back, q_mixed)
    piece, sent = sliced_pieces(*grads, tok, count)
    query_grad = (tn(q_gate_back[:, :own], f1t) + tn(q_up_back[:, :own], f3t)).astype(BF16)
    fast_grad = total_of(piece, over_chips(sent, count), tok)
    cotangent, owned = packed_owner_backward(prior, moved, fast_grad, fh)
    blocks = gather_blocks(jnp.tile(cotangent, (chips, 1)), count)
    c1t, c3t, c2t = whole_matrices(*blocks, tok, count, fh)
    dbb, upb, gpb = second_adjoint(
        c1t, c3t, c2t, keys, push, up_slope, silu, back_slope, back_curve
    )
    bars = nn(gpb, keys), nn(upb, keys), nt(push, dbb)
    piece, sent = sliced_pieces(*bars, tok, count)
    value_grad, key_grad = token_grads(
        rates, mixed[:, :own], dbb[:, :own], upb[:, :own], gpb[:, :own],
        gate_back[:, :own], up_back[:, :own], c1t, c3t, c2t, w1t, w3t, w2,
    )
    results = unpack(owned - total_of(piece, over_chips(sent, count), tok), fh)
    return query_grad, key_grad, value_grad, *results


def solution(mesh):
    tokens = P("tok", "head")
    in_specs = (tokens,) * 5 + (P("head"),) + (P("head", None, None),) * 3
    out_specs = (tokens,) * 3 + (P("head", None, "tok"),) * 3
    return jax.shard_map(
        per_device, mesh=mesh, in_specs=in_specs, out_specs=out_specs, check_vma=False
    )
```

```python
import functools

import jax
import jax.numpy as jnp
from jax import lax
from jax.experimental import pallas as pl
from jax.experimental.pallas import tpu as pltpu
from jax.sharding import PartitionSpec as P

EPSILON = 1e-06
CORES = 2
ROW_TILE = 16
VMEM_LIMIT = 24 * 1024 * 1024
BF16, F32 = jnp.bfloat16, jnp.float32


def nn(a, b):
    return lax.dot_general(a, b, (((1,), (0,)), ((), ())), preferred_element_type=F32)


def nt(a, b):
    return lax.dot_general(a, b, (((1,), (1,)), ((), ())), preferred_element_type=F32)


def tn(a, b):
    return lax.dot_general(a, b, (((0,), (0,)), ((), ())), preferred_element_type=F32)


def silu_parts(hidden):
    sigmoid_value = jax.nn.sigmoid(hidden)
    silu_value = hidden * sigmoid_value
    silu_slope = sigmoid_value * (1.0 + hidden * (1.0 - sigmoid_value))
    curvature = sigmoid_value * (1.0 - sigmoid_value) * (2.0 + hidden * (1.0 - 2.0 * sigmoid_value))
    return silu_value, silu_slope, curvature


def partner(index, step, count):
    return index ^ step if count & (count - 1) == 0 else (index + step) % count


def source(index, step, count):
    return index ^ step if count & (count - 1) == 0 else (index + count - step) % count


def chip_perm(count, step):
    chips = count // CORES
    return [(t, partner(t // CORES, step, chips) * CORES + t % CORES) for t in range(count)]


def core_perm(count):
    return [(t, t ^ 1) for t in range(count)]


def pack(gate, up, down):
    folds = gate.shape[1] // down.shape[1]
    rows = down.shape[0] // folds
    down = jnp.concatenate([down[i * rows : (i + 1) * rows] for i in range(folds)], axis=1)
    return jnp.concatenate([gate, up, down], axis=0)


def unpack(packed, fh):
    g = packed.shape[0] // 3
    folds = packed.shape[1] // fh
    down = packed[2 * g :]
    down = jnp.concatenate([down[:, i * fh : (i + 1) * fh] for i in range(folds)], axis=0)
    return packed[:g], packed[g : 2 * g], down


def gate_and_up(w1t, w3t, keys):
    gate_pre, up_pre = nt(w1t, keys), nt(w3t, keys)
    silu, slope, curvature = silu_parts(gate_pre)
    return up_pre, silu, slope, curvature, (silu * up_pre).astype(BF16)


def back_through_down(w2, push, up_slope, silu):
    down_back = nn(w2, push)
    return down_back, (down_back * up_slope).astype(BF16), (down_back * silu).astype(BF16)


def update_forward(w1t, w3t, w2, keys, push):
    up_pre, silu, slope, curvature, mixed = gate_and_up(w1t, w3t, keys)
    down_back, gate_back, up_back = back_through_down(w2, push, up_pre * slope, silu)
    return up_pre, silu, slope, curvature, mixed, down_back, down_back * slope, gate_back, up_back


def apply_forward(f1t, f3t, f2t, queries, weighted):
    q_gate, q_up = nt(f1t, queries), nt(f3t, queries)
    silu, slope, _ = silu_parts(q_gate)
    mixed = (silu * q_up).astype(BF16)
    output = nn(f2t, mixed)
    square = jnp.sum(output * output, axis=0, keepdims=True)
    dot = jnp.sum(weighted * output, axis=0, keepdims=True)
    return output, mixed, q_up * slope, silu, jnp.concatenate([square, dot], axis=0)


def output_back(sums, full_width, output, weighted):
    inverse = lax.rsqrt(sums[0:1] / full_width + EPSILON)
    scale = inverse * inverse * inverse * sums[1:2] / full_width
    return (inverse * weighted - output * scale).astype(BF16)


def apply_backward(f2t, out_back, up_slope, silu):
    q_back = tn(f2t, out_back)
    return (q_back * up_slope).astype(BF16), (q_back * silu).astype(BF16)


def second_adjoint(c1t, c3t, c2t, keys, push, up_slope, silu, back_slope, back_curve):
    gate_bar, up_bar, mixed_bar = nt(c1t, keys), nt(c3t, keys), tn(c2t, push)
    down_back_bar = (gate_bar * up_slope + up_bar * silu).astype(BF16)
    up_pre_bar = (gate_bar * back_slope + mixed_bar * silu).astype(BF16)
    gate_pre_bar = (up_bar * back_slope + mixed_bar * up_slope + gate_bar * back_curve).astype(BF16)
    return down_back_bar, up_pre_bar, gate_pre_bar


def folds_of(rows, folds):
    width = rows.shape[1] // folds
    return [rows[:, i * width : (i + 1) * width] for i in range(folds)]


def norm_of(rows):
    return jnp.sqrt(jnp.sum(rows * rows, axis=1, keepdims=True) + EPSILON)


def owner_forward(prior, update, folds):
    moved = prior - update
    fast = [
        m * (norm_of(p) / norm_of(m)) for p, m in zip(folds_of(prior, folds), folds_of(moved, folds))
    ]
    return jnp.concatenate(fast, axis=1).astype(BF16), moved


def owner_backward(prior, moved, fast_grad, folds):
    cotangent, owned = [], []
    for p, m, fg in zip(*(folds_of(x, folds) for x in (prior, moved, fast_grad))):
        prior_norm, moved_norm = norm_of(p), norm_of(m)
        column_dot = jnp.sum(fg * m, axis=1, keepdims=True)
        moved_grad = (prior_norm / moved_norm) * (fg - m * (column_dot / (moved_norm * moved_norm)))
        cotangent.append(moved_grad)
        owned.append(moved_grad + p * (column_dot / (moved_norm * prior_norm)))
    return jnp.concatenate(cotangent, axis=1).astype(BF16), jnp.concatenate(owned, axis=1)


def push_of(rates, values):
    return (-rates * values.T.astype(F32)).astype(BF16)


def both(own_ref, other_ref, axis=0):
    return jnp.concatenate([own_ref[...], other_ref[...]], axis=axis)


def rows_of(ref, chip, core, chips, folds, i):
    rows = ref.shape[0] // (chips * CORES)
    height = rows // folds
    return pl.ds(pl.multiple_of((chip * CORES + core) * rows + i * height, height), height)


def cut_half(out, ref, parity, chips, folds):
    core = lax.axis_index("tok") % CORES
    height, width = ref.shape[0] // (chips * CORES * folds), ref.shape[1]
    for k in range(chips // 2):
        for i in range(folds):
            out[k * height : (k + 1) * height, i * width : (i + 1) * width] = ref[
                rows_of(ref, 2 * k + parity, core, chips, folds, i), :
            ].astype(out.dtype)


def place_half(ref, half, parity, core, chips, folds):
    height, width = ref.shape[0] // (chips * CORES * folds), ref.shape[1]
    for k in range(chips // 2):
        for i in range(folds):
            ref[rows_of(ref, 2 * k + parity, core, chips, folds, i), :] = half[
                k * height : (k + 1) * height, i * width : (i + 1) * width
            ]


def place_halves(chips, folds, halves, matrices):
    tok = lax.axis_index("tok")
    parity, core = tok // CORES % 2, tok % CORES
    for k, ref in enumerate(matrices):
        whose = ((parity, core), (1 - parity, core), (parity, 1 - core), (1 - parity, 1 - core))
        for half, (p, c) in zip(halves[4 * k : 4 * k + 4], whose):
            place_half(ref, half, p, c, chips, folds if k == 2 else 1)


def rows_of_core(ref, order, chips):
    core = lax.axis_index("tok") % CORES
    rows = ref.shape[0] // (chips * CORES)
    blocks = [
        ref[pl.ds(pl.multiple_of((chip * CORES + core) * rows, rows), rows), :] for chip in order
    ]
    return jnp.concatenate(blocks, axis=0)


def fold(rows, chips, folds):
    height = rows.shape[0] // (chips * folds)
    parts = [rows[i * height : (i + 1) * height] for i in range(chips * folds)]
    wide = [jnp.concatenate(parts[k : k + folds], axis=1) for k in range(0, len(parts), folds)]
    return jnp.concatenate(wide, axis=0)


def send_pieces(chips, folds, operands, outs):
    gate_ref, up_ref, down_ref, tokens, hidden = operands
    chip = lax.axis_index("tok") // CORES
    order = [partner(chip, step, chips) for step in range(chips)]
    sums = [nn(rows_of_core(ref, order, chips), tokens) for ref in (gate_ref, up_ref)]
    sums.append(fold(nt(rows_of_core(down_ref, order, chips), hidden), chips, folds))
    g = sums[0].shape[0] // chips
    for k, out in enumerate(outs):
        parts = [x[k * g : (k + 1) * g] for x in sums]
        out[...] = jnp.concatenate(parts, axis=0).astype(out.dtype)


def halves_order(chips):
    parity = lax.axis_index("tok") // CORES % 2
    return [2 * k + p for p in (parity, 1 - parity) for k in range(chips // 2)]


def send_halves(sums, kept, given):
    half = kept.shape[0]
    kept[...], given[...] = sums[:half], sums[half:].astype(BF16)


def send_down(chips, folds, rows_ref, hidden, kept, given):
    sums = nt(rows_of_core(rows_ref, halves_order(chips), chips), hidden)
    send_halves(fold(sums, chips, folds), kept, given)


def send_gate_and_up(chips, gate_ref, up_ref, tokens, gate_kept, up_kept, gate_given, up_given):
    order = halves_order(chips)
    send_halves(nn(rows_of_core(gate_ref, order, chips), tokens), gate_kept, gate_given)
    send_halves(nn(rows_of_core(up_ref, order, chips), tokens), up_kept, up_given)


def update_down_kernel(
    chips, folds, ko, kx, vo, vx, ro, rx, w1t, w3t, kept, given, push, up_slope_ref, silu_ref
):
    push[...] = push_of(both(ro, rx, 1), both(vo, vx))
    up_pre, silu, slope, _, mixed = gate_and_up(w1t[...], w3t[...], both(ko, kx))
    send_down(chips, folds, push, mixed, kept, given)
    up_slope_ref[...], silu_ref[...] = up_pre * slope, silu


def update_gate_kernel(chips, ko, kx, w2, push, up_slope, silu, *rest):
    outs, (gate, up) = rest[:4], rest[4:]
    _, gate[...], up[...] = back_through_down(w2[...], push[...], up_slope[...], silu[...])
    send_gate_and_up(chips, gate, up, both(ko, kx), *outs)


def saved_kernel(
    chips, folds, ko, kx, vo, vx, ro, rx, w1t, w3t, w2, go, gx, gain,
    push_ref, up_slope_ref, silu_ref, back_slope_ref, back_curve_ref,
    mixed_ref, gate_back_ref, up_back_ref, weighted_ref, p1_ref, p3_ref, p2_ref,
    gate_ref, up_ref, down_ref,
):
    push = push_of(both(ro, rx, 1), both(vo, vx))
    push_ref[...] = push
    up_pre, silu, slope, curvature, mixed, down_back, back_slope, gate_back, up_back = (
        update_forward(w1t[...], w3t[...], w2[...], both(ko, kx), push)
    )
    up_slope_ref[...] = up_pre * slope
    silu_ref[...] = silu
    back_slope_ref[...] = back_slope
    back_curve_ref[...] = down_back * up_pre * curvature
    own = mixed_ref.shape[1]
    mixed_ref[...] = mixed[:, :own]
    gate_back_ref[...] = gate_back[:, :own]
    up_back_ref[...] = up_back[:, :own]
    weighted_ref[...] = (both(go, gx).astype(F32) * gain[...]).T
    gate_ref[...] = w1t[...].astype(F32)
    up_ref[...] = w3t[...].astype(F32)
    down_ref[...] = w2[...].astype(F32).T
    parity = lax.axis_index("tok") // CORES % 2
    cut_half(p1_ref, gate_ref, parity, chips, 1)
    cut_half(p3_ref, up_ref, parity, chips, 1)
    cut_half(p2_ref, down_ref, parity, chips, folds)


def carry_kernel(own, got, out):
    out[...] = (own[...] + got[...].astype(F32)).astype(BF16)


def total_of_halves(halves):
    total = halves[0][...].astype(F32)
    for half in halves[1:]:
        total = total + half[...].astype(F32)
    return total


def owner_forward_kernel(folds, prior, *refs):
    fast, moved = refs[-2:]
    total = total_of_halves(refs[:-2])
    fast[...], moved[...] = owner_forward(prior[...], total, folds)


def owner_backward_kernel(folds, prior, moved, *refs):
    cotangent, owned = refs[-2:]
    total = total_of_halves(refs[:-2])
    cotangent[...], owned[...] = owner_backward(prior[...], moved[...], total, folds)


def owner_result_kernel(chips, folds, *refs):
    owned, pieces, outs = refs[:3], refs[3:-3], refs[-3:]
    bars = pieces[0][...]
    for piece in pieces[1:]:
        bars = bars + piece[...].astype(F32)
    g = outs[0].shape[0]
    block = lax.axis_index("tok") // (2 * CORES)
    for k, out in enumerate(outs):
        result = owned[k][pl.ds(pl.multiple_of(block * g, g), g), :] - bars[k * g : (k + 1) * g]
        for i, rows in enumerate(folds_of(result, folds if k == 2 else 1)):
            out[i * g : (i + 1) * g] = rows


def apply_kernel(chips, folds, *refs):
    halves, refs = refs[:12], refs[12:]
    qo, qx, weighted, f1t, f3t, f2t, output, mixed, up_slope, silu, sums = refs
    place_halves(chips, folds, halves, (f1t, f3t, f2t))
    output[...], mixed[...], up_slope[...], silu[...], sums[...] = apply_forward(
        f1t[...], f3t[...], f2t[...], both(qo, qx), weighted[...]
    )


def back_kernel(chips, folds, heads, *refs):
    parts, refs = refs[:heads], refs[heads:]
    sums = parts[0][...]
    for part in parts[1:]:
        sums = sums + part[...]
    f2t, output, weighted, mixed, up_slope, silu, qo, qx, gate_back, up_back = refs[:10]
    down_kept, down_given, *outs = refs[10:16]
    gate, up, out_back = refs[16:]
    out_back[...] = output_back(sums, heads * output.shape[0], output[...], weighted[...])
    send_down(chips, folds, out_back, mixed[...], down_kept, down_given)
    gate[...], up[...] = apply_backward(f2t[...], out_back[...], up_slope[...], silu[...])
    send_gate_and_up(chips, gate, up, both(qo, qx), *outs)
    own = gate_back.shape[1]
    gate_back[...], up_back[...] = gate[:, :own], up[:, :own]


def query_kernel(gate_back, up_back, f1t, f3t, out):
    out[...] = (tn(gate_back[...], f1t[...]) + tn(up_back[...], f3t[...])).astype(BF16)


def second_kernel(chips, folds, *refs):
    halves, refs = refs[:12], refs[12:]
    ko, kx, push, up_slope, silu, back_slope, back_curve = refs[:7]
    c1t, c3t, c2t, dbb_ref, upb_ref, gpb_ref = refs[7:13]
    outs, (gate, up) = refs[13 : 13 + chips], refs[13 + chips :]
    place_halves(chips, folds, halves, (c1t, c3t, c2t))
    keys = both(ko, kx)
    dbb, up[...], gate[...] = second_adjoint(
        c1t[...], c3t[...], c2t[...], keys, push[...],
        up_slope[...], silu[...], back_slope[...], back_curve[...],
    )
    send_pieces(chips, folds, (gate, up, push, keys, dbb), outs)
    own = dbb_ref.shape[1]
    dbb_ref[...], upb_ref[...], gpb_ref[...] = dbb[:, :own], up[:, :own], gate[:, :own]


def token_grads(rates, mixed, dbb, upb, gpb, gate_back, up_back, c1t, c3t, c2t, w1t, w3t, w2):
    value_grad = (rates * (nn(c2t, mixed) + tn(w2, dbb))).T.astype(BF16)
    key_total = tn(gate_back, c1t) + tn(up_back, c3t) + tn(gpb, w1t) + tn(upb, w3t)
    return value_grad, (-key_total).astype(BF16)


def token_kernel(*refs):
    value_grad, key_grad = refs[-2:]
    value_grad[...], key_grad[...] = token_grads(*(r[...] for r in refs[:-2]))


def call(kernel, outs, args, scratch=(), name=None, flops=0):
    vmem = pl.BlockSpec(memory_space=pltpu.VMEM)
    return pl.pallas_call(
        kernel,
        out_shape=[jax.ShapeDtypeStruct(s, t) for s, t in outs],
        in_specs=[vmem] * len(args),
        out_specs=[vmem] * len(outs),
        scratch_shapes=[pltpu.VMEM(s, t) for s, t in scratch],
        compiler_params=pltpu.CompilerParams(vmem_limit_bytes=VMEM_LIMIT),
        cost_estimate=pl.CostEstimate(
            flops=flops,
            bytes_accessed=sum(a.size * a.dtype.itemsize for a in args),
            transcendentals=0,
        ),
        name=name,
    )(*args)


def exchange(pieces, chips):
    count = chips * CORES
    got = [lax.ppermute(pieces[s], "tok", chip_perm(count, s)) for s in reversed(range(1, chips))]
    return [pieces[0], *got]


def to_chip(x, step, chips):
    return lax.ppermute(x, "tok", chip_perm(chips * CORES, step))


def half_sums(kept, given, chips):
    (mine,) = call(carry_kernel, [(given.shape, BF16)], (kept, to_chip(given, 1, chips)), name="carry")
    return [mine, *(to_chip(mine, step, chips) for step in range(2, chips, 2))]


def from_owners(halves, chips):
    others = [to_chip(half, 1, chips) for half in halves]
    *later, others[0] = lax.optimization_barrier((*halves, others[0]))
    cross = lambda x: lax.ppermute(x, "tok", core_perm(chips * CORES))
    parts = zip(halves, others, map(cross, later), map(cross, others))
    return [x for part in parts for x in part]


def head_parts(part, heads):
    got = [
        lax.ppermute(part, "head", [(h, partner(h, step, heads)) for h in range(heads)])
        for step in range(1, heads)
    ]
    return [part, *got]


def over_chips(blocks, count):
    groups = [list(range(core, count, CORES)) for core in range(CORES)]
    return lax.all_to_all(blocks, "tok", 0, 0, axis_index_groups=groups, tiled=True)


def gather_blocks(copies, count):
    mine = over_chips(copies, count)
    return mine, lax.ppermute(mine, "tok", core_perm(count))


def sliced_pieces(gate, up, down, tok, count):
    g, d = gate.shape[0] // count, down.shape[0] // count
    rows = lambda x, size, t: lax.dynamic_slice_in_dim(x, t * size, size, 0)
    piece = lambda t: pack(rows(gate, g, t), rows(up, g, t), rows(down, d, t))
    sent = [piece(t + tok % CORES) for t in range(0, count, CORES)]
    return piece(tok), jnp.concatenate(sent, axis=0).astype(BF16)


def total_of(own, got, tok):
    blocks = got.reshape((-1,) + own.shape)
    chip = lax.broadcasted_iota(jnp.int32, (blocks.shape[0], 1, 1), 0)
    others = jnp.where(chip == tok // CORES, 0.0, blocks.astype(F32))
    return own + jnp.sum(others, axis=0)


def whole_matrices(mine, other, tok, count, fh):
    shape = (count // CORES, -1, mine.shape[1])
    pair = jnp.stack([mine.reshape(shape), other.reshape(shape)], axis=1)
    pair = jnp.where(tok % CORES == 0, pair, pair[:, ::-1])
    held = pair.reshape((count, -1, mine.shape[1]))
    parts = jax.vmap(lambda x: unpack(x, fh))(held)
    return tuple(x.reshape((-1, x.shape[-1])) for x in parts)


def packed_owner_forward(prior, update, fh):
    fast, moved = zip(*(owner_forward(p, u, 1) for p, u in zip(unpack(prior, fh), unpack(update, fh))))
    return pack(*fast), pack(*moved)


def packed_owner_backward(prior, moved, fast_grad, fh):
    parts = (unpack(x, fh) for x in (prior, moved, fast_grad))
    cotangent, owned = zip(*(owner_backward(p, m, f, 1) for p, m, f in zip(*parts)))
    return pack(*cotangent), pack(*owned)


def per_device(
    query_input,
    key_input,
    value_input,
    out_grad,
    token_rates,
    out_gain,
    gate_prior,
    up_prior,
    down_prior,
):
    count, heads = lax.axis_size("tok"), lax.axis_size("head")
    tok = lax.axis_index("tok")
    chips = count // CORES
    own, dh = key_input.shape
    n = own * CORES
    w1, w3, w2 = gate_prior[0], up_prior[0], down_prior[0]
    fh = w2.shape[0]
    g, d = fh // count, dh // count
    rates = token_rates.T
    gain = out_gain[None, :]
    inputs = query_input, key_input, value_input, out_grad, rates, gain, w1, w3, w2

    if g % ROW_TILE or d % g or dh * g != fh * d or chips & (chips - 1) or chips < 2:
        query_grad, key_grad, value_grad, *results = by_blocks(inputs, tok, count, heads)
    else:
        query_grad, key_grad, value_grad, *results = by_line(inputs, chips, heads)
    return (query_grad, key_grad, value_grad, *(r.T[None] for r in results))


def by_line(inputs, chips, heads):
    query_input, key_input, value_input, out_grad, rates, gain, w1, w3, w2 = inputs
    count = chips * CORES
    own, dh = key_input.shape
    n, fh = own * CORES, w2.shape[0]
    g, d, folds = fh // count, dh // count, dh // fh
    product = 2 * n * dh * fh

    half = (g * chips // 2, dh)
    down_halves = [(half, F32), (half, BF16)]
    gate_halves = [(half, F32)] * 2 + [(half, BF16)] * 2
    matrices = [((fh, dh), BF16), ((fh, dh), BF16), ((dh, fh), BF16)]
    sums_scratch = [((fh, dh), F32), ((fh, dh), F32), ((dh, fh), F32)]
    operands = [((fh, n), BF16), ((fh, n), BF16), ((dh, n), BF16)]
    hidden = ((fh, n), F32)
    own_hidden = ((fh, own), BF16)
    folds_by_matrix = (1, 1, folds)

    pair = lambda x: lax.ppermute(x, "tok", core_perm(count))
    key_other, value_other, rate_other = pair(key_input), pair(value_input), pair(rates)
    w1t, w3t = w1.T, w3.T
    query_other, grad_other = pair(query_input), pair(out_grad)
    keys_values = (
        key_input, key_other, value_input, value_other, rates, rate_other, w1t, w3t, w2,
    )
    down_kept, down_given, push, up_slope, silu = call(
        functools.partial(update_down_kernel, chips, folds),
        down_halves + [((dh, n), BF16), hidden, hidden],
        keys_values[:-1],
        name="update_down",
        flops=3 * product,
    )
    gate_kept, up_kept, gate_given, up_given = call(
        functools.partial(update_gate_kernel, chips),
        gate_halves,
        (key_input, key_other, w2, push, up_slope, silu),
        operands[:2],
        "update_gate",
        3 * product,
    )
    sums = gate_kept, up_kept, down_kept, gate_given, up_given, down_given
    *saved, weighted, p1, p3, p2 = call(
        functools.partial(saved_kernel, chips, folds),
        [((dh, n), BF16)] + [hidden] * 4 + [own_hidden] * 3 + [((dh, n), F32)] + [(half, F32)] * 3,
        (*keys_values, out_grad, grad_other, gain),
        sums_scratch,
        "saved",
        3 * product,
    )
    push, up_slope, silu, back_slope, back_curve, mixed, gate_back, up_back = saved
    priors = p1, p3, p2

    fast, moved = [], []
    for k in range(3):
        totals = half_sums(sums[k], sums[3 + k], chips)
        rows, rows_moved = call(
            functools.partial(owner_forward_kernel, folds_by_matrix[k]),
            [(half, BF16), (half, F32)],
            (priors[k], *totals),
            name="owner_forward",
        )
        moved.append(rows_moved)
        fast.append(rows)
    f1t, f3t, f2t, output, q_mixed, q_slope, q_silu, part = call(
        functools.partial(apply_kernel, chips, folds),
        matrices + [((dh, n), F32), ((fh, n), BF16), hidden, hidden, ((2, n), F32)],
        (*from_owners(fast, chips), query_input, query_other, weighted),
        name="apply",
        flops=3 * product,
    )
    q_gate_back, q_up_back, down_kept, down_given, gate_kept, up_kept, gate_given, up_given = call(
        functools.partial(back_kernel, chips, folds, heads),
        [own_hidden] * 2 + down_halves + gate_halves,
        (
            *head_parts(part, heads),
            f2t, output, weighted, q_mixed, q_slope, q_silu, query_input, query_other,
        ),
        operands,
        "apply_back",
        4 * product,
    )
    sums = gate_kept, up_kept, down_kept, gate_given, up_given, down_given
    (query_grad,) = call(
        query_kernel,
        [((own, dh), BF16)],
        (q_gate_back, q_up_back, f1t, f3t),
        name="query_grad",
        flops=product,
    )

    cotangent, owned = [], []
    for k in range(3):
        totals = half_sums(sums[k], sums[3 + k], chips)
        rows, rows_owned = call(
            functools.partial(owner_backward_kernel, folds_by_matrix[k]),
            [(half, BF16), (half, F32)],
            (priors[k], moved[k], *totals),
            name="owner_backward",
        )
        owned.append(rows_owned)
        cotangent.append(rows)
    c1t, c3t, c2t, dbb, upb, gpb, *pieces = call(
        functools.partial(second_kernel, chips, folds),
        matrices + [own_hidden] * 3 + [((3 * g, dh), F32)] + [((3 * g, dh), BF16)] * (chips - 1),
        (
            *from_owners(cotangent, chips),
            key_input, key_other, push, up_slope, silu, back_slope, back_curve,
        ),
        operands[:2],
        "second_adjoint",
        6 * product,
    )
    value_grad, key_grad = call(
        token_kernel,
        [((own, dh), BF16)] * 2,
        (rates, mixed, dbb, upb, gpb, gate_back, up_back, c1t, c3t, c2t, w1t, w3t, w2),
        name="token_grads",
        flops=3 * product,
    )
    results = call(
        functools.partial(owner_result_kernel, chips, folds),
        [((g, dh), F32)] * 2 + [((d, fh), F32)],
        (*owned, *exchange(pieces, chips)),
        name="owner_result",
    )
    return query_grad, key_grad, value_grad, *results


def by_blocks(inputs, tok, count, heads):
    query_input, key_input, value_input, out_grad, rates, gain, w1, w3, w2 = inputs
    own, dh = key_input.shape
    fh, chips = w2.shape[0], count // CORES
    g, d = fh // count, dh // count
    w1t, w3t = w1.T, w3.T
    pair = lambda x, axis=0: jnp.concatenate(
        [x, lax.ppermute(x, "tok", core_perm(count))], axis=axis
    )
    keys, values, queries, rate = pair(key_input), pair(value_input), pair(query_input), pair(rates, 1)
    weighted = (pair(out_grad).astype(F32) * gain).T
    push = push_of(rate, values)
    up_pre, silu, slope, curvature, mixed, down_back, back_slope, gate_back, up_back = (
        update_forward(w1t, w3t, w2, keys, push)
    )
    up_slope, back_curve = up_pre * slope, down_back * up_pre * curvature
    sums = nn(gate_back, keys), nn(up_back, keys), nt(push, mixed)
    piece, sent = sliced_pieces(*sums, tok, count)
    prior = pack(
        *(
            lax.dynamic_slice_in_dim(x, tok * rows, rows, 0).astype(F32)
            for x, rows in ((w1t, g), (w3t, g), (w2.T, d))
        )
    )
    update = total_of(piece, over_chips(sent, count), tok)
    fast, moved = packed_owner_forward(prior, update, fh)
    blocks = gather_blocks(jnp.tile(fast, (chips, 1)), count)
    f1t, f3t, f2t = whole_matrices(*blocks, tok, count, fh)
    output, q_mixed, q_slope, q_silu, part = apply_forward(f1t, f3t, f2t, queries, weighted)
    sums = lax.psum(part, "head")
    out_back = output_back(sums, heads * dh, output, weighted)
    q_gate_back, q_up_back = apply_backward(f2t, out_back, q_slope, q_silu)
    grads = nn(q_gate_back, queries), nn(q_up_back, queries), nt(out_back, q_mixed)
    piece, sent = sliced_pieces(*grads, tok, count)
    query_grad = (tn(q_gate_back[:, :own], f1t) + tn(q_up_back[:, :own], f3t)).astype(BF16)
    fast_grad = total_of(piece, over_chips(sent, count), tok)
    cotangent, owned = packed_owner_backward(prior, moved, fast_grad, fh)
    blocks = gather_blocks(jnp.tile(cotangent, (chips, 1)), count)
    c1t, c3t, c2t = whole_matrices(*blocks, tok, count, fh)
    dbb, upb, gpb = second_adjoint(
        c1t, c3t, c2t, keys, push, up_slope, silu, back_slope, back_curve
    )
    bars = nn(gpb, keys), nn(upb, keys), nt(push, dbb)
    piece, sent = sliced_pieces(*bars, tok, count)
    value_grad, key_grad = token_grads(
        rates, mixed[:, :own], dbb[:, :own], upb[:, :own], gpb[:, :own],
        gate_back[:, :own], up_back[:, :own], c1t, c3t, c2t, w1t, w3t, w2,
    )
    results = unpack(owned - total_of(piece, over_chips(sent, count), tok), fh)
    return query_grad, key_grad, value_grad, *results


def solution(mesh):
    tokens = P("tok", "head")
    in_specs = (tokens,) * 5 + (P("head"),) + (P("head", None, None),) * 3
    out_specs = (tokens,) * 3 + (P("head", None, "tok"),) * 3
    return jax.shard_map(
        per_device, mesh=mesh, in_specs=in_specs, out_specs=out_specs, check_vma=False
    )
```

```python
import functools

import jax
import jax.numpy as jnp
from jax import lax
from jax.experimental import pallas as pl
from jax.experimental.pallas import tpu as pltpu
from jax.sharding import PartitionSpec as P

EPSILON = 1e-06
CORES = 2
ROW_TILE = 16
VMEM_LIMIT = 24 * 1024 * 1024
BF16, F32 = jnp.bfloat16, jnp.float32


def nn(a, b):
    return lax.dot_general(a, b, (((1,), (0,)), ((), ())), preferred_element_type=F32)


def nt(a, b):
    return lax.dot_general(a, b, (((1,), (1,)), ((), ())), preferred_element_type=F32)


def tn(a, b):
    return lax.dot_general(a, b, (((0,), (0,)), ((), ())), preferred_element_type=F32)


def silu_parts(hidden):
    sigmoid_value = jax.nn.sigmoid(hidden)
    silu_value = hidden * sigmoid_value
    silu_slope = sigmoid_value * (1.0 + hidden * (1.0 - sigmoid_value))
    curvature = sigmoid_value * (1.0 - sigmoid_value) * (2.0 + hidden * (1.0 - 2.0 * sigmoid_value))
    return silu_value, silu_slope, curvature


def partner(index, step, count):
    return index ^ step if count & (count - 1) == 0 else (index + step) % count


def source(index, step, count):
    return index ^ step if count & (count - 1) == 0 else (index + count - step) % count


def chip_perm(count, step):
    chips = count // CORES
    return [(t, partner(t // CORES, step, chips) * CORES + t % CORES) for t in range(count)]


def core_perm(count):
    return [(t, t ^ 1) for t in range(count)]


def pack(gate, up, down):
    folds = gate.shape[1] // down.shape[1]
    rows = down.shape[0] // folds
    down = jnp.concatenate([down[i * rows : (i + 1) * rows] for i in range(folds)], axis=1)
    return jnp.concatenate([gate, up, down], axis=0)


def unpack(packed, fh):
    g = packed.shape[0] // 3
    folds = packed.shape[1] // fh
    down = packed[2 * g :]
    down = jnp.concatenate([down[:, i * fh : (i + 1) * fh] for i in range(folds)], axis=0)
    return packed[:g], packed[g : 2 * g], down


def update_forward(w1t, w3t, w2, keys, push):
    gate_pre, up_pre = nt(w1t, keys), nt(w3t, keys)
    silu, slope, curvature = silu_parts(gate_pre)
    mixed = (silu * up_pre).astype(BF16)
    down_back = nn(w2, push)
    back_slope = down_back * slope
    gate_back = (down_back * up_pre * slope).astype(BF16)
    up_back = (down_back * silu).astype(BF16)
    return up_pre, silu, slope, curvature, mixed, down_back, back_slope, gate_back, up_back


def apply_forward(f1t, f3t, f2t, queries, weighted):
    q_gate, q_up = nt(f1t, queries), nt(f3t, queries)
    silu, slope, _ = silu_parts(q_gate)
    mixed = (silu * q_up).astype(BF16)
    output = nn(f2t, mixed)
    square = jnp.sum(output * output, axis=0, keepdims=True)
    dot = jnp.sum(weighted * output, axis=0, keepdims=True)
    return output, mixed, q_up * slope, silu, jnp.concatenate([square, dot], axis=0)


def apply_backward(f2t, sums, full_width, output, weighted, up_slope, silu):
    inverse = lax.rsqrt(sums[0:1] / full_width + EPSILON)
    scale = inverse * inverse * inverse * sums[1:2] / full_width
    out_back = (inverse * weighted - output * scale).astype(BF16)
    q_back = tn(f2t, out_back)
    gate_back = (q_back * up_slope).astype(BF16)
    up_back = (q_back * silu).astype(BF16)
    return gate_back, up_back, out_back


def second_by_gate_and_up(c1t, c3t, keys, up_slope, silu, back_slope, back_curve):
    gate_bar, up_bar = nt(c1t, keys), nt(c3t, keys)
    down_back_bar = (gate_bar * up_slope + up_bar * silu).astype(BF16)
    return down_back_bar, gate_bar * back_slope, up_bar * back_slope + gate_bar * back_curve


def second_by_down(c2t, push, up_slope, silu, up_part, gate_part):
    mixed_bar = tn(c2t, push)
    return (up_part + mixed_bar * silu).astype(BF16), (gate_part + mixed_bar * up_slope).astype(BF16)


def folds_of(rows, folds):
    width = rows.shape[1] // folds
    return [rows[:, i * width : (i + 1) * width] for i in range(folds)]


def norm_of(rows):
    return jnp.sqrt(jnp.sum(rows * rows, axis=1, keepdims=True) + EPSILON)


def owner_forward(prior, update, folds):
    moved = prior - update
    fast = [
        m * (norm_of(p) / norm_of(m)) for p, m in zip(folds_of(prior, folds), folds_of(moved, folds))
    ]
    return jnp.concatenate(fast, axis=1).astype(BF16), moved


def owner_backward(prior, moved, fast_grad, folds):
    cotangent, owned = [], []
    for p, m, fg in zip(*(folds_of(x, folds) for x in (prior, moved, fast_grad))):
        prior_norm, moved_norm = norm_of(p), norm_of(m)
        column_dot = jnp.sum(fg * m, axis=1, keepdims=True)
        moved_grad = (prior_norm / moved_norm) * (fg - m * (column_dot / (moved_norm * moved_norm)))
        cotangent.append(moved_grad)
        owned.append(moved_grad + p * (column_dot / (moved_norm * prior_norm)))
    return jnp.concatenate(cotangent, axis=1).astype(BF16), jnp.concatenate(owned, axis=1)


def push_of(rates, values):
    return (-rates * values.T.astype(F32)).astype(BF16)


def both(own_ref, other_ref, axis=0):
    return jnp.concatenate([own_ref[...], other_ref[...]], axis=axis)


def rows_of(ref, chip, core, chips, folds, i):
    rows = ref.shape[0] // (chips * CORES)
    height = rows // folds
    return pl.ds(pl.multiple_of((chip * CORES + core) * rows + i * height, height), height)


def cut_half(out, ref, parity, chips, folds):
    core = lax.axis_index("tok") % CORES
    height, width = ref.shape[0] // (chips * CORES * folds), ref.shape[1]
    for k in range(chips // 2):
        for i in range(folds):
            out[k * height : (k + 1) * height, i * width : (i + 1) * width] = ref[
                rows_of(ref, 2 * k + parity, core, chips, folds, i), :
            ].astype(out.dtype)


def place_half(ref, half, parity, core, chips, folds):
    height, width = ref.shape[0] // (chips * CORES * folds), ref.shape[1]
    for k in range(chips // 2):
        for i in range(folds):
            ref[rows_of(ref, 2 * k + parity, core, chips, folds, i), :] = half[
                k * height : (k + 1) * height, i * width : (i + 1) * width
            ]


def place_halves(chips, folds, halves, ref):
    tok = lax.axis_index("tok")
    parity, core = tok // CORES % 2, tok % CORES
    whose = ((parity, core), (1 - parity, core), (parity, 1 - core), (1 - parity, 1 - core))
    for half, (p, c) in zip(halves, whose):
        place_half(ref, half, p, c, chips, folds)


def rows_of_core(ref, order, chips):
    core = lax.axis_index("tok") % CORES
    rows = ref.shape[0] // (chips * CORES)
    blocks = [
        ref[pl.ds(pl.multiple_of((chip * CORES + core) * rows, rows), rows), :] for chip in order
    ]
    return jnp.concatenate(blocks, axis=0)


def fold(rows, chips, folds):
    height = rows.shape[0] // (chips * folds)
    parts = [rows[i * height : (i + 1) * height] for i in range(chips * folds)]
    wide = [jnp.concatenate(parts[k : k + folds], axis=1) for k in range(0, len(parts), folds)]
    return jnp.concatenate(wide, axis=0)


def pieces_order(chips):
    chip = lax.axis_index("tok") // CORES
    return [partner(chip, step, chips) for step in range(chips)]


def send_halves(chips, folds, operands, outs):
    gate_ref, up_ref, down_ref, tokens, hidden = operands
    parity = lax.axis_index("tok") // CORES % 2
    order = [2 * k + p for p in (parity, 1 - parity) for k in range(chips // 2)]
    sums = [nn(rows_of_core(ref, order, chips), tokens) for ref in (gate_ref, up_ref)]
    sums.append(fold(nt(rows_of_core(down_ref, order, chips), hidden), chips, folds))
    half = outs[0].shape[0]
    for k, total in enumerate(sums):
        outs[k][...] = total[:half]
        outs[3 + k][...] = total[half:].astype(BF16)


def update_kernel(chips, folds, ko, kx, vo, vx, ro, rx, w1t, w3t, w2, *rest):
    outs, (gate, up, push) = rest[:6], rest[6:]
    keys = both(ko, kx)
    push[...] = push_of(both(ro, rx, 1), both(vo, vx))
    *_, mixed, _, _, gate[...], up[...] = update_forward(w1t[...], w3t[...], w2[...], keys, push[...])
    send_halves(chips, folds, (gate, up, push, keys, mixed), outs)


def saved_kernel(
    chips, folds, ko, kx, vo, vx, ro, rx, w1t, w3t, w2, go, gx, gain,
    push_ref, up_slope_ref, silu_ref, back_slope_ref, back_curve_ref,
    mixed_ref, gate_back_ref, up_back_ref, weighted_ref, p1_ref, p3_ref, p2_ref,
    gate_ref, up_ref, down_ref,
):
    push = push_of(both(ro, rx, 1), both(vo, vx))
    push_ref[...] = push
    up_pre, silu, slope, curvature, mixed, down_back, back_slope, gate_back, up_back = (
        update_forward(w1t[...], w3t[...], w2[...], both(ko, kx), push)
    )
    up_slope_ref[...] = up_pre * slope
    silu_ref[...] = silu
    back_slope_ref[...] = back_slope
    back_curve_ref[...] = down_back * up_pre * curvature
    own = mixed_ref.shape[1]
    mixed_ref[...] = mixed[:, :own]
    gate_back_ref[...] = gate_back[:, :own]
    up_back_ref[...] = up_back[:, :own]
    weighted_ref[...] = (both(go, gx).astype(F32) * gain[...]).T
    gate_ref[...] = w1t[...].astype(F32)
    up_ref[...] = w3t[...].astype(F32)
    down_ref[...] = w2[...].astype(F32).T
    parity = lax.axis_index("tok") // CORES % 2
    cut_half(p1_ref, gate_ref, parity, chips, 1)
    cut_half(p3_ref, up_ref, parity, chips, 1)
    cut_half(p2_ref, down_ref, parity, chips, folds)


def carry_kernel(own, got, out):
    out[...] = (own[...] + got[...].astype(F32)).astype(BF16)


def total_of_halves(halves):
    total = halves[0][...].astype(F32)
    for half in halves[1:]:
        total = total + half[...].astype(F32)
    return total


def owner_forward_kernel(folds, prior, *refs):
    fast, moved = refs[-2:]
    total = total_of_halves(refs[:-2])
    fast[...], moved[...] = owner_forward(prior[...], total, folds)


def owner_backward_kernel(folds, prior, moved, *refs):
    cotangent, owned = refs[-2:]
    total = total_of_halves(refs[:-2])
    cotangent[...], owned[...] = owner_backward(prior[...], moved[...], total, folds)


def owner_result_kernel(chips, folds, *refs):
    owned, pieces, outs = refs[:3], refs[3:-3], refs[-3:]
    bars = pieces[0][...]
    for piece in pieces[1:]:
        bars = bars + piece[...].astype(F32)
    g = outs[0].shape[0]
    block = lax.axis_index("tok") // (2 * CORES)
    for k, out in enumerate(outs):
        result = owned[k][pl.ds(pl.multiple_of(block * g, g), g), :] - bars[k * g : (k + 1) * g]
        for i, rows in enumerate(folds_of(result, folds if k == 2 else 1)):
            out[i * g : (i + 1) * g] = rows


def apply_kernel(chips, folds, *refs):
    halves, refs = refs[:12], refs[12:]
    qo, qx, weighted, f1t, f3t, f2t, output, mixed, up_slope, silu, sums = refs
    place_halves(chips, 1, halves[:4], f1t)
    place_halves(chips, 1, halves[4:8], f3t)
    place_halves(chips, folds, halves[8:], f2t)
    output[...], mixed[...], up_slope[...], silu[...], sums[...] = apply_forward(
        f1t[...], f3t[...], f2t[...], both(qo, qx), weighted[...]
    )


def back_kernel(chips, folds, heads, *refs):
    parts, refs = refs[:heads], refs[heads:]
    sums = parts[0][...]
    for part in parts[1:]:
        sums = sums + part[...]
    f2t, output, weighted, mixed, up_slope, silu, qo, qx, gate_back, up_back = refs[:10]
    outs, (gate, up, down) = refs[10:16], refs[16:]
    width = heads * output.shape[0]
    gate[...], up[...], down[...] = apply_backward(
        f2t[...], sums, width, output[...], weighted[...], up_slope[...], silu[...]
    )
    send_halves(chips, folds, (gate, up, down, both(qo, qx), mixed[...]), outs)
    own = gate_back.shape[1]
    gate_back[...], up_back[...] = gate[:, :own], up[:, :own]


def query_kernel(gate_back, up_back, f1t, f3t, out):
    out[...] = (tn(gate_back[...], f1t[...]) + tn(up_back[...], f3t[...])).astype(BF16)


def second_first_kernel(chips, folds, *refs):
    halves, refs = refs[:8], refs[8:]
    ko, kx, push, up_slope, silu, back_slope, back_curve = refs[:7]
    c1t, c3t, dbb_ref, down, up_part, gate_part = refs[7:]
    place_halves(chips, 1, halves[:4], c1t)
    place_halves(chips, 1, halves[4:], c3t)
    dbb, up_part[...], gate_part[...] = second_by_gate_and_up(
        c1t[...], c3t[...], both(ko, kx),
        up_slope[...], silu[...], back_slope[...], back_curve[...],
    )
    down[...] = fold(nt(rows_of_core(push, pieces_order(chips), chips), dbb), chips, folds)
    dbb_ref[...] = dbb[:, : dbb_ref.shape[1]]


def second_last_kernel(chips, folds, *refs):
    halves, refs = refs[:4], refs[4:]
    ko, kx, push, up_slope, silu, up_part, gate_part, down = refs[:8]
    c2t, upb_ref, gpb_ref = refs[8:11]
    outs, (gate, up) = refs[11 : 11 + chips], refs[11 + chips :]
    place_halves(chips, folds, halves, c2t)
    up[...], gate[...] = second_by_down(
        c2t[...], push[...], up_slope[...], silu[...], up_part[...], gate_part[...]
    )
    keys, order = both(ko, kx), pieces_order(chips)
    sums = [nn(rows_of_core(ref, order, chips), keys) for ref in (gate, up)] + [down[...]]
    g = sums[0].shape[0] // chips
    for k, out in enumerate(outs):
        parts = [x[k * g : (k + 1) * g] for x in sums]
        out[...] = jnp.concatenate(parts, axis=0).astype(out.dtype)
    own = upb_ref.shape[1]
    upb_ref[...], gpb_ref[...] = up[:, :own], gate[:, :own]


def token_grads(rates, mixed, dbb, upb, gpb, gate_back, up_back, c1t, c3t, c2t, w1t, w3t, w2):
    value_grad = (rates * (nn(c2t, mixed) + tn(w2, dbb))).T.astype(BF16)
    key_total = tn(gate_back, c1t) + tn(up_back, c3t) + tn(gpb, w1t) + tn(upb, w3t)
    return value_grad, (-key_total).astype(BF16)


def token_kernel(*refs):
    value_grad, key_grad = refs[-2:]
    value_grad[...], key_grad[...] = token_grads(*(r[...] for r in refs[:-2]))


def call(kernel, outs, args, scratch=(), name=None, flops=0):
    vmem = pl.BlockSpec(memory_space=pltpu.VMEM)
    return pl.pallas_call(
        kernel,
        out_shape=[jax.ShapeDtypeStruct(s, t) for s, t in outs],
        in_specs=[vmem] * len(args),
        out_specs=[vmem] * len(outs),
        scratch_shapes=[pltpu.VMEM(s, t) for s, t in scratch],
        compiler_params=pltpu.CompilerParams(vmem_limit_bytes=VMEM_LIMIT),
        cost_estimate=pl.CostEstimate(
            flops=flops,
            bytes_accessed=sum(a.size * a.dtype.itemsize for a in args),
            transcendentals=0,
        ),
        name=name,
    )(*args)


def exchange(pieces, chips):
    count = chips * CORES
    got = [lax.ppermute(pieces[s], "tok", chip_perm(count, s)) for s in reversed(range(1, chips))]
    return [pieces[0], *got]


def to_chip(x, step, chips):
    return lax.ppermute(x, "tok", chip_perm(chips * CORES, step))


def half_sums(kept, given, chips):
    (mine,) = call(carry_kernel, [(given.shape, BF16)], (kept, to_chip(given, 1, chips)), name="carry")
    return [mine, *(to_chip(mine, step, chips) for step in range(2, chips, 2))]


def from_owners(halves, chips):
    others = [to_chip(half, 1, chips) for half in halves]
    *later, others[0] = lax.optimization_barrier((*halves, others[0]))
    cross = lambda x: lax.ppermute(x, "tok", core_perm(chips * CORES))
    parts = zip(halves, others, map(cross, later), map(cross, others))
    return [x for part in parts for x in part]


def head_parts(part, heads):
    got = [
        lax.ppermute(part, "head", [(h, partner(h, step, heads)) for h in range(heads)])
        for step in range(1, heads)
    ]
    return [part, *got]


def over_chips(blocks, count):
    groups = [list(range(core, count, CORES)) for core in range(CORES)]
    return lax.all_to_all(blocks, "tok", 0, 0, axis_index_groups=groups, tiled=True)


def gather_blocks(copies, count):
    mine = over_chips(copies, count)
    return mine, lax.ppermute(mine, "tok", core_perm(count))


def sliced_pieces(gate, up, down, tok, count):
    g, d = gate.shape[0] // count, down.shape[0] // count
    rows = lambda x, size, t: lax.dynamic_slice_in_dim(x, t * size, size, 0)
    piece = lambda t: pack(rows(gate, g, t), rows(up, g, t), rows(down, d, t))
    sent = [piece(t + tok % CORES) for t in range(0, count, CORES)]
    return piece(tok), jnp.concatenate(sent, axis=0).astype(BF16)


def total_of(own, got, tok):
    blocks = got.reshape((-1,) + own.shape)
    chip = lax.broadcasted_iota(jnp.int32, (blocks.shape[0], 1, 1), 0)
    others = jnp.where(chip == tok // CORES, 0.0, blocks.astype(F32))
    return own + jnp.sum(others, axis=0)


def whole_matrices(mine, other, tok, count, fh):
    shape = (count // CORES, -1, mine.shape[1])
    pair = jnp.stack([mine.reshape(shape), other.reshape(shape)], axis=1)
    pair = jnp.where(tok % CORES == 0, pair, pair[:, ::-1])
    held = pair.reshape((count, -1, mine.shape[1]))
    parts = jax.vmap(lambda x: unpack(x, fh))(held)
    return tuple(x.reshape((-1, x.shape[-1])) for x in parts)


def packed_owner_forward(prior, update, fh):
    fast, moved = zip(*(owner_forward(p, u, 1) for p, u in zip(unpack(prior, fh), unpack(update, fh))))
    return pack(*fast), pack(*moved)


def packed_owner_backward(prior, moved, fast_grad, fh):
    parts = (unpack(x, fh) for x in (prior, moved, fast_grad))
    cotangent, owned = zip(*(owner_backward(p, m, f, 1) for p, m, f in zip(*parts)))
    return pack(*cotangent), pack(*owned)


def per_device(
    query_input,
    key_input,
    value_input,
    out_grad,
    token_rates,
    out_gain,
    gate_prior,
    up_prior,
    down_prior,
):
    count, heads = lax.axis_size("tok"), lax.axis_size("head")
    tok = lax.axis_index("tok")
    chips = count // CORES
    own, dh = key_input.shape
    n = own * CORES
    w1, w3, w2 = gate_prior[0], up_prior[0], down_prior[0]
    fh = w2.shape[0]
    g, d = fh // count, dh // count
    rates = token_rates.T
    gain = out_gain[None, :]
    inputs = query_input, key_input, value_input, out_grad, rates, gain, w1, w3, w2

    if g % ROW_TILE or d % g or dh * g != fh * d or chips & (chips - 1) or chips < 2:
        query_grad, key_grad, value_grad, *results = by_blocks(inputs, tok, count, heads)
    else:
        query_grad, key_grad, value_grad, *results = by_line(inputs, chips, heads)
    return (query_grad, key_grad, value_grad, *(r.T[None] for r in results))


def by_line(inputs, chips, heads):
    query_input, key_input, value_input, out_grad, rates, gain, w1, w3, w2 = inputs
    count = chips * CORES
    own, dh = key_input.shape
    n, fh = own * CORES, w2.shape[0]
    g, d, folds = fh // count, dh // count, dh // fh
    product = 2 * n * dh * fh

    half = (g * chips // 2, dh)
    half_shares = [(half, F32)] * 3 + [(half, BF16)] * 3
    matrices = [((fh, dh), BF16), ((fh, dh), BF16), ((dh, fh), BF16)]
    sums_scratch = [((fh, dh), F32), ((fh, dh), F32), ((dh, fh), F32)]
    operands = [((fh, n), BF16), ((fh, n), BF16), ((dh, n), BF16)]
    hidden = ((fh, n), F32)
    own_hidden = ((fh, own), BF16)
    folds_by_matrix = (1, 1, folds)

    pair = lambda x: lax.ppermute(x, "tok", core_perm(count))
    key_other, value_other, rate_other = pair(key_input), pair(value_input), pair(rates)
    w1t, w3t = w1.T, w3.T
    query_other, grad_other = pair(query_input), pair(out_grad)
    keys_values = (
        key_input, key_other, value_input, value_other, rates, rate_other, w1t, w3t, w2,
    )
    sums = call(
        functools.partial(update_kernel, chips, folds),
        half_shares,
        keys_values,
        operands,
        "update",
        6 * product,
    )
    *saved, weighted, p1, p3, p2 = call(
        functools.partial(saved_kernel, chips, folds),
        [((dh, n), BF16)] + [hidden] * 4 + [own_hidden] * 3 + [((dh, n), F32)] + [(half, F32)] * 3,
        (*keys_values, out_grad, grad_other, gain),
        sums_scratch,
        "saved",
        3 * product,
    )
    push, up_slope, silu, back_slope, back_curve, mixed, gate_back, up_back = saved
    priors = p1, p3, p2

    fast, moved = [], []
    for k in range(3):
        totals = half_sums(sums[k], sums[3 + k], chips)
        rows, rows_moved = call(
            functools.partial(owner_forward_kernel, folds_by_matrix[k]),
            [(half, BF16), (half, F32)],
            (priors[k], *totals),
            name="owner_forward",
        )
        moved.append(rows_moved)
        fast.append(rows)
    f1t, f3t, f2t, output, q_mixed, q_slope, q_silu, part = call(
        functools.partial(apply_kernel, chips, folds),
        matrices + [((dh, n), F32), ((fh, n), BF16), hidden, hidden, ((2, n), F32)],
        (*from_owners(fast, chips), query_input, query_other, weighted),
        name="apply",
        flops=3 * product,
    )
    q_gate_back, q_up_back, *sums = call(
        functools.partial(back_kernel, chips, folds, heads),
        [own_hidden] * 2 + half_shares,
        (
            *head_parts(part, heads),
            f2t, output, weighted, q_mixed, q_slope, q_silu, query_input, query_other,
        ),
        operands,
        "apply_back",
        4 * product,
    )
    (query_grad,) = call(
        query_kernel,
        [((own, dh), BF16)],
        (q_gate_back, q_up_back, f1t, f3t),
        name="query_grad",
        flops=product,
    )

    cotangent, owned = [], []
    for k in range(3):
        totals = half_sums(sums[k], sums[3 + k], chips)
        rows, rows_owned = call(
            functools.partial(owner_backward_kernel, folds_by_matrix[k]),
            [(half, BF16), (half, F32)],
            (priors[k], moved[k], *totals),
            name="owner_backward",
        )
        owned.append(rows_owned)
        cotangent.append(rows)
    arrived = from_owners(cotangent, chips)
    c1t, c3t, dbb, down_sums, up_part, gate_part = call(
        functools.partial(second_first_kernel, chips, folds),
        matrices[:2] + [own_hidden, ((g * chips, dh), F32), hidden, hidden],
        (*arrived[:8], key_input, key_other, push, up_slope, silu, back_slope, back_curve),
        name="second_first",
        flops=3 * product,
    )
    c2t, upb, gpb, *pieces = call(
        functools.partial(second_last_kernel, chips, folds),
        matrices[2:] + [own_hidden] * 2 + [((3 * g, dh), F32)] + [((3 * g, dh), BF16)] * (chips - 1),
        (
            *arrived[8:], key_input, key_other, push, up_slope, silu, up_part, gate_part, down_sums,
        ),
        operands[:2],
        "second_last",
        3 * product,
    )
    value_grad, key_grad = call(
        token_kernel,
        [((own, dh), BF16)] * 2,
        (rates, mixed, dbb, upb, gpb, gate_back, up_back, c1t, c3t, c2t, w1t, w3t, w2),
        name="token_grads",
        flops=3 * product,
    )
    results = call(
        functools.partial(owner_result_kernel, chips, folds),
        [((g, dh), F32)] * 2 + [((d, fh), F32)],
        (*owned, *exchange(pieces, chips)),
        name="owner_result",
    )
    return query_grad, key_grad, value_grad, *results


def by_blocks(inputs, tok, count, heads):
    query_input, key_input, value_input, out_grad, rates, gain, w1, w3, w2 = inputs
    own, dh = key_input.shape
    fh, chips = w2.shape[0], count // CORES
    g, d = fh // count, dh // count
    w1t, w3t = w1.T, w3.T
    pair = lambda x, axis=0: jnp.concatenate(
        [x, lax.ppermute(x, "tok", core_perm(count))], axis=axis
    )
    keys, values, queries, rate = pair(key_input), pair(value_input), pair(query_input), pair(rates, 1)
    weighted = (pair(out_grad).astype(F32) * gain).T
    push = push_of(rate, values)
    up_pre, silu, slope, curvature, mixed, down_back, back_slope, gate_back, up_back = (
        update_forward(w1t, w3t, w2, keys, push)
    )
    up_slope, back_curve = up_pre * slope, down_back * up_pre * curvature
    sums = nn(gate_back, keys), nn(up_back, keys), nt(push, mixed)
    piece, sent = sliced_pieces(*sums, tok, count)
    prior = pack(
        *(
            lax.dynamic_slice_in_dim(x, tok * rows, rows, 0).astype(F32)
            for x, rows in ((w1t, g), (w3t, g), (w2.T, d))
        )
    )
    update = total_of(piece, over_chips(sent, count), tok)
    fast, moved = packed_owner_forward(prior, update, fh)
    blocks = gather_blocks(jnp.tile(fast, (chips, 1)), count)
    f1t, f3t, f2t = whole_matrices(*blocks, tok, count, fh)
    output, q_mixed, q_slope, q_silu, part = apply_forward(f1t, f3t, f2t, queries, weighted)
    sums = lax.psum(part, "head")
    q_gate_back, q_up_back, out_back = apply_backward(
        f2t, sums, heads * dh, output, weighted, q_slope, q_silu
    )
    grads = nn(q_gate_back, queries), nn(q_up_back, queries), nt(out_back, q_mixed)
    piece, sent = sliced_pieces(*grads, tok, count)
    query_grad = (tn(q_gate_back[:, :own], f1t) + tn(q_up_back[:, :own], f3t)).astype(BF16)
    fast_grad = total_of(piece, over_chips(sent, count), tok)
    cotangent, owned = packed_owner_backward(prior, moved, fast_grad, fh)
    blocks = gather_blocks(jnp.tile(cotangent, (chips, 1)), count)
    c1t, c3t, c2t = whole_matrices(*blocks, tok, count, fh)
    dbb, *parts = second_by_gate_and_up(c1t, c3t, keys, up_slope, silu, back_slope, back_curve)
    upb, gpb = second_by_down(c2t, push, up_slope, silu, *parts)
    bars = nn(gpb, keys), nn(upb, keys), nt(push, dbb)
    piece, sent = sliced_pieces(*bars, tok, count)
    value_grad, key_grad = token_grads(
        rates, mixed[:, :own], dbb[:, :own], upb[:, :own], gpb[:, :own],
        gate_back[:, :own], up_back[:, :own], c1t, c3t, c2t, w1t, w3t, w2,
    )
    results = unpack(owned - total_of(piece, over_chips(sent, count), tok), fh)
    return query_grad, key_grad, value_grad, *results


def solution(mesh):
    tokens = P("tok", "head")
    in_specs = (tokens,) * 5 + (P("head"),) + (P("head", None, None),) * 3
    out_specs = (tokens,) * 3 + (P("head", None, "tok"),) * 3
    return jax.shard_map(
        per_device, mesh=mesh, in_specs=in_specs, out_specs=out_specs, check_vma=False
    )
```

```python
import functools

import jax
import jax.numpy as jnp
from jax import lax
from jax.experimental import pallas as pl
from jax.experimental.pallas import tpu as pltpu
from jax.sharding import PartitionSpec as P

EPSILON = 1e-06
CORES = 2
ROW_TILE = 16
VMEM_LIMIT = 24 * 1024 * 1024
BF16, F32 = jnp.bfloat16, jnp.float32


def nn(a, b):
    return lax.dot_general(a, b, (((1,), (0,)), ((), ())), preferred_element_type=F32)


def nt(a, b):
    return lax.dot_general(a, b, (((1,), (1,)), ((), ())), preferred_element_type=F32)


def tn(a, b):
    return lax.dot_general(a, b, (((0,), (0,)), ((), ())), preferred_element_type=F32)


def silu_parts(hidden):
    sigmoid_value = jax.nn.sigmoid(hidden)
    silu_value = hidden * sigmoid_value
    silu_slope = sigmoid_value * (1.0 + hidden * (1.0 - sigmoid_value))
    curvature = sigmoid_value * (1.0 - sigmoid_value) * (2.0 + hidden * (1.0 - 2.0 * sigmoid_value))
    return silu_value, silu_slope, curvature


def partner(index, step, count):
    return index ^ step if count & (count - 1) == 0 else (index + step) % count


def source(index, step, count):
    return index ^ step if count & (count - 1) == 0 else (index + count - step) % count


def chip_perm(count, step):
    chips = count // CORES
    return [(t, partner(t // CORES, step, chips) * CORES + t % CORES) for t in range(count)]


def core_perm(count):
    return [(t, t ^ 1) for t in range(count)]


def pack(gate, up, down):
    folds = gate.shape[1] // down.shape[1]
    rows = down.shape[0] // folds
    down = jnp.concatenate([down[i * rows : (i + 1) * rows] for i in range(folds)], axis=1)
    return jnp.concatenate([gate, up, down], axis=0)


def unpack(packed, fh):
    g = packed.shape[0] // 3
    folds = packed.shape[1] // fh
    down = packed[2 * g :]
    down = jnp.concatenate([down[:, i * fh : (i + 1) * fh] for i in range(folds)], axis=0)
    return packed[:g], packed[g : 2 * g], down


def update_forward(w1t, w3t, w2, keys, push):
    gate_pre, up_pre = nt(w1t, keys), nt(w3t, keys)
    silu, slope, curvature = silu_parts(gate_pre)
    mixed = (silu * up_pre).astype(BF16)
    down_back = nn(w2, push)
    back_slope = down_back * slope
    gate_back = (down_back * up_pre * slope).astype(BF16)
    up_back = (down_back * silu).astype(BF16)
    return up_pre, silu, slope, curvature, mixed, down_back, back_slope, gate_back, up_back


def apply_gate_and_up(f1t, f3t, queries):
    q_gate, q_up = nt(f1t, queries), nt(f3t, queries)
    silu, slope, _ = silu_parts(q_gate)
    return (silu * q_up).astype(BF16), q_up * slope, silu


def apply_down(f2t, mixed, weighted):
    output = nn(f2t, mixed)
    square = jnp.sum(output * output, axis=0, keepdims=True)
    dot = jnp.sum(weighted * output, axis=0, keepdims=True)
    return output, jnp.concatenate([square, dot], axis=0)


def apply_backward(f2t, sums, full_width, output, weighted, up_slope, silu):
    inverse = lax.rsqrt(sums[0:1] / full_width + EPSILON)
    scale = inverse * inverse * inverse * sums[1:2] / full_width
    out_back = (inverse * weighted - output * scale).astype(BF16)
    q_back = tn(f2t, out_back)
    gate_back = (q_back * up_slope).astype(BF16)
    up_back = (q_back * silu).astype(BF16)
    return gate_back, up_back, out_back


def second_by_gate_and_up(c1t, c3t, keys, up_slope, silu, back_slope, back_curve):
    gate_bar, up_bar = nt(c1t, keys), nt(c3t, keys)
    down_back_bar = (gate_bar * up_slope + up_bar * silu).astype(BF16)
    return down_back_bar, gate_bar * back_slope, up_bar * back_slope + gate_bar * back_curve


def second_by_down(c2t, push, up_slope, silu, up_part, gate_part):
    mixed_bar = tn(c2t, push)
    return (up_part + mixed_bar * silu).astype(BF16), (gate_part + mixed_bar * up_slope).astype(BF16)


def folds_of(rows, folds):
    width = rows.shape[1] // folds
    return [rows[:, i * width : (i + 1) * width] for i in range(folds)]


def norm_of(rows):
    return jnp.sqrt(jnp.sum(rows * rows, axis=1, keepdims=True) + EPSILON)


def owner_forward(prior, update, folds):
    moved = prior - update
    fast = [
        m * (norm_of(p) / norm_of(m)) for p, m in zip(folds_of(prior, folds), folds_of(moved, folds))
    ]
    return jnp.concatenate(fast, axis=1).astype(BF16), moved


def owner_backward(prior, moved, fast_grad, folds):
    cotangent, owned = [], []
    for p, m, fg in zip(*(folds_of(x, folds) for x in (prior, moved, fast_grad))):
        prior_norm, moved_norm = norm_of(p), norm_of(m)
        column_dot = jnp.sum(fg * m, axis=1, keepdims=True)
        moved_grad = (prior_norm / moved_norm) * (fg - m * (column_dot / (moved_norm * moved_norm)))
        cotangent.append(moved_grad)
        owned.append(moved_grad + p * (column_dot / (moved_norm * prior_norm)))
    return jnp.concatenate(cotangent, axis=1).astype(BF16), jnp.concatenate(owned, axis=1)


def push_of(rates, values):
    return (-rates * values.T.astype(F32)).astype(BF16)


def both(own_ref, other_ref, axis=0):
    return jnp.concatenate([own_ref[...], other_ref[...]], axis=axis)


def rows_of(ref, chip, core, chips, folds, i):
    rows = ref.shape[0] // (chips * CORES)
    height = rows // folds
    return pl.ds(pl.multiple_of((chip * CORES + core) * rows + i * height, height), height)


def cut_half(out, ref, parity, chips, folds):
    core = lax.axis_index("tok") % CORES
    height, width = ref.shape[0] // (chips * CORES * folds), ref.shape[1]
    for k in range(chips // 2):
        for i in range(folds):
            out[k * height : (k + 1) * height, i * width : (i + 1) * width] = ref[
                rows_of(ref, 2 * k + parity, core, chips, folds, i), :
            ].astype(out.dtype)


def place_half(ref, half, parity, core, chips, folds):
    height, width = ref.shape[0] // (chips * CORES * folds), ref.shape[1]
    for k in range(chips // 2):
        for i in range(folds):
            ref[rows_of(ref, 2 * k + parity, core, chips, folds, i), :] = half[
                k * height : (k + 1) * height, i * width : (i + 1) * width
            ]


def place_halves(chips, folds, halves, ref):
    tok = lax.axis_index("tok")
    parity, core = tok // CORES % 2, tok % CORES
    whose = ((parity, core), (1 - parity, core), (parity, 1 - core), (1 - parity, 1 - core))
    for half, (p, c) in zip(halves, whose):
        place_half(ref, half, p, c, chips, folds)


def rows_of_core(ref, order, chips):
    core = lax.axis_index("tok") % CORES
    rows = ref.shape[0] // (chips * CORES)
    blocks = [
        ref[pl.ds(pl.multiple_of((chip * CORES + core) * rows, rows), rows), :] for chip in order
    ]
    return jnp.concatenate(blocks, axis=0)


def fold(rows, chips, folds):
    height = rows.shape[0] // (chips * folds)
    parts = [rows[i * height : (i + 1) * height] for i in range(chips * folds)]
    wide = [jnp.concatenate(parts[k : k + folds], axis=1) for k in range(0, len(parts), folds)]
    return jnp.concatenate(wide, axis=0)


def pieces_order(chips):
    chip = lax.axis_index("tok") // CORES
    return [partner(chip, step, chips) for step in range(chips)]


def send_halves(chips, folds, operands, outs):
    gate_ref, up_ref, down_ref, tokens, hidden = operands
    parity = lax.axis_index("tok") // CORES % 2
    order = [2 * k + p for p in (parity, 1 - parity) for k in range(chips // 2)]
    sums = [nn(rows_of_core(ref, order, chips), tokens) for ref in (gate_ref, up_ref)]
    sums.append(fold(nt(rows_of_core(down_ref, order, chips), hidden), chips, folds))
    half = outs[0].shape[0]
    for k, total in enumerate(sums):
        outs[k][...] = total[:half]
        outs[3 + k][...] = total[half:].astype(BF16)


def update_kernel(chips, folds, ko, kx, vo, vx, ro, rx, w1t, w3t, w2, *rest):
    outs, (gate, up, push) = rest[:6], rest[6:]
    keys = both(ko, kx)
    push[...] = push_of(both(ro, rx, 1), both(vo, vx))
    *_, mixed, _, _, gate[...], up[...] = update_forward(w1t[...], w3t[...], w2[...], keys, push[...])
    send_halves(chips, folds, (gate, up, push, keys, mixed), outs)


def saved_kernel(
    chips, folds, ko, kx, vo, vx, ro, rx, w1t, w3t, w2, go, gx, gain,
    push_ref, up_slope_ref, silu_ref, back_slope_ref, back_curve_ref,
    mixed_ref, gate_back_ref, up_back_ref, weighted_ref, p1_ref, p3_ref, p2_ref,
    gate_ref, up_ref, down_ref,
):
    push = push_of(both(ro, rx, 1), both(vo, vx))
    push_ref[...] = push
    up_pre, silu, slope, curvature, mixed, down_back, back_slope, gate_back, up_back = (
        update_forward(w1t[...], w3t[...], w2[...], both(ko, kx), push)
    )
    up_slope_ref[...] = up_pre * slope
    silu_ref[...] = silu
    back_slope_ref[...] = back_slope
    back_curve_ref[...] = down_back * up_pre * curvature
    own = mixed_ref.shape[1]
    mixed_ref[...] = mixed[:, :own]
    gate_back_ref[...] = gate_back[:, :own]
    up_back_ref[...] = up_back[:, :own]
    weighted_ref[...] = (both(go, gx).astype(F32) * gain[...]).T
    gate_ref[...] = w1t[...].astype(F32)
    up_ref[...] = w3t[...].astype(F32)
    down_ref[...] = w2[...].astype(F32).T
    parity = lax.axis_index("tok") // CORES % 2
    cut_half(p1_ref, gate_ref, parity, chips, 1)
    cut_half(p3_ref, up_ref, parity, chips, 1)
    cut_half(p2_ref, down_ref, parity, chips, folds)


def carry_kernel(own, got, out):
    out[...] = (own[...] + got[...].astype(F32)).astype(BF16)


def total_of_halves(halves):
    total = halves[0][...].astype(F32)
    for half in halves[1:]:
        total = total + half[...].astype(F32)
    return total


def owner_forward_kernel(folds, prior, *refs):
    fast, moved = refs[-2:]
    total = total_of_halves(refs[:-2])
    fast[...], moved[...] = owner_forward(prior[...], total, folds)


def owner_backward_kernel(folds, prior, moved, *refs):
    cotangent, owned = refs[-2:]
    total = total_of_halves(refs[:-2])
    cotangent[...], owned[...] = owner_backward(prior[...], moved[...], total, folds)


def owner_result_kernel(chips, folds, *refs):
    owned, pieces, outs = refs[:3], refs[3:-3], refs[-3:]
    bars = pieces[0][...]
    for piece in pieces[1:]:
        bars = bars + piece[...].astype(F32)
    g = outs[0].shape[0]
    block = lax.axis_index("tok") // (2 * CORES)
    for k, out in enumerate(outs):
        result = owned[k][pl.ds(pl.multiple_of(block * g, g), g), :] - bars[k * g : (k + 1) * g]
        for i, rows in enumerate(folds_of(result, folds if k == 2 else 1)):
            out[i * g : (i + 1) * g] = rows


def apply_first_kernel(chips, *refs):
    halves, (qo, qx, f1t, f3t, mixed, up_slope, silu) = refs[:8], refs[8:]
    place_halves(chips, 1, halves[:4], f1t)
    place_halves(chips, 1, halves[4:], f3t)
    mixed[...], up_slope[...], silu[...] = apply_gate_and_up(f1t[...], f3t[...], both(qo, qx))


def apply_last_kernel(chips, folds, *refs):
    halves, (mixed, weighted, f2t, output, sums) = refs[:4], refs[4:]
    place_halves(chips, folds, halves, f2t)
    output[...], sums[...] = apply_down(f2t[...], mixed[...], weighted[...])


def back_kernel(chips, folds, heads, *refs):
    parts, refs = refs[:heads], refs[heads:]
    sums = parts[0][...]
    for part in parts[1:]:
        sums = sums + part[...]
    f2t, output, weighted, mixed, up_slope, silu, qo, qx, gate_back, up_back = refs[:10]
    outs, (gate, up, down) = refs[10:16], refs[16:]
    width = heads * output.shape[0]
    gate[...], up[...], down[...] = apply_backward(
        f2t[...], sums, width, output[...], weighted[...], up_slope[...], silu[...]
    )
    send_halves(chips, folds, (gate, up, down, both(qo, qx), mixed[...]), outs)
    own = gate_back.shape[1]
    gate_back[...], up_back[...] = gate[:, :own], up[:, :own]


def query_kernel(gate_back, up_back, f1t, f3t, out):
    out[...] = (tn(gate_back[...], f1t[...]) + tn(up_back[...], f3t[...])).astype(BF16)


def second_first_kernel(chips, folds, *refs):
    halves, refs = refs[:8], refs[8:]
    ko, kx, push, up_slope, silu, back_slope, back_curve = refs[:7]
    c1t, c3t, dbb_ref, down, up_part, gate_part = refs[7:]
    place_halves(chips, 1, halves[:4], c1t)
    place_halves(chips, 1, halves[4:], c3t)
    dbb, up_part[...], gate_part[...] = second_by_gate_and_up(
        c1t[...], c3t[...], both(ko, kx),
        up_slope[...], silu[...], back_slope[...], back_curve[...],
    )
    down[...] = fold(nt(rows_of_core(push, pieces_order(chips), chips), dbb), chips, folds)
    dbb_ref[...] = dbb[:, : dbb_ref.shape[1]]


def second_last_kernel(chips, folds, *refs):
    halves, refs = refs[:4], refs[4:]
    ko, kx, push, up_slope, silu, up_part, gate_part, down = refs[:8]
    c2t, upb_ref, gpb_ref = refs[8:11]
    outs, (gate, up) = refs[11 : 11 + chips], refs[11 + chips :]
    place_halves(chips, folds, halves, c2t)
    up[...], gate[...] = second_by_down(
        c2t[...], push[...], up_slope[...], silu[...], up_part[...], gate_part[...]
    )
    keys, order = both(ko, kx), pieces_order(chips)
    sums = [nn(rows_of_core(ref, order, chips), keys) for ref in (gate, up)] + [down[...]]
    g = sums[0].shape[0] // chips
    for k, out in enumerate(outs):
        parts = [x[k * g : (k + 1) * g] for x in sums]
        out[...] = jnp.concatenate(parts, axis=0).astype(out.dtype)
    own = upb_ref.shape[1]
    upb_ref[...], gpb_ref[...] = up[:, :own], gate[:, :own]


def token_grads(rates, mixed, dbb, upb, gpb, gate_back, up_back, c1t, c3t, c2t, w1t, w3t, w2):
    value_grad = (rates * (nn(c2t, mixed) + tn(w2, dbb))).T.astype(BF16)
    key_total = tn(gate_back, c1t) + tn(up_back, c3t) + tn(gpb, w1t) + tn(upb, w3t)
    return value_grad, (-key_total).astype(BF16)


def token_kernel(*refs):
    value_grad, key_grad = refs[-2:]
    value_grad[...], key_grad[...] = token_grads(*(r[...] for r in refs[:-2]))


def call(kernel, outs, args, scratch=(), name=None, flops=0):
    vmem = pl.BlockSpec(memory_space=pltpu.VMEM)
    return pl.pallas_call(
        kernel,
        out_shape=[jax.ShapeDtypeStruct(s, t) for s, t in outs],
        in_specs=[vmem] * len(args),
        out_specs=[vmem] * len(outs),
        scratch_shapes=[pltpu.VMEM(s, t) for s, t in scratch],
        compiler_params=pltpu.CompilerParams(vmem_limit_bytes=VMEM_LIMIT),
        cost_estimate=pl.CostEstimate(
            flops=flops,
            bytes_accessed=sum(a.size * a.dtype.itemsize for a in args),
            transcendentals=0,
        ),
        name=name,
    )(*args)


def exchange(pieces, chips):
    count = chips * CORES
    got = [lax.ppermute(pieces[s], "tok", chip_perm(count, s)) for s in reversed(range(1, chips))]
    return [pieces[0], *got]


def to_chip(x, step, chips):
    return lax.ppermute(x, "tok", chip_perm(chips * CORES, step))


def half_sums(kept, given, chips):
    (mine,) = call(carry_kernel, [(given.shape, BF16)], (kept, to_chip(given, 1, chips)), name="carry")
    return [mine, *(to_chip(mine, step, chips) for step in range(2, chips, 2))]


def from_owners(halves, chips):
    others = [to_chip(half, 1, chips) for half in halves]
    *later, others[0] = lax.optimization_barrier((*halves, others[0]))
    cross = lambda x: lax.ppermute(x, "tok", core_perm(chips * CORES))
    parts = zip(halves, others, map(cross, later), map(cross, others))
    return [x for part in parts for x in part]


def head_parts(part, heads):
    got = [
        lax.ppermute(part, "head", [(h, partner(h, step, heads)) for h in range(heads)])
        for step in range(1, heads)
    ]
    return [part, *got]


def over_chips(blocks, count):
    groups = [list(range(core, count, CORES)) for core in range(CORES)]
    return lax.all_to_all(blocks, "tok", 0, 0, axis_index_groups=groups, tiled=True)


def gather_blocks(copies, count):
    mine = over_chips(copies, count)
    return mine, lax.ppermute(mine, "tok", core_perm(count))


def sliced_pieces(gate, up, down, tok, count):
    g, d = gate.shape[0] // count, down.shape[0] // count
    rows = lambda x, size, t: lax.dynamic_slice_in_dim(x, t * size, size, 0)
    piece = lambda t: pack(rows(gate, g, t), rows(up, g, t), rows(down, d, t))
    sent = [piece(t + tok % CORES) for t in range(0, count, CORES)]
    return piece(tok), jnp.concatenate(sent, axis=0).astype(BF16)


def total_of(own, got, tok):
    blocks = got.reshape((-1,) + own.shape)
    chip = lax.broadcasted_iota(jnp.int32, (blocks.shape[0], 1, 1), 0)
    others = jnp.where(chip == tok // CORES, 0.0, blocks.astype(F32))
    return own + jnp.sum(others, axis=0)


def whole_matrices(mine, other, tok, count, fh):
    shape = (count // CORES, -1, mine.shape[1])
    pair = jnp.stack([mine.reshape(shape), other.reshape(shape)], axis=1)
    pair = jnp.where(tok % CORES == 0, pair, pair[:, ::-1])
    held = pair.reshape((count, -1, mine.shape[1]))
    parts = jax.vmap(lambda x: unpack(x, fh))(held)
    return tuple(x.reshape((-1, x.shape[-1])) for x in parts)


def packed_owner_forward(prior, update, fh):
    fast, moved = zip(*(owner_forward(p, u, 1) for p, u in zip(unpack(prior, fh), unpack(update, fh))))
    return pack(*fast), pack(*moved)


def packed_owner_backward(prior, moved, fast_grad, fh):
    parts = (unpack(x, fh) for x in (prior, moved, fast_grad))
    cotangent, owned = zip(*(owner_backward(p, m, f, 1) for p, m, f in zip(*parts)))
    return pack(*cotangent), pack(*owned)


def per_device(
    query_input,
    key_input,
    value_input,
    out_grad,
    token_rates,
    out_gain,
    gate_prior,
    up_prior,
    down_prior,
):
    count, heads = lax.axis_size("tok"), lax.axis_size("head")
    tok = lax.axis_index("tok")
    chips = count // CORES
    own, dh = key_input.shape
    n = own * CORES
    w1, w3, w2 = gate_prior[0], up_prior[0], down_prior[0]
    fh = w2.shape[0]
    g, d = fh // count, dh // count
    rates = token_rates.T
    gain = out_gain[None, :]
    inputs = query_input, key_input, value_input, out_grad, rates, gain, w1, w3, w2

    if g % ROW_TILE or d % g or dh * g != fh * d or chips & (chips - 1) or chips < 2:
        query_grad, key_grad, value_grad, *results = by_blocks(inputs, tok, count, heads)
    else:
        query_grad, key_grad, value_grad, *results = by_line(inputs, chips, heads)
    return (query_grad, key_grad, value_grad, *(r.T[None] for r in results))


def by_line(inputs, chips, heads):
    query_input, key_input, value_input, out_grad, rates, gain, w1, w3, w2 = inputs
    count = chips * CORES
    own, dh = key_input.shape
    n, fh = own * CORES, w2.shape[0]
    g, d, folds = fh // count, dh // count, dh // fh
    product = 2 * n * dh * fh

    half = (g * chips // 2, dh)
    half_shares = [(half, F32)] * 3 + [(half, BF16)] * 3
    matrices = [((fh, dh), BF16), ((fh, dh), BF16), ((dh, fh), BF16)]
    sums_scratch = [((fh, dh), F32), ((fh, dh), F32), ((dh, fh), F32)]
    operands = [((fh, n), BF16), ((fh, n), BF16), ((dh, n), BF16)]
    hidden = ((fh, n), F32)
    own_hidden = ((fh, own), BF16)
    folds_by_matrix = (1, 1, folds)

    pair = lambda x: lax.ppermute(x, "tok", core_perm(count))
    key_other, value_other, rate_other = pair(key_input), pair(value_input), pair(rates)
    w1t, w3t = w1.T, w3.T
    query_other, grad_other = pair(query_input), pair(out_grad)
    keys_values = (
        key_input, key_other, value_input, value_other, rates, rate_other, w1t, w3t, w2,
    )
    sums = call(
        functools.partial(update_kernel, chips, folds),
        half_shares,
        keys_values,
        operands,
        "update",
        6 * product,
    )
    *saved, weighted, p1, p3, p2 = call(
        functools.partial(saved_kernel, chips, folds),
        [((dh, n), BF16)] + [hidden] * 4 + [own_hidden] * 3 + [((dh, n), F32)] + [(half, F32)] * 3,
        (*keys_values, out_grad, grad_other, gain),
        sums_scratch,
        "saved",
        3 * product,
    )
    push, up_slope, silu, back_slope, back_curve, mixed, gate_back, up_back = saved
    priors = p1, p3, p2

    fast, moved = [], []
    for k in range(3):
        totals = half_sums(sums[k], sums[3 + k], chips)
        rows, rows_moved = call(
            functools.partial(owner_forward_kernel, folds_by_matrix[k]),
            [(half, BF16), (half, F32)],
            (priors[k], *totals),
            name="owner_forward",
        )
        moved.append(rows_moved)
        fast.append(rows)
    arrived = from_owners(fast, chips)
    f1t, f3t, q_mixed, q_slope, q_silu = call(
        functools.partial(apply_first_kernel, chips),
        matrices[:2] + [((fh, n), BF16), hidden, hidden],
        (*arrived[:8], query_input, query_other),
        name="apply_first",
        flops=2 * product,
    )
    f2t, output, part = call(
        functools.partial(apply_last_kernel, chips, folds),
        matrices[2:] + [((dh, n), F32), ((2, n), F32)],
        (*arrived[8:], q_mixed, weighted),
        name="apply_last",
        flops=product,
    )
    q_gate_back, q_up_back, *sums = call(
        functools.partial(back_kernel, chips, folds, heads),
        [own_hidden] * 2 + half_shares,
        (
            *head_parts(part, heads),
            f2t, output, weighted, q_mixed, q_slope, q_silu, query_input, query_other,
        ),
        operands,
        "apply_back",
        4 * product,
    )
    (query_grad,) = call(
        query_kernel,
        [((own, dh), BF16)],
        (q_gate_back, q_up_back, f1t, f3t),
        name="query_grad",
        flops=product,
    )

    cotangent, owned = [], []
    for k in range(3):
        totals = half_sums(sums[k], sums[3 + k], chips)
        rows, rows_owned = call(
            functools.partial(owner_backward_kernel, folds_by_matrix[k]),
            [(half, BF16), (half, F32)],
            (priors[k], moved[k], *totals),
            name="owner_backward",
        )
        owned.append(rows_owned)
        cotangent.append(rows)
    arrived = from_owners(cotangent, chips)
    c1t, c3t, dbb, down_sums, up_part, gate_part = call(
        functools.partial(second_first_kernel, chips, folds),
        matrices[:2] + [own_hidden, ((g * chips, dh), F32), hidden, hidden],
        (*arrived[:8], key_input, key_other, push, up_slope, silu, back_slope, back_curve),
        name="second_first",
        flops=3 * product,
    )
    c2t, upb, gpb, *pieces = call(
        functools.partial(second_last_kernel, chips, folds),
        matrices[2:] + [own_hidden] * 2 + [((3 * g, dh), F32)] + [((3 * g, dh), BF16)] * (chips - 1),
        (
            *arrived[8:], key_input, key_other, push, up_slope, silu, up_part, gate_part, down_sums,
        ),
        operands[:2],
        "second_last",
        3 * product,
    )
    value_grad, key_grad = call(
        token_kernel,
        [((own, dh), BF16)] * 2,
        (rates, mixed, dbb, upb, gpb, gate_back, up_back, c1t, c3t, c2t, w1t, w3t, w2),
        name="token_grads",
        flops=3 * product,
    )
    results = call(
        functools.partial(owner_result_kernel, chips, folds),
        [((g, dh), F32)] * 2 + [((d, fh), F32)],
        (*owned, *exchange(pieces, chips)),
        name="owner_result",
    )
    return query_grad, key_grad, value_grad, *results


def by_blocks(inputs, tok, count, heads):
    query_input, key_input, value_input, out_grad, rates, gain, w1, w3, w2 = inputs
    own, dh = key_input.shape
    fh, chips = w2.shape[0], count // CORES
    g, d = fh // count, dh // count
    w1t, w3t = w1.T, w3.T
    pair = lambda x, axis=0: jnp.concatenate(
        [x, lax.ppermute(x, "tok", core_perm(count))], axis=axis
    )
    keys, values, queries, rate = pair(key_input), pair(value_input), pair(query_input), pair(rates, 1)
    weighted = (pair(out_grad).astype(F32) * gain).T
    push = push_of(rate, values)
    up_pre, silu, slope, curvature, mixed, down_back, back_slope, gate_back, up_back = (
        update_forward(w1t, w3t, w2, keys, push)
    )
    up_slope, back_curve = up_pre * slope, down_back * up_pre * curvature
    sums = nn(gate_back, keys), nn(up_back, keys), nt(push, mixed)
    piece, sent = sliced_pieces(*sums, tok, count)
    prior = pack(
        *(
            lax.dynamic_slice_in_dim(x, tok * rows, rows, 0).astype(F32)
            for x, rows in ((w1t, g), (w3t, g), (w2.T, d))
        )
    )
    update = total_of(piece, over_chips(sent, count), tok)
    fast, moved = packed_owner_forward(prior, update, fh)
    blocks = gather_blocks(jnp.tile(fast, (chips, 1)), count)
    f1t, f3t, f2t = whole_matrices(*blocks, tok, count, fh)
    q_mixed, q_slope, q_silu = apply_gate_and_up(f1t, f3t, queries)
    output, part = apply_down(f2t, q_mixed, weighted)
    sums = lax.psum(part, "head")
    q_gate_back, q_up_back, out_back = apply_backward(
        f2t, sums, heads * dh, output, weighted, q_slope, q_silu
    )
    grads = nn(q_gate_back, queries), nn(q_up_back, queries), nt(out_back, q_mixed)
    piece, sent = sliced_pieces(*grads, tok, count)
    query_grad = (tn(q_gate_back[:, :own], f1t) + tn(q_up_back[:, :own], f3t)).astype(BF16)
    fast_grad = total_of(piece, over_chips(sent, count), tok)
    cotangent, owned = packed_owner_backward(prior, moved, fast_grad, fh)
    blocks = gather_blocks(jnp.tile(cotangent, (chips, 1)), count)
    c1t, c3t, c2t = whole_matrices(*blocks, tok, count, fh)
    dbb, *parts = second_by_gate_and_up(c1t, c3t, keys, up_slope, silu, back_slope, back_curve)
    upb, gpb = second_by_down(c2t, push, up_slope, silu, *parts)
    bars = nn(gpb, keys), nn(upb, keys), nt(push, dbb)
    piece, sent = sliced_pieces(*bars, tok, count)
    value_grad, key_grad = token_grads(
        rates, mixed[:, :own], dbb[:, :own], upb[:, :own], gpb[:, :own],
        gate_back[:, :own], up_back[:, :own], c1t, c3t, c2t, w1t, w3t, w2,
    )
    results = unpack(owned - total_of(piece, over_chips(sent, count), tok), fh)
    return query_grad, key_grad, value_grad, *results


def solution(mesh):
    tokens = P("tok", "head")
    in_specs = (tokens,) * 5 + (P("head"),) + (P("head", None, None),) * 3
    out_specs = (tokens,) * 3 + (P("head", None, "tok"),) * 3
    return jax.shard_map(
        per_device, mesh=mesh, in_specs=in_specs, out_specs=out_specs, check_vma=False
    )
```

```python
import functools

import jax
import jax.numpy as jnp
from jax import lax
from jax.experimental import pallas as pl
from jax.experimental.pallas import tpu as pltpu
from jax.sharding import PartitionSpec as P

EPSILON = 1e-06
CORES = 2
ROW_TILE = 16
VMEM_LIMIT = 24 * 1024 * 1024
BF16, F32 = jnp.bfloat16, jnp.float32


def nn(a, b):
    return lax.dot_general(a, b, (((1,), (0,)), ((), ())), preferred_element_type=F32)


def nt(a, b):
    return lax.dot_general(a, b, (((1,), (1,)), ((), ())), preferred_element_type=F32)


def tn(a, b):
    return lax.dot_general(a, b, (((0,), (0,)), ((), ())), preferred_element_type=F32)


def silu_parts(hidden):
    sigmoid_value = jax.nn.sigmoid(hidden)
    silu_value = hidden * sigmoid_value
    silu_slope = sigmoid_value * (1.0 + hidden * (1.0 - sigmoid_value))
    curvature = sigmoid_value * (1.0 - sigmoid_value) * (2.0 + hidden * (1.0 - 2.0 * sigmoid_value))
    return silu_value, silu_slope, curvature


def partner(index, step, count):
    return index ^ step if count & (count - 1) == 0 else (index + step) % count


def source(index, step, count):
    return index ^ step if count & (count - 1) == 0 else (index + count - step) % count


def chip_perm(count, step):
    chips = count // CORES
    return [(t, partner(t // CORES, step, chips) * CORES + t % CORES) for t in range(count)]


def core_perm(count):
    return [(t, t ^ 1) for t in range(count)]


def pack(gate, up, down):
    folds = gate.shape[1] // down.shape[1]
    rows = down.shape[0] // folds
    down = jnp.concatenate([down[i * rows : (i + 1) * rows] for i in range(folds)], axis=1)
    return jnp.concatenate([gate, up, down], axis=0)


def unpack(packed, fh):
    g = packed.shape[0] // 3
    folds = packed.shape[1] // fh
    down = packed[2 * g :]
    down = jnp.concatenate([down[:, i * fh : (i + 1) * fh] for i in range(folds)], axis=0)
    return packed[:g], packed[g : 2 * g], down


def update_forward(w1t, w3t, w2, keys, push):
    gate_pre, up_pre = nt(w1t, keys), nt(w3t, keys)
    silu, slope, curvature = silu_parts(gate_pre)
    mixed = (silu * up_pre).astype(BF16)
    down_back = nn(w2, push)
    back_slope = down_back * slope
    gate_back = (down_back * up_pre * slope).astype(BF16)
    up_back = (down_back * silu).astype(BF16)
    return up_pre, silu, slope, curvature, mixed, down_back, back_slope, gate_back, up_back


def apply_forward(f1t, f3t, f2t, queries, weighted):
    q_gate, q_up = nt(f1t, queries), nt(f3t, queries)
    silu, slope, _ = silu_parts(q_gate)
    mixed = (silu * q_up).astype(BF16)
    output = nn(f2t, mixed)
    square = jnp.sum(output * output, axis=0, keepdims=True)
    dot = jnp.sum(weighted * output, axis=0, keepdims=True)
    return output, mixed, q_up * slope, silu, jnp.concatenate([square, dot], axis=0)


def apply_backward(f2, sums, full_width, output, weighted, up_slope, silu):
    inverse = lax.rsqrt(sums[0:1] / full_width + EPSILON)
    scale = inverse * inverse * inverse * sums[1:2] / full_width
    out_back = (inverse * weighted - output * scale).astype(BF16)
    q_back = nn(f2, out_back)
    gate_back = (q_back * up_slope).astype(BF16)
    up_back = (q_back * silu).astype(BF16)
    return gate_back, up_back, out_back


def second_by_gate_and_up(c1t, c3t, keys, up_slope, silu, back_slope, back_curve):
    gate_bar, up_bar = nt(c1t, keys), nt(c3t, keys)
    down_back_bar = (gate_bar * up_slope + up_bar * silu).astype(BF16)
    return down_back_bar, gate_bar * back_slope, up_bar * back_slope + gate_bar * back_curve


def second_by_down(c2t, push, up_slope, silu, up_part, gate_part):
    mixed_bar = tn(c2t, push)
    return (up_part + mixed_bar * silu).astype(BF16), (gate_part + mixed_bar * up_slope).astype(BF16)


def folds_of(rows, folds):
    width = rows.shape[1] // folds
    return [rows[:, i * width : (i + 1) * width] for i in range(folds)]


def norm_of(rows):
    return jnp.sqrt(jnp.sum(rows * rows, axis=1, keepdims=True) + EPSILON)


def owner_forward(prior, update, folds):
    moved = prior - update
    fast = [
        m * (norm_of(p) / norm_of(m)) for p, m in zip(folds_of(prior, folds), folds_of(moved, folds))
    ]
    return jnp.concatenate(fast, axis=1).astype(BF16), moved


def owner_backward(prior, moved, fast_grad, folds):
    cotangent, owned = [], []
    for p, m, fg in zip(*(folds_of(x, folds) for x in (prior, moved, fast_grad))):
        prior_norm, moved_norm = norm_of(p), norm_of(m)
        column_dot = jnp.sum(fg * m, axis=1, keepdims=True)
        moved_grad = (prior_norm / moved_norm) * (fg - m * (column_dot / (moved_norm * moved_norm)))
        cotangent.append(moved_grad)
        owned.append(moved_grad + p * (column_dot / (moved_norm * prior_norm)))
    return jnp.concatenate(cotangent, axis=1).astype(BF16), jnp.concatenate(owned, axis=1)


def push_of(rates, values):
    return (-rates * values.T.astype(F32)).astype(BF16)


def both(own_ref, other_ref, axis=0):
    return jnp.concatenate([own_ref[...], other_ref[...]], axis=axis)


def rows_of(ref, chip, core, chips, folds, i):
    rows = ref.shape[0] // (chips * CORES)
    height = rows // folds
    return pl.ds(pl.multiple_of((chip * CORES + core) * rows + i * height, height), height)


def cut_half(out, ref, parity, chips, folds):
    core = lax.axis_index("tok") % CORES
    height, width = ref.shape[0] // (chips * CORES * folds), ref.shape[1]
    for k in range(chips // 2):
        for i in range(folds):
            out[k * height : (k + 1) * height, i * width : (i + 1) * width] = ref[
                rows_of(ref, 2 * k + parity, core, chips, folds, i), :
            ].astype(out.dtype)


def place_half(ref, half, parity, core, chips, folds):
    height, width = ref.shape[0] // (chips * CORES * folds), ref.shape[1]
    for k in range(chips // 2):
        for i in range(folds):
            ref[rows_of(ref, 2 * k + parity, core, chips, folds, i), :] = half[
                k * height : (k + 1) * height, i * width : (i + 1) * width
            ]


def place_halves(chips, folds, halves, ref):
    tok = lax.axis_index("tok")
    parity, core = tok // CORES % 2, tok % CORES
    whose = ((parity, core), (1 - parity, core), (parity, 1 - core), (1 - parity, 1 - core))
    for half, (p, c) in zip(halves, whose):
        place_half(ref, half, p, c, chips, folds)


def rows_of_core(ref, order, chips):
    core = lax.axis_index("tok") % CORES
    rows = ref.shape[0] // (chips * CORES)
    blocks = [
        ref[pl.ds(pl.multiple_of((chip * CORES + core) * rows, rows), rows), :] for chip in order
    ]
    return jnp.concatenate(blocks, axis=0)


def fold(rows, chips, folds):
    height = rows.shape[0] // (chips * folds)
    parts = [rows[i * height : (i + 1) * height] for i in range(chips * folds)]
    wide = [jnp.concatenate(parts[k : k + folds], axis=1) for k in range(0, len(parts), folds)]
    return jnp.concatenate(wide, axis=0)


def pieces_order(chips):
    chip = lax.axis_index("tok") // CORES
    return [partner(chip, step, chips) for step in range(chips)]


def send_halves(chips, folds, operands, outs):
    gate_ref, up_ref, down_ref, tokens, hidden = operands
    parity = lax.axis_index("tok") // CORES % 2
    order = [2 * k + p for p in (parity, 1 - parity) for k in range(chips // 2)]
    sums = [nn(rows_of_core(ref, order, chips), tokens) for ref in (gate_ref, up_ref)]
    sums.append(fold(nt(rows_of_core(down_ref, order, chips), hidden), chips, folds))
    half = outs[0].shape[0]
    for k, total in enumerate(sums):
        outs[k][...] = total[:half]
        outs[3 + k][...] = total[half:].astype(BF16)


def push_kernel(vo, vx, ro, rx, push):
    push[...] = push_of(both(ro, rx, 1), both(vo, vx))


def transpose_kernel(x, out):
    out[...] = x[...].T


def update_kernel(chips, folds, ko, kx, push, w1t, w3t, w2, *rest):
    outs, (gate, up) = rest[:6], rest[6:]
    keys = both(ko, kx)
    *_, mixed, _, _, gate[...], up[...] = update_forward(w1t[...], w3t[...], w2[...], keys, push[...])
    send_halves(chips, folds, (gate, up, push, keys, mixed), outs)


def saved_kernel(
    chips, folds, ko, kx, push, w1t, w3t, w2, go, gx, gain,
    up_slope_ref, silu_ref, back_slope_ref, back_curve_ref,
    mixed_ref, gate_back_ref, up_back_ref, weighted_ref, p1_ref, p3_ref, p2_ref,
    gate_ref, up_ref, down_ref,
):
    up_pre, silu, slope, curvature, mixed, down_back, back_slope, gate_back, up_back = (
        update_forward(w1t[...], w3t[...], w2[...], both(ko, kx), push[...])
    )
    up_slope_ref[...] = up_pre * slope
    silu_ref[...] = silu
    back_slope_ref[...] = back_slope
    back_curve_ref[...] = down_back * up_pre * curvature
    own = mixed_ref.shape[1]
    mixed_ref[...] = mixed[:, :own]
    gate_back_ref[...] = gate_back[:, :own]
    up_back_ref[...] = up_back[:, :own]
    weighted_ref[...] = (both(go, gx).astype(F32) * gain[...]).T
    gate_ref[...] = w1t[...].astype(F32)
    up_ref[...] = w3t[...].astype(F32)
    down_ref[...] = w2[...].astype(F32).T
    parity = lax.axis_index("tok") // CORES % 2
    cut_half(p1_ref, gate_ref, parity, chips, 1)
    cut_half(p3_ref, up_ref, parity, chips, 1)
    cut_half(p2_ref, down_ref, parity, chips, folds)


def carry_kernel(own, got, out):
    out[...] = (own[...] + got[...].astype(F32)).astype(BF16)


def total_of_halves(halves):
    total = halves[0][...].astype(F32)
    for half in halves[1:]:
        total = total + half[...].astype(F32)
    return total


def owner_forward_kernel(folds, prior, *refs):
    fast, moved = refs[-2:]
    total = total_of_halves(refs[:-2])
    fast[...], moved[...] = owner_forward(prior[...], total, folds)


def owner_backward_kernel(folds, prior, moved, *refs):
    cotangent, owned = refs[-2:]
    total = total_of_halves(refs[:-2])
    cotangent[...], owned[...] = owner_backward(prior[...], moved[...], total, folds)


def owner_result_kernel(chips, folds, *refs):
    owned, pieces, outs = refs[:3], refs[3:-3], refs[-3:]
    bars = pieces[0][...]
    for piece in pieces[1:]:
        bars = bars + piece[...].astype(F32)
    g = outs[0].shape[0]
    block = lax.axis_index("tok") // (2 * CORES)
    for k, out in enumerate(outs):
        result = owned[k][pl.ds(pl.multiple_of(block * g, g), g), :] - bars[k * g : (k + 1) * g]
        for i, rows in enumerate(folds_of(result, folds if k == 2 else 1)):
            out[i * g : (i + 1) * g] = rows


def apply_kernel(chips, folds, *refs):
    halves, refs = refs[:12], refs[12:]
    qo, qx, weighted, f1t, f3t, f2t, output, mixed, up_slope, silu, sums = refs
    place_halves(chips, 1, halves[:4], f1t)
    place_halves(chips, 1, halves[4:8], f3t)
    place_halves(chips, folds, halves[8:], f2t)
    output[...], mixed[...], up_slope[...], silu[...], sums[...] = apply_forward(
        f1t[...], f3t[...], f2t[...], both(qo, qx), weighted[...]
    )


def back_kernel(chips, folds, heads, *refs):
    parts, refs = refs[:heads], refs[heads:]
    sums = parts[0][...]
    for part in parts[1:]:
        sums = sums + part[...]
    f2, output, weighted, mixed, up_slope, silu, qo, qx, gate_back, up_back = refs[:10]
    outs, (gate, up, down) = refs[10:16], refs[16:]
    width = heads * output.shape[0]
    gate[...], up[...], down[...] = apply_backward(
        f2[...], sums, width, output[...], weighted[...], up_slope[...], silu[...]
    )
    send_halves(chips, folds, (gate, up, down, both(qo, qx), mixed[...]), outs)
    own = gate_back.shape[1]
    gate_back[...], up_back[...] = gate[:, :own], up[:, :own]


def query_kernel(gate_back, up_back, f1t, f3t, out):
    out[...] = (tn(gate_back[...], f1t[...]) + tn(up_back[...], f3t[...])).astype(BF16)


def second_first_kernel(chips, folds, *refs):
    halves, refs = refs[:8], refs[8:]
    ko, kx, push, up_slope, silu, back_slope, back_curve = refs[:7]
    c1t, c3t, dbb_ref, down, up_part, gate_part = refs[7:]
    place_halves(chips, 1, halves[:4], c1t)
    place_halves(chips, 1, halves[4:], c3t)
    dbb, up_part[...], gate_part[...] = second_by_gate_and_up(
        c1t[...], c3t[...], both(ko, kx),
        up_slope[...], silu[...], back_slope[...], back_curve[...],
    )
    down[...] = fold(nt(rows_of_core(push, pieces_order(chips), chips), dbb), chips, folds)
    dbb_ref[...] = dbb[:, : dbb_ref.shape[1]]


def second_last_kernel(chips, folds, *refs):
    halves, refs = refs[:4], refs[4:]
    ko, kx, push, up_slope, silu, up_part, gate_part, down = refs[:8]
    c2t, upb_ref, gpb_ref = refs[8:11]
    outs, (gate, up) = refs[11 : 11 + chips], refs[11 + chips :]
    place_halves(chips, folds, halves, c2t)
    up[...], gate[...] = second_by_down(
        c2t[...], push[...], up_slope[...], silu[...], up_part[...], gate_part[...]
    )
    keys, order = both(ko, kx), pieces_order(chips)
    sums = [nn(rows_of_core(ref, order, chips), keys) for ref in (gate, up)] + [down[...]]
    g = sums[0].shape[0] // chips
    for k, out in enumerate(outs):
        parts = [x[k * g : (k + 1) * g] for x in sums]
        out[...] = jnp.concatenate(parts, axis=0).astype(out.dtype)
    own = upb_ref.shape[1]
    upb_ref[...], gpb_ref[...] = up[:, :own], gate[:, :own]


def token_grads(rates, mixed, dbb, upb, gpb, gate_back, up_back, c1t, c3t, c2t, w1t, w3t, w2):
    value_grad = (rates * (nn(c2t, mixed) + tn(w2, dbb))).T.astype(BF16)
    key_total = tn(gate_back, c1t) + tn(up_back, c3t) + tn(gpb, w1t) + tn(upb, w3t)
    return value_grad, (-key_total).astype(BF16)


def token_kernel(*refs):
    value_grad, key_grad = refs[-2:]
    value_grad[...], key_grad[...] = token_grads(*(r[...] for r in refs[:-2]))


def call(kernel, outs, args, scratch=(), name=None, flops=0):
    vmem = pl.BlockSpec(memory_space=pltpu.VMEM)
    return pl.pallas_call(
        kernel,
        out_shape=[jax.ShapeDtypeStruct(s, t) for s, t in outs],
        in_specs=[vmem] * len(args),
        out_specs=[vmem] * len(outs),
        scratch_shapes=[pltpu.VMEM(s, t) for s, t in scratch],
        compiler_params=pltpu.CompilerParams(vmem_limit_bytes=VMEM_LIMIT),
        cost_estimate=pl.CostEstimate(
            flops=flops,
            bytes_accessed=sum(a.size * a.dtype.itemsize for a in args),
            transcendentals=0,
        ),
        name=name,
    )(*args)


def exchange(pieces, chips):
    count = chips * CORES
    got = [lax.ppermute(pieces[s], "tok", chip_perm(count, s)) for s in reversed(range(1, chips))]
    return [pieces[0], *got]


def to_chip(x, step, chips):
    return lax.ppermute(x, "tok", chip_perm(chips * CORES, step))


def half_sums(kept, given, chips):
    (mine,) = call(carry_kernel, [(given.shape, BF16)], (kept, to_chip(given, 1, chips)), name="carry")
    return [mine, *(to_chip(mine, step, chips) for step in range(2, chips, 2))]


def from_owners(halves, chips):
    others = [to_chip(half, 1, chips) for half in halves]
    *later, others[0] = lax.optimization_barrier((*halves, others[0]))
    cross = lambda x: lax.ppermute(x, "tok", core_perm(chips * CORES))
    parts = zip(halves, others, map(cross, later), map(cross, others))
    return [x for part in parts for x in part]


def head_parts(part, heads):
    got = [
        lax.ppermute(part, "head", [(h, partner(h, step, heads)) for h in range(heads)])
        for step in range(1, heads)
    ]
    return [part, *got]


def over_chips(blocks, count):
    groups = [list(range(core, count, CORES)) for core in range(CORES)]
    return lax.all_to_all(blocks, "tok", 0, 0, axis_index_groups=groups, tiled=True)


def gather_blocks(copies, count):
    mine = over_chips(copies, count)
    return mine, lax.ppermute(mine, "tok", core_perm(count))


def sliced_pieces(gate, up, down, tok, count):
    g, d = gate.shape[0] // count, down.shape[0] // count
    rows = lambda x, size, t: lax.dynamic_slice_in_dim(x, t * size, size, 0)
    piece = lambda t: pack(rows(gate, g, t), rows(up, g, t), rows(down, d, t))
    sent = [piece(t + tok % CORES) for t in range(0, count, CORES)]
    return piece(tok), jnp.concatenate(sent, axis=0).astype(BF16)


def total_of(own, got, tok):
    blocks = got.reshape((-1,) + own.shape)
    chip = lax.broadcasted_iota(jnp.int32, (blocks.shape[0], 1, 1), 0)
    others = jnp.where(chip == tok // CORES, 0.0, blocks.astype(F32))
    return own + jnp.sum(others, axis=0)


def whole_matrices(mine, other, tok, count, fh):
    shape = (count // CORES, -1, mine.shape[1])
    pair = jnp.stack([mine.reshape(shape), other.reshape(shape)], axis=1)
    pair = jnp.where(tok % CORES == 0, pair, pair[:, ::-1])
    held = pair.reshape((count, -1, mine.shape[1]))
    parts = jax.vmap(lambda x: unpack(x, fh))(held)
    return tuple(x.reshape((-1, x.shape[-1])) for x in parts)


def packed_owner_forward(prior, update, fh):
    fast, moved = zip(*(owner_forward(p, u, 1) for p, u in zip(unpack(prior, fh), unpack(update, fh))))
    return pack(*fast), pack(*moved)


def packed_owner_backward(prior, moved, fast_grad, fh):
    parts = (unpack(x, fh) for x in (prior, moved, fast_grad))
    cotangent, owned = zip(*(owner_backward(p, m, f, 1) for p, m, f in zip(*parts)))
    return pack(*cotangent), pack(*owned)


def per_device(
    query_input,
    key_input,
    value_input,
    out_grad,
    token_rates,
    out_gain,
    gate_prior,
    up_prior,
    down_prior,
):
    count, heads = lax.axis_size("tok"), lax.axis_size("head")
    tok = lax.axis_index("tok")
    chips = count // CORES
    own, dh = key_input.shape
    n = own * CORES
    w1, w3, w2 = gate_prior[0], up_prior[0], down_prior[0]
    fh = w2.shape[0]
    g, d = fh // count, dh // count
    rates = token_rates.T
    gain = out_gain[None, :]
    inputs = query_input, key_input, value_input, out_grad, rates, gain, w1, w3, w2

    if g % ROW_TILE or d % g or dh * g != fh * d or chips & (chips - 1) or chips < 2:
        query_grad, key_grad, value_grad, *results = by_blocks(inputs, tok, count, heads)
    else:
        query_grad, key_grad, value_grad, *results = by_line(inputs, chips, heads)
    return (query_grad, key_grad, value_grad, *(r.T[None] for r in results))


def by_line(inputs, chips, heads):
    query_input, key_input, value_input, out_grad, rates, gain, w1, w3, w2 = inputs
    count = chips * CORES
    own, dh = key_input.shape
    n, fh = own * CORES, w2.shape[0]
    g, d, folds = fh // count, dh // count, dh // fh
    product = 2 * n * dh * fh

    half = (g * chips // 2, dh)
    half_shares = [(half, F32)] * 3 + [(half, BF16)] * 3
    matrices = [((fh, dh), BF16), ((fh, dh), BF16), ((dh, fh), BF16)]
    sums_scratch = [((fh, dh), F32), ((fh, dh), F32), ((dh, fh), F32)]
    operands = [((fh, n), BF16), ((fh, n), BF16), ((dh, n), BF16)]
    hidden = ((fh, n), F32)
    own_hidden = ((fh, own), BF16)
    folds_by_matrix = (1, 1, folds)

    pair = lambda x: lax.ppermute(x, "tok", core_perm(count))
    key_other, value_other, rate_other = pair(key_input), pair(value_input), pair(rates)
    w1t, w3t = w1.T, w3.T
    query_other, grad_other = pair(query_input), pair(out_grad)
    (push,) = call(
        push_kernel,
        [((dh, n), BF16)],
        (value_input, value_other, rates, rate_other),
        name="push",
    )
    keys_values = key_input, key_other, push, w1t, w3t, w2
    sums = call(
        functools.partial(update_kernel, chips, folds),
        half_shares,
        keys_values,
        operands[:2],
        "update",
        6 * product,
    )
    *saved, weighted, p1, p3, p2 = call(
        functools.partial(saved_kernel, chips, folds),
        [hidden] * 4 + [own_hidden] * 3 + [((dh, n), F32)] + [(half, F32)] * 3,
        (*keys_values, out_grad, grad_other, gain),
        sums_scratch,
        "saved",
        3 * product,
    )
    up_slope, silu, back_slope, back_curve, mixed, gate_back, up_back = saved
    priors = p1, p3, p2

    fast, moved = [], []
    for k in range(3):
        totals = half_sums(sums[k], sums[3 + k], chips)
        rows, rows_moved = call(
            functools.partial(owner_forward_kernel, folds_by_matrix[k]),
            [(half, BF16), (half, F32)],
            (priors[k], *totals),
            name="owner_forward",
        )
        moved.append(rows_moved)
        fast.append(rows)
    f1t, f3t, f2t, output, q_mixed, q_slope, q_silu, part = call(
        functools.partial(apply_kernel, chips, folds),
        matrices + [((dh, n), F32), ((fh, n), BF16), hidden, hidden, ((2, n), F32)],
        (*from_owners(fast, chips), query_input, query_other, weighted),
        name="apply",
        flops=3 * product,
    )
    (f2,) = call(transpose_kernel, [((fh, dh), BF16)], (f2t,), name="fast_down", flops=product)
    q_gate_back, q_up_back, *sums = call(
        functools.partial(back_kernel, chips, folds, heads),
        [own_hidden] * 2 + half_shares,
        (
            *head_parts(part, heads),
            f2, output, weighted, q_mixed, q_slope, q_silu, query_input, query_other,
        ),
        operands,
        "apply_back",
        4 * product,
    )
    (query_grad,) = call(
        query_kernel,
        [((own, dh), BF16)],
        (q_gate_back, q_up_back, f1t, f3t),
        name="query_grad",
        flops=product,
    )

    cotangent, owned = [], []
    for k in range(3):
        totals = half_sums(sums[k], sums[3 + k], chips)
        rows, rows_owned = call(
            functools.partial(owner_backward_kernel, folds_by_matrix[k]),
            [(half, BF16), (half, F32)],
            (priors[k], moved[k], *totals),
            name="owner_backward",
        )
        owned.append(rows_owned)
        cotangent.append(rows)
    arrived = from_owners(cotangent, chips)
    c1t, c3t, dbb, down_sums, up_part, gate_part = call(
        functools.partial(second_first_kernel, chips, folds),
        matrices[:2] + [own_hidden, ((g * chips, dh), F32), hidden, hidden],
        (*arrived[:8], key_input, key_other, push, up_slope, silu, back_slope, back_curve),
        name="second_first",
        flops=3 * product,
    )
    c2t, upb, gpb, *pieces = call(
        functools.partial(second_last_kernel, chips, folds),
        matrices[2:] + [own_hidden] * 2 + [((3 * g, dh), F32)] + [((3 * g, dh), BF16)] * (chips - 1),
        (
            *arrived[8:], key_input, key_other, push, up_slope, silu, up_part, gate_part, down_sums,
        ),
        operands[:2],
        "second_last",
        3 * product,
    )
    value_grad, key_grad = call(
        token_kernel,
        [((own, dh), BF16)] * 2,
        (rates, mixed, dbb, upb, gpb, gate_back, up_back, c1t, c3t, c2t, w1t, w3t, w2),
        name="token_grads",
        flops=3 * product,
    )
    results = call(
        functools.partial(owner_result_kernel, chips, folds),
        [((g, dh), F32)] * 2 + [((d, fh), F32)],
        (*owned, *exchange(pieces, chips)),
        name="owner_result",
    )
    return query_grad, key_grad, value_grad, *results


def by_blocks(inputs, tok, count, heads):
    query_input, key_input, value_input, out_grad, rates, gain, w1, w3, w2 = inputs
    own, dh = key_input.shape
    fh, chips = w2.shape[0], count // CORES
    g, d = fh // count, dh // count
    w1t, w3t = w1.T, w3.T
    pair = lambda x, axis=0: jnp.concatenate(
        [x, lax.ppermute(x, "tok", core_perm(count))], axis=axis
    )
    keys, values, queries, rate = pair(key_input), pair(value_input), pair(query_input), pair(rates, 1)
    weighted = (pair(out_grad).astype(F32) * gain).T
    push = push_of(rate, values)
    up_pre, silu, slope, curvature, mixed, down_back, back_slope, gate_back, up_back = (
        update_forward(w1t, w3t, w2, keys, push)
    )
    up_slope, back_curve = up_pre * slope, down_back * up_pre * curvature
    sums = nn(gate_back, keys), nn(up_back, keys), nt(push, mixed)
    piece, sent = sliced_pieces(*sums, tok, count)
    prior = pack(
        *(
            lax.dynamic_slice_in_dim(x, tok * rows, rows, 0).astype(F32)
            for x, rows in ((w1t, g), (w3t, g), (w2.T, d))
        )
    )
    update = total_of(piece, over_chips(sent, count), tok)
    fast, moved = packed_owner_forward(prior, update, fh)
    blocks = gather_blocks(jnp.tile(fast, (chips, 1)), count)
    f1t, f3t, f2t = whole_matrices(*blocks, tok, count, fh)
    output, q_mixed, q_slope, q_silu, part = apply_forward(f1t, f3t, f2t, queries, weighted)
    sums = lax.psum(part, "head")
    q_gate_back, q_up_back, out_back = apply_backward(
        f2t.T, sums, heads * dh, output, weighted, q_slope, q_silu
    )
    grads = nn(q_gate_back, queries), nn(q_up_back, queries), nt(out_back, q_mixed)
    piece, sent = sliced_pieces(*grads, tok, count)
    query_grad = (tn(q_gate_back[:, :own], f1t) + tn(q_up_back[:, :own], f3t)).astype(BF16)
    fast_grad = total_of(piece, over_chips(sent, count), tok)
    cotangent, owned = packed_owner_backward(prior, moved, fast_grad, fh)
    blocks = gather_blocks(jnp.tile(cotangent, (chips, 1)), count)
    c1t, c3t, c2t = whole_matrices(*blocks, tok, count, fh)
    dbb, *parts = second_by_gate_and_up(c1t, c3t, keys, up_slope, silu, back_slope, back_curve)
    upb, gpb = second_by_down(c2t, push, up_slope, silu, *parts)
    bars = nn(gpb, keys), nn(upb, keys), nt(push, dbb)
    piece, sent = sliced_pieces(*bars, tok, count)
    value_grad, key_grad = token_grads(
        rates, mixed[:, :own], dbb[:, :own], upb[:, :own], gpb[:, :own],
        gate_back[:, :own], up_back[:, :own], c1t, c3t, c2t, w1t, w3t, w2,
    )
    results = unpack(owned - total_of(piece, over_chips(sent, count), tok), fh)
    return query_grad, key_grad, value_grad, *results


def solution(mesh):
    tokens = P("tok", "head")
    in_specs = (tokens,) * 5 + (P("head"),) + (P("head", None, None),) * 3
    out_specs = (tokens,) * 3 + (P("head", None, "tok"),) * 3
    return jax.shard_map(
        per_device, mesh=mesh, in_specs=in_specs, out_specs=out_specs, check_vma=False
    )
```

```python
import functools

import jax
import jax.numpy as jnp
from jax import lax
from jax.experimental import pallas as pl
from jax.experimental.pallas import tpu as pltpu
from jax.sharding import PartitionSpec as P

EPSILON = 1e-06
CORES = 2
ROW_TILE = 16
VMEM_LIMIT = 24 * 1024 * 1024
BF16, F32 = jnp.bfloat16, jnp.float32


def nn(a, b):
    return lax.dot_general(a, b, (((1,), (0,)), ((), ())), preferred_element_type=F32)


def nt(a, b):
    return lax.dot_general(a, b, (((1,), (1,)), ((), ())), preferred_element_type=F32)


def tn(a, b):
    return lax.dot_general(a, b, (((0,), (0,)), ((), ())), preferred_element_type=F32)


def stacked(product, first, second, tokens):
    both_rows = product(jnp.concatenate([first, second], axis=0), tokens)
    return both_rows[: first.shape[0]], both_rows[first.shape[0] :]


def silu_parts(hidden):
    sigmoid_value = jax.nn.sigmoid(hidden)
    silu_value = hidden * sigmoid_value
    silu_slope = sigmoid_value * (1.0 + hidden * (1.0 - sigmoid_value))
    curvature = sigmoid_value * (1.0 - sigmoid_value) * (2.0 + hidden * (1.0 - 2.0 * sigmoid_value))
    return silu_value, silu_slope, curvature


def partner(index, step, count):
    return index ^ step if count & (count - 1) == 0 else (index + step) % count


def source(index, step, count):
    return index ^ step if count & (count - 1) == 0 else (index + count - step) % count


def chip_perm(count, step):
    chips = count // CORES
    return [(t, partner(t // CORES, step, chips) * CORES + t % CORES) for t in range(count)]


def core_perm(count):
    return [(t, t ^ 1) for t in range(count)]


def pack(gate, up, down):
    folds = gate.shape[1] // down.shape[1]
    rows = down.shape[0] // folds
    down = jnp.concatenate([down[i * rows : (i + 1) * rows] for i in range(folds)], axis=1)
    return jnp.concatenate([gate, up, down], axis=0)


def unpack(packed, fh):
    g = packed.shape[0] // 3
    folds = packed.shape[1] // fh
    down = packed[2 * g :]
    down = jnp.concatenate([down[:, i * fh : (i + 1) * fh] for i in range(folds)], axis=0)
    return packed[:g], packed[g : 2 * g], down


def update_forward(w1t, w3t, w2, keys, push):
    gate_pre, up_pre = stacked(nt, w1t, w3t, keys)
    silu, slope, curvature = silu_parts(gate_pre)
    mixed = (silu * up_pre).astype(BF16)
    down_back = nn(w2, push)
    back_slope = down_back * slope
    gate_back = (down_back * up_pre * slope).astype(BF16)
    up_back = (down_back * silu).astype(BF16)
    return up_pre, silu, slope, curvature, mixed, down_back, back_slope, gate_back, up_back


def apply_forward(f1t, f3t, f2t, queries, weighted):
    q_gate, q_up = stacked(nt, f1t, f3t, queries)
    silu, slope, _ = silu_parts(q_gate)
    mixed = (silu * q_up).astype(BF16)
    output = nn(f2t, mixed)
    square = jnp.sum(output * output, axis=0, keepdims=True)
    dot = jnp.sum(weighted * output, axis=0, keepdims=True)
    return output, mixed, q_up * slope, silu, jnp.concatenate([square, dot], axis=0)


def apply_backward(f2t, sums, full_width, output, weighted, up_slope, silu):
    inverse = lax.rsqrt(sums[0:1] / full_width + EPSILON)
    scale = inverse * inverse * inverse * sums[1:2] / full_width
    out_back = (inverse * weighted - output * scale).astype(BF16)
    q_back = tn(f2t, out_back)
    gate_back = (q_back * up_slope).astype(BF16)
    up_back = (q_back * silu).astype(BF16)
    return gate_back, up_back, out_back


def second_by_gate_and_up(c1t, c3t, keys, up_slope, silu, back_slope, back_curve):
    gate_bar, up_bar = stacked(nt, c1t, c3t, keys)
    down_back_bar = (gate_bar * up_slope + up_bar * silu).astype(BF16)
    return down_back_bar, gate_bar * back_slope, up_bar * back_slope + gate_bar * back_curve


def second_by_down(c2t, push, up_slope, silu, up_part, gate_part):
    mixed_bar = tn(c2t, push)
    return (up_part + mixed_bar * silu).astype(BF16), (gate_part + mixed_bar * up_slope).astype(BF16)


def folds_of(rows, folds):
    width = rows.shape[1] // folds
    return [rows[:, i * width : (i + 1) * width] for i in range(folds)]


def norm_of(rows):
    return jnp.sqrt(jnp.sum(rows * rows, axis=1, keepdims=True) + EPSILON)


def owner_forward(prior, update, folds):
    moved = prior - update
    fast = [
        m * (norm_of(p) / norm_of(m)) for p, m in zip(folds_of(prior, folds), folds_of(moved, folds))
    ]
    return jnp.concatenate(fast, axis=1).astype(BF16), moved


def owner_backward(prior, moved, fast_grad, folds):
    cotangent, owned = [], []
    for p, m, fg in zip(*(folds_of(x, folds) for x in (prior, moved, fast_grad))):
        prior_norm, moved_norm = norm_of(p), norm_of(m)
        column_dot = jnp.sum(fg * m, axis=1, keepdims=True)
        moved_grad = (prior_norm / moved_norm) * (fg - m * (column_dot / (moved_norm * moved_norm)))
        cotangent.append(moved_grad)
        owned.append(moved_grad + p * (column_dot / (moved_norm * prior_norm)))
    return jnp.concatenate(cotangent, axis=1).astype(BF16), jnp.concatenate(owned, axis=1)


def push_of(rates, values):
    return (-rates * values.T.astype(F32)).astype(BF16)


def both(own_ref, other_ref, axis=0):
    return jnp.concatenate([own_ref[...], other_ref[...]], axis=axis)


def rows_of(ref, chip, core, chips, folds, i):
    rows = ref.shape[0] // (chips * CORES)
    height = rows // folds
    return pl.ds(pl.multiple_of((chip * CORES + core) * rows + i * height, height), height)


def cut_half(out, ref, parity, chips, folds):
    core = lax.axis_index("tok") % CORES
    height, width = ref.shape[0] // (chips * CORES * folds), ref.shape[1]
    for k in range(chips // 2):
        for i in range(folds):
            out[k * height : (k + 1) * height, i * width : (i + 1) * width] = ref[
                rows_of(ref, 2 * k + parity, core, chips, folds, i), :
            ].astype(out.dtype)


def place_half(ref, half, parity, core, chips, folds):
    height, width = ref.shape[0] // (chips * CORES * folds), ref.shape[1]
    for k in range(chips // 2):
        for i in range(folds):
            ref[rows_of(ref, 2 * k + parity, core, chips, folds, i), :] = half[
                k * height : (k + 1) * height, i * width : (i + 1) * width
            ]


def place_halves(chips, folds, halves, ref):
    tok = lax.axis_index("tok")
    parity, core = tok // CORES % 2, tok % CORES
    whose = ((parity, core), (1 - parity, core), (parity, 1 - core), (1 - parity, 1 - core))
    for half, (p, c) in zip(halves, whose):
        place_half(ref, half, p, c, chips, folds)


def rows_of_core(ref, order, chips):
    core = lax.axis_index("tok") % CORES
    rows = ref.shape[0] // (chips * CORES)
    blocks = [
        ref[pl.ds(pl.multiple_of((chip * CORES + core) * rows, rows), rows), :] for chip in order
    ]
    return jnp.concatenate(blocks, axis=0)


def fold(rows, chips, folds):
    height = rows.shape[0] // (chips * folds)
    parts = [rows[i * height : (i + 1) * height] for i in range(chips * folds)]
    wide = [jnp.concatenate(parts[k : k + folds], axis=1) for k in range(0, len(parts), folds)]
    return jnp.concatenate(wide, axis=0)


def pieces_order(chips):
    chip = lax.axis_index("tok") // CORES
    return [partner(chip, step, chips) for step in range(chips)]


def send_halves(chips, folds, operands, outs):
    gate_ref, up_ref, down_ref, tokens, hidden = operands
    parity = lax.axis_index("tok") // CORES % 2
    order = [2 * k + p for p in (parity, 1 - parity) for k in range(chips // 2)]
    sums = list(stacked(nn, *(rows_of_core(x, order, chips) for x in (gate_ref, up_ref)), tokens))
    sums.append(fold(nt(rows_of_core(down_ref, order, chips), hidden), chips, folds))
    half = outs[0].shape[0]
    for k, total in enumerate(sums):
        outs[k][...] = total[:half]
        outs[3 + k][...] = total[half:].astype(BF16)


def update_kernel(chips, folds, ko, kx, vo, vx, ro, rx, w1t, w3t, w2, *rest):
    outs, (gate, up, push) = rest[:6], rest[6:]
    keys = both(ko, kx)
    push[...] = push_of(both(ro, rx, 1), both(vo, vx))
    *_, mixed, _, _, gate[...], up[...] = update_forward(w1t[...], w3t[...], w2[...], keys, push[...])
    send_halves(chips, folds, (gate, up, push, keys, mixed), outs)


def saved_kernel(
    chips, folds, ko, kx, vo, vx, ro, rx, w1t, w3t, w2, go, gx, gain,
    push_ref, up_slope_ref, silu_ref, back_slope_ref, back_curve_ref,
    mixed_ref, gate_back_ref, up_back_ref, weighted_ref, p1_ref, p3_ref, p2_ref,
    gate_ref, up_ref, down_ref,
):
    push = push_of(both(ro, rx, 1), both(vo, vx))
    push_ref[...] = push
    up_pre, silu, slope, curvature, mixed, down_back, back_slope, gate_back, up_back = (
        update_forward(w1t[...], w3t[...], w2[...], both(ko, kx), push)
    )
    up_slope_ref[...] = up_pre * slope
    silu_ref[...] = silu
    back_slope_ref[...] = back_slope
    back_curve_ref[...] = down_back * up_pre * curvature
    own = mixed_ref.shape[1]
    mixed_ref[...] = mixed[:, :own]
    gate_back_ref[...] = gate_back[:, :own]
    up_back_ref[...] = up_back[:, :own]
    weighted_ref[...] = (both(go, gx).astype(F32) * gain[...]).T
    gate_ref[...] = w1t[...].astype(F32)
    up_ref[...] = w3t[...].astype(F32)
    down_ref[...] = w2[...].astype(F32).T
    parity = lax.axis_index("tok") // CORES % 2
    cut_half(p1_ref, gate_ref, parity, chips, 1)
    cut_half(p3_ref, up_ref, parity, chips, 1)
    cut_half(p2_ref, down_ref, parity, chips, folds)


def carry_kernel(own, got, out):
    out[...] = (own[...] + got[...].astype(F32)).astype(BF16)


def total_of_halves(halves):
    total = halves[0][...].astype(F32)
    for half in halves[1:]:
        total = total + half[...].astype(F32)
    return total


def owner_forward_kernel(folds, prior, *refs):
    fast, moved = refs[-2:]
    total = total_of_halves(refs[:-2])
    fast[...], moved[...] = owner_forward(prior[...], total, folds)


def owner_backward_kernel(folds, prior, moved, *refs):
    cotangent, owned = refs[-2:]
    total = total_of_halves(refs[:-2])
    cotangent[...], owned[...] = owner_backward(prior[...], moved[...], total, folds)


def owner_result_kernel(chips, folds, *refs):
    owned, pieces, outs = refs[:3], refs[3:-3], refs[-3:]
    bars = pieces[0][...]
    for piece in pieces[1:]:
        bars = bars + piece[...].astype(F32)
    g = outs[0].shape[0]
    block = lax.axis_index("tok") // (2 * CORES)
    for k, out in enumerate(outs):
        result = owned[k][pl.ds(pl.multiple_of(block * g, g), g), :] - bars[k * g : (k + 1) * g]
        for i, rows in enumerate(folds_of(result, folds if k == 2 else 1)):
            out[i * g : (i + 1) * g] = rows


def apply_kernel(chips, folds, *refs):
    halves, refs = refs[:12], refs[12:]
    qo, qx, weighted, f1t, f3t, f2t, output, mixed, up_slope, silu, sums = refs
    place_halves(chips, 1, halves[:4], f1t)
    place_halves(chips, 1, halves[4:8], f3t)
    place_halves(chips, folds, halves[8:], f2t)
    output[...], mixed[...], up_slope[...], silu[...], sums[...] = apply_forward(
        f1t[...], f3t[...], f2t[...], both(qo, qx), weighted[...]
    )


def back_kernel(chips, folds, heads, *refs):
    parts, refs = refs[:heads], refs[heads:]
    sums = parts[0][...]
    for part in parts[1:]:
        sums = sums + part[...]
    f2t, output, weighted, mixed, up_slope, silu, qo, qx, gate_back, up_back = refs[:10]
    outs, (gate, up, down) = refs[10:16], refs[16:]
    width = heads * output.shape[0]
    gate[...], up[...], down[...] = apply_backward(
        f2t[...], sums, width, output[...], weighted[...], up_slope[...], silu[...]
    )
    send_halves(chips, folds, (gate, up, down, both(qo, qx), mixed[...]), outs)
    own = gate_back.shape[1]
    gate_back[...], up_back[...] = gate[:, :own], up[:, :own]


def query_kernel(gate_back, up_back, f1t, f3t, out):
    out[...] = (tn(gate_back[...], f1t[...]) + tn(up_back[...], f3t[...])).astype(BF16)


def second_first_kernel(chips, folds, *refs):
    halves, refs = refs[:8], refs[8:]
    ko, kx, push, up_slope, silu, back_slope, back_curve = refs[:7]
    c1t, c3t, dbb_ref, down, up_part, gate_part = refs[7:]
    place_halves(chips, 1, halves[:4], c1t)
    place_halves(chips, 1, halves[4:], c3t)
    dbb, up_part[...], gate_part[...] = second_by_gate_and_up(
        c1t[...], c3t[...], both(ko, kx),
        up_slope[...], silu[...], back_slope[...], back_curve[...],
    )
    down[...] = fold(nt(rows_of_core(push, pieces_order(chips), chips), dbb), chips, folds)
    dbb_ref[...] = dbb[:, : dbb_ref.shape[1]]


def second_last_kernel(chips, folds, *refs):
    halves, refs = refs[:4], refs[4:]
    ko, kx, push, up_slope, silu, up_part, gate_part, down = refs[:8]
    c2t, upb_ref, gpb_ref = refs[8:11]
    outs, (gate, up) = refs[11 : 11 + chips], refs[11 + chips :]
    place_halves(chips, folds, halves, c2t)
    up[...], gate[...] = second_by_down(
        c2t[...], push[...], up_slope[...], silu[...], up_part[...], gate_part[...]
    )
    keys, order = both(ko, kx), pieces_order(chips)
    sums = [*stacked(nn, *(rows_of_core(x, order, chips) for x in (gate, up)), keys), down[...]]
    g = sums[0].shape[0] // chips
    for k, out in enumerate(outs):
        parts = [x[k * g : (k + 1) * g] for x in sums]
        out[...] = jnp.concatenate(parts, axis=0).astype(out.dtype)
    own = upb_ref.shape[1]
    upb_ref[...], gpb_ref[...] = up[:, :own], gate[:, :own]


def token_grads(rates, mixed, dbb, upb, gpb, gate_back, up_back, c1t, c3t, c2t, w1t, w3t, w2):
    value_grad = (rates * (nn(c2t, mixed) + tn(w2, dbb))).T.astype(BF16)
    key_total = tn(gate_back, c1t) + tn(up_back, c3t) + tn(gpb, w1t) + tn(upb, w3t)
    return value_grad, (-key_total).astype(BF16)


def token_kernel(*refs):
    value_grad, key_grad = refs[-2:]
    value_grad[...], key_grad[...] = token_grads(*(r[...] for r in refs[:-2]))


def call(kernel, outs, args, scratch=(), name=None, flops=0):
    vmem = pl.BlockSpec(memory_space=pltpu.VMEM)
    return pl.pallas_call(
        kernel,
        out_shape=[jax.ShapeDtypeStruct(s, t) for s, t in outs],
        in_specs=[vmem] * len(args),
        out_specs=[vmem] * len(outs),
        scratch_shapes=[pltpu.VMEM(s, t) for s, t in scratch],
        compiler_params=pltpu.CompilerParams(vmem_limit_bytes=VMEM_LIMIT),
        cost_estimate=pl.CostEstimate(
            flops=flops,
            bytes_accessed=sum(a.size * a.dtype.itemsize for a in args),
            transcendentals=0,
        ),
        name=name,
    )(*args)


def exchange(pieces, chips):
    count = chips * CORES
    got = [lax.ppermute(pieces[s], "tok", chip_perm(count, s)) for s in reversed(range(1, chips))]
    return [pieces[0], *got]


def to_chip(x, step, chips):
    return lax.ppermute(x, "tok", chip_perm(chips * CORES, step))


def half_sums(kept, given, chips):
    (mine,) = call(carry_kernel, [(given.shape, BF16)], (kept, to_chip(given, 1, chips)), name="carry")
    return [mine, *(to_chip(mine, step, chips) for step in range(2, chips, 2))]


def from_owners(halves, chips):
    others = [to_chip(half, 1, chips) for half in halves]
    *later, others[0] = lax.optimization_barrier((*halves, others[0]))
    cross = lambda x: lax.ppermute(x, "tok", core_perm(chips * CORES))
    parts = zip(halves, others, map(cross, later), map(cross, others))
    return [x for part in parts for x in part]


def head_parts(part, heads):
    got = [
        lax.ppermute(part, "head", [(h, partner(h, step, heads)) for h in range(heads)])
        for step in range(1, heads)
    ]
    return [part, *got]


def over_chips(blocks, count):
    groups = [list(range(core, count, CORES)) for core in range(CORES)]
    return lax.all_to_all(blocks, "tok", 0, 0, axis_index_groups=groups, tiled=True)


def gather_blocks(copies, count):
    mine = over_chips(copies, count)
    return mine, lax.ppermute(mine, "tok", core_perm(count))


def sliced_pieces(gate, up, down, tok, count):
    g, d = gate.shape[0] // count, down.shape[0] // count
    rows = lambda x, size, t: lax.dynamic_slice_in_dim(x, t * size, size, 0)
    piece = lambda t: pack(rows(gate, g, t), rows(up, g, t), rows(down, d, t))
    sent = [piece(t + tok % CORES) for t in range(0, count, CORES)]
    return piece(tok), jnp.concatenate(sent, axis=0).astype(BF16)


def total_of(own, got, tok):
    blocks = got.reshape((-1,) + own.shape)
    chip = lax.broadcasted_iota(jnp.int32, (blocks.shape[0], 1, 1), 0)
    others = jnp.where(chip == tok // CORES, 0.0, blocks.astype(F32))
    return own + jnp.sum(others, axis=0)


def whole_matrices(mine, other, tok, count, fh):
    shape = (count // CORES, -1, mine.shape[1])
    pair = jnp.stack([mine.reshape(shape), other.reshape(shape)], axis=1)
    pair = jnp.where(tok % CORES == 0, pair, pair[:, ::-1])
    held = pair.reshape((count, -1, mine.shape[1]))
    parts = jax.vmap(lambda x: unpack(x, fh))(held)
    return tuple(x.reshape((-1, x.shape[-1])) for x in parts)


def packed_owner_forward(prior, update, fh):
    fast, moved = zip(*(owner_forward(p, u, 1) for p, u in zip(unpack(prior, fh), unpack(update, fh))))
    return pack(*fast), pack(*moved)


def packed_owner_backward(prior, moved, fast_grad, fh):
    parts = (unpack(x, fh) for x in (prior, moved, fast_grad))
    cotangent, owned = zip(*(owner_backward(p, m, f, 1) for p, m, f in zip(*parts)))
    return pack(*cotangent), pack(*owned)


def per_device(
    query_input,
    key_input,
    value_input,
    out_grad,
    token_rates,
    out_gain,
    gate_prior,
    up_prior,
    down_prior,
):
    count, heads = lax.axis_size("tok"), lax.axis_size("head")
    tok = lax.axis_index("tok")
    chips = count // CORES
    own, dh = key_input.shape
    n = own * CORES
    w1, w3, w2 = gate_prior[0], up_prior[0], down_prior[0]
    fh = w2.shape[0]
    g, d = fh // count, dh // count
    rates = token_rates.T
    gain = out_gain[None, :]
    inputs = query_input, key_input, value_input, out_grad, rates, gain, w1, w3, w2

    if g % ROW_TILE or d % g or dh * g != fh * d or chips & (chips - 1) or chips < 2:
        query_grad, key_grad, value_grad, *results = by_blocks(inputs, tok, count, heads)
    else:
        query_grad, key_grad, value_grad, *results = by_line(inputs, chips, heads)
    return (query_grad, key_grad, value_grad, *(r.T[None] for r in results))


def by_line(inputs, chips, heads):
    query_input, key_input, value_input, out_grad, rates, gain, w1, w3, w2 = inputs
    count = chips * CORES
    own, dh = key_input.shape
    n, fh = own * CORES, w2.shape[0]
    g, d, folds = fh // count, dh // count, dh // fh
    product = 2 * n * dh * fh

    half = (g * chips // 2, dh)
    half_shares = [(half, F32)] * 3 + [(half, BF16)] * 3
    matrices = [((fh, dh), BF16), ((fh, dh), BF16), ((dh, fh), BF16)]
    sums_scratch = [((fh, dh), F32), ((fh, dh), F32), ((dh, fh), F32)]
    operands = [((fh, n), BF16), ((fh, n), BF16), ((dh, n), BF16)]
    hidden = ((fh, n), F32)
    own_hidden = ((fh, own), BF16)
    folds_by_matrix = (1, 1, folds)

    pair = lambda x: lax.ppermute(x, "tok", core_perm(count))
    key_other, value_other, rate_other = pair(key_input), pair(value_input), pair(rates)
    w1t, w3t = w1.T, w3.T
    query_other, grad_other = pair(query_input), pair(out_grad)
    keys_values = (
        key_input, key_other, value_input, value_other, rates, rate_other, w1t, w3t, w2,
    )
    sums = call(
        functools.partial(update_kernel, chips, folds),
        half_shares,
        keys_values,
        operands,
        "update",
        6 * product,
    )
    *saved, weighted, p1, p3, p2 = call(
        functools.partial(saved_kernel, chips, folds),
        [((dh, n), BF16)] + [hidden] * 4 + [own_hidden] * 3 + [((dh, n), F32)] + [(half, F32)] * 3,
        (*keys_values, out_grad, grad_other, gain),
        sums_scratch,
        "saved",
        3 * product,
    )
    push, up_slope, silu, back_slope, back_curve, mixed, gate_back, up_back = saved
    priors = p1, p3, p2

    fast, moved = [], []
    for k in range(3):
        totals = half_sums(sums[k], sums[3 + k], chips)
        rows, rows_moved = call(
            functools.partial(owner_forward_kernel, folds_by_matrix[k]),
            [(half, BF16), (half, F32)],
            (priors[k], *totals),
            name="owner_forward",
        )
        moved.append(rows_moved)
        fast.append(rows)
    f1t, f3t, f2t, output, q_mixed, q_slope, q_silu, part = call(
        functools.partial(apply_kernel, chips, folds),
        matrices + [((dh, n), F32), ((fh, n), BF16), hidden, hidden, ((2, n), F32)],
        (*from_owners(fast, chips), query_input, query_other, weighted),
        name="apply",
        flops=3 * product,
    )
    q_gate_back, q_up_back, *sums = call(
        functools.partial(back_kernel, chips, folds, heads),
        [own_hidden] * 2 + half_shares,
        (
            *head_parts(part, heads),
            f2t, output, weighted, q_mixed, q_slope, q_silu, query_input, query_other,
        ),
        operands,
        "apply_back",
        4 * product,
    )
    (query_grad,) = call(
        query_kernel,
        [((own, dh), BF16)],
        (q_gate_back, q_up_back, f1t, f3t),
        name="query_grad",
        flops=product,
    )

    cotangent, owned = [], []
    for k in range(3):
        totals = half_sums(sums[k], sums[3 + k], chips)
        rows, rows_owned = call(
            functools.partial(owner_backward_kernel, folds_by_matrix[k]),
            [(half, BF16), (half, F32)],
            (priors[k], moved[k], *totals),
            name="owner_backward",
        )
        owned.append(rows_owned)
        cotangent.append(rows)
    arrived = from_owners(cotangent, chips)
    c1t, c3t, dbb, down_sums, up_part, gate_part = call(
        functools.partial(second_first_kernel, chips, folds),
        matrices[:2] + [own_hidden, ((g * chips, dh), F32), hidden, hidden],
        (*arrived[:8], key_input, key_other, push, up_slope, silu, back_slope, back_curve),
        name="second_first",
        flops=3 * product,
    )
    c2t, upb, gpb, *pieces = call(
        functools.partial(second_last_kernel, chips, folds),
        matrices[2:] + [own_hidden] * 2 + [((3 * g, dh), F32)] + [((3 * g, dh), BF16)] * (chips - 1),
        (
            *arrived[8:], key_input, key_other, push, up_slope, silu, up_part, gate_part, down_sums,
        ),
        operands[:2],
        "second_last",
        3 * product,
    )
    value_grad, key_grad = call(
        token_kernel,
        [((own, dh), BF16)] * 2,
        (rates, mixed, dbb, upb, gpb, gate_back, up_back, c1t, c3t, c2t, w1t, w3t, w2),
        name="token_grads",
        flops=3 * product,
    )
    results = call(
        functools.partial(owner_result_kernel, chips, folds),
        [((g, dh), F32)] * 2 + [((d, fh), F32)],
        (*owned, *exchange(pieces, chips)),
        name="owner_result",
    )
    return query_grad, key_grad, value_grad, *results


def by_blocks(inputs, tok, count, heads):
    query_input, key_input, value_input, out_grad, rates, gain, w1, w3, w2 = inputs
    own, dh = key_input.shape
    fh, chips = w2.shape[0], count // CORES
    g, d = fh // count, dh // count
    w1t, w3t = w1.T, w3.T
    pair = lambda x, axis=0: jnp.concatenate(
        [x, lax.ppermute(x, "tok", core_perm(count))], axis=axis
    )
    keys, values, queries, rate = pair(key_input), pair(value_input), pair(query_input), pair(rates, 1)
    weighted = (pair(out_grad).astype(F32) * gain).T
    push = push_of(rate, values)
    up_pre, silu, slope, curvature, mixed, down_back, back_slope, gate_back, up_back = (
        update_forward(w1t, w3t, w2, keys, push)
    )
    up_slope, back_curve = up_pre * slope, down_back * up_pre * curvature
    sums = nn(gate_back, keys), nn(up_back, keys), nt(push, mixed)
    piece, sent = sliced_pieces(*sums, tok, count)
    prior = pack(
        *(
            lax.dynamic_slice_in_dim(x, tok * rows, rows, 0).astype(F32)
            for x, rows in ((w1t, g), (w3t, g), (w2.T, d))
        )
    )
    update = total_of(piece, over_chips(sent, count), tok)
    fast, moved = packed_owner_forward(prior, update, fh)
    blocks = gather_blocks(jnp.tile(fast, (chips, 1)), count)
    f1t, f3t, f2t = whole_matrices(*blocks, tok, count, fh)
    output, q_mixed, q_slope, q_silu, part = apply_forward(f1t, f3t, f2t, queries, weighted)
    sums = lax.psum(part, "head")
    q_gate_back, q_up_back, out_back = apply_backward(
        f2t, sums, heads * dh, output, weighted, q_slope, q_silu
    )
    grads = nn(q_gate_back, queries), nn(q_up_back, queries), nt(out_back, q_mixed)
    piece, sent = sliced_pieces(*grads, tok, count)
    query_grad = (tn(q_gate_back[:, :own], f1t) + tn(q_up_back[:, :own], f3t)).astype(BF16)
    fast_grad = total_of(piece, over_chips(sent, count), tok)
    cotangent, owned = packed_owner_backward(prior, moved, fast_grad, fh)
    blocks = gather_blocks(jnp.tile(cotangent, (chips, 1)), count)
    c1t, c3t, c2t = whole_matrices(*blocks, tok, count, fh)
    dbb, *parts = second_by_gate_and_up(c1t, c3t, keys, up_slope, silu, back_slope, back_curve)
    upb, gpb = second_by_down(c2t, push, up_slope, silu, *parts)
    bars = nn(gpb, keys), nn(upb, keys), nt(push, dbb)
    piece, sent = sliced_pieces(*bars, tok, count)
    value_grad, key_grad = token_grads(
        rates, mixed[:, :own], dbb[:, :own], upb[:, :own], gpb[:, :own],
        gate_back[:, :own], up_back[:, :own], c1t, c3t, c2t, w1t, w3t, w2,
    )
    results = unpack(owned - total_of(piece, over_chips(sent, count), tok), fh)
    return query_grad, key_grad, value_grad, *results


def solution(mesh):
    tokens = P("tok", "head")
    in_specs = (tokens,) * 5 + (P("head"),) + (P("head", None, None),) * 3
    out_specs = (tokens,) * 3 + (P("head", None, "tok"),) * 3
    return jax.shard_map(
        per_device, mesh=mesh, in_specs=in_specs, out_specs=out_specs, check_vma=False
    )
```

```python
import functools

import jax
import jax.numpy as jnp
from jax import lax
from jax.experimental import pallas as pl
from jax.experimental.pallas import tpu as pltpu
from jax.sharding import PartitionSpec as P

EPSILON = 1e-06
CORES = 2
ROW_TILE = 16
VMEM_LIMIT = 24 * 1024 * 1024
BF16, F32 = jnp.bfloat16, jnp.float32


def nn(a, b):
    return lax.dot_general(a, b, (((1,), (0,)), ((), ())), preferred_element_type=F32)


def nt(a, b):
    return lax.dot_general(a, b, (((1,), (1,)), ((), ())), preferred_element_type=F32)


def tn(a, b):
    return lax.dot_general(a, b, (((0,), (0,)), ((), ())), preferred_element_type=F32)


def stacked(product, first, second, tokens):
    both_rows = product(jnp.concatenate([first, second], axis=0), tokens)
    return both_rows[: first.shape[0]], both_rows[first.shape[0] :]


def silu_parts(hidden):
    sigmoid_value = jax.nn.sigmoid(hidden)
    silu_value = hidden * sigmoid_value
    silu_slope = sigmoid_value * (1.0 + hidden * (1.0 - sigmoid_value))
    curvature = sigmoid_value * (1.0 - sigmoid_value) * (2.0 + hidden * (1.0 - 2.0 * sigmoid_value))
    return silu_value, silu_slope, curvature


def partner(index, step, count):
    return index ^ step if count & (count - 1) == 0 else (index + step) % count


def source(index, step, count):
    return index ^ step if count & (count - 1) == 0 else (index + count - step) % count


def chip_perm(count, step):
    chips = count // CORES
    return [(t, partner(t // CORES, step, chips) * CORES + t % CORES) for t in range(count)]


def core_perm(count):
    return [(t, t ^ 1) for t in range(count)]


def pack(gate, up, down):
    folds = gate.shape[1] // down.shape[1]
    rows = down.shape[0] // folds
    down = jnp.concatenate([down[i * rows : (i + 1) * rows] for i in range(folds)], axis=1)
    return jnp.concatenate([gate, up, down], axis=0)


def unpack(packed, fh):
    g = packed.shape[0] // 3
    folds = packed.shape[1] // fh
    down = packed[2 * g :]
    down = jnp.concatenate([down[:, i * fh : (i + 1) * fh] for i in range(folds)], axis=0)
    return packed[:g], packed[g : 2 * g], down


def update_forward(w1t, w3t, w2, keys, push):
    gate_pre, up_pre = stacked(nt, w1t, w3t, keys)
    silu, slope, curvature = silu_parts(gate_pre)
    mixed = (silu * up_pre).astype(BF16)
    down_back = nn(w2, push)
    back_slope = down_back * slope
    gate_back = (down_back * up_pre * slope).astype(BF16)
    up_back = (down_back * silu).astype(BF16)
    return up_pre, silu, slope, curvature, mixed, down_back, back_slope, gate_back, up_back


def apply_forward(f1t, f3t, f2t, queries, weighted):
    q_gate, q_up = nt(f1t, queries), nt(f3t, queries)
    silu, slope, _ = silu_parts(q_gate)
    mixed = (silu * q_up).astype(BF16)
    output = nn(f2t, mixed)
    square = jnp.sum(output * output, axis=0, keepdims=True)
    dot = jnp.sum(weighted * output, axis=0, keepdims=True)
    return output, mixed, q_up * slope, silu, jnp.concatenate([square, dot], axis=0)


def apply_backward(f2t, sums, full_width, output, weighted, up_slope, silu):
    inverse = lax.rsqrt(sums[0:1] / full_width + EPSILON)
    scale = inverse * inverse * inverse * sums[1:2] / full_width
    out_back = (inverse * weighted - output * scale).astype(BF16)
    q_back = tn(f2t, out_back)
    gate_back = (q_back * up_slope).astype(BF16)
    up_back = (q_back * silu).astype(BF16)
    return gate_back, up_back, out_back


def second_by_gate_and_up(c1t, c3t, keys, up_slope, silu, back_slope, back_curve):
    gate_bar, up_bar = stacked(nt, c1t, c3t, keys)
    down_back_bar = (gate_bar * up_slope + up_bar * silu).astype(BF16)
    return down_back_bar, gate_bar * back_slope, up_bar * back_slope + gate_bar * back_curve


def second_by_down(c2t, push, up_slope, silu, up_part, gate_part):
    mixed_bar = tn(c2t, push)
    return (up_part + mixed_bar * silu).astype(BF16), (gate_part + mixed_bar * up_slope).astype(BF16)


def folds_of(rows, folds):
    width = rows.shape[1] // folds
    return [rows[:, i * width : (i + 1) * width] for i in range(folds)]


def norm_of(rows):
    return jnp.sqrt(jnp.sum(rows * rows, axis=1, keepdims=True) + EPSILON)


def owner_forward(prior, update, folds):
    moved = prior - update
    fast = [
        m * (norm_of(p) / norm_of(m)) for p, m in zip(folds_of(prior, folds), folds_of(moved, folds))
    ]
    return jnp.concatenate(fast, axis=1).astype(BF16), moved


def owner_backward(prior, moved, fast_grad, folds):
    cotangent, owned = [], []
    for p, m, fg in zip(*(folds_of(x, folds) for x in (prior, moved, fast_grad))):
        prior_norm, moved_norm = norm_of(p), norm_of(m)
        column_dot = jnp.sum(fg * m, axis=1, keepdims=True)
        moved_grad = (prior_norm / moved_norm) * (fg - m * (column_dot / (moved_norm * moved_norm)))
        cotangent.append(moved_grad)
        owned.append(moved_grad + p * (column_dot / (moved_norm * prior_norm)))
    return jnp.concatenate(cotangent, axis=1).astype(BF16), jnp.concatenate(owned, axis=1)


def push_of(rates, values):
    return (-rates * values.T.astype(F32)).astype(BF16)


def both(own_ref, other_ref, axis=0):
    return jnp.concatenate([own_ref[...], other_ref[...]], axis=axis)


def rows_of(ref, chip, core, chips, folds, i):
    rows = ref.shape[0] // (chips * CORES)
    height = rows // folds
    return pl.ds(pl.multiple_of((chip * CORES + core) * rows + i * height, height), height)


def cut_half(out, ref, parity, chips, folds):
    core = lax.axis_index("tok") % CORES
    height, width = ref.shape[0] // (chips * CORES * folds), ref.shape[1]
    for k in range(chips // 2):
        for i in range(folds):
            out[k * height : (k + 1) * height, i * width : (i + 1) * width] = ref[
                rows_of(ref, 2 * k + parity, core, chips, folds, i), :
            ].astype(out.dtype)


def place_half(ref, half, parity, core, chips, folds):
    height, width = ref.shape[0] // (chips * CORES * folds), ref.shape[1]
    for k in range(chips // 2):
        for i in range(folds):
            ref[rows_of(ref, 2 * k + parity, core, chips, folds, i), :] = half[
                k * height : (k + 1) * height, i * width : (i + 1) * width
            ]


def place_halves(chips, folds, halves, ref):
    tok = lax.axis_index("tok")
    parity, core = tok // CORES % 2, tok % CORES
    whose = ((parity, core), (1 - parity, core), (parity, 1 - core), (1 - parity, 1 - core))
    for half, (p, c) in zip(halves, whose):
        place_half(ref, half, p, c, chips, folds)


def rows_of_core(ref, order, chips):
    core = lax.axis_index("tok") % CORES
    rows = ref.shape[0] // (chips * CORES)
    blocks = [
        ref[pl.ds(pl.multiple_of((chip * CORES + core) * rows, rows), rows), :] for chip in order
    ]
    return jnp.concatenate(blocks, axis=0)


def fold(rows, chips, folds):
    height = rows.shape[0] // (chips * folds)
    parts = [rows[i * height : (i + 1) * height] for i in range(chips * folds)]
    wide = [jnp.concatenate(parts[k : k + folds], axis=1) for k in range(0, len(parts), folds)]
    return jnp.concatenate(wide, axis=0)


def pieces_order(chips):
    chip = lax.axis_index("tok") // CORES
    return [partner(chip, step, chips) for step in range(chips)]


def send_halves(chips, folds, operands, outs):
    gate_ref, up_ref, down_ref, tokens, hidden = operands
    parity = lax.axis_index("tok") // CORES % 2
    order = [2 * k + p for p in (parity, 1 - parity) for k in range(chips // 2)]
    sums = list(stacked(nn, *(rows_of_core(x, order, chips) for x in (gate_ref, up_ref)), tokens))
    sums.append(fold(nt(rows_of_core(down_ref, order, chips), hidden), chips, folds))
    half = outs[0].shape[0]
    for k, total in enumerate(sums):
        outs[k][...] = total[:half]
        outs[3 + k][...] = total[half:].astype(BF16)


def update_kernel(chips, folds, ko, kx, vo, vx, ro, rx, w1t, w3t, w2, *rest):
    outs, (gate, up, push) = rest[:6], rest[6:]
    keys = both(ko, kx)
    push[...] = push_of(both(ro, rx, 1), both(vo, vx))
    *_, mixed, _, _, gate[...], up[...] = update_forward(w1t[...], w3t[...], w2[...], keys, push[...])
    send_halves(chips, folds, (gate, up, push, keys, mixed), outs)


def saved_kernel(
    chips, folds, ko, kx, vo, vx, ro, rx, w1t, w3t, w2, go, gx, gain,
    push_ref, up_slope_ref, silu_ref, back_slope_ref, back_curve_ref,
    mixed_ref, gate_back_ref, up_back_ref, weighted_ref, p1_ref, p3_ref, p2_ref,
    gate_ref, up_ref, down_ref,
):
    push = push_of(both(ro, rx, 1), both(vo, vx))
    push_ref[...] = push
    up_pre, silu, slope, curvature, mixed, down_back, back_slope, gate_back, up_back = (
        update_forward(w1t[...], w3t[...], w2[...], both(ko, kx), push)
    )
    up_slope_ref[...] = up_pre * slope
    silu_ref[...] = silu
    back_slope_ref[...] = back_slope
    back_curve_ref[...] = down_back * up_pre * curvature
    own = mixed_ref.shape[1]
    mixed_ref[...] = mixed[:, :own]
    gate_back_ref[...] = gate_back[:, :own]
    up_back_ref[...] = up_back[:, :own]
    weighted_ref[...] = (both(go, gx).astype(F32) * gain[...]).T
    gate_ref[...] = w1t[...].astype(F32)
    up_ref[...] = w3t[...].astype(F32)
    down_ref[...] = w2[...].astype(F32).T
    parity = lax.axis_index("tok") // CORES % 2
    cut_half(p1_ref, gate_ref, parity, chips, 1)
    cut_half(p3_ref, up_ref, parity, chips, 1)
    cut_half(p2_ref, down_ref, parity, chips, folds)


def carry_kernel(own, got, out):
    out[...] = (own[...] + got[...].astype(F32)).astype(BF16)


def total_of_halves(halves):
    total = halves[0][...].astype(F32)
    for half in halves[1:]:
        total = total + half[...].astype(F32)
    return total


def owner_forward_kernel(folds, prior, *refs):
    fast, moved = refs[-2:]
    total = total_of_halves(refs[:-2])
    fast[...], moved[...] = owner_forward(prior[...], total, folds)


def owner_backward_kernel(folds, prior, moved, *refs):
    cotangent, owned = refs[-2:]
    total = total_of_halves(refs[:-2])
    cotangent[...], owned[...] = owner_backward(prior[...], moved[...], total, folds)


def owner_result_kernel(chips, folds, *refs):
    owned, pieces, outs = refs[:3], refs[3:-3], refs[-3:]
    bars = pieces[0][...]
    for piece in pieces[1:]:
        bars = bars + piece[...].astype(F32)
    g = outs[0].shape[0]
    block = lax.axis_index("tok") // (2 * CORES)
    for k, out in enumerate(outs):
        result = owned[k][pl.ds(pl.multiple_of(block * g, g), g), :] - bars[k * g : (k + 1) * g]
        for i, rows in enumerate(folds_of(result, folds if k == 2 else 1)):
            out[i * g : (i + 1) * g] = rows


def apply_kernel(chips, folds, *refs):
    halves, refs = refs[:12], refs[12:]
    qo, qx, weighted, f1t, f3t, f2t, output, mixed, up_slope, silu, sums = refs
    place_halves(chips, 1, halves[:4], f1t)
    place_halves(chips, 1, halves[4:8], f3t)
    place_halves(chips, folds, halves[8:], f2t)
    output[...], mixed[...], up_slope[...], silu[...], sums[...] = apply_forward(
        f1t[...], f3t[...], f2t[...], both(qo, qx), weighted[...]
    )


def back_kernel(chips, folds, heads, *refs):
    parts, refs = refs[:heads], refs[heads:]
    sums = parts[0][...]
    for part in parts[1:]:
        sums = sums + part[...]
    f2t, output, weighted, mixed, up_slope, silu, qo, qx, gate_back, up_back = refs[:10]
    outs, (gate, up, down) = refs[10:16], refs[16:]
    width = heads * output.shape[0]
    gate[...], up[...], down[...] = apply_backward(
        f2t[...], sums, width, output[...], weighted[...], up_slope[...], silu[...]
    )
    send_halves(chips, folds, (gate, up, down, both(qo, qx), mixed[...]), outs)
    own = gate_back.shape[1]
    gate_back[...], up_back[...] = gate[:, :own], up[:, :own]


def query_kernel(gate_back, up_back, f1t, f3t, out):
    out[...] = (tn(gate_back[...], f1t[...]) + tn(up_back[...], f3t[...])).astype(BF16)


def second_first_kernel(chips, folds, *refs):
    halves, refs = refs[:8], refs[8:]
    ko, kx, push, up_slope, silu, back_slope, back_curve = refs[:7]
    c1t, c3t, dbb_ref, down, up_part, gate_part = refs[7:]
    place_halves(chips, 1, halves[:4], c1t)
    place_halves(chips, 1, halves[4:], c3t)
    dbb, up_part[...], gate_part[...] = second_by_gate_and_up(
        c1t[...], c3t[...], both(ko, kx),
        up_slope[...], silu[...], back_slope[...], back_curve[...],
    )
    down[...] = fold(nt(rows_of_core(push, pieces_order(chips), chips), dbb), chips, folds)
    dbb_ref[...] = dbb[:, : dbb_ref.shape[1]]


def second_last_kernel(chips, folds, *refs):
    halves, refs = refs[:4], refs[4:]
    ko, kx, push, up_slope, silu, up_part, gate_part, down = refs[:8]
    c2t, upb_ref, gpb_ref = refs[8:11]
    outs, (gate, up) = refs[11 : 11 + chips], refs[11 + chips :]
    place_halves(chips, folds, halves, c2t)
    up[...], gate[...] = second_by_down(
        c2t[...], push[...], up_slope[...], silu[...], up_part[...], gate_part[...]
    )
    keys, order = both(ko, kx), pieces_order(chips)
    sums = [*stacked(nn, *(rows_of_core(x, order, chips) for x in (gate, up)), keys), down[...]]
    g = sums[0].shape[0] // chips
    for k, out in enumerate(outs):
        parts = [x[k * g : (k + 1) * g] for x in sums]
        out[...] = jnp.concatenate(parts, axis=0).astype(out.dtype)
    own = upb_ref.shape[1]
    upb_ref[...], gpb_ref[...] = up[:, :own], gate[:, :own]


def token_grads(rates, mixed, dbb, upb, gpb, gate_back, up_back, c1t, c3t, c2t, w1t, w3t, w2):
    value_grad = (rates * (nn(c2t, mixed) + tn(w2, dbb))).T.astype(BF16)
    key_total = tn(gate_back, c1t) + tn(up_back, c3t) + tn(gpb, w1t) + tn(upb, w3t)
    return value_grad, (-key_total).astype(BF16)


def token_kernel(*refs):
    value_grad, key_grad = refs[-2:]
    value_grad[...], key_grad[...] = token_grads(*(r[...] for r in refs[:-2]))


def call(kernel, outs, args, scratch=(), name=None, flops=0):
    vmem = pl.BlockSpec(memory_space=pltpu.VMEM)
    return pl.pallas_call(
        kernel,
        out_shape=[jax.ShapeDtypeStruct(s, t) for s, t in outs],
        in_specs=[vmem] * len(args),
        out_specs=[vmem] * len(outs),
        scratch_shapes=[pltpu.VMEM(s, t) for s, t in scratch],
        compiler_params=pltpu.CompilerParams(vmem_limit_bytes=VMEM_LIMIT),
        cost_estimate=pl.CostEstimate(
            flops=flops,
            bytes_accessed=sum(a.size * a.dtype.itemsize for a in args),
            transcendentals=0,
        ),
        name=name,
    )(*args)


def exchange(pieces, chips):
    count = chips * CORES
    got = [lax.ppermute(pieces[s], "tok", chip_perm(count, s)) for s in reversed(range(1, chips))]
    return [pieces[0], *got]


def to_chip(x, step, chips):
    return lax.ppermute(x, "tok", chip_perm(chips * CORES, step))


def half_sums(kept, given, chips):
    (mine,) = call(carry_kernel, [(given.shape, BF16)], (kept, to_chip(given, 1, chips)), name="carry")
    return [mine, *(to_chip(mine, step, chips) for step in range(2, chips, 2))]


def from_owners(halves, chips):
    others = [to_chip(half, 1, chips) for half in halves]
    *later, others[0] = lax.optimization_barrier((*halves, others[0]))
    cross = lambda x: lax.ppermute(x, "tok", core_perm(chips * CORES))
    parts = zip(halves, others, map(cross, later), map(cross, others))
    return [x for part in parts for x in part]


def head_parts(part, heads):
    got = [
        lax.ppermute(part, "head", [(h, partner(h, step, heads)) for h in range(heads)])
        for step in range(1, heads)
    ]
    return [part, *got]


def over_chips(blocks, count):
    groups = [list(range(core, count, CORES)) for core in range(CORES)]
    return lax.all_to_all(blocks, "tok", 0, 0, axis_index_groups=groups, tiled=True)


def gather_blocks(copies, count):
    mine = over_chips(copies, count)
    return mine, lax.ppermute(mine, "tok", core_perm(count))


def sliced_pieces(gate, up, down, tok, count):
    g, d = gate.shape[0] // count, down.shape[0] // count
    rows = lambda x, size, t: lax.dynamic_slice_in_dim(x, t * size, size, 0)
    piece = lambda t: pack(rows(gate, g, t), rows(up, g, t), rows(down, d, t))
    sent = [piece(t + tok % CORES) for t in range(0, count, CORES)]
    return piece(tok), jnp.concatenate(sent, axis=0).astype(BF16)


def total_of(own, got, tok):
    blocks = got.reshape((-1,) + own.shape)
    chip = lax.broadcasted_iota(jnp.int32, (blocks.shape[0], 1, 1), 0)
    others = jnp.where(chip == tok // CORES, 0.0, blocks.astype(F32))
    return own + jnp.sum(others, axis=0)


def whole_matrices(mine, other, tok, count, fh):
    shape = (count // CORES, -1, mine.shape[1])
    pair = jnp.stack([mine.reshape(shape), other.reshape(shape)], axis=1)
    pair = jnp.where(tok % CORES == 0, pair, pair[:, ::-1])
    held = pair.reshape((count, -1, mine.shape[1]))
    parts = jax.vmap(lambda x: unpack(x, fh))(held)
    return tuple(x.reshape((-1, x.shape[-1])) for x in parts)


def packed_owner_forward(prior, update, fh):
    fast, moved = zip(*(owner_forward(p, u, 1) for p, u in zip(unpack(prior, fh), unpack(update, fh))))
    return pack(*fast), pack(*moved)


def packed_owner_backward(prior, moved, fast_grad, fh):
    parts = (unpack(x, fh) for x in (prior, moved, fast_grad))
    cotangent, owned = zip(*(owner_backward(p, m, f, 1) for p, m, f in zip(*parts)))
    return pack(*cotangent), pack(*owned)


def per_device(
    query_input,
    key_input,
    value_input,
    out_grad,
    token_rates,
    out_gain,
    gate_prior,
    up_prior,
    down_prior,
):
    count, heads = lax.axis_size("tok"), lax.axis_size("head")
    tok = lax.axis_index("tok")
    chips = count // CORES
    own, dh = key_input.shape
    n = own * CORES
    w1, w3, w2 = gate_prior[0], up_prior[0], down_prior[0]
    fh = w2.shape[0]
    g, d = fh // count, dh // count
    rates = token_rates.T
    gain = out_gain[None, :]
    inputs = query_input, key_input, value_input, out_grad, rates, gain, w1, w3, w2

    if g % ROW_TILE or d % g or dh * g != fh * d or chips & (chips - 1) or chips < 2:
        query_grad, key_grad, value_grad, *results = by_blocks(inputs, tok, count, heads)
    else:
        query_grad, key_grad, value_grad, *results = by_line(inputs, chips, heads)
    return (query_grad, key_grad, value_grad, *(r.T[None] for r in results))


def by_line(inputs, chips, heads):
    query_input, key_input, value_input, out_grad, rates, gain, w1, w3, w2 = inputs
    count = chips * CORES
    own, dh = key_input.shape
    n, fh = own * CORES, w2.shape[0]
    g, d, folds = fh // count, dh // count, dh // fh
    product = 2 * n * dh * fh

    half = (g * chips // 2, dh)
    half_shares = [(half, F32)] * 3 + [(half, BF16)] * 3
    matrices = [((fh, dh), BF16), ((fh, dh), BF16), ((dh, fh), BF16)]
    sums_scratch = [((fh, dh), F32), ((fh, dh), F32), ((dh, fh), F32)]
    operands = [((fh, n), BF16), ((fh, n), BF16), ((dh, n), BF16)]
    hidden = ((fh, n), F32)
    own_hidden = ((fh, own), BF16)
    folds_by_matrix = (1, 1, folds)

    pair = lambda x: lax.ppermute(x, "tok", core_perm(count))
    key_other, value_other, rate_other = pair(key_input), pair(value_input), pair(rates)
    w1t, w3t = w1.T, w3.T
    grad_other = pair(out_grad)
    keys_values = (
        key_input, key_other, value_input, value_other, rates, rate_other, w1t, w3t, w2,
    )
    sums = call(
        functools.partial(update_kernel, chips, folds),
        half_shares,
        keys_values,
        operands,
        "update",
        6 * product,
    )
    *saved, weighted, p1, p3, p2 = call(
        functools.partial(saved_kernel, chips, folds),
        [((dh, n), BF16)] + [hidden] * 4 + [own_hidden] * 3 + [((dh, n), F32)] + [(half, F32)] * 3,
        (*keys_values, out_grad, grad_other, gain),
        sums_scratch,
        "saved",
        3 * product,
    )
    push, up_slope, silu, back_slope, back_curve, mixed, gate_back, up_back = saved
    priors = p1, p3, p2

    fast, moved = [], []
    for k in range(3):
        totals = half_sums(sums[k], sums[3 + k], chips)
        rows, rows_moved = call(
            functools.partial(owner_forward_kernel, folds_by_matrix[k]),
            [(half, BF16), (half, F32)],
            (priors[k], *totals),
            name="owner_forward",
        )
        moved.append(rows_moved)
        fast.append(rows)
    query_later, weighted = lax.optimization_barrier((query_input, weighted))
    query_other = pair(query_later)
    f1t, f3t, f2t, output, q_mixed, q_slope, q_silu, part = call(
        functools.partial(apply_kernel, chips, folds),
        matrices + [((dh, n), F32), ((fh, n), BF16), hidden, hidden, ((2, n), F32)],
        (*from_owners(fast, chips), query_input, query_other, weighted),
        name="apply",
        flops=3 * product,
    )
    q_gate_back, q_up_back, *sums = call(
        functools.partial(back_kernel, chips, folds, heads),
        [own_hidden] * 2 + half_shares,
        (
            *head_parts(part, heads),
            f2t, output, weighted, q_mixed, q_slope, q_silu, query_input, query_other,
        ),
        operands,
        "apply_back",
        4 * product,
    )
    (query_grad,) = call(
        query_kernel,
        [((own, dh), BF16)],
        (q_gate_back, q_up_back, f1t, f3t),
        name="query_grad",
        flops=product,
    )

    cotangent, owned = [], []
    for k in range(3):
        totals = half_sums(sums[k], sums[3 + k], chips)
        rows, rows_owned = call(
            functools.partial(owner_backward_kernel, folds_by_matrix[k]),
            [(half, BF16), (half, F32)],
            (priors[k], moved[k], *totals),
            name="owner_backward",
        )
        owned.append(rows_owned)
        cotangent.append(rows)
    arrived = from_owners(cotangent, chips)
    c1t, c3t, dbb, down_sums, up_part, gate_part = call(
        functools.partial(second_first_kernel, chips, folds),
        matrices[:2] + [own_hidden, ((g * chips, dh), F32), hidden, hidden],
        (*arrived[:8], key_input, key_other, push, up_slope, silu, back_slope, back_curve),
        name="second_first",
        flops=3 * product,
    )
    c2t, upb, gpb, *pieces = call(
        functools.partial(second_last_kernel, chips, folds),
        matrices[2:] + [own_hidden] * 2 + [((3 * g, dh), F32)] + [((3 * g, dh), BF16)] * (chips - 1),
        (
            *arrived[8:], key_input, key_other, push, up_slope, silu, up_part, gate_part, down_sums,
        ),
        operands[:2],
        "second_last",
        3 * product,
    )
    value_grad, key_grad = call(
        token_kernel,
        [((own, dh), BF16)] * 2,
        (rates, mixed, dbb, upb, gpb, gate_back, up_back, c1t, c3t, c2t, w1t, w3t, w2),
        name="token_grads",
        flops=3 * product,
    )
    results = call(
        functools.partial(owner_result_kernel, chips, folds),
        [((g, dh), F32)] * 2 + [((d, fh), F32)],
        (*owned, *exchange(pieces, chips)),
        name="owner_result",
    )
    return query_grad, key_grad, value_grad, *results


def by_blocks(inputs, tok, count, heads):
    query_input, key_input, value_input, out_grad, rates, gain, w1, w3, w2 = inputs
    own, dh = key_input.shape
    fh, chips = w2.shape[0], count // CORES
    g, d = fh // count, dh // count
    w1t, w3t = w1.T, w3.T
    pair = lambda x, axis=0: jnp.concatenate(
        [x, lax.ppermute(x, "tok", core_perm(count))], axis=axis
    )
    keys, values, queries, rate = pair(key_input), pair(value_input), pair(query_input), pair(rates, 1)
    weighted = (pair(out_grad).astype(F32) * gain).T
    push = push_of(rate, values)
    up_pre, silu, slope, curvature, mixed, down_back, back_slope, gate_back, up_back = (
        update_forward(w1t, w3t, w2, keys, push)
    )
    up_slope, back_curve = up_pre * slope, down_back * up_pre * curvature
    sums = nn(gate_back, keys), nn(up_back, keys), nt(push, mixed)
    piece, sent = sliced_pieces(*sums, tok, count)
    prior = pack(
        *(
            lax.dynamic_slice_in_dim(x, tok * rows, rows, 0).astype(F32)
            for x, rows in ((w1t, g), (w3t, g), (w2.T, d))
        )
    )
    update = total_of(piece, over_chips(sent, count), tok)
    fast, moved = packed_owner_forward(prior, update, fh)
    blocks = gather_blocks(jnp.tile(fast, (chips, 1)), count)
    f1t, f3t, f2t = whole_matrices(*blocks, tok, count, fh)
    output, q_mixed, q_slope, q_silu, part = apply_forward(f1t, f3t, f2t, queries, weighted)
    sums = lax.psum(part, "head")
    q_gate_back, q_up_back, out_back = apply_backward(
        f2t, sums, heads * dh, output, weighted, q_slope, q_silu
    )
    grads = nn(q_gate_back, queries), nn(q_up_back, queries), nt(out_back, q_mixed)
    piece, sent = sliced_pieces(*grads, tok, count)
    query_grad = (tn(q_gate_back[:, :own], f1t) + tn(q_up_back[:, :own], f3t)).astype(BF16)
    fast_grad = total_of(piece, over_chips(sent, count), tok)
    cotangent, owned = packed_owner_backward(prior, moved, fast_grad, fh)
    blocks = gather_blocks(jnp.tile(cotangent, (chips, 1)), count)
    c1t, c3t, c2t = whole_matrices(*blocks, tok, count, fh)
    dbb, *parts = second_by_gate_and_up(c1t, c3t, keys, up_slope, silu, back_slope, back_curve)
    upb, gpb = second_by_down(c2t, push, up_slope, silu, *parts)
    bars = nn(gpb, keys), nn(upb, keys), nt(push, dbb)
    piece, sent = sliced_pieces(*bars, tok, count)
    value_grad, key_grad = token_grads(
        rates, mixed[:, :own], dbb[:, :own], upb[:, :own], gpb[:, :own],
        gate_back[:, :own], up_back[:, :own], c1t, c3t, c2t, w1t, w3t, w2,
    )
    results = unpack(owned - total_of(piece, over_chips(sent, count), tok), fh)
    return query_grad, key_grad, value_grad, *results


def solution(mesh):
    tokens = P("tok", "head")
    in_specs = (tokens,) * 5 + (P("head"),) + (P("head", None, None),) * 3
    out_specs = (tokens,) * 3 + (P("head", None, "tok"),) * 3
    return jax.shard_map(
        per_device, mesh=mesh, in_specs=in_specs, out_specs=out_specs, check_vma=False
    )
```

```python
import functools

import jax
import jax.numpy as jnp
from jax import lax
from jax.experimental import pallas as pl
from jax.experimental.pallas import tpu as pltpu
from jax.sharding import PartitionSpec as P

EPSILON = 1e-06
CORES = 2
ROW_TILE = 16
VMEM_LIMIT = 24 * 1024 * 1024
BF16, F32 = jnp.bfloat16, jnp.float32


def nn(a, b):
    return lax.dot_general(a, b, (((1,), (0,)), ((), ())), preferred_element_type=F32)


def nt(a, b):
    return lax.dot_general(a, b, (((1,), (1,)), ((), ())), preferred_element_type=F32)


def tn(a, b):
    return lax.dot_general(a, b, (((0,), (0,)), ((), ())), preferred_element_type=F32)


def stacked(product, first, second, tokens):
    both_rows = product(jnp.concatenate([first, second], axis=0), tokens)
    return both_rows[: first.shape[0]], both_rows[first.shape[0] :]


def silu_parts(hidden):
    sigmoid_value = jax.nn.sigmoid(hidden)
    silu_value = hidden * sigmoid_value
    silu_slope = sigmoid_value * (1.0 + hidden * (1.0 - sigmoid_value))
    curvature = sigmoid_value * (1.0 - sigmoid_value) * (2.0 + hidden * (1.0 - 2.0 * sigmoid_value))
    return silu_value, silu_slope, curvature


def partner(index, step, count):
    return index ^ step if count & (count - 1) == 0 else (index + step) % count


def source(index, step, count):
    return index ^ step if count & (count - 1) == 0 else (index + count - step) % count


def chip_perm(count, step):
    chips = count // CORES
    return [(t, partner(t // CORES, step, chips) * CORES + t % CORES) for t in range(count)]


def core_perm(count):
    return [(t, t ^ 1) for t in range(count)]


def pack(gate, up, down):
    folds = gate.shape[1] // down.shape[1]
    rows = down.shape[0] // folds
    down = jnp.concatenate([down[i * rows : (i + 1) * rows] for i in range(folds)], axis=1)
    return jnp.concatenate([gate, up, down], axis=0)


def unpack(packed, fh):
    g = packed.shape[0] // 3
    folds = packed.shape[1] // fh
    down = packed[2 * g :]
    down = jnp.concatenate([down[:, i * fh : (i + 1) * fh] for i in range(folds)], axis=0)
    return packed[:g], packed[g : 2 * g], down


def update_forward(w1t, w3t, w2, keys, push):
    gate_pre, up_pre = stacked(nt, w1t, w3t, keys)
    silu, slope, curvature = silu_parts(gate_pre)
    mixed = (silu * up_pre).astype(BF16)
    down_back = nn(w2, push)
    back_slope = down_back * slope
    gate_back = (down_back * up_pre * slope).astype(BF16)
    up_back = (down_back * silu).astype(BF16)
    return up_pre, silu, slope, curvature, mixed, down_back, back_slope, gate_back, up_back


def apply_forward(f1t, f3t, f2t, queries, weighted):
    q_gate, q_up = nt(f1t, queries), nt(f3t, queries)
    silu, slope, _ = silu_parts(q_gate)
    mixed = (silu * q_up).astype(BF16)
    output = nn(f2t, mixed)
    square = jnp.sum(output * output, axis=0, keepdims=True)
    dot = jnp.sum(weighted * output, axis=0, keepdims=True)
    return output, mixed, q_up * slope, silu, jnp.concatenate([square, dot], axis=0)


def apply_backward(f2t, sums, full_width, output, weighted, up_slope, silu):
    inverse = lax.rsqrt(sums[0:1] / full_width + EPSILON)
    scale = inverse * inverse * inverse * sums[1:2] / full_width
    out_back = (inverse * weighted - output * scale).astype(BF16)
    q_back = tn(f2t, out_back)
    gate_back = (q_back * up_slope).astype(BF16)
    up_back = (q_back * silu).astype(BF16)
    return gate_back, up_back, out_back


def second_by_gate_and_up(c1t, c3t, keys, up_slope, silu, back_slope, back_curve):
    gate_bar, up_bar = stacked(nt, c1t, c3t, keys)
    down_back_bar = (gate_bar * up_slope + up_bar * silu).astype(BF16)
    return down_back_bar, gate_bar * back_slope, up_bar * back_slope + gate_bar * back_curve


def second_by_down(c2t, push, up_slope, silu, up_part, gate_part):
    mixed_bar = tn(c2t, push)
    return (up_part + mixed_bar * silu).astype(BF16), (gate_part + mixed_bar * up_slope).astype(BF16)


def folds_of(rows, folds):
    width = rows.shape[1] // folds
    return [rows[:, i * width : (i + 1) * width] for i in range(folds)]


def norm_of(rows):
    return jnp.sqrt(jnp.sum(rows * rows, axis=1, keepdims=True) + EPSILON)


def owner_forward(prior, update, folds):
    moved = prior - update
    fast = [
        m * (norm_of(p) / norm_of(m)) for p, m in zip(folds_of(prior, folds), folds_of(moved, folds))
    ]
    return jnp.concatenate(fast, axis=1).astype(BF16), moved


def owner_backward(prior, moved, fast_grad, folds):
    cotangent, owned = [], []
    for p, m, fg in zip(*(folds_of(x, folds) for x in (prior, moved, fast_grad))):
        prior_norm, moved_norm = norm_of(p), norm_of(m)
        column_dot = jnp.sum(fg * m, axis=1, keepdims=True)
        moved_grad = (prior_norm / moved_norm) * (fg - m * (column_dot / (moved_norm * moved_norm)))
        cotangent.append(moved_grad)
        owned.append(moved_grad + p * (column_dot / (moved_norm * prior_norm)))
    return jnp.concatenate(cotangent, axis=1).astype(BF16), jnp.concatenate(owned, axis=1)


def push_of(rates, values):
    return (-rates * values.T.astype(F32)).astype(BF16)


def both(own_ref, other_ref, axis=0):
    return jnp.concatenate([own_ref[...], other_ref[...]], axis=axis)


def rows_of(ref, chip, core, chips, folds, i):
    rows = ref.shape[0] // (chips * CORES)
    height = rows // folds
    return pl.ds(pl.multiple_of((chip * CORES + core) * rows + i * height, height), height)


def cut_half(out, ref, parity, chips, folds):
    core = lax.axis_index("tok") % CORES
    height, width = ref.shape[0] // (chips * CORES * folds), ref.shape[1]
    for k in range(chips // 2):
        for i in range(folds):
            out[k * height : (k + 1) * height, i * width : (i + 1) * width] = ref[
                rows_of(ref, 2 * k + parity, core, chips, folds, i), :
            ].astype(out.dtype)


def place_half(ref, half, parity, core, chips, folds):
    height, width = ref.shape[0] // (chips * CORES * folds), ref.shape[1]
    for k in range(chips // 2):
        for i in range(folds):
            ref[rows_of(ref, 2 * k + parity, core, chips, folds, i), :] = half[
                k * height : (k + 1) * height, i * width : (i + 1) * width
            ]


def place_halves(chips, folds, halves, ref):
    tok = lax.axis_index("tok")
    parity, core = tok // CORES % 2, tok % CORES
    whose = ((parity, core), (1 - parity, core), (parity, 1 - core), (1 - parity, 1 - core))
    for half, (p, c) in zip(halves, whose):
        place_half(ref, half, p, c, chips, folds)


def rows_of_core(ref, order, chips):
    core = lax.axis_index("tok") % CORES
    rows = ref.shape[0] // (chips * CORES)
    blocks = [
        ref[pl.ds(pl.multiple_of((chip * CORES + core) * rows, rows), rows), :] for chip in order
    ]
    return jnp.concatenate(blocks, axis=0)


def fold(rows, chips, folds):
    height = rows.shape[0] // (chips * folds)
    parts = [rows[i * height : (i + 1) * height] for i in range(chips * folds)]
    wide = [jnp.concatenate(parts[k : k + folds], axis=1) for k in range(0, len(parts), folds)]
    return jnp.concatenate(wide, axis=0)


def pieces_order(chips):
    chip = lax.axis_index("tok") // CORES
    return [partner(chip, step, chips) for step in range(chips)]


def send_halves(chips, folds, operands, outs):
    gate_ref, up_ref, down_ref, tokens, hidden = operands
    parity = lax.axis_index("tok") // CORES % 2
    order = [2 * k + p for p in (parity, 1 - parity) for k in range(chips // 2)]
    sums = list(stacked(nn, *(rows_of_core(x, order, chips) for x in (gate_ref, up_ref)), tokens))
    sums.append(fold(nt(rows_of_core(down_ref, order, chips), hidden), chips, folds))
    half = outs[0].shape[0]
    for k, total in enumerate(sums):
        outs[k][...] = total[:half]
        outs[3 + k][...] = total[half:].astype(BF16)


def update_kernel(chips, folds, ko, kx, vo, vx, ro, rx, w1t, w3t, w2, *rest):
    outs, (gate, up, push) = rest[:6], rest[6:]
    keys = both(ko, kx)
    push[...] = push_of(both(ro, rx, 1), both(vo, vx))
    *_, mixed, _, _, gate[...], up[...] = update_forward(w1t[...], w3t[...], w2[...], keys, push[...])
    send_halves(chips, folds, (gate, up, push, keys, mixed), outs)


def prior_kernel(
    chips, folds, w1t, w3t, w2, go, gx, gain, weighted_ref, p1_ref, p3_ref, p2_ref, gate_ref, up_ref, down_ref
):
    weighted_ref[...] = (both(go, gx).astype(F32) * gain[...]).T
    gate_ref[...] = w1t[...].astype(F32)
    up_ref[...] = w3t[...].astype(F32)
    down_ref[...] = w2[...].astype(F32).T
    parity = lax.axis_index("tok") // CORES % 2
    cut_half(p1_ref, gate_ref, parity, chips, 1)
    cut_half(p3_ref, up_ref, parity, chips, 1)
    cut_half(p2_ref, down_ref, parity, chips, folds)


def saved_kernel(
    ko, kx, vo, vx, ro, rx, w1t, w3t, w2,
    push_ref, up_slope_ref, silu_ref, back_slope_ref, back_curve_ref,
    mixed_ref, gate_back_ref, up_back_ref,
):
    push = push_of(both(ro, rx, 1), both(vo, vx))
    push_ref[...] = push
    up_pre, silu, slope, curvature, mixed, down_back, back_slope, gate_back, up_back = (
        update_forward(w1t[...], w3t[...], w2[...], both(ko, kx), push)
    )
    up_slope_ref[...] = up_pre * slope
    silu_ref[...] = silu
    back_slope_ref[...] = back_slope
    back_curve_ref[...] = down_back * up_pre * curvature
    own = mixed_ref.shape[1]
    mixed_ref[...] = mixed[:, :own]
    gate_back_ref[...] = gate_back[:, :own]
    up_back_ref[...] = up_back[:, :own]


def carry_kernel(own, got, out):
    out[...] = (own[...] + got[...].astype(F32)).astype(BF16)


def total_of_halves(halves):
    total = halves[0][...].astype(F32)
    for half in halves[1:]:
        total = total + half[...].astype(F32)
    return total


def owner_forward_kernel(folds, prior, *refs):
    fast, moved = refs[-2:]
    total = total_of_halves(refs[:-2])
    fast[...], moved[...] = owner_forward(prior[...], total, folds)


def owner_backward_kernel(folds, prior, moved, *refs):
    cotangent, owned = refs[-2:]
    total = total_of_halves(refs[:-2])
    cotangent[...], owned[...] = owner_backward(prior[...], moved[...], total, folds)


def owner_result_kernel(chips, folds, *refs):
    owned, pieces, outs = refs[:3], refs[3:-3], refs[-3:]
    bars = pieces[0][...]
    for piece in pieces[1:]:
        bars = bars + piece[...].astype(F32)
    g = outs[0].shape[0]
    block = lax.axis_index("tok") // (2 * CORES)
    for k, out in enumerate(outs):
        result = owned[k][pl.ds(pl.multiple_of(block * g, g), g), :] - bars[k * g : (k + 1) * g]
        for i, rows in enumerate(folds_of(result, folds if k == 2 else 1)):
            out[i * g : (i + 1) * g] = rows


def apply_kernel(chips, folds, *refs):
    halves, refs = refs[:12], refs[12:]
    qo, qx, weighted, f1t, f3t, f2t, output, mixed, up_slope, silu, sums = refs
    place_halves(chips, 1, halves[:4], f1t)
    place_halves(chips, 1, halves[4:8], f3t)
    place_halves(chips, folds, halves[8:], f2t)
    output[...], mixed[...], up_slope[...], silu[...], sums[...] = apply_forward(
        f1t[...], f3t[...], f2t[...], both(qo, qx), weighted[...]
    )


def back_kernel(chips, folds, heads, *refs):
    parts, refs = refs[:heads], refs[heads + 1 :]
    sums = parts[0][...]
    for part in parts[1:]:
        sums = sums + part[...]
    f2t, output, weighted, mixed, up_slope, silu, qo, qx, gate_back, up_back = refs[:10]
    outs, (gate, up, down) = refs[10:16], refs[16:]
    width = heads * output.shape[0]
    gate[...], up[...], down[...] = apply_backward(
        f2t[...], sums, width, output[...], weighted[...], up_slope[...], silu[...]
    )
    send_halves(chips, folds, (gate, up, down, both(qo, qx), mixed[...]), outs)
    own = gate_back.shape[1]
    gate_back[...], up_back[...] = gate[:, :own], up[:, :own]


def query_kernel(gate_back, up_back, f1t, f3t, out):
    out[...] = (tn(gate_back[...], f1t[...]) + tn(up_back[...], f3t[...])).astype(BF16)


def second_first_kernel(chips, folds, *refs):
    halves, refs = refs[:8], refs[8:]
    ko, kx, push, up_slope, silu, back_slope, back_curve = refs[:7]
    c1t, c3t, dbb_ref, down, up_part, gate_part = refs[7:]
    place_halves(chips, 1, halves[:4], c1t)
    place_halves(chips, 1, halves[4:], c3t)
    dbb, up_part[...], gate_part[...] = second_by_gate_and_up(
        c1t[...], c3t[...], both(ko, kx),
        up_slope[...], silu[...], back_slope[...], back_curve[...],
    )
    down[...] = fold(nt(rows_of_core(push, pieces_order(chips), chips), dbb), chips, folds)
    dbb_ref[...] = dbb[:, : dbb_ref.shape[1]]


def second_last_kernel(chips, folds, *refs):
    halves, refs = refs[:4], refs[4:]
    ko, kx, push, up_slope, silu, up_part, gate_part, down = refs[:8]
    c2t, upb_ref, gpb_ref = refs[8:11]
    outs, (gate, up) = refs[11 : 11 + chips], refs[11 + chips :]
    place_halves(chips, folds, halves, c2t)
    up[...], gate[...] = second_by_down(
        c2t[...], push[...], up_slope[...], silu[...], up_part[...], gate_part[...]
    )
    keys, order = both(ko, kx), pieces_order(chips)
    sums = [*stacked(nn, *(rows_of_core(x, order, chips) for x in (gate, up)), keys), down[...]]
    g = sums[0].shape[0] // chips
    for k, out in enumerate(outs):
        parts = [x[k * g : (k + 1) * g] for x in sums]
        out[...] = jnp.concatenate(parts, axis=0).astype(out.dtype)
    own = upb_ref.shape[1]
    upb_ref[...], gpb_ref[...] = up[:, :own], gate[:, :own]


def token_grads(rates, mixed, dbb, upb, gpb, gate_back, up_back, c1t, c3t, c2t, w1t, w3t, w2):
    value_grad = (rates * (nn(c2t, mixed) + tn(w2, dbb))).T.astype(BF16)
    key_total = tn(gate_back, c1t) + tn(up_back, c3t) + tn(gpb, w1t) + tn(upb, w3t)
    return value_grad, (-key_total).astype(BF16)


def token_kernel(*refs):
    value_grad, key_grad = refs[-2:]
    value_grad[...], key_grad[...] = token_grads(*(r[...] for r in refs[:-2]))


def call(kernel, outs, args, scratch=(), name=None, flops=0):
    vmem = pl.BlockSpec(memory_space=pltpu.VMEM)
    return pl.pallas_call(
        kernel,
        out_shape=[jax.ShapeDtypeStruct(s, t) for s, t in outs],
        in_specs=[vmem] * len(args),
        out_specs=[vmem] * len(outs),
        scratch_shapes=[pltpu.VMEM(s, t) for s, t in scratch],
        compiler_params=pltpu.CompilerParams(vmem_limit_bytes=VMEM_LIMIT),
        cost_estimate=pl.CostEstimate(
            flops=flops,
            bytes_accessed=sum(a.size * a.dtype.itemsize for a in args),
            transcendentals=0,
        ),
        name=name,
    )(*args)


def exchange(pieces, chips):
    count = chips * CORES
    got = [lax.ppermute(pieces[s], "tok", chip_perm(count, s)) for s in reversed(range(1, chips))]
    return [pieces[0], *got]


def to_chip(x, step, chips):
    return lax.ppermute(x, "tok", chip_perm(chips * CORES, step))


def half_sums(kept, given, chips):
    (mine,) = call(carry_kernel, [(given.shape, BF16)], (kept, to_chip(given, 1, chips)), name="carry")
    return [mine, *(to_chip(mine, step, chips) for step in range(2, chips, 2))]


def from_owners(halves, chips):
    others = [to_chip(half, 1, chips) for half in halves]
    *later, others[0] = lax.optimization_barrier((*halves, others[0]))
    cross = lambda x: lax.ppermute(x, "tok", core_perm(chips * CORES))
    parts = zip(halves, others, map(cross, later), map(cross, others))
    return [x for part in parts for x in part]


def head_parts(part, heads):
    got = [
        lax.ppermute(part, "head", [(h, partner(h, step, heads)) for h in range(heads)])
        for step in range(1, heads)
    ]
    return [part, *got]


def over_chips(blocks, count):
    groups = [list(range(core, count, CORES)) for core in range(CORES)]
    return lax.all_to_all(blocks, "tok", 0, 0, axis_index_groups=groups, tiled=True)


def gather_blocks(copies, count):
    mine = over_chips(copies, count)
    return mine, lax.ppermute(mine, "tok", core_perm(count))


def sliced_pieces(gate, up, down, tok, count):
    g, d = gate.shape[0] // count, down.shape[0] // count
    rows = lambda x, size, t: lax.dynamic_slice_in_dim(x, t * size, size, 0)
    piece = lambda t: pack(rows(gate, g, t), rows(up, g, t), rows(down, d, t))
    sent = [piece(t + tok % CORES) for t in range(0, count, CORES)]
    return piece(tok), jnp.concatenate(sent, axis=0).astype(BF16)


def total_of(own, got, tok):
    blocks = got.reshape((-1,) + own.shape)
    chip = lax.broadcasted_iota(jnp.int32, (blocks.shape[0], 1, 1), 0)
    others = jnp.where(chip == tok // CORES, 0.0, blocks.astype(F32))
    return own + jnp.sum(others, axis=0)


def whole_matrices(mine, other, tok, count, fh):
    shape = (count // CORES, -1, mine.shape[1])
    pair = jnp.stack([mine.reshape(shape), other.reshape(shape)], axis=1)
    pair = jnp.where(tok % CORES == 0, pair, pair[:, ::-1])
    held = pair.reshape((count, -1, mine.shape[1]))
    parts = jax.vmap(lambda x: unpack(x, fh))(held)
    return tuple(x.reshape((-1, x.shape[-1])) for x in parts)


def packed_owner_forward(prior, update, fh):
    fast, moved = zip(*(owner_forward(p, u, 1) for p, u in zip(unpack(prior, fh), unpack(update, fh))))
    return pack(*fast), pack(*moved)


def packed_owner_backward(prior, moved, fast_grad, fh):
    parts = (unpack(x, fh) for x in (prior, moved, fast_grad))
    cotangent, owned = zip(*(owner_backward(p, m, f, 1) for p, m, f in zip(*parts)))
    return pack(*cotangent), pack(*owned)


def per_device(
    query_input,
    key_input,
    value_input,
    out_grad,
    token_rates,
    out_gain,
    gate_prior,
    up_prior,
    down_prior,
):
    count, heads = lax.axis_size("tok"), lax.axis_size("head")
    tok = lax.axis_index("tok")
    chips = count // CORES
    own, dh = key_input.shape
    n = own * CORES
    w1, w3, w2 = gate_prior[0], up_prior[0], down_prior[0]
    fh = w2.shape[0]
    g, d = fh // count, dh // count
    rates = token_rates.T
    gain = out_gain[None, :]
    inputs = query_input, key_input, value_input, out_grad, rates, gain, w1, w3, w2

    if g % ROW_TILE or d % g or dh * g != fh * d or chips & (chips - 1) or chips < 2:
        query_grad, key_grad, value_grad, *results = by_blocks(inputs, tok, count, heads)
    else:
        query_grad, key_grad, value_grad, *results = by_line(inputs, chips, heads)
    return (query_grad, key_grad, value_grad, *(r.T[None] for r in results))


def by_line(inputs, chips, heads):
    query_input, key_input, value_input, out_grad, rates, gain, w1, w3, w2 = inputs
    count = chips * CORES
    own, dh = key_input.shape
    n, fh = own * CORES, w2.shape[0]
    g, d, folds = fh // count, dh // count, dh // fh
    product = 2 * n * dh * fh

    half = (g * chips // 2, dh)
    half_shares = [(half, F32)] * 3 + [(half, BF16)] * 3
    matrices = [((fh, dh), BF16), ((fh, dh), BF16), ((dh, fh), BF16)]
    sums_scratch = [((fh, dh), F32), ((fh, dh), F32), ((dh, fh), F32)]
    operands = [((fh, n), BF16), ((fh, n), BF16), ((dh, n), BF16)]
    hidden = ((fh, n), F32)
    own_hidden = ((fh, own), BF16)
    folds_by_matrix = (1, 1, folds)

    pair = lambda x: lax.ppermute(x, "tok", core_perm(count))
    key_other, value_other, rate_other = pair(key_input), pair(value_input), pair(rates)
    w1t, w3t = w1.T, w3.T
    grad_other = pair(out_grad)
    keys_values = (
        key_input, key_other, value_input, value_other, rates, rate_other, w1t, w3t, w2,
    )
    sums = call(
        functools.partial(update_kernel, chips, folds),
        half_shares,
        keys_values,
        operands,
        "update",
        6 * product,
    )
    weighted, *priors = call(
        functools.partial(prior_kernel, chips, folds),
        [((dh, n), F32)] + [(half, F32)] * 3,
        (w1t, w3t, w2, out_grad, grad_other, gain),
        sums_scratch,
        "priors",
    )
    push, up_slope, silu, back_slope, back_curve, mixed, gate_back, up_back = call(
        saved_kernel,
        [((dh, n), BF16)] + [hidden] * 4 + [own_hidden] * 3,
        keys_values,
        name="saved",
        flops=3 * product,
    )

    fast, moved = [], []
    for k in range(3):
        totals = half_sums(sums[k], sums[3 + k], chips)
        rows, rows_moved = call(
            functools.partial(owner_forward_kernel, folds_by_matrix[k]),
            [(half, BF16), (half, F32)],
            (priors[k], *totals),
            name="owner_forward",
        )
        moved.append(rows_moved)
        fast.append(rows)
    query_later, weighted = lax.optimization_barrier((query_input, weighted))
    query_other = pair(query_later)
    f1t, f3t, f2t, output, q_mixed, q_slope, q_silu, part = call(
        functools.partial(apply_kernel, chips, folds),
        matrices + [((dh, n), F32), ((fh, n), BF16), hidden, hidden, ((2, n), F32)],
        (*from_owners(fast, chips), query_input, query_other, weighted),
        name="apply",
        flops=3 * product,
    )
    q_gate_back, q_up_back, *sums = call(
        functools.partial(back_kernel, chips, folds, heads),
        [own_hidden] * 2 + half_shares,
        (
            *head_parts(part, heads), up_back,
            f2t, output, weighted, q_mixed, q_slope, q_silu, query_input, query_other,
        ),
        operands,
        "apply_back",
        4 * product,
    )
    (query_grad,) = call(
        query_kernel,
        [((own, dh), BF16)],
        (q_gate_back, q_up_back, f1t, f3t),
        name="query_grad",
        flops=product,
    )

    cotangent, owned = [], []
    for k in range(3):
        totals = half_sums(sums[k], sums[3 + k], chips)
        rows, rows_owned = call(
            functools.partial(owner_backward_kernel, folds_by_matrix[k]),
            [(half, BF16), (half, F32)],
            (priors[k], moved[k], *totals),
            name="owner_backward",
        )
        owned.append(rows_owned)
        cotangent.append(rows)
    arrived = from_owners(cotangent, chips)
    c1t, c3t, dbb, down_sums, up_part, gate_part = call(
        functools.partial(second_first_kernel, chips, folds),
        matrices[:2] + [own_hidden, ((g * chips, dh), F32), hidden, hidden],
        (*arrived[:8], key_input, key_other, push, up_slope, silu, back_slope, back_curve),
        name="second_first",
        flops=3 * product,
    )
    c2t, upb, gpb, *pieces = call(
        functools.partial(second_last_kernel, chips, folds),
        matrices[2:] + [own_hidden] * 2 + [((3 * g, dh), F32)] + [((3 * g, dh), BF16)] * (chips - 1),
        (
            *arrived[8:], key_input, key_other, push, up_slope, silu, up_part, gate_part, down_sums,
        ),
        operands[:2],
        "second_last",
        3 * product,
    )
    value_grad, key_grad = call(
        token_kernel,
        [((own, dh), BF16)] * 2,
        (rates, mixed, dbb, upb, gpb, gate_back, up_back, c1t, c3t, c2t, w1t, w3t, w2),
        name="token_grads",
        flops=3 * product,
    )
    results = call(
        functools.partial(owner_result_kernel, chips, folds),
        [((g, dh), F32)] * 2 + [((d, fh), F32)],
        (*owned, *exchange(pieces, chips)),
        name="owner_result",
    )
    return query_grad, key_grad, value_grad, *results


def by_blocks(inputs, tok, count, heads):
    query_input, key_input, value_input, out_grad, rates, gain, w1, w3, w2 = inputs
    own, dh = key_input.shape
    fh, chips = w2.shape[0], count // CORES
    g, d = fh // count, dh // count
    w1t, w3t = w1.T, w3.T
    pair = lambda x, axis=0: jnp.concatenate(
        [x, lax.ppermute(x, "tok", core_perm(count))], axis=axis
    )
    keys, values, queries, rate = pair(key_input), pair(value_input), pair(query_input), pair(rates, 1)
    weighted = (pair(out_grad).astype(F32) * gain).T
    push = push_of(rate, values)
    up_pre, silu, slope, curvature, mixed, down_back, back_slope, gate_back, up_back = (
        update_forward(w1t, w3t, w2, keys, push)
    )
    up_slope, back_curve = up_pre * slope, down_back * up_pre * curvature
    sums = nn(gate_back, keys), nn(up_back, keys), nt(push, mixed)
    piece, sent = sliced_pieces(*sums, tok, count)
    prior = pack(
        *(
            lax.dynamic_slice_in_dim(x, tok * rows, rows, 0).astype(F32)
            for x, rows in ((w1t, g), (w3t, g), (w2.T, d))
        )
    )
    update = total_of(piece, over_chips(sent, count), tok)
    fast, moved = packed_owner_forward(prior, update, fh)
    blocks = gather_blocks(jnp.tile(fast, (chips, 1)), count)
    f1t, f3t, f2t = whole_matrices(*blocks, tok, count, fh)
    output, q_mixed, q_slope, q_silu, part = apply_forward(f1t, f3t, f2t, queries, weighted)
    sums = lax.psum(part, "head")
    q_gate_back, q_up_back, out_back = apply_backward(
        f2t, sums, heads * dh, output, weighted, q_slope, q_silu
    )
    grads = nn(q_gate_back, queries), nn(q_up_back, queries), nt(out_back, q_mixed)
    piece, sent = sliced_pieces(*grads, tok, count)
    query_grad = (tn(q_gate_back[:, :own], f1t) + tn(q_up_back[:, :own], f3t)).astype(BF16)
    fast_grad = total_of(piece, over_chips(sent, count), tok)
    cotangent, owned = packed_owner_backward(prior, moved, fast_grad, fh)
    blocks = gather_blocks(jnp.tile(cotangent, (chips, 1)), count)
    c1t, c3t, c2t = whole_matrices(*blocks, tok, count, fh)
    dbb, *parts = second_by_gate_and_up(c1t, c3t, keys, up_slope, silu, back_slope, back_curve)
    upb, gpb = second_by_down(c2t, push, up_slope, silu, *parts)
    bars = nn(gpb, keys), nn(upb, keys), nt(push, dbb)
    piece, sent = sliced_pieces(*bars, tok, count)
    value_grad, key_grad = token_grads(
        rates, mixed[:, :own], dbb[:, :own], upb[:, :own], gpb[:, :own],
        gate_back[:, :own], up_back[:, :own], c1t, c3t, c2t, w1t, w3t, w2,
    )
    results = unpack(owned - total_of(piece, over_chips(sent, count), tok), fh)
    return query_grad, key_grad, value_grad, *results


def solution(mesh):
    tokens = P("tok", "head")
    in_specs = (tokens,) * 5 + (P("head"),) + (P("head", None, None),) * 3
    out_specs = (tokens,) * 3 + (P("head", None, "tok"),) * 3
    return jax.shard_map(
        per_device, mesh=mesh, in_specs=in_specs, out_specs=out_specs, check_vma=False
    )
```

```python
import functools

import jax
import jax.numpy as jnp
from jax import lax
from jax.experimental import pallas as pl
from jax.experimental.pallas import tpu as pltpu
from jax.sharding import PartitionSpec as P

EPSILON = 1e-06
CORES = 2
ROW_TILE = 16
VMEM_LIMIT = 24 * 1024 * 1024
BF16, F32 = jnp.bfloat16, jnp.float32


def nn(a, b):
    return lax.dot_general(a, b, (((1,), (0,)), ((), ())), preferred_element_type=F32)


def nt(a, b):
    return lax.dot_general(a, b, (((1,), (1,)), ((), ())), preferred_element_type=F32)


def tn(a, b):
    return lax.dot_general(a, b, (((0,), (0,)), ((), ())), preferred_element_type=F32)


def stacked(product, first, second, tokens):
    both_rows = product(jnp.concatenate([first, second], axis=0), tokens)
    return both_rows[: first.shape[0]], both_rows[first.shape[0] :]


def silu_parts(hidden):
    sigmoid_value = jax.nn.sigmoid(hidden)
    silu_value = hidden * sigmoid_value
    silu_slope = sigmoid_value * (1.0 + hidden * (1.0 - sigmoid_value))
    curvature = sigmoid_value * (1.0 - sigmoid_value) * (2.0 + hidden * (1.0 - 2.0 * sigmoid_value))
    return silu_value, silu_slope, curvature


def partner(index, step, count):
    return index ^ step if count & (count - 1) == 0 else (index + step) % count


def source(index, step, count):
    return index ^ step if count & (count - 1) == 0 else (index + count - step) % count


def chip_perm(count, step):
    chips = count // CORES
    return [(t, partner(t // CORES, step, chips) * CORES + t % CORES) for t in range(count)]


def core_perm(count):
    return [(t, t ^ 1) for t in range(count)]


def pack(gate, up, down):
    folds = gate.shape[1] // down.shape[1]
    rows = down.shape[0] // folds
    down = jnp.concatenate([down[i * rows : (i + 1) * rows] for i in range(folds)], axis=1)
    return jnp.concatenate([gate, up, down], axis=0)


def unpack(packed, fh):
    g = packed.shape[0] // 3
    folds = packed.shape[1] // fh
    down = packed[2 * g :]
    down = jnp.concatenate([down[:, i * fh : (i + 1) * fh] for i in range(folds)], axis=0)
    return packed[:g], packed[g : 2 * g], down


def update_forward(w1t, w3t, w2, keys, push):
    gate_pre, up_pre = stacked(nt, w1t, w3t, keys)
    silu, slope, curvature = silu_parts(gate_pre)
    mixed = (silu * up_pre).astype(BF16)
    down_back = nn(w2, push)
    back_slope = down_back * slope
    gate_back = (down_back * up_pre * slope).astype(BF16)
    up_back = (down_back * silu).astype(BF16)
    return up_pre, silu, slope, curvature, mixed, down_back, back_slope, gate_back, up_back


def apply_forward(f1t, f3t, f2t, queries, weighted):
    q_gate, q_up = nt(f1t, queries), nt(f3t, queries)
    silu, slope, _ = silu_parts(q_gate)
    mixed = (silu * q_up).astype(BF16)
    output = nn(f2t, mixed)
    square = jnp.sum(output * output, axis=0, keepdims=True)
    dot = jnp.sum(weighted * output, axis=0, keepdims=True)
    return output, mixed, q_up * slope, silu, jnp.concatenate([square, dot], axis=0)


def apply_backward(f2t, sums, full_width, output, weighted, up_slope, silu):
    inverse = lax.rsqrt(sums[0:1] / full_width + EPSILON)
    scale = inverse * inverse * inverse * sums[1:2] / full_width
    out_back = (inverse * weighted - output * scale).astype(BF16)
    q_back = tn(f2t, out_back)
    gate_back = (q_back * up_slope).astype(BF16)
    up_back = (q_back * silu).astype(BF16)
    return gate_back, up_back, out_back


def second_by_gate_and_up(c1t, c3t, keys, up_slope, silu, back_slope, back_curve):
    gate_bar, up_bar = stacked(nt, c1t, c3t, keys)
    down_back_bar = (gate_bar * up_slope + up_bar * silu).astype(BF16)
    return down_back_bar, gate_bar * back_slope, up_bar * back_slope + gate_bar * back_curve


def second_by_down(c2t, push, up_slope, silu, up_part, gate_part):
    mixed_bar = tn(c2t, push)
    return (up_part + mixed_bar * silu).astype(BF16), (gate_part + mixed_bar * up_slope).astype(BF16)


def folds_of(rows, folds):
    width = rows.shape[1] // folds
    return [rows[:, i * width : (i + 1) * width] for i in range(folds)]


def norm_of(rows):
    return jnp.sqrt(jnp.sum(rows * rows, axis=1, keepdims=True) + EPSILON)


def owner_forward(prior, update, folds):
    moved = prior - update
    fast = [
        m * (norm_of(p) / norm_of(m)) for p, m in zip(folds_of(prior, folds), folds_of(moved, folds))
    ]
    return jnp.concatenate(fast, axis=1).astype(BF16), moved


def owner_backward(prior, moved, fast_grad, folds):
    cotangent, owned = [], []
    for p, m, fg in zip(*(folds_of(x, folds) for x in (prior, moved, fast_grad))):
        prior_norm, moved_norm = norm_of(p), norm_of(m)
        column_dot = jnp.sum(fg * m, axis=1, keepdims=True)
        moved_grad = (prior_norm / moved_norm) * (fg - m * (column_dot / (moved_norm * moved_norm)))
        cotangent.append(moved_grad)
        owned.append(moved_grad + p * (column_dot / (moved_norm * prior_norm)))
    return jnp.concatenate(cotangent, axis=1).astype(BF16), jnp.concatenate(owned, axis=1)


def push_of(rates, values):
    return (-rates * values.T.astype(F32)).astype(BF16)


def both(own_ref, other_ref, axis=0):
    return jnp.concatenate([own_ref[...], other_ref[...]], axis=axis)


def rows_of(ref, chip, core, chips, folds, i):
    rows = ref.shape[0] // (chips * CORES)
    height = rows // folds
    return pl.ds(pl.multiple_of((chip * CORES + core) * rows + i * height, height), height)


def cut_half(out, ref, parity, chips, folds):
    core = lax.axis_index("tok") % CORES
    height, width = ref.shape[0] // (chips * CORES * folds), ref.shape[1]
    for k in range(chips // 2):
        for i in range(folds):
            out[k * height : (k + 1) * height, i * width : (i + 1) * width] = ref[
                rows_of(ref, 2 * k + parity, core, chips, folds, i), :
            ].astype(out.dtype)


def place_half(ref, half, parity, core, chips, folds):
    height, width = ref.shape[0] // (chips * CORES * folds), ref.shape[1]
    for k in range(chips // 2):
        for i in range(folds):
            ref[rows_of(ref, 2 * k + parity, core, chips, folds, i), :] = half[
                k * height : (k + 1) * height, i * width : (i + 1) * width
            ]


def place_halves(chips, folds, halves, ref):
    tok = lax.axis_index("tok")
    parity, core = tok // CORES % 2, tok % CORES
    whose = ((parity, core), (1 - parity, core), (parity, 1 - core), (1 - parity, 1 - core))
    for half, (p, c) in zip(halves, whose):
        place_half(ref, half, p, c, chips, folds)


def rows_of_core(ref, order, chips):
    core = lax.axis_index("tok") % CORES
    rows = ref.shape[0] // (chips * CORES)
    blocks = [
        ref[pl.ds(pl.multiple_of((chip * CORES + core) * rows, rows), rows), :] for chip in order
    ]
    return jnp.concatenate(blocks, axis=0)


def fold(rows, chips, folds):
    height = rows.shape[0] // (chips * folds)
    parts = [rows[i * height : (i + 1) * height] for i in range(chips * folds)]
    wide = [jnp.concatenate(parts[k : k + folds], axis=1) for k in range(0, len(parts), folds)]
    return jnp.concatenate(wide, axis=0)


def pieces_order(chips):
    chip = lax.axis_index("tok") // CORES
    return [partner(chip, step, chips) for step in range(chips)]


def send_halves(chips, folds, operands, outs):
    gate_ref, up_ref, down_ref, tokens, hidden = operands
    parity = lax.axis_index("tok") // CORES % 2
    order = [2 * k + p for p in (parity, 1 - parity) for k in range(chips // 2)]
    sums = list(stacked(nn, *(rows_of_core(x, order, chips) for x in (gate_ref, up_ref)), tokens))
    sums.append(fold(nt(rows_of_core(down_ref, order, chips), hidden), chips, folds))
    half = outs[0].shape[0]
    for k, total in enumerate(sums):
        outs[k][...] = total[:half]
        outs[3 + k][...] = total[half:].astype(BF16)


def update_kernel(chips, folds, ko, kx, vo, vx, ro, rx, w1t, w3t, w2, *rest):
    outs, (gate, up, push) = rest[:6], rest[6:]
    keys = both(ko, kx)
    push[...] = push_of(both(ro, rx, 1), both(vo, vx))
    *_, mixed, _, _, gate[...], up[...] = update_forward(w1t[...], w3t[...], w2[...], keys, push[...])
    send_halves(chips, folds, (gate, up, push, keys, mixed), outs)


def prior_kernel(
    chips, folds, w1t, w3t, w2, go, gx, gain, weighted_ref, p1_ref, p3_ref, p2_ref, gate_ref, up_ref, down_ref
):
    weighted_ref[...] = (both(go, gx).astype(F32) * gain[...]).T
    gate_ref[...] = w1t[...].astype(F32)
    up_ref[...] = w3t[...].astype(F32)
    down_ref[...] = w2[...].astype(F32).T
    parity = lax.axis_index("tok") // CORES % 2
    cut_half(p1_ref, gate_ref, parity, chips, 1)
    cut_half(p3_ref, up_ref, parity, chips, 1)
    cut_half(p2_ref, down_ref, parity, chips, folds)


def saved_kernel(
    ko, kx, vo, vx, ro, rx, w1t, w3t, w2,
    push_ref, up_slope_ref, silu_ref, back_slope_ref, back_curve_ref,
    mixed_ref, gate_back_ref, up_back_ref,
):
    push = push_of(both(ro, rx, 1), both(vo, vx))
    push_ref[...] = push
    up_pre, silu, slope, curvature, mixed, down_back, back_slope, gate_back, up_back = (
        update_forward(w1t[...], w3t[...], w2[...], both(ko, kx), push)
    )
    up_slope_ref[...] = up_pre * slope
    silu_ref[...] = silu
    back_slope_ref[...] = back_slope
    back_curve_ref[...] = down_back * up_pre * curvature
    own = mixed_ref.shape[1]
    mixed_ref[...] = mixed[:, :own]
    gate_back_ref[...] = gate_back[:, :own]
    up_back_ref[...] = up_back[:, :own]


def carry_kernel(own, got, out):
    out[...] = (own[...] + got[...].astype(F32)).astype(BF16)


def total_of_halves(halves):
    total = halves[0][...].astype(F32)
    for half in halves[1:]:
        total = total + half[...].astype(F32)
    return total


def owner_forward_kernel(folds, prior, *refs):
    fast, moved = refs[-2:]
    total = total_of_halves(refs[:-2])
    fast[...], moved[...] = owner_forward(prior[...], total, folds)


def owner_backward_kernel(folds, prior, moved, *refs):
    cotangent, owned = refs[-2:]
    total = total_of_halves(refs[:-2])
    cotangent[...], owned[...] = owner_backward(prior[...], moved[...], total, folds)


def owner_result_kernel(chips, folds, *refs):
    owned, pieces, outs = refs[:3], refs[3:-3], refs[-3:]
    bars = pieces[0][...]
    for piece in pieces[1:]:
        bars = bars + piece[...].astype(F32)
    g = outs[0].shape[0]
    block = lax.axis_index("tok") // (2 * CORES)
    for k, out in enumerate(outs):
        result = owned[k][pl.ds(pl.multiple_of(block * g, g), g), :] - bars[k * g : (k + 1) * g]
        for i, rows in enumerate(folds_of(result, folds if k == 2 else 1)):
            out[i * g : (i + 1) * g] = rows


def apply_kernel(chips, folds, *refs):
    halves, refs = refs[:12], refs[12:]
    qo, qx, weighted, f1t, f3t, f2t, output, mixed, up_slope, silu, sums = refs
    place_halves(chips, 1, halves[:4], f1t)
    place_halves(chips, 1, halves[4:8], f3t)
    place_halves(chips, folds, halves[8:], f2t)
    output[...], mixed[...], up_slope[...], silu[...], sums[...] = apply_forward(
        f1t[...], f3t[...], f2t[...], both(qo, qx), weighted[...]
    )


def back_kernel(chips, folds, heads, *refs):
    parts, refs = refs[:heads], refs[heads + 1 :]
    sums = parts[0][...]
    for part in parts[1:]:
        sums = sums + part[...]
    f2t, output, weighted, mixed, up_slope, silu, qo, qx, gate_back, up_back = refs[:10]
    outs, (gate, up, down) = refs[10:16], refs[16:]
    width = heads * output.shape[0]
    gate[...], up[...], down[...] = apply_backward(
        f2t[...], sums, width, output[...], weighted[...], up_slope[...], silu[...]
    )
    send_halves(chips, folds, (gate, up, down, both(qo, qx), mixed[...]), outs)
    own = gate_back.shape[1]
    gate_back[...], up_back[...] = gate[:, :own], up[:, :own]


def query_kernel(gate_back, up_back, f1t, f3t, out):
    out[...] = (tn(gate_back[...], f1t[...]) + tn(up_back[...], f3t[...])).astype(BF16)


def second_first_kernel(chips, folds, *refs):
    halves, refs = refs[:8], refs[8:]
    ko, kx, push, up_slope, silu, back_slope, back_curve = refs[:7]
    c1t, c3t, dbb_ref, down, up_part, gate_part = refs[7:]
    place_halves(chips, 1, halves[:4], c1t)
    place_halves(chips, 1, halves[4:], c3t)
    dbb, up_part[...], gate_part[...] = second_by_gate_and_up(
        c1t[...], c3t[...], both(ko, kx),
        up_slope[...], silu[...], back_slope[...], back_curve[...],
    )
    down[...] = fold(nt(rows_of_core(push, pieces_order(chips), chips), dbb), chips, folds)
    dbb_ref[...] = dbb[:, : dbb_ref.shape[1]]


def second_last_kernel(chips, folds, *refs):
    halves, refs = refs[:4], refs[4:]
    ko, kx, push, up_slope, silu, up_part, gate_part, down = refs[:8]
    c2t, upb_ref, gpb_ref = refs[8:11]
    outs, (gate, up) = refs[11 : 11 + chips], refs[11 + chips :]
    place_halves(chips, folds, halves, c2t)
    up[...], gate[...] = second_by_down(
        c2t[...], push[...], up_slope[...], silu[...], up_part[...], gate_part[...]
    )
    keys, order = both(ko, kx), pieces_order(chips)
    sums = [*stacked(nn, *(rows_of_core(x, order, chips) for x in (gate, up)), keys), down[...]]
    g = sums[0].shape[0] // chips
    for k, out in enumerate(outs):
        parts = [x[k * g : (k + 1) * g] for x in sums]
        out[...] = jnp.concatenate(parts, axis=0).astype(out.dtype)
    own = upb_ref.shape[1]
    upb_ref[...], gpb_ref[...] = up[:, :own], gate[:, :own]


def token_grads(rates, mixed, dbb, upb, gpb, gate_back, up_back, c1t, c3t, c2t, w1t, w3t, w2):
    value_grad = (rates * (nn(c2t, mixed) + tn(w2, dbb))).T.astype(BF16)
    key_total = tn(gate_back, c1t) + tn(up_back, c3t) + tn(gpb, w1t) + tn(upb, w3t)
    return value_grad, (-key_total).astype(BF16)


def token_kernel(*refs):
    value_grad, key_grad = refs[-2:]
    value_grad[...], key_grad[...] = token_grads(*(r[...] for r in refs[:-2]))


def call(kernel, outs, args, scratch=(), name=None, flops=0):
    vmem = pl.BlockSpec(memory_space=pltpu.VMEM)
    return pl.pallas_call(
        kernel,
        out_shape=[jax.ShapeDtypeStruct(s, t) for s, t in outs],
        in_specs=[vmem] * len(args),
        out_specs=[vmem] * len(outs),
        scratch_shapes=[pltpu.VMEM(s, t) for s, t in scratch],
        compiler_params=pltpu.CompilerParams(vmem_limit_bytes=VMEM_LIMIT),
        cost_estimate=pl.CostEstimate(
            flops=flops,
            bytes_accessed=sum(a.size * a.dtype.itemsize for a in args),
            transcendentals=0,
        ),
        name=name,
    )(*args)


def exchange(pieces, chips):
    count = chips * CORES
    got = [lax.ppermute(pieces[s], "tok", chip_perm(count, s)) for s in reversed(range(1, chips))]
    return [pieces[0], *got]


def to_chip(x, step, chips):
    return lax.ppermute(x, "tok", chip_perm(chips * CORES, step))


def half_sums(kept, given, chips):
    (mine,) = call(carry_kernel, [(given.shape, BF16)], (kept, to_chip(given, 1, chips)), name="carry")
    return [mine, *(to_chip(mine, step, chips) for step in range(2, chips, 2))]


def from_owners(halves, chips):
    others = [to_chip(half, 1, chips) for half in halves]
    *later, others[0] = lax.optimization_barrier((*halves, others[0]))
    cross = lambda x: lax.ppermute(x, "tok", core_perm(chips * CORES))
    parts = zip(halves, others, map(cross, later), map(cross, others))
    return [x for part in parts for x in part]


def head_parts(part, heads):
    got = [
        lax.ppermute(part, "head", [(h, partner(h, step, heads)) for h in range(heads)])
        for step in range(1, heads)
    ]
    return [part, *got]


def over_chips(blocks, count):
    groups = [list(range(core, count, CORES)) for core in range(CORES)]
    return lax.all_to_all(blocks, "tok", 0, 0, axis_index_groups=groups, tiled=True)


def gather_blocks(copies, count):
    mine = over_chips(copies, count)
    return mine, lax.ppermute(mine, "tok", core_perm(count))


def sliced_pieces(gate, up, down, tok, count):
    g, d = gate.shape[0] // count, down.shape[0] // count
    rows = lambda x, size, t: lax.dynamic_slice_in_dim(x, t * size, size, 0)
    piece = lambda t: pack(rows(gate, g, t), rows(up, g, t), rows(down, d, t))
    sent = [piece(t + tok % CORES) for t in range(0, count, CORES)]
    return piece(tok), jnp.concatenate(sent, axis=0).astype(BF16)


def total_of(own, got, tok):
    blocks = got.reshape((-1,) + own.shape)
    chip = lax.broadcasted_iota(jnp.int32, (blocks.shape[0], 1, 1), 0)
    others = jnp.where(chip == tok // CORES, 0.0, blocks.astype(F32))
    return own + jnp.sum(others, axis=0)


def whole_matrices(mine, other, tok, count, fh):
    shape = (count // CORES, -1, mine.shape[1])
    pair = jnp.stack([mine.reshape(shape), other.reshape(shape)], axis=1)
    pair = jnp.where(tok % CORES == 0, pair, pair[:, ::-1])
    held = pair.reshape((count, -1, mine.shape[1]))
    parts = jax.vmap(lambda x: unpack(x, fh))(held)
    return tuple(x.reshape((-1, x.shape[-1])) for x in parts)


def packed_owner_forward(prior, update, fh):
    fast, moved = zip(*(owner_forward(p, u, 1) for p, u in zip(unpack(prior, fh), unpack(update, fh))))
    return pack(*fast), pack(*moved)


def packed_owner_backward(prior, moved, fast_grad, fh):
    parts = (unpack(x, fh) for x in (prior, moved, fast_grad))
    cotangent, owned = zip(*(owner_backward(p, m, f, 1) for p, m, f in zip(*parts)))
    return pack(*cotangent), pack(*owned)


def per_device(
    query_input,
    key_input,
    value_input,
    out_grad,
    token_rates,
    out_gain,
    gate_prior,
    up_prior,
    down_prior,
):
    count, heads = lax.axis_size("tok"), lax.axis_size("head")
    tok = lax.axis_index("tok")
    chips = count // CORES
    own, dh = key_input.shape
    n = own * CORES
    w1, w3, w2 = gate_prior[0], up_prior[0], down_prior[0]
    fh = w2.shape[0]
    g, d = fh // count, dh // count
    rates = token_rates.T
    gain = out_gain[None, :]
    inputs = query_input, key_input, value_input, out_grad, rates, gain, w1, w3, w2

    if g % ROW_TILE or d % g or dh * g != fh * d or chips & (chips - 1) or chips < 2:
        query_grad, key_grad, value_grad, *results = by_blocks(inputs, tok, count, heads)
    else:
        query_grad, key_grad, value_grad, *results = by_line(inputs, chips, heads)
    return (query_grad, key_grad, value_grad, *(r.T[None] for r in results))


def by_line(inputs, chips, heads):
    query_input, key_input, value_input, out_grad, rates, gain, w1, w3, w2 = inputs
    count = chips * CORES
    own, dh = key_input.shape
    n, fh = own * CORES, w2.shape[0]
    g, d, folds = fh // count, dh // count, dh // fh
    product = 2 * n * dh * fh

    half = (g * chips // 2, dh)
    half_shares = [(half, F32)] * 3 + [(half, BF16)] * 3
    matrices = [((fh, dh), BF16), ((fh, dh), BF16), ((dh, fh), BF16)]
    sums_scratch = [((fh, dh), F32), ((fh, dh), F32), ((dh, fh), F32)]
    operands = [((fh, n), BF16), ((fh, n), BF16), ((dh, n), BF16)]
    hidden = ((fh, n), F32)
    own_hidden = ((fh, own), BF16)
    folds_by_matrix = (1, 1, folds)

    pair = lambda x: lax.ppermute(x, "tok", core_perm(count))
    key_other, value_other, rate_other = pair(key_input), pair(value_input), pair(rates)
    w1t, w3t = w1.T, w3.T
    query_other, grad_other = pair(query_input), pair(out_grad)
    keys_values = (
        key_input, key_other, value_input, value_other, rates, rate_other, w1t, w3t, w2,
    )
    sums = call(
        functools.partial(update_kernel, chips, folds),
        half_shares,
        keys_values,
        operands,
        "update",
        6 * product,
    )
    weighted, *priors = call(
        functools.partial(prior_kernel, chips, folds),
        [((dh, n), F32)] + [(half, F32)] * 3,
        (w1t, w3t, w2, out_grad, grad_other, gain),
        sums_scratch,
        "priors",
    )
    push, up_slope, silu, back_slope, back_curve, mixed, gate_back, up_back = call(
        saved_kernel,
        [((dh, n), BF16)] + [hidden] * 4 + [own_hidden] * 3,
        keys_values,
        name="saved",
        flops=3 * product,
    )

    fast, moved = [], []
    for k in range(3):
        totals = half_sums(sums[k], sums[3 + k], chips)
        rows, rows_moved = call(
            functools.partial(owner_forward_kernel, folds_by_matrix[k]),
            [(half, BF16), (half, F32)],
            (priors[k], *totals),
            name="owner_forward",
        )
        moved.append(rows_moved)
        fast.append(rows)
    f1t, f3t, f2t, output, q_mixed, q_slope, q_silu, part = call(
        functools.partial(apply_kernel, chips, folds),
        matrices + [((dh, n), F32), ((fh, n), BF16), hidden, hidden, ((2, n), F32)],
        (*from_owners(fast, chips), query_input, query_other, weighted),
        name="apply",
        flops=3 * product,
    )
    q_gate_back, q_up_back, *sums = call(
        functools.partial(back_kernel, chips, folds, heads),
        [own_hidden] * 2 + half_shares,
        (
            *head_parts(part, heads), up_back,
            f2t, output, weighted, q_mixed, q_slope, q_silu, query_input, query_other,
        ),
        operands,
        "apply_back",
        4 * product,
    )
    (query_grad,) = call(
        query_kernel,
        [((own, dh), BF16)],
        (q_gate_back, q_up_back, f1t, f3t),
        name="query_grad",
        flops=product,
    )

    cotangent, owned = [], []
    for k in range(3):
        totals = half_sums(sums[k], sums[3 + k], chips)
        rows, rows_owned = call(
            functools.partial(owner_backward_kernel, folds_by_matrix[k]),
            [(half, BF16), (half, F32)],
            (priors[k], moved[k], *totals),
            name="owner_backward",
        )
        owned.append(rows_owned)
        cotangent.append(rows)
    arrived = from_owners(cotangent, chips)
    c1t, c3t, dbb, down_sums, up_part, gate_part = call(
        functools.partial(second_first_kernel, chips, folds),
        matrices[:2] + [own_hidden, ((g * chips, dh), F32), hidden, hidden],
        (*arrived[:8], key_input, key_other, push, up_slope, silu, back_slope, back_curve),
        name="second_first",
        flops=3 * product,
    )
    c2t, upb, gpb, *pieces = call(
        functools.partial(second_last_kernel, chips, folds),
        matrices[2:] + [own_hidden] * 2 + [((3 * g, dh), F32)] + [((3 * g, dh), BF16)] * (chips - 1),
        (
            *arrived[8:], key_input, key_other, push, up_slope, silu, up_part, gate_part, down_sums,
        ),
        operands[:2],
        "second_last",
        3 * product,
    )
    value_grad, key_grad = call(
        token_kernel,
        [((own, dh), BF16)] * 2,
        (rates, mixed, dbb, upb, gpb, gate_back, up_back, c1t, c3t, c2t, w1t, w3t, w2),
        name="token_grads",
        flops=3 * product,
    )
    results = call(
        functools.partial(owner_result_kernel, chips, folds),
        [((g, dh), F32)] * 2 + [((d, fh), F32)],
        (*owned, *exchange(pieces, chips)),
        name="owner_result",
    )
    return query_grad, key_grad, value_grad, *results


def by_blocks(inputs, tok, count, heads):
    query_input, key_input, value_input, out_grad, rates, gain, w1, w3, w2 = inputs
    own, dh = key_input.shape
    fh, chips = w2.shape[0], count // CORES
    g, d = fh // count, dh // count
    w1t, w3t = w1.T, w3.T
    pair = lambda x, axis=0: jnp.concatenate(
        [x, lax.ppermute(x, "tok", core_perm(count))], axis=axis
    )
    keys, values, queries, rate = pair(key_input), pair(value_input), pair(query_input), pair(rates, 1)
    weighted = (pair(out_grad).astype(F32) * gain).T
    push = push_of(rate, values)
    up_pre, silu, slope, curvature, mixed, down_back, back_slope, gate_back, up_back = (
        update_forward(w1t, w3t, w2, keys, push)
    )
    up_slope, back_curve = up_pre * slope, down_back * up_pre * curvature
    sums = nn(gate_back, keys), nn(up_back, keys), nt(push, mixed)
    piece, sent = sliced_pieces(*sums, tok, count)
    prior = pack(
        *(
            lax.dynamic_slice_in_dim(x, tok * rows, rows, 0).astype(F32)
            for x, rows in ((w1t, g), (w3t, g), (w2.T, d))
        )
    )
    update = total_of(piece, over_chips(sent, count), tok)
    fast, moved = packed_owner_forward(prior, update, fh)
    blocks = gather_blocks(jnp.tile(fast, (chips, 1)), count)
    f1t, f3t, f2t = whole_matrices(*blocks, tok, count, fh)
    output, q_mixed, q_slope, q_silu, part = apply_forward(f1t, f3t, f2t, queries, weighted)
    sums = lax.psum(part, "head")
    q_gate_back, q_up_back, out_back = apply_backward(
        f2t, sums, heads * dh, output, weighted, q_slope, q_silu
    )
    grads = nn(q_gate_back, queries), nn(q_up_back, queries), nt(out_back, q_mixed)
    piece, sent = sliced_pieces(*grads, tok, count)
    query_grad = (tn(q_gate_back[:, :own], f1t) + tn(q_up_back[:, :own], f3t)).astype(BF16)
    fast_grad = total_of(piece, over_chips(sent, count), tok)
    cotangent, owned = packed_owner_backward(prior, moved, fast_grad, fh)
    blocks = gather_blocks(jnp.tile(cotangent, (chips, 1)), count)
    c1t, c3t, c2t = whole_matrices(*blocks, tok, count, fh)
    dbb, *parts = second_by_gate_and_up(c1t, c3t, keys, up_slope, silu, back_slope, back_curve)
    upb, gpb = second_by_down(c2t, push, up_slope, silu, *parts)
    bars = nn(gpb, keys), nn(upb, keys), nt(push, dbb)
    piece, sent = sliced_pieces(*bars, tok, count)
    value_grad, key_grad = token_grads(
        rates, mixed[:, :own], dbb[:, :own], upb[:, :own], gpb[:, :own],
        gate_back[:, :own], up_back[:, :own], c1t, c3t, c2t, w1t, w3t, w2,
    )
    results = unpack(owned - total_of(piece, over_chips(sent, count), tok), fh)
    return query_grad, key_grad, value_grad, *results


def solution(mesh):
    tokens = P("tok", "head")
    in_specs = (tokens,) * 5 + (P("head"),) + (P("head", None, None),) * 3
    out_specs = (tokens,) * 3 + (P("head", None, "tok"),) * 3
    return jax.shard_map(
        per_device, mesh=mesh, in_specs=in_specs, out_specs=out_specs, check_vma=False
    )
```

```python
import functools

import jax
import jax.numpy as jnp
from jax import lax
from jax.experimental import pallas as pl
from jax.experimental.pallas import tpu as pltpu
from jax.sharding import PartitionSpec as P

EPSILON = 1e-06
CORES = 2
ROW_TILE = 16
VMEM_LIMIT = 24 * 1024 * 1024
BF16, F32 = jnp.bfloat16, jnp.float32


def nn(a, b):
    return lax.dot_general(a, b, (((1,), (0,)), ((), ())), preferred_element_type=F32)


def nt(a, b):
    return lax.dot_general(a, b, (((1,), (1,)), ((), ())), preferred_element_type=F32)


def tn(a, b):
    return lax.dot_general(a, b, (((0,), (0,)), ((), ())), preferred_element_type=F32)


def stacked(product, first, second, tokens):
    both_rows = product(jnp.concatenate([first, second], axis=0), tokens)
    return both_rows[: first.shape[0]], both_rows[first.shape[0] :]


def silu_parts(hidden):
    sigmoid_value = jax.nn.sigmoid(hidden)
    silu_value = hidden * sigmoid_value
    silu_slope = sigmoid_value * (1.0 + hidden * (1.0 - sigmoid_value))
    curvature = sigmoid_value * (1.0 - sigmoid_value) * (2.0 + hidden * (1.0 - 2.0 * sigmoid_value))
    return silu_value, silu_slope, curvature


def partner(index, step, count):
    return index ^ step if count & (count - 1) == 0 else (index + step) % count


def source(index, step, count):
    return index ^ step if count & (count - 1) == 0 else (index + count - step) % count


def chip_perm(count, step):
    chips = count // CORES
    return [(t, partner(t // CORES, step, chips) * CORES + t % CORES) for t in range(count)]


def core_perm(count):
    return [(t, t ^ 1) for t in range(count)]


def pack(gate, up, down):
    folds = gate.shape[1] // down.shape[1]
    rows = down.shape[0] // folds
    down = jnp.concatenate([down[i * rows : (i + 1) * rows] for i in range(folds)], axis=1)
    return jnp.concatenate([gate, up, down], axis=0)


def unpack(packed, fh):
    g = packed.shape[0] // 3
    folds = packed.shape[1] // fh
    down = packed[2 * g :]
    down = jnp.concatenate([down[:, i * fh : (i + 1) * fh] for i in range(folds)], axis=0)
    return packed[:g], packed[g : 2 * g], down


def update_forward(w1t, w3t, w2, keys, push):
    gate_pre, up_pre = stacked(nt, w1t, w3t, keys)
    silu, slope, curvature = silu_parts(gate_pre)
    mixed = (silu * up_pre).astype(BF16)
    down_back = nn(w2, push)
    back_slope = down_back * slope
    gate_back = (down_back * up_pre * slope).astype(BF16)
    up_back = (down_back * silu).astype(BF16)
    return up_pre, silu, slope, curvature, mixed, down_back, back_slope, gate_back, up_back


def apply_forward(f1t, f3t, f2t, queries, weighted):
    q_gate, q_up = nt(f1t, queries), nt(f3t, queries)
    silu, slope, _ = silu_parts(q_gate)
    mixed = (silu * q_up).astype(BF16)
    output = nn(f2t, mixed)
    square = jnp.sum(output * output, axis=0, keepdims=True)
    dot = jnp.sum(weighted * output, axis=0, keepdims=True)
    return output, mixed, q_up * slope, silu, jnp.concatenate([square, dot], axis=0)


def apply_backward(f2t, sums, full_width, output, weighted, up_slope, silu):
    inverse = lax.rsqrt(sums[0:1] / full_width + EPSILON)
    scale = inverse * inverse * inverse * sums[1:2] / full_width
    out_back = (inverse * weighted - output * scale).astype(BF16)
    q_back = tn(f2t, out_back)
    gate_back = (q_back * up_slope).astype(BF16)
    up_back = (q_back * silu).astype(BF16)
    return gate_back, up_back, out_back


def second_by_gate_and_up(c1t, c3t, keys, up_slope, silu, back_slope, back_curve):
    gate_bar, up_bar = stacked(nt, c1t, c3t, keys)
    down_back_bar = (gate_bar * up_slope + up_bar * silu).astype(BF16)
    return down_back_bar, gate_bar * back_slope, up_bar * back_slope + gate_bar * back_curve


def second_by_down(c2t, push, up_slope, silu, up_part, gate_part):
    mixed_bar = tn(c2t, push)
    return (up_part + mixed_bar * silu).astype(BF16), (gate_part + mixed_bar * up_slope).astype(BF16)


def folds_of(rows, folds):
    width = rows.shape[1] // folds
    return [rows[:, i * width : (i + 1) * width] for i in range(folds)]


def norm_of(rows):
    return jnp.sqrt(jnp.sum(rows * rows, axis=1, keepdims=True) + EPSILON)


def owner_forward(prior, update, folds):
    moved = prior - update
    fast = [
        m * (norm_of(p) / norm_of(m)) for p, m in zip(folds_of(prior, folds), folds_of(moved, folds))
    ]
    return jnp.concatenate(fast, axis=1).astype(BF16), moved


def owner_backward(prior, moved, fast_grad, folds):
    cotangent, owned = [], []
    for p, m, fg in zip(*(folds_of(x, folds) for x in (prior, moved, fast_grad))):
        prior_norm, moved_norm = norm_of(p), norm_of(m)
        column_dot = jnp.sum(fg * m, axis=1, keepdims=True)
        moved_grad = (prior_norm / moved_norm) * (fg - m * (column_dot / (moved_norm * moved_norm)))
        cotangent.append(moved_grad)
        owned.append(moved_grad + p * (column_dot / (moved_norm * prior_norm)))
    return jnp.concatenate(cotangent, axis=1).astype(BF16), jnp.concatenate(owned, axis=1)


def push_of(rates, values):
    return (-rates * values.T.astype(F32)).astype(BF16)


def both(own_ref, other_ref, axis=0):
    return jnp.concatenate([own_ref[...], other_ref[...]], axis=axis)


def rows_of(ref, chip, core, chips, folds, i):
    rows = ref.shape[0] // (chips * CORES)
    height = rows // folds
    return pl.ds(pl.multiple_of((chip * CORES + core) * rows + i * height, height), height)


def cut_half(out, ref, parity, chips, folds):
    core = lax.axis_index("tok") % CORES
    height, width = ref.shape[0] // (chips * CORES * folds), ref.shape[1]
    for k in range(chips // 2):
        for i in range(folds):
            out[k * height : (k + 1) * height, i * width : (i + 1) * width] = ref[
                rows_of(ref, 2 * k + parity, core, chips, folds, i), :
            ].astype(out.dtype)


def place_half(ref, half, parity, core, chips, folds):
    height, width = ref.shape[0] // (chips * CORES * folds), ref.shape[1]
    for k in range(chips // 2):
        for i in range(folds):
            ref[rows_of(ref, 2 * k + parity, core, chips, folds, i), :] = half[
                k * height : (k + 1) * height, i * width : (i + 1) * width
            ]


def place_halves(chips, folds, halves, ref):
    tok = lax.axis_index("tok")
    parity, core = tok // CORES % 2, tok % CORES
    whose = ((parity, core), (1 - parity, core), (parity, 1 - core), (1 - parity, 1 - core))
    for half, (p, c) in zip(halves, whose):
        place_half(ref, half, p, c, chips, folds)


def rows_of_core(ref, order, chips):
    core = lax.axis_index("tok") % CORES
    rows = ref.shape[0] // (chips * CORES)
    blocks = [
        ref[pl.ds(pl.multiple_of((chip * CORES + core) * rows, rows), rows), :] for chip in order
    ]
    return jnp.concatenate(blocks, axis=0)


def fold(rows, chips, folds):
    height = rows.shape[0] // (chips * folds)
    parts = [rows[i * height : (i + 1) * height] for i in range(chips * folds)]
    wide = [jnp.concatenate(parts[k : k + folds], axis=1) for k in range(0, len(parts), folds)]
    return jnp.concatenate(wide, axis=0)


def pieces_order(chips):
    chip = lax.axis_index("tok") // CORES
    return [partner(chip, step, chips) for step in range(chips)]


def send_halves(chips, folds, operands, outs):
    gate_ref, up_ref, down_ref, tokens, hidden = operands
    parity = lax.axis_index("tok") // CORES % 2
    order = [2 * k + p for p in (parity, 1 - parity) for k in range(chips // 2)]
    sums = list(stacked(nn, *(rows_of_core(x, order, chips) for x in (gate_ref, up_ref)), tokens))
    sums.append(fold(nt(rows_of_core(down_ref, order, chips), hidden), chips, folds))
    half = outs[0].shape[0]
    for k, total in enumerate(sums):
        outs[k][...] = total[:half]
        outs[3 + k][...] = total[half:].astype(BF16)


def update_kernel(chips, folds, ko, kx, vo, vx, ro, rx, w1t, w3t, w2, *rest):
    outs, (gate, up, push) = rest[:6], rest[6:]
    keys = both(ko, kx)
    push[...] = push_of(both(ro, rx, 1), both(vo, vx))
    *_, mixed, _, _, gate[...], up[...] = update_forward(w1t[...], w3t[...], w2[...], keys, push[...])
    send_halves(chips, folds, (gate, up, push, keys, mixed), outs)


def prior_kernel(
    chips, folds, w1t, w3t, w2, go, gx, gain, weighted_ref, p1_ref, p3_ref, p2_ref, gate_ref, up_ref, down_ref
):
    weighted_ref[...] = (both(go, gx).astype(F32) * gain[...]).T
    gate_ref[...] = w1t[...].astype(F32)
    up_ref[...] = w3t[...].astype(F32)
    down_ref[...] = w2[...].astype(F32).T
    parity = lax.axis_index("tok") // CORES % 2
    cut_half(p1_ref, gate_ref, parity, chips, 1)
    cut_half(p3_ref, up_ref, parity, chips, 1)
    cut_half(p2_ref, down_ref, parity, chips, folds)


def saved_kernel(
    ko, kx, vo, vx, ro, rx, w1t, w3t, w2,
    push_ref, up_slope_ref, silu_ref, back_slope_ref, back_curve_ref,
    mixed_ref, gate_back_ref, up_back_ref,
):
    push = push_of(both(ro, rx, 1), both(vo, vx))
    push_ref[...] = push
    up_pre, silu, slope, curvature, mixed, down_back, back_slope, gate_back, up_back = (
        update_forward(w1t[...], w3t[...], w2[...], both(ko, kx), push)
    )
    up_slope_ref[...] = up_pre * slope
    silu_ref[...] = silu
    back_slope_ref[...] = back_slope
    back_curve_ref[...] = down_back * up_pre * curvature
    own = mixed_ref.shape[1]
    mixed_ref[...] = mixed[:, :own]
    gate_back_ref[...] = gate_back[:, :own]
    up_back_ref[...] = up_back[:, :own]


def carry_kernel(own, got, out):
    out[...] = (own[...] + got[...].astype(F32)).astype(BF16)


def total_of_halves(halves):
    total = halves[0][...].astype(F32)
    for half in halves[1:]:
        total = total + half[...].astype(F32)
    return total


def owner_forward_kernel(folds, prior, *refs):
    fast, moved = refs[-2:]
    total = total_of_halves(refs[:-2])
    fast[...], moved[...] = owner_forward(prior[...], total, folds)


def owner_backward_kernel(folds, prior, moved, *refs):
    cotangent, owned = refs[-2:]
    total = total_of_halves(refs[:-2])
    cotangent[...], owned[...] = owner_backward(prior[...], moved[...], total, folds)


def owner_result_kernel(chips, folds, *refs):
    owned, pieces, outs = refs[:3], refs[3:-3], refs[-3:]
    bars = pieces[0][...]
    for piece in pieces[1:]:
        bars = bars + piece[...].astype(F32)
    g = outs[0].shape[0]
    block = lax.axis_index("tok") // (2 * CORES)
    for k, out in enumerate(outs):
        result = owned[k][pl.ds(pl.multiple_of(block * g, g), g), :] - bars[k * g : (k + 1) * g]
        for i, rows in enumerate(folds_of(result, folds if k == 2 else 1)):
            out[i * g : (i + 1) * g] = rows


def apply_kernel(chips, folds, *refs):
    halves, refs = refs[:12], refs[12:]
    qo, qx, weighted, f1t, f3t, f2t, output, mixed, up_slope, silu, sums = refs
    place_halves(chips, 1, halves[:4], f1t)
    place_halves(chips, 1, halves[4:8], f3t)
    place_halves(chips, folds, halves[8:], f2t)
    output[...], mixed[...], up_slope[...], silu[...], sums[...] = apply_forward(
        f1t[...], f3t[...], f2t[...], both(qo, qx), weighted[...]
    )


def back_kernel(chips, folds, heads, *refs):
    parts, refs = refs[:heads], refs[heads + 1 :]
    sums = parts[0][...]
    for part in parts[1:]:
        sums = sums + part[...]
    f2t, output, weighted, mixed, up_slope, silu, qo, qx, gate_back, up_back = refs[:10]
    outs, (gate, up, down) = refs[10:16], refs[16:]
    width = heads * output.shape[0]
    gate[...], up[...], down[...] = apply_backward(
        f2t[...], sums, width, output[...], weighted[...], up_slope[...], silu[...]
    )
    send_halves(chips, folds, (gate, up, down, both(qo, qx), mixed[...]), outs)
    own = gate_back.shape[1]
    gate_back[...], up_back[...] = gate[:, :own], up[:, :own]


def query_kernel(gate_back, up_back, f1t, f3t, out):
    out[...] = (tn(gate_back[...], f1t[...]) + tn(up_back[...], f3t[...])).astype(BF16)


def second_first_kernel(chips, folds, *refs):
    halves, refs = refs[:8], refs[8:]
    ko, kx, push, up_slope, silu, back_slope, back_curve = refs[:7]
    c1t, c3t, dbb_ref, down, up_part, gate_part = refs[7:]
    place_halves(chips, 1, halves[:4], c1t)
    place_halves(chips, 1, halves[4:], c3t)
    dbb, up_part[...], gate_part[...] = second_by_gate_and_up(
        c1t[...], c3t[...], both(ko, kx),
        up_slope[...], silu[...], back_slope[...], back_curve[...],
    )
    down[...] = fold(nt(rows_of_core(push, pieces_order(chips), chips), dbb), chips, folds)
    dbb_ref[...] = dbb[:, : dbb_ref.shape[1]]


def second_last_kernel(chips, folds, *refs):
    halves, refs = refs[:4], refs[4:]
    ko, kx, push, up_slope, silu, up_part, gate_part, down = refs[:8]
    c2t, upb_ref, gpb_ref = refs[8:11]
    outs, (gate, up) = refs[11 : 11 + chips], refs[11 + chips :]
    place_halves(chips, folds, halves, c2t)
    up[...], gate[...] = second_by_down(
        c2t[...], push[...], up_slope[...], silu[...], up_part[...], gate_part[...]
    )
    keys, order = both(ko, kx), pieces_order(chips)
    sums = [*stacked(nn, *(rows_of_core(x, order, chips) for x in (gate, up)), keys), down[...]]
    g = sums[0].shape[0] // chips
    for k, out in enumerate(outs):
        parts = [x[k * g : (k + 1) * g] for x in sums]
        out[...] = jnp.concatenate(parts, axis=0).astype(out.dtype)
    own = upb_ref.shape[1]
    upb_ref[...], gpb_ref[...] = up[:, :own], gate[:, :own]


def token_grads(rates, mixed, dbb, upb, gpb, gate_back, up_back, c1t, c3t, c2t, w1t, w3t, w2):
    value_grad = (rates * (nn(c2t, mixed) + tn(w2, dbb))).T.astype(BF16)
    key_total = tn(gate_back, c1t) + tn(up_back, c3t) + tn(gpb, w1t) + tn(upb, w3t)
    return value_grad, (-key_total).astype(BF16)


def token_kernel(*refs):
    value_grad, key_grad = refs[-2:]
    value_grad[...], key_grad[...] = token_grads(*(r[...] for r in refs[:-2]))


def call(kernel, outs, args, scratch=(), name=None, flops=0):
    vmem = pl.BlockSpec(memory_space=pltpu.VMEM)
    return pl.pallas_call(
        kernel,
        out_shape=[jax.ShapeDtypeStruct(s, t) for s, t in outs],
        in_specs=[vmem] * len(args),
        out_specs=[vmem] * len(outs),
        scratch_shapes=[pltpu.VMEM(s, t) for s, t in scratch],
        compiler_params=pltpu.CompilerParams(vmem_limit_bytes=VMEM_LIMIT),
        cost_estimate=pl.CostEstimate(
            flops=flops,
            bytes_accessed=sum(a.size * a.dtype.itemsize for a in args),
            transcendentals=0,
        ),
        name=name,
    )(*args)


def exchange(pieces, chips):
    count = chips * CORES
    got = [lax.ppermute(pieces[s], "tok", chip_perm(count, s)) for s in reversed(range(1, chips))]
    return [pieces[0], *got]


def to_chip(x, step, chips):
    return lax.ppermute(x, "tok", chip_perm(chips * CORES, step))


def half_sums(kept, given, chips):
    (mine,) = call(carry_kernel, [(given.shape, BF16)], (kept, to_chip(given, 1, chips)), name="carry")
    return [mine, *(to_chip(mine, step, chips) for step in range(2, chips, 2))]


def from_owners(halves, chips, first):
    others = [to_chip(half, 1, chips) for half in halves]
    *later, others[first] = lax.optimization_barrier((*halves, others[first]))
    cross = lambda x: lax.ppermute(x, "tok", core_perm(chips * CORES))
    parts = zip(halves, others, map(cross, later), map(cross, others))
    return [x for part in parts for x in part]


def head_parts(part, heads):
    got = [
        lax.ppermute(part, "head", [(h, partner(h, step, heads)) for h in range(heads)])
        for step in range(1, heads)
    ]
    return [part, *got]


def over_chips(blocks, count):
    groups = [list(range(core, count, CORES)) for core in range(CORES)]
    return lax.all_to_all(blocks, "tok", 0, 0, axis_index_groups=groups, tiled=True)


def gather_blocks(copies, count):
    mine = over_chips(copies, count)
    return mine, lax.ppermute(mine, "tok", core_perm(count))


def sliced_pieces(gate, up, down, tok, count):
    g, d = gate.shape[0] // count, down.shape[0] // count
    rows = lambda x, size, t: lax.dynamic_slice_in_dim(x, t * size, size, 0)
    piece = lambda t: pack(rows(gate, g, t), rows(up, g, t), rows(down, d, t))
    sent = [piece(t + tok % CORES) for t in range(0, count, CORES)]
    return piece(tok), jnp.concatenate(sent, axis=0).astype(BF16)


def total_of(own, got, tok):
    blocks = got.reshape((-1,) + own.shape)
    chip = lax.broadcasted_iota(jnp.int32, (blocks.shape[0], 1, 1), 0)
    others = jnp.where(chip == tok // CORES, 0.0, blocks.astype(F32))
    return own + jnp.sum(others, axis=0)


def whole_matrices(mine, other, tok, count, fh):
    shape = (count // CORES, -1, mine.shape[1])
    pair = jnp.stack([mine.reshape(shape), other.reshape(shape)], axis=1)
    pair = jnp.where(tok % CORES == 0, pair, pair[:, ::-1])
    held = pair.reshape((count, -1, mine.shape[1]))
    parts = jax.vmap(lambda x: unpack(x, fh))(held)
    return tuple(x.reshape((-1, x.shape[-1])) for x in parts)


def packed_owner_forward(prior, update, fh):
    fast, moved = zip(*(owner_forward(p, u, 1) for p, u in zip(unpack(prior, fh), unpack(update, fh))))
    return pack(*fast), pack(*moved)


def packed_owner_backward(prior, moved, fast_grad, fh):
    parts = (unpack(x, fh) for x in (prior, moved, fast_grad))
    cotangent, owned = zip(*(owner_backward(p, m, f, 1) for p, m, f in zip(*parts)))
    return pack(*cotangent), pack(*owned)


def per_device(
    query_input,
    key_input,
    value_input,
    out_grad,
    token_rates,
    out_gain,
    gate_prior,
    up_prior,
    down_prior,
):
    count, heads = lax.axis_size("tok"), lax.axis_size("head")
    tok = lax.axis_index("tok")
    chips = count // CORES
    own, dh = key_input.shape
    n = own * CORES
    w1, w3, w2 = gate_prior[0], up_prior[0], down_prior[0]
    fh = w2.shape[0]
    g, d = fh // count, dh // count
    rates = token_rates.T
    gain = out_gain[None, :]
    inputs = query_input, key_input, value_input, out_grad, rates, gain, w1, w3, w2

    if g % ROW_TILE or d % g or dh * g != fh * d or chips & (chips - 1) or chips < 2:
        query_grad, key_grad, value_grad, *results = by_blocks(inputs, tok, count, heads)
    else:
        query_grad, key_grad, value_grad, *results = by_line(inputs, chips, heads)
    return (query_grad, key_grad, value_grad, *(r.T[None] for r in results))


def by_line(inputs, chips, heads):
    query_input, key_input, value_input, out_grad, rates, gain, w1, w3, w2 = inputs
    count = chips * CORES
    own, dh = key_input.shape
    n, fh = own * CORES, w2.shape[0]
    g, d, folds = fh // count, dh // count, dh // fh
    product = 2 * n * dh * fh

    half = (g * chips // 2, dh)
    half_shares = [(half, F32)] * 3 + [(half, BF16)] * 3
    matrices = [((fh, dh), BF16), ((fh, dh), BF16), ((dh, fh), BF16)]
    sums_scratch = [((fh, dh), F32), ((fh, dh), F32), ((dh, fh), F32)]
    operands = [((fh, n), BF16), ((fh, n), BF16), ((dh, n), BF16)]
    hidden = ((fh, n), F32)
    own_hidden = ((fh, own), BF16)
    folds_by_matrix = (1, 1, folds)

    pair = lambda x: lax.ppermute(x, "tok", core_perm(count))
    key_other, value_other, rate_other = pair(key_input), pair(value_input), pair(rates)
    w1t, w3t = w1.T, w3.T
    grad_other = pair(out_grad)
    keys_values = (
        key_input, key_other, value_input, value_other, rates, rate_other, w1t, w3t, w2,
    )
    sums = call(
        functools.partial(update_kernel, chips, folds),
        half_shares,
        keys_values,
        operands,
        "update",
        6 * product,
    )
    weighted, *priors = call(
        functools.partial(prior_kernel, chips, folds),
        [((dh, n), F32)] + [(half, F32)] * 3,
        (w1t, w3t, w2, out_grad, grad_other, gain),
        sums_scratch,
        "priors",
    )
    push, up_slope, silu, back_slope, back_curve, mixed, gate_back, up_back = call(
        saved_kernel,
        [((dh, n), BF16)] + [hidden] * 4 + [own_hidden] * 3,
        keys_values,
        name="saved",
        flops=3 * product,
    )

    fast, moved = [], []
    for k in range(3):
        totals = half_sums(sums[k], sums[3 + k], chips)
        rows, rows_moved = call(
            functools.partial(owner_forward_kernel, folds_by_matrix[k]),
            [(half, BF16), (half, F32)],
            (priors[k], *totals),
            name="owner_forward",
        )
        moved.append(rows_moved)
        fast.append(rows)
    query_later, weighted = lax.optimization_barrier((query_input, weighted))
    query_other = pair(query_later)
    f1t, f3t, f2t, output, q_mixed, q_slope, q_silu, part = call(
        functools.partial(apply_kernel, chips, folds),
        matrices + [((dh, n), F32), ((fh, n), BF16), hidden, hidden, ((2, n), F32)],
        (*from_owners(fast, chips, 2), query_input, query_other, weighted),
        name="apply",
        flops=3 * product,
    )
    q_gate_back, q_up_back, *sums = call(
        functools.partial(back_kernel, chips, folds, heads),
        [own_hidden] * 2 + half_shares,
        (
            *head_parts(part, heads), up_back,
            f2t, output, weighted, q_mixed, q_slope, q_silu, query_input, query_other,
        ),
        operands,
        "apply_back",
        4 * product,
    )
    (query_grad,) = call(
        query_kernel,
        [((own, dh), BF16)],
        (q_gate_back, q_up_back, f1t, f3t),
        name="query_grad",
        flops=product,
    )

    cotangent, owned = [], []
    for k in range(3):
        totals = half_sums(sums[k], sums[3 + k], chips)
        rows, rows_owned = call(
            functools.partial(owner_backward_kernel, folds_by_matrix[k]),
            [(half, BF16), (half, F32)],
            (priors[k], moved[k], *totals),
            name="owner_backward",
        )
        owned.append(rows_owned)
        cotangent.append(rows)
    arrived = from_owners(cotangent, chips, 0)
    c1t, c3t, dbb, down_sums, up_part, gate_part = call(
        functools.partial(second_first_kernel, chips, folds),
        matrices[:2] + [own_hidden, ((g * chips, dh), F32), hidden, hidden],
        (*arrived[:8], key_input, key_other, push, up_slope, silu, back_slope, back_curve),
        name="second_first",
        flops=3 * product,
    )
    c2t, upb, gpb, *pieces = call(
        functools.partial(second_last_kernel, chips, folds),
        matrices[2:] + [own_hidden] * 2 + [((3 * g, dh), F32)] + [((3 * g, dh), BF16)] * (chips - 1),
        (
            *arrived[8:], key_input, key_other, push, up_slope, silu, up_part, gate_part, down_sums,
        ),
        operands[:2],
        "second_last",
        3 * product,
    )
    value_grad, key_grad = call(
        token_kernel,
        [((own, dh), BF16)] * 2,
        (rates, mixed, dbb, upb, gpb, gate_back, up_back, c1t, c3t, c2t, w1t, w3t, w2),
        name="token_grads",
        flops=3 * product,
    )
    results = call(
        functools.partial(owner_result_kernel, chips, folds),
        [((g, dh), F32)] * 2 + [((d, fh), F32)],
        (*owned, *exchange(pieces, chips)),
        name="owner_result",
    )
    return query_grad, key_grad, value_grad, *results


def by_blocks(inputs, tok, count, heads):
    query_input, key_input, value_input, out_grad, rates, gain, w1, w3, w2 = inputs
    own, dh = key_input.shape
    fh, chips = w2.shape[0], count // CORES
    g, d = fh // count, dh // count
    w1t, w3t = w1.T, w3.T
    pair = lambda x, axis=0: jnp.concatenate(
        [x, lax.ppermute(x, "tok", core_perm(count))], axis=axis
    )
    keys, values, queries, rate = pair(key_input), pair(value_input), pair(query_input), pair(rates, 1)
    weighted = (pair(out_grad).astype(F32) * gain).T
    push = push_of(rate, values)
    up_pre, silu, slope, curvature, mixed, down_back, back_slope, gate_back, up_back = (
        update_forward(w1t, w3t, w2, keys, push)
    )
    up_slope, back_curve = up_pre * slope, down_back * up_pre * curvature
    sums = nn(gate_back, keys), nn(up_back, keys), nt(push, mixed)
    piece, sent = sliced_pieces(*sums, tok, count)
    prior = pack(
        *(
            lax.dynamic_slice_in_dim(x, tok * rows, rows, 0).astype(F32)
            for x, rows in ((w1t, g), (w3t, g), (w2.T, d))
        )
    )
    update = total_of(piece, over_chips(sent, count), tok)
    fast, moved = packed_owner_forward(prior, update, fh)
    blocks = gather_blocks(jnp.tile(fast, (chips, 1)), count)
    f1t, f3t, f2t = whole_matrices(*blocks, tok, count, fh)
    output, q_mixed, q_slope, q_silu, part = apply_forward(f1t, f3t, f2t, queries, weighted)
    sums = lax.psum(part, "head")
    q_gate_back, q_up_back, out_back = apply_backward(
        f2t, sums, heads * dh, output, weighted, q_slope, q_silu
    )
    grads = nn(q_gate_back, queries), nn(q_up_back, queries), nt(out_back, q_mixed)
    piece, sent = sliced_pieces(*grads, tok, count)
    query_grad = (tn(q_gate_back[:, :own], f1t) + tn(q_up_back[:, :own], f3t)).astype(BF16)
    fast_grad = total_of(piece, over_chips(sent, count), tok)
    cotangent, owned = packed_owner_backward(prior, moved, fast_grad, fh)
    blocks = gather_blocks(jnp.tile(cotangent, (chips, 1)), count)
    c1t, c3t, c2t = whole_matrices(*blocks, tok, count, fh)
    dbb, *parts = second_by_gate_and_up(c1t, c3t, keys, up_slope, silu, back_slope, back_curve)
    upb, gpb = second_by_down(c2t, push, up_slope, silu, *parts)
    bars = nn(gpb, keys), nn(upb, keys), nt(push, dbb)
    piece, sent = sliced_pieces(*bars, tok, count)
    value_grad, key_grad = token_grads(
        rates, mixed[:, :own], dbb[:, :own], upb[:, :own], gpb[:, :own],
        gate_back[:, :own], up_back[:, :own], c1t, c3t, c2t, w1t, w3t, w2,
    )
    results = unpack(owned - total_of(piece, over_chips(sent, count), tok), fh)
    return query_grad, key_grad, value_grad, *results


def solution(mesh):
    tokens = P("tok", "head")
    in_specs = (tokens,) * 5 + (P("head"),) + (P("head", None, None),) * 3
    out_specs = (tokens,) * 3 + (P("head", None, "tok"),) * 3
    return jax.shard_map(
        per_device, mesh=mesh, in_specs=in_specs, out_specs=out_specs, check_vma=False
    )
```
